32 devices in a mesh: items: 8 (over y, x, core), band: 4 (over z).
Axes of the slice: x: 2, y: 2, z: 4, core: 2. Of those that a mesh axis runs over, the one named last changes fastest.
Arguments:
- tokens: bfloat16 [16, 1024, 1024], P('items', 'band'), may hold values from -17 to 17
- cotangent: bfloat16 [16, 1024, 1024], P('items', 'band'), may hold values from -6 to 6
- running_mean: float32 [1024], replicated, may hold values from -3 to 3
- running_var: float32 [1024], replicated, may hold values from 0.5 to 4
- slot_table: int32 [16], replicated, may hold values from 0 to 15, as said below
- patch_counts: int32 [16], replicated, may hold values from 128 to 1024, as said below
- ln1_gain: bfloat16 [1024], replicated, may hold values from 0.5 to 1.5
- ln1_bias: bfloat16 [1024], replicated, may hold values from -1.75 to 1.75
- w_query: bfloat16 [1024, 1024], replicated, may hold values from -0.1875 to 0.1875
- b_query: bfloat16 [1024], replicated, may hold values from -1.75 to 1.75
- w_key: bfloat16 [1024, 1024], replicated, may hold values from -0.1875 to 0.1875
- w_value: bfloat16 [1024, 1024], replicated, may hold values from -0.1875 to 0.1875
- b_value: bfloat16 [1024], replicated, may hold values from -1.75 to 1.75
- w_out: bfloat16 [1024, 1024], replicated, may hold values from -0.75 to 0.75
- b_out: bfloat16 [1024], replicated, may hold values from -1.75 to 1.75
- ln2_gain: bfloat16 [1024], replicated, may hold values from 0.5 to 1.5
- ln2_bias: bfloat16 [1024], replicated, may hold values from -1.75 to 1.75
- w_up: bfloat16 [1024, 4096], replicated, may hold values from -0.1875 to 0.1875
- b_up: bfloat16 [4096], replicated, may hold values from -1.75 to 1.75
- w_down: bfloat16 [4096, 1024], replicated, may hold values from -0.09375 to 0.09375
- b_down: bfloat16 [1024], replicated, may hold values from -1.75 to 1.75
Outputs:
- output: bfloat16 [16, 1024, 1024], P('items', 'band')
- d_tokens: bfloat16 [16, 1024, 1024], P('items', 'band')
- new_mean: float32 [1024], replicated
- new_var: float32 [1024], replicated
- d_ln1_gain: float32 [1024], replicated
- d_ln1_bias: float32 [1024], replicated
- d_w_query: float32 [1024, 1024], P('items', 'band')
- d_b_query: float32 [1024], replicated
- d_w_key: float32 [1024, 1024], P('items', 'band')
- d_w_value: float32 [1024, 1024], P('items', 'band')
- d_b_value: float32 [1024], replicated
- d_w_out: float32 [1024, 1024], P('items', 'band')
- d_b_out: float32 [1024], replicated
- d_ln2_gain: float32 [1024], replicated
- d_ln2_bias: float32 [1024], replicated
- d_w_up: float32 [1024, 4096], P('items', 'band')
- d_b_up: float32 [4096], replicated
- d_w_down: float32 [4096, 1024], P('items', 'band')
- d_b_down: float32 [1024], replicated
The draws below stay inside these ranges and needn't reach their ends.
Inputs may be any that keep to these rules, and one draw needn't show every extreme that they name: `slot_table`: a permutation: each group of 2 slots 2g, 2g + 1 holds one item of 1024 patches and one shorter item. `patch_counts`: the items named in the first half of the ids have 1024 patches.
All inputs are finite; a program needn't handle non-finite values.
Results may differ from the reference program's by a relative error of at most 0.024.
Values may be sent and summed in bfloat16 or wider, within the bound.
A program may use at most 320 MiB of HBM per device.

```python
import math
import jax
import jax.numpy as jnp
from jax import lax

D = 1024
HEADS = 16
HEAD_DIM = 64
FF = 4096
SLOTS = 2
LMAX = 1024
ITEMS = 16


def layout_draw(key):
    groups = ITEMS // SLOTS
    key_long, key_short, key_flip, key_len = jax.random.split(key, 4)
    long_ids = jax.random.permutation(key_long, groups).astype(jnp.int32)
    short_ids = (groups + jax.random.permutation(key_short, groups)).astype(jnp.int32)
    flipped = jax.random.randint(key_flip, (groups,), 0, 2)
    first_slot = jnp.where(flipped == 1, short_ids, long_ids)
    second_slot = jnp.where(flipped == 1, long_ids, short_ids)
    slot_table = jnp.stack([first_slot, second_slot], 1).reshape(ITEMS).astype(jnp.int32)
    short_lengths = jax.random.randint(key_len, (groups,), LMAX // 8, LMAX // 2 + 1).astype(jnp.int32)
    patch_counts = jnp.concatenate([jnp.full((groups,), LMAX, jnp.int32), short_lengths])
    return (slot_table, patch_counts)


def draw_slot_table(key, part):
    return layout_draw(key)[0]


def draw_patch_counts(key, part):
    return layout_draw(key)[1]


def draw_tokens(key, part):
    key = jax.random.fold_in(key, 11)
    key_base, key_scale, key_shift = jax.random.split(key, 3)
    base_draw = jnp.clip(jax.random.normal(key_base, (ITEMS, LMAX, D), jnp.float32), -5.0, 5.0)
    spread = 3.0
    shift_scale = 0.5
    scales = jnp.exp(jax.random.uniform(key_scale, (ITEMS, 1, 1), jnp.float32) * math.log(spread))
    shift_draw = jnp.clip(jax.random.normal(key_shift, (1, 1, D), jnp.float32), -3.0, 3.0) * shift_scale
    return (base_draw * scales + shift_draw).astype(jnp.bfloat16)


def level_of(own_key, extent, pieces, low, top_value):
    def one(dim, shards_of):
        heights = jax.random.uniform(jax.random.fold_in(jax.random.fold_in(own_key, 6), dim), (shards_of,), jnp.float32, low / len(pieces), top_value / len(pieces))
        return jnp.repeat(jnp.exp(heights), extent[dim] // shards_of).reshape((-1,) + (1,) * (len(extent) - dim - 1))

    level = one(*pieces[0])
    for cut in pieces[1:]:
        level = level * one(*cut)
    return level


def scatter_about(own_key, dims, width, most, cuts=(), kind=jnp.bfloat16):
    entries = jax.random.normal(own_key, dims, jnp.float32) * width
    if len(cuts) > 0:
        entries = level_of(own_key, dims, cuts, -0.22, 0.18) * entries
    return jnp.clip(entries, min=-most, max=most).astype(kind)


def setup_inputs(seed: int = 0) -> dict:
    key_list = jax.random.split(jax.random.key(seed), 22)
    return {
        "tokens": draw_tokens(jax.random.fold_in(key_list[21], 71), 0),
        "cotangent": scatter_about(key_list[1], (ITEMS, LMAX, D), 1.0, 6.0, ((0, 8), (1, 4))),
        "running_mean": scatter_about(key_list[2], (D,), 0.5, 3.0, (), jnp.float32),
        "running_var": jnp.clip(jnp.exp(jax.random.uniform(key_list[3], (D,), jnp.float32, math.log(0.5), math.log(4.0))), 0.5, 4.0),
        "slot_table": draw_slot_table(jax.random.fold_in(key_list[21], 71), 0),
        "patch_counts": draw_patch_counts(jax.random.fold_in(key_list[21], 71), 0),
        "ln1_gain": jnp.clip(1.0 + 0.1 * jax.random.normal(key_list[6], (D,), jnp.float32), 0.5, 1.5).astype(jnp.bfloat16),
        "ln1_bias": scatter_about(key_list[7], (D,), 0.3, 1.75),
        "w_query": scatter_about(key_list[8], (D, D), D ** -0.5, 0.1875),
        "b_query": scatter_about(key_list[9], (D,), 0.3, 1.75),
        "w_key": scatter_about(key_list[10], (D, D), D ** -0.5, 0.1875),
        "w_value": scatter_about(key_list[11], (D, D), D ** -0.5, 0.1875),
        "b_value": scatter_about(key_list[12], (D,), 0.3, 1.75),
        "w_out": scatter_about(key_list[13], (D, D), (D // 16) ** -0.5, 0.75),
        "b_out": scatter_about(key_list[14], (D,), 0.3, 1.75),
        "ln2_gain": jnp.clip(1.0 + 0.1 * jax.random.normal(key_list[15], (D,), jnp.float32), 0.5, 1.5).astype(jnp.bfloat16),
        "ln2_bias": scatter_about(key_list[16], (D,), 0.3, 1.75),
        "w_up": scatter_about(key_list[17], (D, FF), D ** -0.5, 0.1875),
        "b_up": scatter_about(key_list[18], (FF,), 0.3, 1.75),
        "w_down": scatter_about(key_list[19], (FF, D), FF ** -0.5, 0.09375),
        "b_down": scatter_about(key_list[20], (D,), 0.3, 1.75),
    }


epsilon = 1e-05
score_scale = 0.125
masked_score = -1e+30
momentum = 0.5

@jax.custom_vjp
def low(v):
    return lax.optimization_barrier(v.astype(jnp.bfloat16)).astype(jnp.float32)

@jax.custom_vjp
def low_back(v):
    return v

def low_keep(v):
    return (low(v), None)

def low_pass(kept, grad):
    return (grad,)

def back_keep(v):
    return (v, None)

def back_low(kept, grad):
    return (low(grad),)
low.defvjp(low_keep, low_pass)
low_back.defvjp(back_keep, back_low)

def round_both(value):
    return low_back(low(value))

def matmul_high(left, right):
    return jnp.dot(left, right, precision=lax.Precision.HIGHEST, preferred_element_type=jnp.float32)

def layer_norm(value, gain, shift):
    centre = value - lax.optimization_barrier(jnp.mean(value, -1, keepdims=True))
    spread = lax.optimization_barrier(jnp.mean(centre * centre, -1, keepdims=True))
    return centre * lax.rsqrt(spread + epsilon) * gain + shift

def gelu_tanh(value):
    return 0.5 * value * (1.0 + jnp.tanh(0.7978845608028654 * (value + 0.044715 * value * value * value)))

def reference(tokens, cotangent, running_mean, running_var, slot_table, patch_counts, ln1_gain, ln1_bias, w_query, b_query, w_key, w_value, b_value, w_out, b_out, ln2_gain, ln2_bias, w_up, b_up, w_down, b_down):
    seq_length = tokens.shape[1]
    model_width = tokens.shape[2]
    lengths = patch_counts[slot_table]
    valid = (jnp.arange(seq_length, dtype=jnp.int32)[None, :] < lengths[:, None]).astype(jnp.float32)
    mean_run = running_mean.astype(jnp.float32)
    var_run = running_var.astype(jnp.float32)
    weights = tuple((w.astype(jnp.float32) for w in (ln1_gain, ln1_bias, w_query, b_query, w_key, w_value, b_value, w_out, b_out, ln2_gain, ln2_bias, w_up, b_up, w_down, b_down)))

    def forward(raw_tokens, gain_one, shift_one, wq_f, bq_f, wk_f, wv_f, bv_f, wo_f, bo_f, gain_two, shift_two, wu_f, bu_f, wd_f, bd_f):
        patch_total = jnp.sum(valid)
        batch_mean = lax.optimization_barrier(jnp.sum(valid[:, :, None] * raw_tokens, (0, 1))) / patch_total
        batch_var = lax.optimization_barrier(jnp.sum(valid[:, :, None] * raw_tokens * raw_tokens, (0, 1))) / patch_total - batch_mean * batch_mean
        new_mean = momentum * mean_run + momentum * batch_mean
        new_var = momentum * var_run + momentum * batch_var
        inverse = lax.rsqrt(new_var + epsilon)
        normed_in = (raw_tokens - new_mean) * inverse

        def item_step(inputs):
            item_start, item_valid = inputs
            h_one = low(layer_norm(item_start, gain_one, shift_one))
            queries = round_both(matmul_high(h_one, wq_f) + bq_f).reshape(seq_length, HEADS, HEAD_DIM)
            keys_all = round_both(matmul_high(h_one, wk_f)).reshape(seq_length, HEADS, HEAD_DIM)
            values_all = round_both(matmul_high(h_one, wv_f) + bv_f).reshape(seq_length, HEADS, HEAD_DIM)
            scores = low_back(jnp.einsum('qhd,khd->hqk', queries, keys_all, precision=lax.Precision.HIGHEST) * score_scale)
            scores = jnp.where(item_valid[None, None, :] > 0, scores, masked_score)
            top_score = lax.optimization_barrier(jnp.max(scores, -1, keepdims=True))
            log_total = top_score + jnp.log(lax.optimization_barrier(jnp.sum(jnp.exp(scores - top_score), -1, keepdims=True)))
            probs = low(jnp.exp(scores - log_total))
            attn = round_both(jnp.einsum('hqk,khd->qhd', probs, values_all, precision=lax.Precision.HIGHEST).reshape(seq_length, model_width))
            residual = item_start + low_back(matmul_high(attn, wo_f) + bo_f)
            h_two = low(layer_norm(residual, gain_two, shift_two))
            up_proj = low_back(matmul_high(h_two, wu_f) + bu_f)
            activated = low(gelu_tanh(up_proj))
            return residual + matmul_high(activated, wd_f) + bd_f
        result = lax.map(jax.checkpoint(item_step), (normed_in, valid))
        return (result, (new_mean, new_var))
    result, pull, stats = jax.vjp(forward, tokens.astype(jnp.float32), *weights, has_aux=True)
    grads = pull(cotangent.astype(jnp.float32))
    return (result.astype(jnp.bfloat16), grads[0].astype(jnp.bfloat16), stats[0], stats[1], grads[1], grads[2], grads[3], grads[4], grads[5], grads[6], grads[7], grads[8], grads[9], grads[10], grads[11], grads[12], grads[13], grads[14], grads[15])
```

```python
import functools
import jax
import jax.numpy as jnp
from jax import lax
from jax.experimental import pallas as pl
from jax.experimental.pallas import tpu as pltpu
from jax.sharding import PartitionSpec as P

HEADS = 16
HEAD_DIM = 64
epsilon = 1e-05
score_scale = 0.125
masked_score = -1e30
momentum = 0.5
f32 = jnp.float32
bf16 = jnp.bfloat16
VMEM_LIMIT = 60 * 2**20


def dot(a, b, ca=1, cb=0):
    return lax.dot_general(a, b, (((ca,), (cb,)), ((), ())), preferred_element_type=f32)


def params(**kw):
    return pltpu.CompilerParams(vmem_limit_bytes=VMEM_LIMIT, **kw)


def project_kernel(core, tok, mean, inv, gain, shift, wq, wk, wv, bq, bv, h1, q, k, v):
    start = (tok[...].astype(f32) - mean[...]) * inv[...]
    centre = start - jnp.mean(start, -1, keepdims=True)
    spread = jnp.mean(centre * centre, -1, keepdims=True)
    h = (centre * lax.rsqrt(spread + epsilon) * gain[...] + shift[...]).astype(bf16)
    h1[...] = h
    q[...] = ((dot(h, wq[...]) + bq[...]).astype(bf16) * score_scale).astype(bf16)
    k[...] = dot(h, wk[...]).astype(bf16)
    v[...] = (dot(h, wv[...]) + bv[...]).astype(bf16)


def project(core, tok, mean, inv, gain, shift, wq, wk, wv, bq, bv, block=256):
    rows, width = tok.shape
    half = width // 2
    row = lambda i, c: (i, 0)
    one = lambda i, c: (0, 0)
    mine = lambda i, c: (0, c[0])
    vec = pl.BlockSpec((1, width), one)
    w = pl.BlockSpec((width, half), mine)
    bias = pl.BlockSpec((1, half), mine)
    return pl.pallas_call(
        project_kernel,
        name="project",
        grid_spec=pltpu.PrefetchScalarGridSpec(
            num_scalar_prefetch=1,
            grid=(rows // block,),
            in_specs=[pl.BlockSpec((block, width), row), vec, vec, vec, vec, w, w, w, bias, bias],
            out_specs=[pl.BlockSpec((block, width), row)] + [pl.BlockSpec((block, half), row)] * 3,
        ),
        out_shape=[jax.ShapeDtypeStruct((rows, width), bf16)]
        + [jax.ShapeDtypeStruct((rows, half), bf16)] * 3,
        compiler_params=params(),
        cost_estimate=pl.CostEstimate(
            flops=2 * rows * width * 3 * half, bytes_accessed=12 * 2**20, transcendentals=0
        ),
    )(core, tok, mean, inv, gain, shift, wq, wk, wv, bq, bv)


def head_lanes(array, head, lane):
    keep = (lane >= head * HEAD_DIM) & (lane < (head + 1) * HEAD_DIM)
    return jnp.where(keep, array, jnp.zeros_like(array))


def scores_keys(k_pair, bias, head, lane):
    spare = (1 - head) * HEAD_DIM
    return jnp.where(lane == spare, bias, head_lanes(k_pair, head, lane))


def scores_queries(q_pair, head, lane):
    spare = (1 - head) * HEAD_DIM
    return jnp.where(lane == spare, jnp.ones_like(q_pair), head_lanes(q_pair, head, lane))


def attend_kernel(qt, q, k, v, bias, out, log_total):
    rows, lanes = q.shape
    lane_k = lax.broadcasted_iota(jnp.int32, (rows, lanes), 1)
    lane_q = lax.broadcasted_iota(jnp.int32, (qt, lanes), 1)
    row_out = lax.broadcasted_iota(jnp.int32, (lanes, qt), 0)
    keys = [scores_keys(k[...], bias[...], hd, lane_k) for hd in range(2)]
    values = [scores_queries(v[...], hd, lane_k).T for hd in range(2)]
    for t in range(rows // qt):
        at = slice(t * qt, (t + 1) * qt)
        scores = [dot(keys[hd], scores_queries(q[at, :], hd, lane_q), 1, 1) for hd in range(2)]
        tops = [jnp.max(s, 0, keepdims=True) for s in scores]
        weights = [jnp.exp(s - top).astype(bf16) for s, top in zip(scores, tops)]
        parts = []
        for hd in range(2):
            part = dot(values[hd], weights[hd])
            spare = (1 - hd) * HEAD_DIM
            total = part[spare : spare + 1, :]
            log_total[0, hd : hd + 1, at] = tops[hd] + jnp.log(total)
            parts.append(part * (1.0 / total))
        out[at, :] = jnp.where(row_out < HEAD_DIM, parts[0], parts[1]).T.astype(bf16)


def attend(q, k, v, bias, qt=512):
    rows, width = q.shape
    pairs = width // 128
    blk = pl.BlockSpec((rows, 128), lambda i: (0, i))
    return pl.pallas_call(
        functools.partial(attend_kernel, qt),
        name="attend",
        grid=(pairs,),
        in_specs=[blk, blk, blk, pl.BlockSpec((rows, 128), lambda i: (0, 0))],
        out_specs=[blk, pl.BlockSpec((1, 2, rows), lambda i: (i, 0, 0))],
        out_shape=[
            jax.ShapeDtypeStruct((rows, width), bf16),
            jax.ShapeDtypeStruct((pairs, 2, rows), f32),
        ],
        compiler_params=params(),
        cost_estimate=pl.CostEstimate(
            flops=16 * rows * rows * width, bytes_accessed=5 * 2**20, transcendentals=0
        ),
    )(q, k, v, bias)


def attend_back_kernel(qt, q, k, v, bias, d_attn, log_total, dq, dk, dv, dk_acc, dv_acc):
    rows, lanes = q.shape
    lane_k = lax.broadcasted_iota(jnp.int32, (rows, lanes), 1)
    lane_q = lax.broadcasted_iota(jnp.int32, (qt, lanes), 1)
    keys = [scores_keys(k[...], bias[...], hd, lane_k) for hd in range(2)]
    keys_only = [head_lanes(k[...], hd, lane_k) for hd in range(2)]
    values = [head_lanes(v[...], hd, lane_k) for hd in range(2)]
    for t in range(rows // qt):
        at = slice(t * qt, (t + 1) * qt)
        q_tile = q[at, :]
        d_tile = d_attn[at, :]
        dq_both = None
        for hd in range(2):
            q_head = head_lanes(q_tile, hd, lane_q)
            d_head = head_lanes(d_tile, hd, lane_q)
            s = dot(keys[hd], scores_queries(q_tile, hd, lane_q), 1, 1)
            p = jnp.exp(s - log_total[0, hd : hd + 1, at])
            d_p = dot(values[hd], d_tile, 1, 1)
            weighted = p * d_p
            delta = jnp.sum(weighted, 0, keepdims=True)
            ds = (weighted - p * delta).astype(bf16)
            dv_part = dot(p.astype(bf16), d_head)
            dk_part = dot(ds, q_head)
            if t == 0 and hd == 0:
                dv_acc[...] = dv_part
                dk_acc[...] = dk_part
            else:
                dv_acc[...] += dv_part
                dk_acc[...] += dk_part
            part = dot(keys_only[hd], ds, 0, 0)
            dq_both = part if dq_both is None else dq_both + part
        dq[at, :] = (dq_both.T * score_scale).astype(bf16)
    dk[...] = dk_acc[...].astype(bf16)
    dv[...] = dv_acc[...].astype(bf16)


def attend_back(q, k, v, bias, d_attn, log_total, qt=512):
    rows, width = q.shape
    pairs = width // 128
    blk = pl.BlockSpec((rows, 128), lambda i: (0, i))
    return pl.pallas_call(
        functools.partial(attend_back_kernel, qt),
        name="attend_back",
        grid=(pairs,),
        in_specs=[
            blk,
            blk,
            blk,
            pl.BlockSpec((rows, 128), lambda i: (0, 0)),
            blk,
            pl.BlockSpec((1, 2, rows), lambda i: (i, 0, 0)),
        ],
        out_specs=[blk] * 3,
        out_shape=[jax.ShapeDtypeStruct((rows, width), bf16)] * 3,
        scratch_shapes=[pltpu.VMEM((rows, 128), f32)] * 2,
        compiler_params=params(),
        cost_estimate=pl.CostEstimate(
            flops=40 * rows * rows * width, bytes_accessed=8 * 2**20, transcendentals=0
        ),
    )(q, k, v, bias, d_attn, log_total)


def gelu_and_slope(u):
    u2 = u * u
    t = jnp.tanh(u * (0.7978845608028654 + (0.7978845608028654 * 0.044715) * u2))
    half = 0.5 + 0.5 * t
    slope = half * (
        1.0 + u * (1.0 - t) * (0.7978845608028654 + (3 * 0.7978845608028654 * 0.044715) * u2)
    )
    return u * half, slope


def mlp_kernel(core, h2, h2p, cot, out_in, dh_in, *refs):
    (wu_a, bu_a, wd_a, wu_b, bu_b, wd_b) = refs[:6]
    (out, dh, dwd_a, dwu_ak, dwu_as, dbu_a, dwd_b, dwu_bk, dwu_bs, dbu_b) = refs[6:]
    step = pl.program_id(0)
    half = h2.shape[1] // 2

    @pl.when(step == 0)
    def _():
        out[...] = out_in[...]
        dh[...] = dh_in[...]

    for wu, bu, wd, dwd, dwu_k, dwu_s, dbu in (
        (wu_a, bu_a, wd_a, dwd_a, dwu_ak, dwu_as, dbu_a),
        (wu_b, bu_b, wd_b, dwd_b, dwu_bk, dwu_bs, dbu_b),
    ):
        up = dot(h2[...], wu[...]) + bu[...]
        d_act = dot(cot[...], wd[...], 1, 1)
        act, slope = gelu_and_slope(up)
        act = act.astype(bf16)
        d_up32 = d_act * slope
        d_up = d_up32.astype(bf16)
        dbu[0] = jnp.sum(d_up32, 0, keepdims=True)
        dwd[0] = dot(cot[...], act, 0, 0).astype(bf16)
        d_wu = dot(h2p[...], d_up, 0, 0).astype(bf16)
        dwu_k[0] = d_wu[:half]
        dwu_s[0] = d_wu[half:]
        out[...] += dot(act, wd[...])
        dh[...] += dot(d_up, wu[...], 1, 1)


def mlp(core, h2, h2p, cot, out_in, dh_in, w_up, b_up, w_down, first, steps):
    rows, width = h2.shape
    ff = w_up.shape[1]
    tile = ff // 8
    half = width // 2
    whole = pl.BlockSpec((rows, width), lambda i, c: (0, 0))
    at_a = lambda i, c: 2 * (first + i) + 1 - c[0]
    at_b = lambda i, c: 2 * (first + i) + c[0]
    w_specs = []
    for at in (at_a, at_b):
        w_specs += [
            pl.BlockSpec((width, tile), lambda i, c, at=at: (0, at(i, c))),
            pl.BlockSpec((1, tile), lambda i, c, at=at: (0, at(i, c))),
            pl.BlockSpec((tile, width), lambda i, c, at=at: (at(i, c), 0)),
        ]
    out_specs = [whole, whole]
    out_shape = [jax.ShapeDtypeStruct((rows, width), f32)] * 2
    for _ in range(2):
        out_specs += [
            pl.BlockSpec((1, width, tile), lambda i, c: (i, 0, 0)),
            pl.BlockSpec((1, half, tile), lambda i, c: (i, 0, 0)),
            pl.BlockSpec((1, half, tile), lambda i, c: (i, 0, 0)),
            pl.BlockSpec((1, 1, tile), lambda i, c: (i, 0, 0)),
        ]
        out_shape += [
            jax.ShapeDtypeStruct((steps, width, tile), bf16),
            jax.ShapeDtypeStruct((steps, half, tile), bf16),
            jax.ShapeDtypeStruct((steps, half, tile), bf16),
            jax.ShapeDtypeStruct((steps, 1, tile), f32),
        ]
    return pl.pallas_call(
        mlp_kernel,
        name="mlp",
        grid_spec=pltpu.PrefetchScalarGridSpec(
            num_scalar_prefetch=1,
            grid=(steps,),
            in_specs=[whole] * 5 + w_specs,
            out_specs=out_specs,
        ),
        out_shape=out_shape,
        compiler_params=params(),
        cost_estimate=pl.CostEstimate(
            flops=2 * 6 * rows * width * 2 * tile * steps, bytes_accessed=20 * 2**20, transcendentals=0
        ),
    )(core, h2, h2p, cot, out_in, dh_in, w_up, b_up, w_down, w_up, b_up, w_down)


def all_sum_kernel(n_items, n_band, x, total, buf_i, buf_b, part, send_i, recv_i, send_b, recv_b):
    it = lax.axis_index("items")
    bd = lax.axis_index("band")
    barrier = pltpu.get_barrier_semaphore()
    for o in range(1, n_items):
        peer = (lax.rem(it + o, n_items), bd)
        pl.semaphore_signal(barrier, inc=1, device_id=peer, device_id_type=pl.DeviceIdType.MESH)
    for o in range(1, n_band):
        peer = (it, lax.rem(bd + o, n_band))
        pl.semaphore_signal(barrier, inc=1, device_id=peer, device_id_type=pl.DeviceIdType.MESH)
    pl.semaphore_wait(barrier, n_items + n_band - 2)

    def share(n, rank, peer_of, src, buf, send, recv):
        copies = []
        for o in range(1, n):
            copy = pltpu.make_async_remote_copy(
                src_ref=src,
                dst_ref=buf.at[rank],
                send_sem=send.at[o],
                recv_sem=recv.at[o],
                device_id=peer_of(lax.rem(rank + o, n)),
                device_id_type=pl.DeviceIdType.MESH,
            )
            copy.start()
            copies.append(copy)
        buf[rank] = src[...]
        for copy in copies:
            copy.wait()
        added = buf[0]
        for i in range(1, n):
            added = added + buf[i]
        return added

    part[...] = share(n_items, it, lambda p: (p, bd), x, buf_i, send_i, recv_i)
    total[...] = share(n_band, bd, lambda p: (it, p), part, buf_b, send_b, recv_b)


def all_sum(x, collective_id):
    n_items, n_band = lax.axis_size("items"), lax.axis_size("band")
    vmem = pl.BlockSpec(memory_space=pltpu.VMEM)
    return pl.pallas_call(
        functools.partial(all_sum_kernel, n_items, n_band),
        name=f"all_sum_{collective_id}",
        out_shape=jax.ShapeDtypeStruct(x.shape, f32),
        in_specs=[vmem],
        out_specs=vmem,
        scratch_shapes=[
            pltpu.VMEM((n_items,) + x.shape, f32),
            pltpu.VMEM((n_band,) + x.shape, f32),
            pltpu.VMEM(x.shape, f32),
            pltpu.SemaphoreType.DMA((n_items,)),
            pltpu.SemaphoreType.DMA((n_items,)),
            pltpu.SemaphoreType.DMA((n_band,)),
            pltpu.SemaphoreType.DMA((n_band,)),
        ],
        compiler_params=params(collective_id=collective_id, has_side_effects=True),
    )(x)


def stats_kernel(left, tok, sums):
    slots, rows, width = tok.shape
    row = lax.broadcasted_iota(jnp.int32, (rows, width), 0)
    one = jnp.zeros((1, width), f32)
    two = jnp.zeros((1, width), f32)
    for s in range(slots):
        x = jnp.where(row < left[s], tok[s].astype(f32), 0.0)
        one = one + jnp.sum(x, 0, keepdims=True)
        two = two + jnp.sum(x * x, 0, keepdims=True)
    sums[0:1, :] = one
    sums[1:2, :] = two


def stats(left, tok):
    width = tok.shape[2]
    vmem = pl.BlockSpec(memory_space=pltpu.VMEM)
    return pl.pallas_call(
        stats_kernel,
        name="stats",
        in_specs=[pl.BlockSpec(memory_space=pltpu.SMEM), vmem],
        out_specs=vmem,
        out_shape=jax.ShapeDtypeStruct((2, width), f32),
        compiler_params=params(),
    )(left, tok)


def join_kernel(core, attn_a, attn_b, wo_a, wo_b, tok, mean, inv, bo, gain, shift, res, h2, h2p):
    start = (tok[...].astype(f32) - mean[...]) * inv[...]
    r = start + (dot(attn_a[...], wo_a[...]) + dot(attn_b[...], wo_b[...])) + bo[...]
    res[...] = r
    centre = r - jnp.mean(r, -1, keepdims=True)
    spread = jnp.mean(centre * centre, -1, keepdims=True)
    h = (centre * lax.rsqrt(spread + epsilon) * gain[...] + shift[...]).astype(bf16)
    h2[...] = h
    half = h.shape[1] // 2
    width = h.shape[1] // 8
    even = core[0] == 0
    for x in range(4):
        first = h[:, 2 * x * width : (2 * x + 1) * width]
        second = h[:, (2 * x + 1) * width : (2 * x + 2) * width]
        h2p[:, x * width : (x + 1) * width] = jnp.where(even, first, second)
        h2p[:, half + x * width : half + (x + 1) * width] = jnp.where(even, second, first)


def join(core, attn, attn_recv, w_out, tok, mean, inv, bo, gain, shift, block=256):
    rows, half = attn_recv.shape
    width = 2 * half
    row = lambda i, c: (i, 0)
    one = lambda i, c: (0, 0)
    vec = pl.BlockSpec((1, width), one)
    act = pl.BlockSpec((block, half), row)
    full = pl.BlockSpec((block, width), row)
    return pl.pallas_call(
        join_kernel,
        name="join",
        grid_spec=pltpu.PrefetchScalarGridSpec(
            num_scalar_prefetch=1,
            grid=(rows // block,),
            in_specs=[
                act,
                act,
                pl.BlockSpec((half, width), lambda i, c: (c[0], 0)),
                pl.BlockSpec((half, width), lambda i, c: (1 - c[0], 0)),
                full,
                vec,
                vec,
                vec,
                vec,
                vec,
            ],
            out_specs=[full] * 3,
        ),
        out_shape=[
            jax.ShapeDtypeStruct((rows, width), f32),
            jax.ShapeDtypeStruct((rows, width), bf16),
            jax.ShapeDtypeStruct((rows, width), bf16),
        ],
        compiler_params=params(),
        cost_estimate=pl.CostEstimate(
            flops=2 * rows * width * width, bytes_accessed=8 * 2**20, transcendentals=0
        ),
    )(core, attn, attn_recv, w_out, w_out, tok, mean, inv, bo, gain, shift)


def unjoin_kernel(
    core, res, dh, cot, gain, attn_a, attn_b, wo_a, wo_b, d_res, da_a, da_b, dwo_a, dwo_b, sums, acc_a, acc_b
):
    step = pl.program_id(0)
    last = pl.num_programs(0) - 1
    r = res[...]
    centre = r - jnp.mean(r, -1, keepdims=True)
    spread = jnp.mean(centre * centre, -1, keepdims=True)
    scale = lax.rsqrt(spread + epsilon)
    z = centre * scale
    d_h = dh[...]
    dz = d_h * gain[...]
    dv = scale * (dz - jnp.mean(dz, -1, keepdims=True) - z * jnp.mean(dz * z, -1, keepdims=True))
    c32 = cot[...].astype(f32)
    full = c32 + dv
    d_res[...] = full
    low = full.astype(bf16)
    add_rows(step, sums, (d_h * z, d_h, low.astype(f32), c32))
    da_a[...] = dot(low, wo_a[...], 1, 1).astype(bf16)
    da_b[...] = dot(low, wo_b[...], 1, 1).astype(bf16)
    part_a = dot(attn_a[...], low, 0, 0)
    part_b = dot(attn_b[...], low, 0, 0)

    @pl.when(step == 0)
    def _():
        acc_a[...] = part_a
        acc_b[...] = part_b

    @pl.when(step > 0)
    def _():
        acc_a[...] += part_a
        acc_b[...] += part_b

    @pl.when(step == last)
    def _():
        dwo_a[...] = acc_a[...].astype(bf16)
        dwo_b[...] = acc_b[...].astype(bf16)


def add_rows(step, sums, arrays):
    for i, a in enumerate(arrays):
        total = jnp.sum(a, 0, keepdims=True)

        @pl.when(step == 0)
        def _():
            sums[i : i + 1, :] = total

        @pl.when(step > 0)
        def _():
            sums[i : i + 1, :] += total


def unjoin(core, res, dh, cot, gain, attn, attn_recv, w_out, block=256):
    rows, half = attn_recv.shape
    width = 2 * half
    row = lambda i, c: (i, 0)
    one = lambda i, c: (0, 0)
    act = pl.BlockSpec((block, half), row)
    full = pl.BlockSpec((block, width), row)
    grad = pl.BlockSpec((half, width), one)
    return pl.pallas_call(
        unjoin_kernel,
        name="unjoin",
        grid_spec=pltpu.PrefetchScalarGridSpec(
            num_scalar_prefetch=1,
            grid=(rows // block,),
            in_specs=[
                full,
                full,
                full,
                pl.BlockSpec((1, width), one),
                act,
                act,
                pl.BlockSpec((half, width), lambda i, c: (c[0], 0)),
                pl.BlockSpec((half, width), lambda i, c: (1 - c[0], 0)),
            ],
            out_specs=[full, act, act, grad, grad, pl.BlockSpec((4, width), one)],
            scratch_shapes=[pltpu.VMEM((half, width), f32)] * 2,
        ),
        out_shape=[
            jax.ShapeDtypeStruct((rows, width), f32),
            jax.ShapeDtypeStruct((rows, half), bf16),
            jax.ShapeDtypeStruct((rows, half), bf16),
            jax.ShapeDtypeStruct((half, width), bf16),
            jax.ShapeDtypeStruct((half, width), bf16),
            jax.ShapeDtypeStruct((4, width), f32),
        ],
        compiler_params=params(),
        cost_estimate=pl.CostEstimate(
            flops=4 * rows * width * width, bytes_accessed=12 * 2**20, transcendentals=0
        ),
    )(core, res, dh, cot, gain, attn, attn_recv, w_out, w_out)


def unproject_kernel(core, h1, dq, dk, dv, dq_r, dk_r, dv_r, wq, wk, wv, dw, dh, sums):
    step = pl.program_id(0)
    for i, d in enumerate((dq, dk, dv)):
        dw[i] = dot(h1[...], d[...], 0, 0).astype(bf16)
    total = dot(dq_r[...], wq[...], 1, 1)
    total = total + dot(dk_r[...], wk[...], 1, 1)
    total = total + dot(dv_r[...], wv[...], 1, 1)
    dh[...] = total.astype(bf16)

    @pl.when(step == 0)
    def _():
        sums[0:1, :] = jnp.sum(dq[...].astype(f32), 0, keepdims=True)
        sums[1:2, :] = jnp.sum(dv[...].astype(f32), 0, keepdims=True)


def unproject(core, h1, dq, dk, dv, wq, wk, wv, blocks=4):
    rows, width = h1.shape
    half = width // 2
    rb, cb = rows // blocks, width // blocks
    one = lambda i, c: (0, 0)
    whole = pl.BlockSpec((rows, half), one)
    part = pl.BlockSpec((rb, half), lambda i, c: (i, 0))
    w = pl.BlockSpec((width, half), lambda i, c: (0, c[0]))
    return pl.pallas_call(
        unproject_kernel,
        name="unproject",
        grid_spec=pltpu.PrefetchScalarGridSpec(
            num_scalar_prefetch=1,
            grid=(blocks,),
            in_specs=[pl.BlockSpec((rows, cb), lambda i, c: (0, i))]
            + [whole] * 3
            + [part] * 3
            + [w] * 3,
            out_specs=[
                pl.BlockSpec((3, cb, half), lambda i, c: (0, i, 0)),
                pl.BlockSpec((rb, width), lambda i, c: (i, 0)),
                pl.BlockSpec((2, half), one),
            ],
        ),
        out_shape=[
            jax.ShapeDtypeStruct((3, width, half), bf16),
            jax.ShapeDtypeStruct((rows, width), bf16),
            jax.ShapeDtypeStruct((2, half), f32),
        ],
        compiler_params=params(),
        cost_estimate=pl.CostEstimate(
            flops=12 * rows * width * half, bytes_accessed=14 * 2**20, transcendentals=0
        ),
    )(core, h1, dq, dk, dv, dq, dk, dv, wq, wk, wv)


def start_back_kernel(tok, mean, inv, gain, dh_a, dh_b, d_res, g_out, sums):
    step = pl.program_id(0)
    centred = tok[...].astype(f32) - mean[...]
    start = centred * inv[...]
    centre = start - jnp.mean(start, -1, keepdims=True)
    spread = jnp.mean(centre * centre, -1, keepdims=True)
    scale = lax.rsqrt(spread + epsilon)
    z = centre * scale
    d_h = dh_a[...].astype(f32) + dh_b[...].astype(f32)
    dz = d_h * gain[...]
    dv = scale * (dz - jnp.mean(dz, -1, keepdims=True) - z * jnp.mean(dz * z, -1, keepdims=True))
    d_start = d_res[...] + dv
    g_out[...] = (d_start * inv[...]).astype(bf16)
    add_rows(step, sums, (d_start, d_start * centred, d_h * z, d_h))


def start_back(tok, mean, inv, gain, dh, dh_recv, d_res, block=256):
    rows, width = d_res.shape
    full = pl.BlockSpec((block, width), lambda i: (i, 0))
    vec = pl.BlockSpec((1, width), lambda i: (0, 0))
    return pl.pallas_call(
        start_back_kernel,
        name="start_back",
        grid=(rows // block,),
        in_specs=[full, vec, vec, vec, full, full, full],
        out_specs=[full, pl.BlockSpec((4, width), lambda i: (0, 0))],
        out_shape=[
            jax.ShapeDtypeStruct((rows, width), bf16),
            jax.ShapeDtypeStruct((4, width), f32),
        ],
        compiler_params=params(),
        cost_estimate=pl.CostEstimate(flops=2**22, bytes_accessed=8 * 2**20, transcendentals=0),
    )(tok, mean, inv, gain, dh, dh_recv, d_res)


def pick(array, index, axis=0):
    return lax.dynamic_index_in_dim(array, index, axis, keepdims=False)


def column_layer(
    tokens, cotangent, running_mean, running_var, slot_table, patch_counts,
    ln1_gain, ln1_bias, w_query, b_query, w_key, w_value, b_value, w_out, b_out,
    ln2_gain, ln2_bias, w_up, b_up, w_down, b_down,
):
    n_items, n_band = lax.axis_size("items"), lax.axis_size("band")
    slots, band_rows, width = tokens.shape
    cut = band_rows // 2
    it = lax.axis_index("items")
    bd = lax.axis_index("band")
    c, yx = lax.rem(it, 2), it // 2
    x, y = lax.rem(yx, 2), yx // 2
    core = c.astype(jnp.int32).reshape(1)
    devices = [(i, b) for i in range(n_items) for b in range(n_band)]

    def permute(array, to):
        pairs = []
        for i, b in devices:
            j, d = to(i, b)
            pairs.append((i * n_band + b, j * n_band + d))
        return lax.ppermute(array, ("items", "band"), pairs)

    to_core = lambda i, b: (i ^ 1, b)
    to_x = lambda i, b: (i ^ 2, b)
    to_y = lambda i, b: (i ^ 4, b)
    to_z1 = lambda i, b: (i, b ^ 1)
    to_z2 = lambda i, b: (i, b ^ 2)

    def out_round(r):
        def to(i, b):
            q = b ^ r
            return ((i // 2) * 2 + (q & 1), 2 * (i % 2) + (q >> 1))

        return to

    def back_round(r):
        there = {out_round(r)(i, b): (i, b) for i, b in devices}
        return lambda i, b: there[(i, b)]

    def gather_rows(array):
        blocks = array.reshape(slots * 2, cut, width)
        return [permute(pick(blocks, bd ^ r), out_round(r)) for r in range(4)]

    def return_rows(rows):
        blocks = rows.reshape(4, cut, width)
        got = jnp.stack([permute(blocks[r], back_round(r)) for r in range(4)])
        return jnp.stack([pick(got, bd ^ q) for q in range(4)]).reshape(slots, band_rows, width)

    counts = patch_counts[slot_table]
    my_counts = lax.dynamic_slice_in_dim(counts, it * slots, slots)
    left = my_counts - bd * band_rows
    item_count = pick(counts, yx * 4 + bd)

    tok_rows = jnp.concatenate(gather_rows(tokens))
    sums = all_sum(stats(left, tokens), 1)
    tok_sib = permute(tok_rows, to_core)
    cot_rows = jnp.concatenate(gather_rows(cotangent))

    patch_total = jnp.sum(patch_counts).astype(f32)
    batch_mean = sums[0] / patch_total
    batch_var = sums[1] / patch_total - batch_mean * batch_mean
    new_mean = momentum * running_mean + momentum * batch_mean
    new_var = momentum * running_var + momentum * batch_var
    inverse = lax.rsqrt(new_var + epsilon)
    mean_row, inv_row = new_mean.reshape(1, -1), inverse.reshape(1, -1)
    as_row = lambda a: a.astype(f32).reshape(1, -1)

    round_of = jnp.arange(4 * cut, dtype=jnp.int32) // cut
    at = jnp.arange(4 * cut, dtype=jnp.int32) % cut
    base = 2 * lax.rem(bd, 2)
    own = ((base + c) ^ round_of) * band_rows + c * cut + at
    sib = ((base + 1 - c) ^ round_of) * band_rows + (1 - c) * cut + at
    bias = jnp.where(jnp.concatenate([own, sib]) < item_count, 0.0, masked_score).astype(bf16)
    bias = jnp.broadcast_to(bias[:, None], (8 * cut, 128))

    tok = jnp.concatenate([tok_rows, tok_sib])
    h1, q, k, v = project(
        core, tok, mean_row, inv_row, as_row(ln1_gain), as_row(ln1_bias),
        w_query, w_key, w_value, as_row(b_query), as_row(b_value),
    )
    attn, log_total = attend(q, k, v, bias)
    rows = 4 * cut
    attn_recv = permute(attn[rows:], to_core)
    res, h2, h2p = join(
        core, attn, attn_recv, w_out, tok, mean_row, inv_row, as_row(b_out), as_row(ln2_gain), as_row(ln2_bias)
    )
    up_bias = as_row(b_up)
    zero = jnp.zeros_like(res)
    d_down_part, d_up_part, d_bias_up = [], [], []
    total, d_h2 = res, zero
    for j in range(2):
        (total, d_h2, dwd_a, dwu_ak, dwu_as, dbu_a, dwd_b, dwu_bk, dwu_bs, dbu_b) = mlp(
            core, h2, h2p, cot_rows, total, d_h2, w_up, up_bias, w_down, 2 * j, 2
        )
        d_down = (dwd_b, permute(dwd_a, to_core))
        got_a, got_b = permute(dwu_as, to_core), permute(dwu_bs, to_core)
        d_up = (jnp.stack([dwu_ak, dwu_bk]), jnp.stack([got_b, got_a]))
        d_bias_up.append(jnp.stack([dbu_a, dbu_b]))
        send = pick(d_down[0], 1 - x) + pick(d_down[1], 1 - x)
        keep = pick(d_down[0], x) + pick(d_down[1], x)
        d_down_part.append((keep, permute(send, to_x)))
        d_up = [a.reshape(2, 2, 2, 2, -1, a.shape[-1]) for a in d_up]
        send = pick(d_up[0], 1 - y, 2) + pick(d_up[1], 1 - y, 2)
        keep = pick(d_up[0], y, 2) + pick(d_up[1], y, 2)
        got = permute(send, to_y)
        send = pick(keep, 1 - x, 2) + pick(got, 1 - x, 2)
        keep = pick(keep, x, 2) + pick(got, x, 2)
        got = permute(send, to_x)
        b_low = lax.rem(bd, 2)
        send = pick(keep, 1 - b_low, 1) + pick(got, 1 - b_low, 1)
        keep = pick(keep, b_low, 1) + pick(got, b_low, 1)
        d_up_part.append((keep, permute(send, to_z1)))
    b_low, b_high = lax.rem(bd, 2), bd // 2

    def add(pair):
        return pair[0] + pair[1]

    def pick_pair(pairs, index):
        keep = jnp.stack([p[0] for p in pairs])
        got = jnp.stack([p[1] for p in pairs])
        return pick(keep, index) + pick(got, index)

    send = pick_pair(d_down_part, 1 - y)
    keep = pick_pair(d_down_part, y)
    got = permute(send, to_y)
    tile = keep.shape[-1]
    keep, got = (a.reshape(2, 2, -1, tile) for a in (keep, got))
    send = pick(keep, 1 - b_low, 1) + pick(got, 1 - b_low, 1)
    keep = pick(keep, b_low, 1) + pick(got, b_low, 1)
    got = permute(send, to_z1)
    send = pick(keep, 1 - b_high) + pick(got, 1 - b_high)
    keep = pick(keep, b_high) + pick(got, b_high)
    got = permute(send, to_z2)
    d_w_down = (keep.astype(f32) + got.astype(f32)).T
    send = pick_pair(d_up_part, 1 - b_high)
    keep = pick_pair(d_up_part, b_high)
    got = permute(send, to_z2)
    d_w_up = keep.astype(f32) + got.astype(f32)
    d_w_up = jnp.where(
        c == 0,
        jnp.concatenate([d_w_up[1], d_w_up[0]], 1),
        jnp.concatenate([d_w_up[0], d_w_up[1]], 1),
    )
    d_bias_up = jnp.stack(d_bias_up)[:, :, :, 0]
    d_bias_up = jnp.where(c == 0, d_bias_up[:, ::-1], d_bias_up)
    d_bias_up = d_bias_up.transpose(0, 2, 1, 3).reshape(-1, width)

    output = return_rows((total + as_row(b_down)).astype(bf16))

    d_res, da_own, da_send, dwo_a, dwo_b, sums_two = unjoin(
        core, res, d_h2, cot_rows, as_row(ln2_gain), attn, attn_recv, w_out
    )
    da_recv = permute(da_send, to_core)
    dq, dk, dv = attend_back(q, k, v, bias, jnp.concatenate([da_own, da_recv]), log_total)
    dw, dh1, sums_qv = unproject(core, h1, dq, dk, dv, w_query, w_key, w_value)

    dwo = jnp.stack([dwo_a, dwo_b]).reshape(2, 2, 2, -1, width)
    got = permute(pick(dwo, 1 - c, 2), to_core)[::-1]
    keep = pick(dwo, c, 2)
    rel = y ^ c
    send = pick(keep, 1 - rel) + pick(got, 1 - rel)
    keep = pick(keep, rel) + pick(got, rel)
    got = permute(send, to_y)
    send = pick(keep, 1 - x) + pick(got, 1 - x)
    keep = pick(keep, x) + pick(got, x)
    got = permute(send, to_x)
    fourth = width // 4
    keep, got = (a.reshape(-1, 2, 2, fourth) for a in (keep, got))
    send = pick(keep, 1 - b_low, 2) + pick(got, 1 - b_low, 2)
    keep = pick(keep, b_low, 2) + pick(got, b_low, 2)
    got = permute(send, to_z1)
    send = pick(keep, 1 - b_high, 1) + pick(got, 1 - b_high, 1)
    keep = pick(keep, b_high, 1) + pick(got, b_high, 1)
    got = permute(send, to_z2)
    d_w_out = keep.astype(f32) + got.astype(f32)

    dw = dw.reshape(3, 2, 2, 2, -1, width // 2)
    got = permute(pick(dw, 1 - c, 3), to_core)
    dw = jnp.stack([pick(dw, c, 3), got])
    send, keep = pick(dw, 1 - x, 3), pick(dw, x, 3)
    got = permute(send, to_x)
    send = pick(keep, 1 - y, 2) + pick(got, 1 - y, 2)
    keep = pick(keep, y, 2) + pick(got, y, 2)
    got = permute(send, to_y)
    rel = b_high ^ c
    keep, got = (a.reshape(2, 3, -1, 2, fourth) for a in (keep, got))
    send = pick(keep, 1 - b_low, 3) + pick(got, 1 - b_low, 3)
    keep = pick(keep, b_low, 3) + pick(got, b_low, 3)
    got = permute(send, to_z1)
    send = pick(keep, 1 - rel) + pick(got, 1 - rel)
    keep = pick(keep, rel) + pick(got, rel)
    got = permute(send, to_z2)
    d_qkv = keep.astype(f32) + got.astype(f32)

    dh_recv = permute(dh1[rows:], to_core)
    g_rows, sums_one = start_back(tok, mean_row, inv_row, as_row(ln1_gain), dh1, dh_recv, d_res)
    g_home = return_rows(g_rows)
    empty = jnp.zeros_like(sums_qv)
    halves = jnp.where(
        c == 0,
        jnp.concatenate([sums_qv, empty], 1),
        jnp.concatenate([empty, sums_qv], 1),
    )
    small = all_sum(jnp.concatenate([sums_one, halves, sums_two, d_bias_up]), 2)
    sum_g, sum_gx, d_gain_one, d_shift_one, d_bq, d_bv, d_gain_two, d_shift_two, d_bo, d_bdown = (
        small[i] for i in range(10)
    )
    d_bup = small[10:].reshape(-1)
    row_keep = (jnp.arange(band_rows, dtype=jnp.int32)[None, :] < left[:, None]).astype(f32)
    cube = inverse * inverse * inverse
    fix = -0.5 * inverse * sum_g / patch_total
    slope = -0.5 * cube * sum_gx / patch_total
    d_tokens = g_home.astype(f32) + row_keep[:, :, None] * (
        fix + slope * (tokens.astype(f32) - batch_mean)
    )
    return (
        output, d_tokens.astype(bf16), new_mean, new_var, d_gain_one, d_shift_one,
        d_qkv[0], d_bq, d_qkv[1], d_qkv[2], d_bv, d_w_out, d_bo, d_gain_two, d_shift_two,
        d_w_up, d_bup, d_w_down, d_bdown,
    )


def layer_norm(value, gain, shift):
    centre = value - jnp.mean(value, -1, keepdims=True)
    spread = jnp.mean(centre * centre, -1, keepdims=True)
    return centre * lax.rsqrt(spread + epsilon) * gain + shift


def gelu_tanh(value):
    return (
        0.5
        * value
        * (1.0 + jnp.tanh(0.7978845608028654 * (value + 0.044715 * value * value * value)))
    )


def head_layout():
    heads_per = 4
    return (heads_per, HEADS // heads_per, heads_per * HEAD_DIM)


def group_scores(q_part, k_part, key_mask):
    scores = (
        jnp.einsum("rhd,khd->hrk", q_part, k_part, preferred_element_type=jnp.float32) * score_scale
    )
    return jnp.where(key_mask[None, None, :], scores, masked_score)


def attend_forward(q_slot, keys_slot, values_slot, key_mask):
    heads_per, groups, group_width = head_layout()
    band_rows = q_slot.shape[0]
    seq_length = keys_slot.shape[0]

    def head_block(group_index):
        begin = group_index * group_width
        q_part = lax.dynamic_slice_in_dim(q_slot, begin, group_width, 1).reshape(
            band_rows, heads_per, HEAD_DIM
        )
        k_part = lax.dynamic_slice_in_dim(keys_slot, begin, group_width, 1).reshape(
            seq_length, heads_per, HEAD_DIM
        )
        v_part = lax.dynamic_slice_in_dim(values_slot, begin, group_width, 1).reshape(
            seq_length, heads_per, HEAD_DIM
        )
        scores = group_scores(q_part, k_part, key_mask)
        top_score = jnp.max(scores, -1, keepdims=True)
        log_total = top_score + jnp.log(jnp.sum(jnp.exp(scores - top_score), -1, keepdims=True))
        probs_low = jnp.exp(scores - log_total).astype(jnp.bfloat16)
        attended = jnp.einsum("hrk,khd->rhd", probs_low, v_part, preferred_element_type=jnp.float32)
        return (attended.reshape(band_rows, group_width), log_total[..., 0])

    attended, log_totals = lax.map(head_block, jnp.arange(groups, dtype=jnp.int32))
    return (attended.transpose(1, 0, 2).reshape(band_rows, groups * group_width), log_totals)


def attend_backward(q_slot, keys_slot, values_slot, key_mask, d_attn_slot, row_delta, log_totals):
    heads_per, groups, group_width = head_layout()
    query_rows = q_slot.shape[0]
    seq_length = keys_slot.shape[0]
    deltas = jnp.transpose(row_delta).reshape(groups, heads_per, query_rows)

    def head_block(inputs):
        group_index, log_total, delta_part = inputs
        begin = group_index * group_width
        q_part = lax.dynamic_slice_in_dim(q_slot, begin, group_width, 1).reshape(
            query_rows, heads_per, HEAD_DIM
        )
        k_part = lax.dynamic_slice_in_dim(keys_slot, begin, group_width, 1).reshape(
            seq_length, heads_per, HEAD_DIM
        )
        v_part = lax.dynamic_slice_in_dim(values_slot, begin, group_width, 1).reshape(
            seq_length, heads_per, HEAD_DIM
        )
        d_part = lax.dynamic_slice_in_dim(d_attn_slot, begin, group_width, 1).reshape(
            query_rows, heads_per, HEAD_DIM
        )
        scores = group_scores(q_part, k_part, key_mask)
        probs = jnp.exp(scores - log_total[..., None])
        d_probs = jnp.einsum("rhd,khd->hrk", d_part, v_part, preferred_element_type=jnp.float32)
        d_scores = (probs * (d_probs - delta_part[..., None])).astype(jnp.bfloat16)
        results = []
        d_q_part = (
            jnp.einsum("hrk,khd->rhd", d_scores, k_part, preferred_element_type=jnp.float32)
            * score_scale
        )
        results.append(d_q_part.reshape(query_rows, group_width))
        probs_low = probs.astype(jnp.bfloat16)
        d_k_part = (
            jnp.einsum("hrk,rhd->khd", d_scores, q_part, preferred_element_type=jnp.float32)
            * score_scale
        )
        d_v_part = jnp.einsum("hrk,rhd->khd", probs_low, d_part, preferred_element_type=jnp.float32)
        results.append(d_k_part.reshape(seq_length, group_width))
        results.append(d_v_part.reshape(seq_length, group_width))
        return tuple(results)

    mapped = lax.map(head_block, (jnp.arange(groups, dtype=jnp.int32), log_totals, deltas))
    full_width = groups * group_width
    return tuple((piece.transpose(1, 0, 2).reshape(piece.shape[1], full_width) for piece in mapped))


def local(
    tokens,
    cotangent,
    running_mean,
    running_var,
    slot_table,
    patch_counts,
    ln1_gain,
    ln1_bias,
    w_query,
    b_query,
    w_key,
    w_value,
    b_value,
    w_out,
    b_out,
    ln2_gain,
    ln2_bias,
    w_up,
    b_up,
    w_down,
    b_down,
):
    slot_count, band_rows, model_width = tokens.shape
    seq_length = band_rows * lax.axis_size("band")
    item_rank = lax.axis_index("items")
    band_rank = lax.axis_index("band")
    every_slot = jnp.arange(slot_table.shape[0], dtype=jnp.int32)
    my_slots = item_rank * slot_count + jnp.arange(slot_count, dtype=jnp.int32)
    item_ids = jnp.sum(
        jnp.where(every_slot[None, :] == my_slots[:, None], slot_table[None, :], 0), 1
    )
    lengths = jnp.sum(
        jnp.where(every_slot[None, :] == item_ids[:, None], patch_counts[None, :], 0), 1
    )
    key_mask = jnp.arange(seq_length, dtype=jnp.int32)[None, :] < lengths[:, None]
    row_mask = (band_rank * band_rows + jnp.arange(band_rows, dtype=jnp.int32))[None, :] < lengths[
        :, None
    ]
    row_keep = row_mask.astype(jnp.float32).reshape(-1, 1)
    raw_flat = tokens.astype(jnp.float32).reshape(-1, model_width)
    part_one = jnp.sum(row_keep * raw_flat, 0)
    part_two = jnp.sum(row_keep * raw_flat * raw_flat, 0)
    total_one, total_two = lax.psum((part_one, part_two), ("items", "band"))
    patch_total = jnp.sum(patch_counts).astype(jnp.float32)
    batch_mean = total_one / patch_total
    batch_var = total_two / patch_total - batch_mean * batch_mean
    new_mean = momentum * running_mean + momentum * batch_mean
    new_var = momentum * running_var + momentum * batch_var
    inverse = lax.rsqrt(new_var + epsilon)
    normed_in = (raw_flat - new_mean) * inverse
    gain_one = ln1_gain.astype(jnp.float32)
    shift_one = ln1_bias.astype(jnp.float32)
    gain_two = ln2_gain.astype(jnp.float32)
    shift_two = ln2_bias.astype(jnp.float32)
    h_one_full, norm_one_back = jax.vjp(layer_norm, normed_in, gain_one, shift_one)
    h_one = h_one_full.astype(jnp.bfloat16)
    queries = (
        jnp.dot(h_one, w_query, preferred_element_type=jnp.float32) + b_query.astype(jnp.float32)
    ).astype(jnp.bfloat16)
    key_local = (
        jnp.dot(h_one, w_key, preferred_element_type=jnp.float32)
        .astype(jnp.bfloat16)
        .reshape(slot_count, band_rows, model_width)
    )
    value_local = (
        (jnp.dot(h_one, w_value, preferred_element_type=jnp.float32) + b_value.astype(jnp.float32))
        .astype(jnp.bfloat16)
        .reshape(slot_count, band_rows, model_width)
    )
    keys_all, values_all = (
        lax.all_gather(key_local, "band", axis=1, tiled=True),
        lax.all_gather(value_local, "band", axis=1, tiled=True),
    )
    q_slots = queries.reshape(slot_count, band_rows, model_width)
    attended_list = []
    totals_list = []
    for slot_index in range(slot_count):
        attended, log_totals = attend_forward(
            q_slots[slot_index], keys_all[slot_index], values_all[slot_index], key_mask[slot_index]
        )
        attended_list.append(attended)
        totals_list.append(log_totals)
    attn_full = jnp.concatenate(attended_list, 0)
    attn_low = attn_full.astype(jnp.bfloat16)
    residual = (
        normed_in
        + jnp.dot(attn_low, w_out, preferred_element_type=jnp.float32)
        + b_out.astype(jnp.float32)
    )
    h_two_full, norm_two_back = jax.vjp(layer_norm, residual, gain_two, shift_two)
    h_two = h_two_full.astype(jnp.bfloat16)
    up_proj = jnp.dot(h_two, w_up, preferred_element_type=jnp.float32) + b_up.astype(jnp.float32)
    activated_full, gelu_back = jax.vjp(gelu_tanh, up_proj)
    activated = activated_full.astype(jnp.bfloat16)
    result = (
        residual
        + jnp.dot(activated, w_down, preferred_element_type=jnp.float32)
        + b_down.astype(jnp.float32)
    )
    output = result.astype(jnp.bfloat16).reshape(slot_count, band_rows, model_width)
    cot_low = cotangent.reshape(-1, model_width)
    cot_full = cot_low.astype(jnp.float32)
    d_w_down = jnp.einsum("tf,td->fd", activated, cot_low, preferred_element_type=jnp.float32)
    d_b_down = jnp.sum(cot_full, 0)
    d_activated = jnp.einsum("td,fd->tf", cot_low, w_down, preferred_element_type=jnp.float32)
    (d_up_full,) = gelu_back(d_activated)
    d_up = d_up_full.astype(jnp.bfloat16)
    d_w_up = jnp.einsum("td,tf->df", h_two, d_up, preferred_element_type=jnp.float32)
    d_b_up = jnp.sum(d_up, 0, dtype=jnp.float32)
    d_h_two = jnp.einsum("tf,df->td", d_up, w_up, preferred_element_type=jnp.float32)
    d_res_norm, d_gain_two, d_shift_two = norm_two_back(d_h_two)
    d_residual = cot_full + d_res_norm
    d_branch = d_residual.astype(jnp.bfloat16)
    d_w_out = jnp.einsum("td,te->de", attn_low, d_branch, preferred_element_type=jnp.float32)
    d_b_out = jnp.sum(d_branch, 0, dtype=jnp.float32)
    d_attn = jnp.einsum("te,de->td", d_branch, w_out, preferred_element_type=jnp.float32).astype(
        jnp.bfloat16
    )
    row_delta = jnp.sum(
        (d_attn.astype(jnp.float32) * attn_full).reshape(slot_count, band_rows, HEADS, HEAD_DIM), -1
    )
    d_attn_slots = d_attn.reshape(slot_count, band_rows, model_width)
    back_keys, back_values = (keys_all, values_all)
    d_q_list = []
    d_k_list = []
    d_v_list = []
    for slot_index in range(slot_count):
        d_q_slot, d_k_slot, d_v_slot = attend_backward(
            q_slots[slot_index],
            back_keys[slot_index],
            back_values[slot_index],
            key_mask[slot_index],
            d_attn_slots[slot_index],
            row_delta[slot_index],
            totals_list[slot_index],
        )
        d_q_list.append(d_q_slot)
        d_k_list.append(d_k_slot)
        d_v_list.append(d_v_slot)
    d_keys_mine, d_values_mine = (
        lax.psum_scatter(
            jnp.stack(d_k_list).astype(jnp.bfloat16), "band", scatter_dimension=1, tiled=True
        ).astype(jnp.float32),
        lax.psum_scatter(
            jnp.stack(d_v_list).astype(jnp.bfloat16), "band", scatter_dimension=1, tiled=True
        ).astype(jnp.float32),
    )
    d_queries = jnp.concatenate(d_q_list, 0).astype(jnp.bfloat16)
    d_keys = d_keys_mine.reshape(-1, model_width).astype(jnp.bfloat16)
    d_values = d_values_mine.reshape(-1, model_width).astype(jnp.bfloat16)
    d_w_query = jnp.einsum("td,te->de", h_one, d_queries, preferred_element_type=jnp.float32)
    d_b_query = jnp.sum(d_queries, 0, dtype=jnp.float32)
    d_w_key = jnp.einsum("td,te->de", h_one, d_keys, preferred_element_type=jnp.float32)
    d_w_value = jnp.einsum("td,te->de", h_one, d_values, preferred_element_type=jnp.float32)
    d_b_value = jnp.sum(d_values, 0, dtype=jnp.float32)
    d_h_one = jnp.einsum("te,de->td", d_queries, w_query, preferred_element_type=jnp.float32)
    d_h_one = d_h_one + jnp.einsum("te,de->td", d_keys, w_key, preferred_element_type=jnp.float32)
    d_h_one = d_h_one + jnp.einsum(
        "te,de->td", d_values, w_value, preferred_element_type=jnp.float32
    )
    d_start_norm, d_gain_one, d_shift_one = norm_one_back(d_h_one)
    d_start = d_residual + d_start_norm
    centred = raw_flat - new_mean
    small_sums = lax.psum(
        (
            jnp.sum(d_start, 0),
            jnp.sum(d_start * centred, 0),
            d_gain_one,
            d_shift_one,
            d_b_query,
            d_b_value,
            d_b_out,
            d_gain_two,
            d_shift_two,
            d_b_up,
            d_b_down,
        ),
        ("items", "band"),
    )
    sum_g = small_sums[0]
    sum_gx = small_sums[1]
    cube = inverse * inverse * inverse
    d_raw = d_start * inverse + row_keep * (
        -0.5 * inverse * sum_g / patch_total
        - 0.5 * cube * sum_gx * (raw_flat - batch_mean) / patch_total
    )
    d_tokens = d_raw.astype(jnp.bfloat16).reshape(slot_count, band_rows, model_width)
    weight_grads = (
        lax.psum_scatter(
            d_w_query.astype(jnp.bfloat16), "items", scatter_dimension=0, tiled=True
        ).astype(jnp.float32),
        lax.psum_scatter(
            d_w_key.astype(jnp.bfloat16), "items", scatter_dimension=0, tiled=True
        ).astype(jnp.float32),
        lax.psum_scatter(
            d_w_value.astype(jnp.bfloat16), "items", scatter_dimension=0, tiled=True
        ).astype(jnp.float32),
        lax.psum_scatter(
            d_w_out.astype(jnp.bfloat16), "items", scatter_dimension=0, tiled=True
        ).astype(jnp.float32),
        lax.psum_scatter(
            d_w_up.astype(jnp.bfloat16), "items", scatter_dimension=0, tiled=True
        ).astype(jnp.float32),
        lax.psum_scatter(
            d_w_down.astype(jnp.bfloat16), "items", scatter_dimension=0, tiled=True
        ).astype(jnp.float32),
    )
    weight_grads = (
        lax.psum_scatter(
            weight_grads[0].astype(jnp.bfloat16), "band", scatter_dimension=1, tiled=True
        ).astype(jnp.float32),
        lax.psum_scatter(
            weight_grads[1].astype(jnp.bfloat16), "band", scatter_dimension=1, tiled=True
        ).astype(jnp.float32),
        lax.psum_scatter(
            weight_grads[2].astype(jnp.bfloat16), "band", scatter_dimension=1, tiled=True
        ).astype(jnp.float32),
        lax.psum_scatter(
            weight_grads[3].astype(jnp.bfloat16), "band", scatter_dimension=1, tiled=True
        ).astype(jnp.float32),
        lax.psum_scatter(
            weight_grads[4].astype(jnp.bfloat16), "band", scatter_dimension=1, tiled=True
        ).astype(jnp.float32),
        lax.psum_scatter(
            weight_grads[5].astype(jnp.bfloat16), "band", scatter_dimension=1, tiled=True
        ).astype(jnp.float32),
    )
    return (
        output,
        d_tokens,
        new_mean,
        new_var,
        small_sums[2],
        small_sums[3],
        weight_grads[0],
        small_sums[4],
        weight_grads[1],
        weight_grads[2],
        small_sums[5],
        weight_grads[3],
        small_sums[6],
        small_sums[7],
        small_sums[8],
        weight_grads[4],
        small_sums[9],
        weight_grads[5],
        small_sums[10],
    )


def solution(mesh):
    columns = mesh.shape["items"] == 8 and mesh.shape["band"] == 4
    return jax.shard_map(
        column_layer if columns else local,
        mesh=mesh,
        in_specs=(
            P("items", "band", None),
            P("items", "band", None),
            P(),
            P(),
            P(),
            P(),
            P(),
            P(),
            P(),
            P(),
            P(),
            P(),
            P(),
            P(),
            P(),
            P(),
            P(),
            P(),
            P(),
            P(),
            P(),
        ),
        out_specs=(
            P("items", "band", None),
            P("items", "band", None),
            P(),
            P(),
            P(),
            P(),
            P("items", "band"),
            P(),
            P("items", "band"),
            P("items", "band"),
            P(),
            P("items", "band"),
            P(),
            P(),
            P(),
            P("items", "band"),
            P(),
            P("items", "band"),
            P(),
        ),
        check_vma=False,
    )
```

```python
import functools
import jax
import jax.numpy as jnp
from jax import lax
from jax.experimental import pallas as pl
from jax.experimental.pallas import tpu as pltpu
from jax.sharding import PartitionSpec as P

HEADS = 16
HEAD_DIM = 64
epsilon = 1e-05
score_scale = 0.125
masked_score = -1e30
momentum = 0.5
f32 = jnp.float32
bf16 = jnp.bfloat16
VMEM_LIMIT = 60 * 2**20


def dot(a, b, ca=1, cb=0):
    return lax.dot_general(a, b, (((ca,), (cb,)), ((), ())), preferred_element_type=f32)


def params(**kw):
    return pltpu.CompilerParams(vmem_limit_bytes=VMEM_LIMIT, **kw)


def place():
    it, bd = lax.axis_index("items"), lax.axis_index("band")
    return it, bd, lax.rem(it, 2), it // 2


def remote(src, dst, send, recv, to):
    return pltpu.make_async_remote_copy(
        src_ref=src,
        dst_ref=dst,
        send_sem=send,
        recv_sem=recv,
        device_id=to,
        device_id_type=pl.DeviceIdType.MESH,
    )


def greet(peers):
    barrier = pltpu.get_barrier_semaphore()
    for peer in peers:
        pl.semaphore_signal(barrier, inc=1, device_id=peer, device_id_type=pl.DeviceIdType.MESH)
    pl.semaphore_wait(barrier, len(peers))


def column_peers():
    it, bd, c, yx = place()
    peers = [(it, lax.rem(bd + o, 4)) for o in range(1, 4)]
    return peers + [(it + 1 - 2 * c, lax.rem(bd + o, 4)) for o in range(4)]


def rows_out(src, dst, send, recv):
    it, bd, c, yx = place()
    cut = src.shape[1] // 2
    for q in range(4):
        s, h = q // 2, q % 2
        block = src.at[s, pl.ds(h * cut, cut)]
        target = dst.at[bd]
        own = (c == h) & (bd == 2 * c + s)

        @pl.when(own)
        def _():
            pltpu.make_async_copy(block, target, recv.at[bd]).start()

        @pl.when(jnp.logical_not(own))
        def _():
            remote(block, target, send.at[q], recv.at[bd], (yx * 2 + h, 2 * c + s)).start()


def rows_out_sent(src, dst, send, recv):
    it, bd, c, yx = place()
    cut = src.shape[1] // 2
    for q in range(4):
        s, h = q // 2, q % 2
        own = (c == h) & (bd == 2 * c + s)

        @pl.when(jnp.logical_not(own))
        def _():
            block = src.at[s, pl.ds(h * cut, cut)]
            remote(block, dst.at[bd], send.at[q], recv.at[bd], (yx * 2 + h, 2 * c + s)).wait_send()


def rows_out_got(src, dst, send, recv, band):
    it, bd, c, yx = place()
    cut = src.shape[1] // 2
    pltpu.make_async_copy(src.at[0, pl.ds(0, cut)], dst.at[band], recv.at[band]).wait()


def rows_back(src, dst, send, recv):
    it, bd, c, yx = place()
    cut = src.shape[1]
    home = bd // 2
    s = lax.rem(bd, 2)
    target = dst.at[s, pl.ds(pl.multiple_of(c * cut, cut), cut)]
    got = recv.at[2 * s + c]
    for r in range(4):
        own = (home == c) & (bd == r)

        @pl.when(own)
        def _():
            pltpu.make_async_copy(src.at[r], target, got).start()

        @pl.when(jnp.logical_not(own))
        def _():
            remote(src.at[r], target, send.at[r], got, (yx * 2 + home, r)).start()


def rows_back_sent(src, dst, send, recv):
    it, bd, c, yx = place()
    cut = src.shape[1]
    home = bd // 2
    for r in range(4):
        own = (home == c) & (bd == r)

        @pl.when(jnp.logical_not(own))
        def _():
            target = dst.at[0, pl.ds(0, cut)]
            remote(src.at[r], target, send.at[r], recv.at[0], (yx * 2 + home, r)).wait_send()


def rows_back_got(src, dst, send, recv, q):
    cut = src.shape[1]
    s, h = q // 2, q % 2
    pltpu.make_async_copy(src.at[0], dst.at[s, pl.ds(h * cut, cut)], recv.at[q]).wait()


def gather_kernel(n_items, n_band, table, counts, tok, rows, sums, one, buf_i, part, buf_b, *sems):
    (send_t, recv_t, send_s, recv_s, send_i, recv_i, send_b, recv_b) = sems
    it, bd, c, yx = place()
    sibling = (it + 1 - 2 * c, bd)
    others = []
    for o in range(1, n_items // 2):
        for k in range(2):
            others.append((lax.rem(yx + o, n_items // 2) * 2 + k, bd))
    greet(column_peers() + others)
    rows_out(tok, rows, send_t, recv_t)
    slots, band_rows, width = tok.shape
    at = lax.broadcasted_iota(jnp.int32, (band_rows, width), 0) + bd * band_rows
    first = jnp.zeros((1, width), f32)
    second = jnp.zeros((1, width), f32)
    for s in range(slots):
        x = jnp.where(at < counts[table[it * slots + s]], tok[s].astype(f32), 0.0)
        first = first + jnp.sum(x, 0, keepdims=True)
        second = second + jnp.sum(x * x, 0, keepdims=True)
    one[0:1, :] = first
    one[1:2, :] = second
    part[...] = share(n_items, it, lambda p: (p, bd), one, buf_i, send_i, recv_i)
    sums[...] = share(n_band, bd, lambda p: (it, p), part, buf_b, send_b, recv_b)
    hand = []
    for o in range(4):
        band = lax.rem(bd + o, 4)
        rows_out_got(tok, rows, send_t, recv_t, band)
        copy = remote(rows.at[band], rows.at[4 + band], send_s.at[o], recv_s.at[o], sibling)
        copy.start()
        hand.append(copy)
    for copy in hand:
        copy.wait()
    rows_out_sent(tok, rows, send_t, recv_t)


def gather(table, counts, tok):
    n_items, n_band = lax.axis_size("items"), lax.axis_size("band")
    slots, band_rows, width = tok.shape
    vmem = pl.BlockSpec(memory_space=pltpu.VMEM)
    smem = pl.BlockSpec(memory_space=pltpu.SMEM)
    dma = pltpu.SemaphoreType.DMA
    return pl.pallas_call(
        functools.partial(gather_kernel, n_items, n_band),
        name="gather",
        in_specs=[smem, smem, vmem],
        out_specs=[pl.BlockSpec(memory_space=pltpu.HBM), vmem],
        out_shape=[
            jax.ShapeDtypeStruct((8, band_rows // 2, width), bf16),
            jax.ShapeDtypeStruct((2, width), f32),
        ],
        scratch_shapes=[
            pltpu.VMEM((2, width), f32),
            pltpu.VMEM((n_items, 2, width), f32),
            pltpu.VMEM((2, width), f32),
            pltpu.VMEM((n_band, 2, width), f32),
        ]
        + [dma((4,))] * 4
        + [dma((n_items,))] * 2
        + [dma((n_band,))] * 2,
        compiler_params=params(collective_id=1, has_side_effects=True),
    )(table, counts, tok)


def project_kernel(core, tok, mean, inv, gain, shift, wq, wk, wv, bq, bv, h1, q, k, v):
    start = (tok[...].astype(f32) - mean[...]) * inv[...]
    centre = start - jnp.mean(start, -1, keepdims=True)
    spread = jnp.mean(centre * centre, -1, keepdims=True)
    h = (centre * lax.rsqrt(spread + epsilon) * gain[...] + shift[...]).astype(bf16)
    h1[...] = h
    q[...] = ((dot(h, wq[...]) + bq[...]).astype(bf16) * score_scale).astype(bf16)
    k[...] = dot(h, wk[...]).astype(bf16)
    v[...] = (dot(h, wv[...]) + bv[...]).astype(bf16)


def project(core, tok, mean, inv, gain, shift, wq, wk, wv, bq, bv, block=256):
    rows, width = tok.shape
    half = width // 2
    row = lambda i, c: (i, 0)
    one = lambda i, c: (0, 0)
    mine = lambda i, c: (0, c[0])
    vec = pl.BlockSpec((1, width), one)
    w = pl.BlockSpec((width, half), mine)
    bias = pl.BlockSpec((1, half), mine)
    return pl.pallas_call(
        project_kernel,
        name="project",
        grid_spec=pltpu.PrefetchScalarGridSpec(
            num_scalar_prefetch=1,
            grid=(rows // block,),
            in_specs=[pl.BlockSpec((block, width), row), vec, vec, vec, vec, w, w, w, bias, bias],
            out_specs=[pl.BlockSpec((block, width), row)] + [pl.BlockSpec((block, half), row)] * 3,
        ),
        out_shape=[jax.ShapeDtypeStruct((rows, width), bf16)]
        + [jax.ShapeDtypeStruct((rows, half), bf16)] * 3,
        compiler_params=params(),
        cost_estimate=pl.CostEstimate(
            flops=2 * rows * width * 3 * half, bytes_accessed=12 * 2**20, transcendentals=0
        ),
    )(core, tok, mean, inv, gain, shift, wq, wk, wv, bq, bv)


def head_lanes(array, head, lane):
    keep = (lane >= head * HEAD_DIM) & (lane < (head + 1) * HEAD_DIM)
    return jnp.where(keep, array, jnp.zeros_like(array))


def scores_keys(k_pair, bias, head, lane):
    spare = (1 - head) * HEAD_DIM
    return jnp.where(lane == spare, bias, head_lanes(k_pair, head, lane))


def scores_queries(q_pair, head, lane):
    spare = (1 - head) * HEAD_DIM
    return jnp.where(lane == spare, jnp.ones_like(q_pair), head_lanes(q_pair, head, lane))


def attend_kernel(qt, q, k, v, bias, cot, out, log_total, cot_rows, send, recv):
    step = pl.program_id(0)

    @pl.when(step == 0)
    def _():
        greet(column_peers())
        rows_out(cot, cot_rows, send, recv)

    rows, lanes = q.shape
    lane_k = lax.broadcasted_iota(jnp.int32, (rows, lanes), 1)
    lane_q = lax.broadcasted_iota(jnp.int32, (qt, lanes), 1)
    row_out = lax.broadcasted_iota(jnp.int32, (lanes, qt), 0)
    keys = [scores_keys(k[...], bias[...], hd, lane_k) for hd in range(2)]
    values = [scores_queries(v[...], hd, lane_k).T for hd in range(2)]
    for t in range(rows // qt):
        at = slice(t * qt, (t + 1) * qt)
        scores = [dot(keys[hd], scores_queries(q[at, :], hd, lane_q), 1, 1) for hd in range(2)]
        tops = [jnp.max(s, 0, keepdims=True) for s in scores]
        weights = [jnp.exp(s - top).astype(bf16) for s, top in zip(scores, tops)]
        parts = []
        for hd in range(2):
            part = dot(values[hd], weights[hd])
            spare = (1 - hd) * HEAD_DIM
            total = part[spare : spare + 1, :]
            log_total[0, hd : hd + 1, at] = tops[hd] + jnp.log(total)
            parts.append(part * (1.0 / total))
        out[at, :] = jnp.where(row_out < HEAD_DIM, parts[0], parts[1]).T.astype(bf16)

    @pl.when(step == pl.num_programs(0) - 1)
    def _():
        for band in range(4):
            rows_out_got(cot, cot_rows, send, recv, band)
        rows_out_sent(cot, cot_rows, send, recv)


def attend(q, k, v, bias, cot, qt=512):
    rows, width = q.shape
    pairs = width // 128
    blk = pl.BlockSpec((rows, 128), lambda i: (0, i))
    hbm = pl.BlockSpec(memory_space=pltpu.HBM)
    return pl.pallas_call(
        functools.partial(attend_kernel, qt),
        name="attend",
        grid=(pairs,),
        in_specs=[blk, blk, blk, pl.BlockSpec((rows, 128), lambda i: (0, 0)), hbm],
        out_specs=[blk, pl.BlockSpec((1, 2, rows), lambda i: (i, 0, 0)), hbm],
        out_shape=[
            jax.ShapeDtypeStruct((rows, width), bf16),
            jax.ShapeDtypeStruct((pairs, 2, rows), f32),
            jax.ShapeDtypeStruct((4, cot.shape[1] // 2, cot.shape[2]), bf16),
        ],
        scratch_shapes=[pltpu.SemaphoreType.DMA((4,))] * 2,
        compiler_params=params(collective_id=3, has_side_effects=True),
        cost_estimate=pl.CostEstimate(
            flops=16 * rows * rows * width, bytes_accessed=5 * 2**20, transcendentals=0
        ),
    )(q, k, v, bias, cot)


def attend_back_kernel(
    qt, q, k, v, bias, d_attn, log_total, out_rows, dq, dk, dv, out_home, dk_acc, dv_acc, send, recv
):
    step = pl.program_id(0)

    @pl.when(step == 0)
    def _():
        greet(column_peers())
        rows_back(out_rows, out_home, send, recv)

    rows, lanes = q.shape
    lane_k = lax.broadcasted_iota(jnp.int32, (rows, lanes), 1)
    lane_q = lax.broadcasted_iota(jnp.int32, (qt, lanes), 1)
    keys = [scores_keys(k[...], bias[...], hd, lane_k) for hd in range(2)]
    keys_only = [head_lanes(k[...], hd, lane_k) for hd in range(2)]
    values = [head_lanes(v[...], hd, lane_k) for hd in range(2)]
    for t in range(rows // qt):
        at = slice(t * qt, (t + 1) * qt)
        q_tile = q[at, :]
        d_tile = d_attn[at, :]
        dq_both = None
        for hd in range(2):
            q_head = head_lanes(q_tile, hd, lane_q)
            d_head = head_lanes(d_tile, hd, lane_q)
            s = dot(keys[hd], scores_queries(q_tile, hd, lane_q), 1, 1)
            p = jnp.exp(s - log_total[0, hd : hd + 1, at])
            d_p = dot(values[hd], d_tile, 1, 1)
            weighted = p * d_p
            delta = jnp.sum(weighted, 0, keepdims=True)
            ds = (weighted - p * delta).astype(bf16)
            dv_part = dot(p.astype(bf16), d_head)
            dk_part = dot(ds, q_head)
            if t == 0 and hd == 0:
                dv_acc[...] = dv_part
                dk_acc[...] = dk_part
            else:
                dv_acc[...] += dv_part
                dk_acc[...] += dk_part
            part = dot(keys_only[hd], ds, 0, 0)
            dq_both = part if dq_both is None else dq_both + part
        dq[at, :] = (dq_both.T * score_scale).astype(bf16)
    dk[...] = dk_acc[...].astype(bf16)
    dv[...] = dv_acc[...].astype(bf16)

    @pl.when(step == pl.num_programs(0) - 1)
    def _():
        for i in range(4):
            rows_back_got(out_rows, out_home, send, recv, i)
        rows_back_sent(out_rows, out_home, send, recv)


def attend_back(q, k, v, bias, d_attn, log_total, out_rows, qt=512):
    rows, width = q.shape
    pairs = width // 128
    blk = pl.BlockSpec((rows, 128), lambda i: (0, i))
    hbm = pl.BlockSpec(memory_space=pltpu.HBM)
    return pl.pallas_call(
        functools.partial(attend_back_kernel, qt),
        name="attend_back",
        grid=(pairs,),
        in_specs=[
            blk,
            blk,
            blk,
            pl.BlockSpec((rows, 128), lambda i: (0, 0)),
            blk,
            pl.BlockSpec((1, 2, rows), lambda i: (i, 0, 0)),
            hbm,
        ],
        out_specs=[blk] * 3 + [hbm],
        out_shape=[jax.ShapeDtypeStruct((rows, width), bf16)] * 3
        + [jax.ShapeDtypeStruct((2, 2 * out_rows.shape[1], out_rows.shape[2]), bf16)],
        scratch_shapes=[pltpu.VMEM((rows, 128), f32)] * 2 + [pltpu.SemaphoreType.DMA((4,))] * 2,
        compiler_params=params(collective_id=5, has_side_effects=True),
        cost_estimate=pl.CostEstimate(
            flops=40 * rows * rows * width, bytes_accessed=8 * 2**20, transcendentals=0
        ),
    )(q, k, v, bias, d_attn, log_total, out_rows)


def gelu_and_slope(u):
    u2 = u * u
    t = jnp.tanh(u * (0.7978845608028654 + (0.7978845608028654 * 0.044715) * u2))
    half = 0.5 + 0.5 * t
    slope = half * (
        1.0 + u * (1.0 - t) * (0.7978845608028654 + (3 * 0.7978845608028654 * 0.044715) * u2)
    )
    return u * half, slope


def mlp_kernel(h2, h2p, cot, res, *refs):
    (wu_a, bu_a, wd_a, wu_b, bu_b, wd_b) = refs[:6]
    (out, dh, dwd, dwu_a, dwu_b, dbu_a, dbu_b) = refs[6:13]
    (send_wd, send_wua, send_wub, got_wd, got_wua, got_wub, keep_a, keep_d, keep_b, send, recv) = refs[13:]
    step = pl.program_id(0)
    steps = pl.num_programs(0) - 1
    half = h2.shape[1] // 2
    it, bd, c, yx = place()
    sibling = (it + 1 - 2 * c, bd)
    slot = lax.rem(step, 2)
    before = 1 - slot

    def copies(at):
        pairs = ((send_wd, got_wd), (send_wua, got_wua), (send_wub, got_wub))
        return [
            remote(src.at[at], dst.at[at], send.at[i, at], recv.at[i, at], sibling)
            for i, (src, dst) in enumerate(pairs)
        ]

    @pl.when(step == 0)
    def _():
        greet([sibling])
        out[...] = res[...]
        dh[...] = jnp.zeros_like(dh)

    def tile(wu, bu, wd, dbu):
        up = dot(h2[...], wu[...]) + bu[...]
        d_act = dot(cot[...], wd[...], 1, 1)
        act, slope = gelu_and_slope(up)
        act = act.astype(bf16)
        d_up32 = d_act * slope
        d_up = d_up32.astype(bf16)
        dbu[0] = jnp.sum(d_up32, 0, keepdims=True)
        d_wd = dot(cot[...], act, 0, 0).astype(bf16)
        d_wu = dot(h2p[...], d_up, 0, 0).astype(bf16)
        out[...] += dot(act, wd[...])
        dh[...] += dot(d_up, wu[...], 1, 1)
        return d_wd, d_wu

    @pl.when(step >= 2)
    def _():
        for copy in copies(slot):
            copy.wait_send()

    @pl.when(step < steps)
    def _():
        d_wd, d_wu = tile(wu_a, bu_a, wd_a, dbu_a)
        send_wd[slot] = d_wd
        send_wua[slot] = d_wu[half:]
        keep_a[slot] = d_wu[:half]

    @pl.when(step > 0)
    def _():
        for copy in copies(before):
            copy.wait_recv()
        dwd[0] = keep_d[...] + got_wd[before]
        dwu_b[0] = keep_b[...] + got_wua[before]
        dwu_a[0] = keep_a[before] + got_wub[before]

    @pl.when(step < steps)
    def _():
        for copy in copies(slot)[:2]:
            copy.start()
        d_wd, d_wu = tile(wu_b, bu_b, wd_b, dbu_b)
        send_wub[slot] = d_wu[half:]
        copies(slot)[2].start()
        keep_b[...] = d_wu[:half]
        keep_d[...] = d_wd

    @pl.when(step == steps)
    def _():
        for copy in copies(before):
            copy.wait_send()


def mlp(core, h2, h2p, cot, res, w_up, b_up, w_down):
    rows, width = h2.shape
    ff = w_up.shape[1]
    tile = ff // 8
    half = width // 2
    steps = 4
    vmem = pl.BlockSpec(memory_space=pltpu.VMEM)
    now = lambda i: jnp.minimum(i, steps - 1)
    last = lambda i: jnp.maximum(i - 1, 0)
    at_a = lambda i: 2 * now(i) + 1 - lax.rem(lax.axis_index("items"), 2)
    at_b = lambda i: 2 * now(i) + lax.rem(lax.axis_index("items"), 2)
    w_specs = []
    for at in (at_a, at_b):
        w_specs += [
            pl.BlockSpec((width, tile), lambda i, at=at: (0, at(i))),
            pl.BlockSpec((1, tile), lambda i, at=at: (0, at(i))),
            pl.BlockSpec((tile, width), lambda i, at=at: (at(i), 0)),
        ]
    bias = pl.BlockSpec((1, 1, tile), lambda i: (now(i), 0, 0))
    up_grad = pl.BlockSpec((1, half, tile), lambda i: (last(i), 0, 0))
    dma = pltpu.SemaphoreType.DMA
    return pl.pallas_call(
        mlp_kernel,
        name="mlp",
        grid=(steps + 1,),
        in_specs=[vmem] * 4 + w_specs,
        out_specs=[
            vmem,
            vmem,
            pl.BlockSpec((1, width, tile), lambda i: (last(i), 0, 0)),
            up_grad,
            up_grad,
            bias,
            bias,
        ],
        out_shape=[jax.ShapeDtypeStruct((rows, width), f32)] * 2
        + [jax.ShapeDtypeStruct((steps, width, tile), bf16)]
        + [jax.ShapeDtypeStruct((steps, half, tile), bf16)] * 2
        + [jax.ShapeDtypeStruct((steps, 1, tile), f32)] * 2,
        scratch_shapes=(
            [pltpu.VMEM((2, width, tile), bf16)]
            + [pltpu.VMEM((2, half, tile), bf16)] * 2
        )
        * 2
        + [
            pltpu.VMEM((2, half, tile), bf16),
            pltpu.VMEM((width, tile), bf16),
            pltpu.VMEM((half, tile), bf16),
            dma((3, 2)),
            dma((3, 2)),
        ],
        compiler_params=params(collective_id=4, has_side_effects=True),
        cost_estimate=pl.CostEstimate(
            flops=2 * 6 * rows * width * ff, bytes_accessed=40 * 2**20, transcendentals=0
        ),
    )(h2, h2p, cot, res, w_up, b_up, w_down, w_up, b_up, w_down)


def share(n, rank, peer_of, src, buf, send, recv):
    copies = []
    for o in range(1, n):
        copy = pltpu.make_async_remote_copy(
            src_ref=src,
            dst_ref=buf.at[rank],
            send_sem=send.at[o],
            recv_sem=recv.at[o],
            device_id=peer_of(lax.rem(rank + o, n)),
            device_id_type=pl.DeviceIdType.MESH,
        )
        copy.start()
        copies.append(copy)
    buf[rank] = src[...]
    for copy in copies:
        copy.wait()
    added = buf[0]
    for i in range(1, n):
        added = added + buf[i]
    return added


def finish_kernel(n_items, n_band, patches, table, counts, g_rows, small, tok, batch, inv, d_tok, total, *refs):
    (got, buf_i, part, buf_b, send_g, recv_g, send_i, recv_i, send_b, recv_b) = refs
    it, bd, c, yx = place()
    others = []
    for o in range(1, n_items // 2):
        for k in range(2):
            others.append((lax.rem(yx + o, n_items // 2) * 2 + k, bd))
    greet(column_peers() + others)
    rows_back(g_rows, got, send_g, recv_g)
    part[...] = share(n_items, it, lambda p: (p, bd), small, buf_i, send_i, recv_i)
    total[...] = share(n_band, bd, lambda p: (it, p), part, buf_b, send_b, recv_b)
    slots, band_rows, width = tok.shape
    cut = band_rows // 2
    scale = inv[...] * patches[0]
    fix = -0.5 * scale * total[0:1, :]
    slope = -0.5 * scale * inv[...] * inv[...] * total[1:2, :]
    at = lax.broadcasted_iota(jnp.int32, (cut, width), 0) + bd * band_rows
    for q in range(4):
        s, h = q // 2, q % 2
        rows_back_got(g_rows, got, send_g, recv_g, q)
        now = pl.ds(h * cut, cut)
        valid = at + h * cut < counts[table[it * slots + s]]
        term = fix + slope * (tok[s, now].astype(f32) - batch[...])
        d_tok[s, now] = (got[s, now].astype(f32) + jnp.where(valid, term, 0.0)).astype(bf16)
    rows_back_sent(g_rows, got, send_g, recv_g)


def finish(patches, table, counts, g_rows, small, tok, batch, inv):
    n_items, n_band = lax.axis_size("items"), lax.axis_size("band")
    vmem = pl.BlockSpec(memory_space=pltpu.VMEM)
    smem = pl.BlockSpec(memory_space=pltpu.SMEM)
    dma = pltpu.SemaphoreType.DMA
    return pl.pallas_call(
        functools.partial(finish_kernel, n_items, n_band),
        name="finish",
        in_specs=[smem, smem, smem, pl.BlockSpec(memory_space=pltpu.HBM), vmem, vmem, vmem, vmem],
        out_specs=[vmem, vmem],
        out_shape=[
            jax.ShapeDtypeStruct(tok.shape, bf16),
            jax.ShapeDtypeStruct(small.shape, f32),
        ],
        scratch_shapes=[
            pltpu.VMEM(tok.shape, bf16),
            pltpu.VMEM((n_items,) + small.shape, f32),
            pltpu.VMEM(small.shape, f32),
            pltpu.VMEM((n_band,) + small.shape, f32),
        ]
        + [dma((4,))] * 2
        + [dma((n_items,))] * 2
        + [dma((n_band,))] * 2,
        compiler_params=params(collective_id=2, has_side_effects=True),
    )(patches, table, counts, g_rows, small, tok, batch, inv)


def join_kernel(core, attn_a, attn_b, wo_a, wo_b, tok, mean, inv, bo, gain, shift, res, h2, h2p):
    start = (tok[...].astype(f32) - mean[...]) * inv[...]
    r = start + (dot(attn_a[...], wo_a[...]) + dot(attn_b[...], wo_b[...])) + bo[...]
    res[...] = r
    centre = r - jnp.mean(r, -1, keepdims=True)
    spread = jnp.mean(centre * centre, -1, keepdims=True)
    h = (centre * lax.rsqrt(spread + epsilon) * gain[...] + shift[...]).astype(bf16)
    h2[...] = h
    half = h.shape[1] // 2
    width = h.shape[1] // 8
    even = core[0] == 0
    for x in range(4):
        first = h[:, 2 * x * width : (2 * x + 1) * width]
        second = h[:, (2 * x + 1) * width : (2 * x + 2) * width]
        h2p[:, x * width : (x + 1) * width] = jnp.where(even, first, second)
        h2p[:, half + x * width : half + (x + 1) * width] = jnp.where(even, second, first)


def join(core, attn, attn_recv, w_out, tok, mean, inv, bo, gain, shift, block=256):
    rows, half = attn_recv.shape
    width = 2 * half
    row = lambda i, c: (i, 0)
    one = lambda i, c: (0, 0)
    vec = pl.BlockSpec((1, width), one)
    act = pl.BlockSpec((block, half), row)
    full = pl.BlockSpec((block, width), row)
    return pl.pallas_call(
        join_kernel,
        name="join",
        grid_spec=pltpu.PrefetchScalarGridSpec(
            num_scalar_prefetch=1,
            grid=(rows // block,),
            in_specs=[
                act,
                act,
                pl.BlockSpec((half, width), lambda i, c: (c[0], 0)),
                pl.BlockSpec((half, width), lambda i, c: (1 - c[0], 0)),
                full,
                vec,
                vec,
                vec,
                vec,
                vec,
            ],
            out_specs=[full] * 3,
        ),
        out_shape=[
            jax.ShapeDtypeStruct((rows, width), f32),
            jax.ShapeDtypeStruct((rows, width), bf16),
            jax.ShapeDtypeStruct((rows, width), bf16),
        ],
        compiler_params=params(),
        cost_estimate=pl.CostEstimate(
            flops=2 * rows * width * width, bytes_accessed=8 * 2**20, transcendentals=0
        ),
    )(core, attn, attn_recv, w_out, w_out, tok, mean, inv, bo, gain, shift)


def unjoin_kernel(
    core, res, dh, cot, gain, attn_a, attn_b, wo_a, wo_b, d_res, da_a, da_b, dwo_a, dwo_b, sums, acc_a, acc_b
):
    step = pl.program_id(0)
    last = pl.num_programs(0) - 1
    r = res[...]
    centre = r - jnp.mean(r, -1, keepdims=True)
    spread = jnp.mean(centre * centre, -1, keepdims=True)
    scale = lax.rsqrt(spread + epsilon)
    z = centre * scale
    d_h = dh[...]
    dz = d_h * gain[...]
    dv = scale * (dz - jnp.mean(dz, -1, keepdims=True) - z * jnp.mean(dz * z, -1, keepdims=True))
    c32 = cot[...].astype(f32)
    full = c32 + dv
    d_res[...] = full
    low = full.astype(bf16)
    add_rows(step, sums, (d_h * z, d_h, low.astype(f32), c32))
    da_a[...] = dot(low, wo_a[...], 1, 1).astype(bf16)
    da_b[...] = dot(low, wo_b[...], 1, 1).astype(bf16)
    part_a = dot(attn_a[...], low, 0, 0)
    part_b = dot(attn_b[...], low, 0, 0)

    @pl.when(step == 0)
    def _():
        acc_a[...] = part_a
        acc_b[...] = part_b

    @pl.when(step > 0)
    def _():
        acc_a[...] += part_a
        acc_b[...] += part_b

    @pl.when(step == last)
    def _():
        dwo_a[...] = acc_a[...].astype(bf16)
        dwo_b[...] = acc_b[...].astype(bf16)


def add_rows(step, sums, arrays):
    for i, a in enumerate(arrays):
        total = jnp.sum(a, 0, keepdims=True)

        @pl.when(step == 0)
        def _():
            sums[i : i + 1, :] = total

        @pl.when(step > 0)
        def _():
            sums[i : i + 1, :] += total


def unjoin(core, res, dh, cot, gain, attn, attn_recv, w_out, block=256):
    rows, half = attn_recv.shape
    width = 2 * half
    row = lambda i, c: (i, 0)
    one = lambda i, c: (0, 0)
    act = pl.BlockSpec((block, half), row)
    full = pl.BlockSpec((block, width), row)
    grad = pl.BlockSpec((half, width), one)
    return pl.pallas_call(
        unjoin_kernel,
        name="unjoin",
        grid_spec=pltpu.PrefetchScalarGridSpec(
            num_scalar_prefetch=1,
            grid=(rows // block,),
            in_specs=[
                full,
                full,
                full,
                pl.BlockSpec((1, width), one),
                act,
                act,
                pl.BlockSpec((half, width), lambda i, c: (c[0], 0)),
                pl.BlockSpec((half, width), lambda i, c: (1 - c[0], 0)),
            ],
            out_specs=[full, act, act, grad, grad, pl.BlockSpec((4, width), one)],
            scratch_shapes=[pltpu.VMEM((half, width), f32)] * 2,
        ),
        out_shape=[
            jax.ShapeDtypeStruct((rows, width), f32),
            jax.ShapeDtypeStruct((rows, half), bf16),
            jax.ShapeDtypeStruct((rows, half), bf16),
            jax.ShapeDtypeStruct((half, width), bf16),
            jax.ShapeDtypeStruct((half, width), bf16),
            jax.ShapeDtypeStruct((4, width), f32),
        ],
        compiler_params=params(),
        cost_estimate=pl.CostEstimate(
            flops=4 * rows * width * width, bytes_accessed=12 * 2**20, transcendentals=0
        ),
    )(core, res, dh, cot, gain, attn, attn_recv, w_out, w_out)


def unproject_kernel(core, h1, dq, dk, dv, dq_r, dk_r, dv_r, wq, wk, wv, dw, dh, sums):
    step = pl.program_id(0)
    for i, d in enumerate((dq, dk, dv)):
        dw[i] = dot(h1[...], d[...], 0, 0).astype(bf16)
    total = dot(dq_r[...], wq[...], 1, 1)
    total = total + dot(dk_r[...], wk[...], 1, 1)
    total = total + dot(dv_r[...], wv[...], 1, 1)
    dh[...] = total.astype(bf16)

    @pl.when(step == 0)
    def _():
        sums[0:1, :] = jnp.sum(dq[...].astype(f32), 0, keepdims=True)
        sums[1:2, :] = jnp.sum(dv[...].astype(f32), 0, keepdims=True)


def unproject(core, h1, dq, dk, dv, wq, wk, wv, blocks=4):
    rows, width = h1.shape
    half = width // 2
    rb, cb = rows // blocks, width // blocks
    one = lambda i, c: (0, 0)
    whole = pl.BlockSpec((rows, half), one)
    part = pl.BlockSpec((rb, half), lambda i, c: (i, 0))
    w = pl.BlockSpec((width, half), lambda i, c: (0, c[0]))
    return pl.pallas_call(
        unproject_kernel,
        name="unproject",
        grid_spec=pltpu.PrefetchScalarGridSpec(
            num_scalar_prefetch=1,
            grid=(blocks,),
            in_specs=[pl.BlockSpec((rows, cb), lambda i, c: (0, i))]
            + [whole] * 3
            + [part] * 3
            + [w] * 3,
            out_specs=[
                pl.BlockSpec((3, cb, half), lambda i, c: (0, i, 0)),
                pl.BlockSpec((rb, width), lambda i, c: (i, 0)),
                pl.BlockSpec((2, half), one),
            ],
        ),
        out_shape=[
            jax.ShapeDtypeStruct((3, width, half), bf16),
            jax.ShapeDtypeStruct((rows, width), bf16),
            jax.ShapeDtypeStruct((2, half), f32),
        ],
        compiler_params=params(),
        cost_estimate=pl.CostEstimate(
            flops=12 * rows * width * half, bytes_accessed=14 * 2**20, transcendentals=0
        ),
    )(core, h1, dq, dk, dv, dq, dk, dv, wq, wk, wv)


def start_back_kernel(tok, mean, inv, gain, dh_a, dh_b, d_res, g_out, sums):
    step = pl.program_id(0)
    centred = tok[...].astype(f32) - mean[...]
    start = centred * inv[...]
    centre = start - jnp.mean(start, -1, keepdims=True)
    spread = jnp.mean(centre * centre, -1, keepdims=True)
    scale = lax.rsqrt(spread + epsilon)
    z = centre * scale
    d_h = dh_a[...].astype(f32) + dh_b[...].astype(f32)
    dz = d_h * gain[...]
    dv = scale * (dz - jnp.mean(dz, -1, keepdims=True) - z * jnp.mean(dz * z, -1, keepdims=True))
    d_start = d_res[...] + dv
    g_out[...] = (d_start * inv[...]).astype(bf16)
    add_rows(step, sums, (d_start, d_start * centred, d_h * z, d_h))


def start_back(tok, mean, inv, gain, dh, dh_recv, d_res, block=256):
    rows, width = d_res.shape
    full = pl.BlockSpec((block, width), lambda i: (i, 0))
    vec = pl.BlockSpec((1, width), lambda i: (0, 0))
    return pl.pallas_call(
        start_back_kernel,
        name="start_back",
        grid=(rows // block,),
        in_specs=[full, vec, vec, vec, full, full, full],
        out_specs=[full, pl.BlockSpec((4, width), lambda i: (0, 0))],
        out_shape=[
            jax.ShapeDtypeStruct((rows, width), bf16),
            jax.ShapeDtypeStruct((4, width), f32),
        ],
        compiler_params=params(),
        cost_estimate=pl.CostEstimate(flops=2**22, bytes_accessed=8 * 2**20, transcendentals=0),
    )(tok, mean, inv, gain, dh, dh_recv, d_res)


def pick(array, index, axis=0):
    return lax.dynamic_index_in_dim(array, index, axis, keepdims=False)


def column_layer(
    tokens, cotangent, running_mean, running_var, slot_table, patch_counts,
    ln1_gain, ln1_bias, w_query, b_query, w_key, w_value, b_value, w_out, b_out,
    ln2_gain, ln2_bias, w_up, b_up, w_down, b_down,
):
    n_items, n_band = lax.axis_size("items"), lax.axis_size("band")
    slots, band_rows, width = tokens.shape
    cut = band_rows // 2
    it = lax.axis_index("items")
    bd = lax.axis_index("band")
    c, yx = lax.rem(it, 2), it // 2
    x, y = lax.rem(yx, 2), yx // 2
    core = c.astype(jnp.int32).reshape(1)
    devices = [(i, b) for i in range(n_items) for b in range(n_band)]

    def permute(array, to):
        pairs = []
        for i, b in devices:
            j, d = to(i, b)
            pairs.append((i * n_band + b, j * n_band + d))
        return lax.ppermute(array, ("items", "band"), pairs)

    to_core = lambda i, b: (i ^ 1, b)
    to_x = lambda i, b: (i ^ 2, b)
    to_y = lambda i, b: (i ^ 4, b)
    to_z1 = lambda i, b: (i, b ^ 1)
    to_z2 = lambda i, b: (i, b ^ 2)

    item_count = pick(patch_counts, pick(slot_table, yx * 4 + bd))
    gathered, sums = gather(slot_table, patch_counts, tokens)
    tok = gathered.reshape(8 * cut, width)

    patch_total = jnp.sum(patch_counts).astype(f32)
    batch_mean = sums[0] / patch_total
    batch_var = sums[1] / patch_total - batch_mean * batch_mean
    new_mean = momentum * running_mean + momentum * batch_mean
    new_var = momentum * running_var + momentum * batch_var
    inverse = lax.rsqrt(new_var + epsilon)
    mean_row, inv_row = new_mean.reshape(1, -1), inverse.reshape(1, -1)
    as_row = lambda a: a.astype(f32).reshape(1, -1)

    at = jnp.arange(4 * cut, dtype=jnp.int32)
    at = (at // cut) * band_rows + at % cut
    at = jnp.concatenate([at + c * cut, at + (1 - c) * cut])
    bias = jnp.where(at < item_count, 0.0, masked_score).astype(bf16)
    bias = jnp.broadcast_to(bias[:, None], (8 * cut, 128))

    h1, q, k, v = project(
        core, tok, mean_row, inv_row, as_row(ln1_gain), as_row(ln1_bias),
        w_query, w_key, w_value, as_row(b_query), as_row(b_value),
    )
    attn, log_total, cot_rows = attend(q, k, v, bias, cotangent)
    rows = 4 * cut
    cot_rows = cot_rows.reshape(rows, width)
    attn_recv = permute(attn[rows:], to_core)
    res, h2, h2p = join(
        core, attn, attn_recv, w_out, tok, mean_row, inv_row, as_row(b_out), as_row(ln2_gain), as_row(ln2_bias)
    )
    total, d_h2, d_down, d_up_a, d_up_b, dbu_a, dbu_b = mlp(
        core, h2, h2p, cot_rows, res, w_up, as_row(b_up), w_down
    )
    d_down_part, d_up_part = [], []
    down = d_down.reshape(2, 2, width, -1)
    up = jnp.stack([d_up_a, d_up_b]).reshape(2, 2, 2, 2, 2, -1, d_up_a.shape[-1])
    for j in range(2):
        d_down_part.append((pick(down[j], x), permute(pick(down[j], 1 - x), to_x)))
        got = permute(pick(up[:, j], 1 - y, 2), to_y)
        keep = pick(up[:, j], y, 2)
        send = pick(keep, 1 - x, 2) + pick(got, 1 - x, 2)
        keep = pick(keep, x, 2) + pick(got, x, 2)
        got = permute(send, to_x)
        b_low = lax.rem(bd, 2)
        send = pick(keep, 1 - b_low, 1) + pick(got, 1 - b_low, 1)
        keep = pick(keep, b_low, 1) + pick(got, b_low, 1)
        d_up_part.append((keep, permute(send, to_z1)))
    b_low, b_high = lax.rem(bd, 2), bd // 2

    def add(pair):
        return pair[0] + pair[1]

    def pick_pair(pairs, index):
        keep = jnp.stack([p[0] for p in pairs])
        got = jnp.stack([p[1] for p in pairs])
        return pick(keep, index) + pick(got, index)

    send = pick_pair(d_down_part, 1 - y)
    keep = pick_pair(d_down_part, y)
    got = permute(send, to_y)
    tile = keep.shape[-1]
    keep, got = (a.reshape(2, 2, -1, tile) for a in (keep, got))
    send = pick(keep, 1 - b_low, 1) + pick(got, 1 - b_low, 1)
    keep = pick(keep, b_low, 1) + pick(got, b_low, 1)
    got = permute(send, to_z1)
    send = pick(keep, 1 - b_high) + pick(got, 1 - b_high)
    keep = pick(keep, b_high) + pick(got, b_high)
    got = permute(send, to_z2)
    d_w_down = (keep.astype(f32) + got.astype(f32)).T
    send = pick_pair(d_up_part, 1 - b_high)
    keep = pick_pair(d_up_part, b_high)
    got = permute(send, to_z2)
    d_w_up = keep.astype(f32) + got.astype(f32)
    d_w_up = jnp.where(
        c == 0,
        jnp.concatenate([d_w_up[1], d_w_up[0]], 1),
        jnp.concatenate([d_w_up[0], d_w_up[1]], 1),
    )
    d_bias_up = jnp.where(
        c == 0,
        jnp.concatenate([dbu_b[:, 0], dbu_a[:, 0]], 1),
        jnp.concatenate([dbu_a[:, 0], dbu_b[:, 0]], 1),
    )
    out_rows = (total + as_row(b_down)).astype(bf16).reshape(4, cut, width)

    d_res, da_own, da_send, dwo_a, dwo_b, sums_two = unjoin(
        core, res, d_h2, cot_rows, as_row(ln2_gain), attn, attn_recv, w_out
    )
    da_recv = permute(da_send, to_core)
    dq, dk, dv, output = attend_back(
        q, k, v, bias, jnp.concatenate([da_own, da_recv]), log_total, out_rows
    )
    dw, dh1, sums_qv = unproject(core, h1, dq, dk, dv, w_query, w_key, w_value)

    dwo = jnp.stack([dwo_a, dwo_b]).reshape(2, 2, 2, -1, width)
    got = permute(pick(dwo, 1 - c, 2), to_core)[::-1]
    keep = pick(dwo, c, 2)
    rel = y ^ c
    send = pick(keep, 1 - rel) + pick(got, 1 - rel)
    keep = pick(keep, rel) + pick(got, rel)
    got = permute(send, to_y)
    send = pick(keep, 1 - x) + pick(got, 1 - x)
    keep = pick(keep, x) + pick(got, x)
    got = permute(send, to_x)
    fourth = width // 4
    keep, got = (a.reshape(-1, 2, 2, fourth) for a in (keep, got))
    send = pick(keep, 1 - b_low, 2) + pick(got, 1 - b_low, 2)
    keep = pick(keep, b_low, 2) + pick(got, b_low, 2)
    got = permute(send, to_z1)
    send = pick(keep, 1 - b_high, 1) + pick(got, 1 - b_high, 1)
    keep = pick(keep, b_high, 1) + pick(got, b_high, 1)
    got = permute(send, to_z2)
    d_w_out = keep.astype(f32) + got.astype(f32)

    dw = dw.reshape(3, 2, 2, 2, -1, width // 2)
    got = permute(pick(dw, 1 - c, 3), to_core)
    dw = jnp.stack([pick(dw, c, 3), got])
    send, keep = pick(dw, 1 - x, 3), pick(dw, x, 3)
    got = permute(send, to_x)
    send = pick(keep, 1 - y, 2) + pick(got, 1 - y, 2)
    keep = pick(keep, y, 2) + pick(got, y, 2)
    got = permute(send, to_y)
    rel = b_high ^ c
    keep, got = (a.reshape(2, 3, -1, 2, fourth) for a in (keep, got))
    send = pick(keep, 1 - b_low, 3) + pick(got, 1 - b_low, 3)
    keep = pick(keep, b_low, 3) + pick(got, b_low, 3)
    got = permute(send, to_z1)
    send = pick(keep, 1 - rel) + pick(got, 1 - rel)
    keep = pick(keep, rel) + pick(got, rel)
    got = permute(send, to_z2)
    d_qkv = keep.astype(f32) + got.astype(f32)

    dh_recv = permute(dh1[rows:], to_core)
    g_rows, sums_one = start_back(tok, mean_row, inv_row, as_row(ln1_gain), dh1, dh_recv, d_res)
    empty = jnp.zeros_like(sums_qv)
    halves = jnp.where(
        c == 0,
        jnp.concatenate([sums_qv, empty], 1),
        jnp.concatenate([empty, sums_qv], 1),
    )
    d_tokens, small = finish(
        (1.0 / patch_total).reshape(1), slot_table, patch_counts, g_rows.reshape(4, cut, width),
        jnp.concatenate([sums_one, halves, sums_two, d_bias_up]), tokens,
        batch_mean.reshape(1, -1), inv_row,
    )
    d_gain_one, d_shift_one, d_bq, d_bv, d_gain_two, d_shift_two, d_bo, d_bdown = (
        small[i] for i in range(2, 10)
    )
    d_bup = small[10:].reshape(-1)
    return (
        output, d_tokens, new_mean, new_var, d_gain_one, d_shift_one,
        d_qkv[0], d_bq, d_qkv[1], d_qkv[2], d_bv, d_w_out, d_bo, d_gain_two, d_shift_two,
        d_w_up, d_bup, d_w_down, d_bdown,
    )


def layer_norm(value, gain, shift):
    centre = value - jnp.mean(value, -1, keepdims=True)
    spread = jnp.mean(centre * centre, -1, keepdims=True)
    return centre * lax.rsqrt(spread + epsilon) * gain + shift


def gelu_tanh(value):
    return (
        0.5
        * value
        * (1.0 + jnp.tanh(0.7978845608028654 * (value + 0.044715 * value * value * value)))
    )


def head_layout():
    heads_per = 4
    return (heads_per, HEADS // heads_per, heads_per * HEAD_DIM)


def group_scores(q_part, k_part, key_mask):
    scores = (
        jnp.einsum("rhd,khd->hrk", q_part, k_part, preferred_element_type=jnp.float32) * score_scale
    )
    return jnp.where(key_mask[None, None, :], scores, masked_score)


def attend_forward(q_slot, keys_slot, values_slot, key_mask):
    heads_per, groups, group_width = head_layout()
    band_rows = q_slot.shape[0]
    seq_length = keys_slot.shape[0]

    def head_block(group_index):
        begin = group_index * group_width
        q_part = lax.dynamic_slice_in_dim(q_slot, begin, group_width, 1).reshape(
            band_rows, heads_per, HEAD_DIM
        )
        k_part = lax.dynamic_slice_in_dim(keys_slot, begin, group_width, 1).reshape(
            seq_length, heads_per, HEAD_DIM
        )
        v_part = lax.dynamic_slice_in_dim(values_slot, begin, group_width, 1).reshape(
            seq_length, heads_per, HEAD_DIM
        )
        scores = group_scores(q_part, k_part, key_mask)
        top_score = jnp.max(scores, -1, keepdims=True)
        log_total = top_score + jnp.log(jnp.sum(jnp.exp(scores - top_score), -1, keepdims=True))
        probs_low = jnp.exp(scores - log_total).astype(jnp.bfloat16)
        attended = jnp.einsum("hrk,khd->rhd", probs_low, v_part, preferred_element_type=jnp.float32)
        return (attended.reshape(band_rows, group_width), log_total[..., 0])

    attended, log_totals = lax.map(head_block, jnp.arange(groups, dtype=jnp.int32))
    return (attended.transpose(1, 0, 2).reshape(band_rows, groups * group_width), log_totals)


def attend_backward(q_slot, keys_slot, values_slot, key_mask, d_attn_slot, row_delta, log_totals):
    heads_per, groups, group_width = head_layout()
    query_rows = q_slot.shape[0]
    seq_length = keys_slot.shape[0]
    deltas = jnp.transpose(row_delta).reshape(groups, heads_per, query_rows)

    def head_block(inputs):
        group_index, log_total, delta_part = inputs
        begin = group_index * group_width
        q_part = lax.dynamic_slice_in_dim(q_slot, begin, group_width, 1).reshape(
            query_rows, heads_per, HEAD_DIM
        )
        k_part = lax.dynamic_slice_in_dim(keys_slot, begin, group_width, 1).reshape(
            seq_length, heads_per, HEAD_DIM
        )
        v_part = lax.dynamic_slice_in_dim(values_slot, begin, group_width, 1).reshape(
            seq_length, heads_per, HEAD_DIM
        )
        d_part = lax.dynamic_slice_in_dim(d_attn_slot, begin, group_width, 1).reshape(
            query_rows, heads_per, HEAD_DIM
        )
        scores = group_scores(q_part, k_part, key_mask)
        probs = jnp.exp(scores - log_total[..., None])
        d_probs = jnp.einsum("rhd,khd->hrk", d_part, v_part, preferred_element_type=jnp.float32)
        d_scores = (probs * (d_probs - delta_part[..., None])).astype(jnp.bfloat16)
        results = []
        d_q_part = (
            jnp.einsum("hrk,khd->rhd", d_scores, k_part, preferred_element_type=jnp.float32)
            * score_scale
        )
        results.append(d_q_part.reshape(query_rows, group_width))
        probs_low = probs.astype(jnp.bfloat16)
        d_k_part = (
            jnp.einsum("hrk,rhd->khd", d_scores, q_part, preferred_element_type=jnp.float32)
            * score_scale
        )
        d_v_part = jnp.einsum("hrk,rhd->khd", probs_low, d_part, preferred_element_type=jnp.float32)
        results.append(d_k_part.reshape(seq_length, group_width))
        results.append(d_v_part.reshape(seq_length, group_width))
        return tuple(results)

    mapped = lax.map(head_block, (jnp.arange(groups, dtype=jnp.int32), log_totals, deltas))
    full_width = groups * group_width
    return tuple((piece.transpose(1, 0, 2).reshape(piece.shape[1], full_width) for piece in mapped))


def local(
    tokens,
    cotangent,
    running_mean,
    running_var,
    slot_table,
    patch_counts,
    ln1_gain,
    ln1_bias,
    w_query,
    b_query,
    w_key,
    w_value,
    b_value,
    w_out,
    b_out,
    ln2_gain,
    ln2_bias,
    w_up,
    b_up,
    w_down,
    b_down,
):
    slot_count, band_rows, model_width = tokens.shape
    seq_length = band_rows * lax.axis_size("band")
    item_rank = lax.axis_index("items")
    band_rank = lax.axis_index("band")
    every_slot = jnp.arange(slot_table.shape[0], dtype=jnp.int32)
    my_slots = item_rank * slot_count + jnp.arange(slot_count, dtype=jnp.int32)
    item_ids = jnp.sum(
        jnp.where(every_slot[None, :] == my_slots[:, None], slot_table[None, :], 0), 1
    )
    lengths = jnp.sum(
        jnp.where(every_slot[None, :] == item_ids[:, None], patch_counts[None, :], 0), 1
    )
    key_mask = jnp.arange(seq_length, dtype=jnp.int32)[None, :] < lengths[:, None]
    row_mask = (band_rank * band_rows + jnp.arange(band_rows, dtype=jnp.int32))[None, :] < lengths[
        :, None
    ]
    row_keep = row_mask.astype(jnp.float32).reshape(-1, 1)
    raw_flat = tokens.astype(jnp.float32).reshape(-1, model_width)
    part_one = jnp.sum(row_keep * raw_flat, 0)
    part_two = jnp.sum(row_keep * raw_flat * raw_flat, 0)
    total_one, total_two = lax.psum((part_one, part_two), ("items", "band"))
    patch_total = jnp.sum(patch_counts).astype(jnp.float32)
    batch_mean = total_one / patch_total
    batch_var = total_two / patch_total - batch_mean * batch_mean
    new_mean = momentum * running_mean + momentum * batch_mean
    new_var = momentum * running_var + momentum * batch_var
    inverse = lax.rsqrt(new_var + epsilon)
    normed_in = (raw_flat - new_mean) * inverse
    gain_one = ln1_gain.astype(jnp.float32)
    shift_one = ln1_bias.astype(jnp.float32)
    gain_two = ln2_gain.astype(jnp.float32)
    shift_two = ln2_bias.astype(jnp.float32)
    h_one_full, norm_one_back = jax.vjp(layer_norm, normed_in, gain_one, shift_one)
    h_one = h_one_full.astype(jnp.bfloat16)
    queries = (
        jnp.dot(h_one, w_query, preferred_element_type=jnp.float32) + b_query.astype(jnp.float32)
    ).astype(jnp.bfloat16)
    key_local = (
        jnp.dot(h_one, w_key, preferred_element_type=jnp.float32)
        .astype(jnp.bfloat16)
        .reshape(slot_count, band_rows, model_width)
    )
    value_local = (
        (jnp.dot(h_one, w_value, preferred_element_type=jnp.float32) + b_value.astype(jnp.float32))
        .astype(jnp.bfloat16)
        .reshape(slot_count, band_rows, model_width)
    )
    keys_all, values_all = (
        lax.all_gather(key_local, "band", axis=1, tiled=True),
        lax.all_gather(value_local, "band", axis=1, tiled=True),
    )
    q_slots = queries.reshape(slot_count, band_rows, model_width)
    attended_list = []
    totals_list = []
    for slot_index in range(slot_count):
        attended, log_totals = attend_forward(
            q_slots[slot_index], keys_all[slot_index], values_all[slot_index], key_mask[slot_index]
        )
        attended_list.append(attended)
        totals_list.append(log_totals)
    attn_full = jnp.concatenate(attended_list, 0)
    attn_low = attn_full.astype(jnp.bfloat16)
    residual = (
        normed_in
        + jnp.dot(attn_low, w_out, preferred_element_type=jnp.float32)
        + b_out.astype(jnp.float32)
    )
    h_two_full, norm_two_back = jax.vjp(layer_norm, residual, gain_two, shift_two)
    h_two = h_two_full.astype(jnp.bfloat16)
    up_proj = jnp.dot(h_two, w_up, preferred_element_type=jnp.float32) + b_up.astype(jnp.float32)
    activated_full, gelu_back = jax.vjp(gelu_tanh, up_proj)
    activated = activated_full.astype(jnp.bfloat16)
    result = (
        residual
        + jnp.dot(activated, w_down, preferred_element_type=jnp.float32)
        + b_down.astype(jnp.float32)
    )
    output = result.astype(jnp.bfloat16).reshape(slot_count, band_rows, model_width)
    cot_low = cotangent.reshape(-1, model_width)
    cot_full = cot_low.astype(jnp.float32)
    d_w_down = jnp.einsum("tf,td->fd", activated, cot_low, preferred_element_type=jnp.float32)
    d_b_down = jnp.sum(cot_full, 0)
    d_activated = jnp.einsum("td,fd->tf", cot_low, w_down, preferred_element_type=jnp.float32)
    (d_up_full,) = gelu_back(d_activated)
    d_up = d_up_full.astype(jnp.bfloat16)
    d_w_up = jnp.einsum("td,tf->df", h_two, d_up, preferred_element_type=jnp.float32)
    d_b_up = jnp.sum(d_up, 0, dtype=jnp.float32)
    d_h_two = jnp.einsum("tf,df->td", d_up, w_up, preferred_element_type=jnp.float32)
    d_res_norm, d_gain_two, d_shift_two = norm_two_back(d_h_two)
    d_residual = cot_full + d_res_norm
    d_branch = d_residual.astype(jnp.bfloat16)
    d_w_out = jnp.einsum("td,te->de", attn_low, d_branch, preferred_element_type=jnp.float32)
    d_b_out = jnp.sum(d_branch, 0, dtype=jnp.float32)
    d_attn = jnp.einsum("te,de->td", d_branch, w_out, preferred_element_type=jnp.float32).astype(
        jnp.bfloat16
    )
    row_delta = jnp.sum(
        (d_attn.astype(jnp.float32) * attn_full).reshape(slot_count, band_rows, HEADS, HEAD_DIM), -1
    )
    d_attn_slots = d_attn.reshape(slot_count, band_rows, model_width)
    back_keys, back_values = (keys_all, values_all)
    d_q_list = []
    d_k_list = []
    d_v_list = []
    for slot_index in range(slot_count):
        d_q_slot, d_k_slot, d_v_slot = attend_backward(
            q_slots[slot_index],
            back_keys[slot_index],
            back_values[slot_index],
            key_mask[slot_index],
            d_attn_slots[slot_index],
            row_delta[slot_index],
            totals_list[slot_index],
        )
        d_q_list.append(d_q_slot)
        d_k_list.append(d_k_slot)
        d_v_list.append(d_v_slot)
    d_keys_mine, d_values_mine = (
        lax.psum_scatter(
            jnp.stack(d_k_list).astype(jnp.bfloat16), "band", scatter_dimension=1, tiled=True
        ).astype(jnp.float32),
        lax.psum_scatter(
            jnp.stack(d_v_list).astype(jnp.bfloat16), "band", scatter_dimension=1, tiled=True
        ).astype(jnp.float32),
    )
    d_queries = jnp.concatenate(d_q_list, 0).astype(jnp.bfloat16)
    d_keys = d_keys_mine.reshape(-1, model_width).astype(jnp.bfloat16)
    d_values = d_values_mine.reshape(-1, model_width).astype(jnp.bfloat16)
    d_w_query = jnp.einsum("td,te->de", h_one, d_queries, preferred_element_type=jnp.float32)
    d_b_query = jnp.sum(d_queries, 0, dtype=jnp.float32)
    d_w_key = jnp.einsum("td,te->de", h_one, d_keys, preferred_element_type=jnp.float32)
    d_w_value = jnp.einsum("td,te->de", h_one, d_values, preferred_element_type=jnp.float32)
    d_b_value = jnp.sum(d_values, 0, dtype=jnp.float32)
    d_h_one = jnp.einsum("te,de->td", d_queries, w_query, preferred_element_type=jnp.float32)
    d_h_one = d_h_one + jnp.einsum("te,de->td", d_keys, w_key, preferred_element_type=jnp.float32)
    d_h_one = d_h_one + jnp.einsum(
        "te,de->td", d_values, w_value, preferred_element_type=jnp.float32
    )
    d_start_norm, d_gain_one, d_shift_one = norm_one_back(d_h_one)
    d_start = d_residual + d_start_norm
    centred = raw_flat - new_mean
    small_sums = lax.psum(
        (
            jnp.sum(d_start, 0),
            jnp.sum(d_start * centred, 0),
            d_gain_one,
            d_shift_one,
            d_b_query,
            d_b_value,
            d_b_out,
            d_gain_two,
            d_shift_two,
            d_b_up,
            d_b_down,
        ),
        ("items", "band"),
    )
    sum_g = small_sums[0]
    sum_gx = small_sums[1]
    cube = inverse * inverse * inverse
    d_raw = d_start * inverse + row_keep * (
        -0.5 * inverse * sum_g / patch_total
        - 0.5 * cube * sum_gx * (raw_flat - batch_mean) / patch_total
    )
    d_tokens = d_raw.astype(jnp.bfloat16).reshape(slot_count, band_rows, model_width)
    weight_grads = (
        lax.psum_scatter(
            d_w_query.astype(jnp.bfloat16), "items", scatter_dimension=0, tiled=True
        ).astype(jnp.float32),
        lax.psum_scatter(
            d_w_key.astype(jnp.bfloat16), "items", scatter_dimension=0, tiled=True
        ).astype(jnp.float32),
        lax.psum_scatter(
            d_w_value.astype(jnp.bfloat16), "items", scatter_dimension=0, tiled=True
        ).astype(jnp.float32),
        lax.psum_scatter(
            d_w_out.astype(jnp.bfloat16), "items", scatter_dimension=0, tiled=True
        ).astype(jnp.float32),
        lax.psum_scatter(
            d_w_up.astype(jnp.bfloat16), "items", scatter_dimension=0, tiled=True
        ).astype(jnp.float32),
        lax.psum_scatter(
            d_w_down.astype(jnp.bfloat16), "items", scatter_dimension=0, tiled=True
        ).astype(jnp.float32),
    )
    weight_grads = (
        lax.psum_scatter(
            weight_grads[0].astype(jnp.bfloat16), "band", scatter_dimension=1, tiled=True
        ).astype(jnp.float32),
        lax.psum_scatter(
            weight_grads[1].astype(jnp.bfloat16), "band", scatter_dimension=1, tiled=True
        ).astype(jnp.float32),
        lax.psum_scatter(
            weight_grads[2].astype(jnp.bfloat16), "band", scatter_dimension=1, tiled=True
        ).astype(jnp.float32),
        lax.psum_scatter(
            weight_grads[3].astype(jnp.bfloat16), "band", scatter_dimension=1, tiled=True
        ).astype(jnp.float32),
        lax.psum_scatter(
            weight_grads[4].astype(jnp.bfloat16), "band", scatter_dimension=1, tiled=True
        ).astype(jnp.float32),
        lax.psum_scatter(
            weight_grads[5].astype(jnp.bfloat16), "band", scatter_dimension=1, tiled=True
        ).astype(jnp.float32),
    )
    return (
        output,
        d_tokens,
        new_mean,
        new_var,
        small_sums[2],
        small_sums[3],
        weight_grads[0],
        small_sums[4],
        weight_grads[1],
        weight_grads[2],
        small_sums[5],
        weight_grads[3],
        small_sums[6],
        small_sums[7],
        small_sums[8],
        weight_grads[4],
        small_sums[9],
        weight_grads[5],
        small_sums[10],
    )


def solution(mesh):
    columns = mesh.shape["items"] == 8 and mesh.shape["band"] == 4
    return jax.shard_map(
        column_layer if columns else local,
        mesh=mesh,
        in_specs=(
            P("items", "band", None),
            P("items", "band", None),
            P(),
            P(),
            P(),
            P(),
            P(),
            P(),
            P(),
            P(),
            P(),
            P(),
            P(),
            P(),
            P(),
            P(),
            P(),
            P(),
            P(),
            P(),
            P(),
        ),
        out_specs=(
            P("items", "band", None),
            P("items", "band", None),
            P(),
            P(),
            P(),
            P(),
            P("items", "band"),
            P(),
            P("items", "band"),
            P("items", "band"),
            P(),
            P("items", "band"),
            P(),
            P(),
            P(),
            P("items", "band"),
            P(),
            P("items", "band"),
            P(),
        ),
        check_vma=False,
    )
```

```python
import functools
import jax
import jax.numpy as jnp
from jax import lax
from jax.experimental import pallas as pl
from jax.experimental.pallas import tpu as pltpu
from jax.sharding import PartitionSpec as P

HEADS = 16
HEAD_DIM = 64
epsilon = 1e-05
score_scale = 0.125
masked_score = -1e30
momentum = 0.5
f32 = jnp.float32
bf16 = jnp.bfloat16
VMEM_LIMIT = 60 * 2**20
R_MEAN, R_VAR, R_G1, R_S1, R_BQ, R_BV, R_BO, R_G2, R_S2, R_BD, R_BU = range(11)
S_MEAN, S_VAR, S_BATCH, S_INV = range(4)


def dot(a, b, ca=1, cb=0):
    return lax.dot_general(a, b, (((ca,), (cb,)), ((), ())), preferred_element_type=f32)


def params(**kw):
    return pltpu.CompilerParams(vmem_limit_bytes=VMEM_LIMIT, **kw)


def place():
    it, bd = lax.axis_index("items"), lax.axis_index("band")
    return it, bd, lax.rem(it, 2), it // 2


def remote(src, dst, send, recv, to):
    return pltpu.make_async_remote_copy(
        src_ref=src,
        dst_ref=dst,
        send_sem=send,
        recv_sem=recv,
        device_id=to,
        device_id_type=pl.DeviceIdType.MESH,
    )


def greet(peers):
    barrier = pltpu.get_barrier_semaphore()
    for peer in peers:
        pl.semaphore_signal(barrier, inc=1, device_id=peer, device_id_type=pl.DeviceIdType.MESH)
    pl.semaphore_wait(barrier, len(peers))


def column_peers():
    it, bd, c, yx = place()
    peers = [(it, lax.rem(bd + o, 4)) for o in range(1, 4)]
    return peers + [(it + 1 - 2 * c, lax.rem(bd + o, 4)) for o in range(4)]


def rows_out(src, dst, send, recv):
    it, bd, c, yx = place()
    cut = src.shape[1] // 2
    for q in range(4):
        s, h = q // 2, q % 2
        block = src.at[s, pl.ds(h * cut, cut)]
        target = dst.at[bd]
        own = (c == h) & (bd == 2 * c + s)

        @pl.when(own)
        def _():
            pltpu.make_async_copy(block, target, recv.at[bd]).start()

        @pl.when(jnp.logical_not(own))
        def _():
            remote(block, target, send.at[q], recv.at[bd], (yx * 2 + h, 2 * c + s)).start()


def rows_out_sent(src, dst, send, recv):
    it, bd, c, yx = place()
    cut = src.shape[1] // 2
    for q in range(4):
        s, h = q // 2, q % 2
        own = (c == h) & (bd == 2 * c + s)

        @pl.when(jnp.logical_not(own))
        def _():
            block = src.at[s, pl.ds(h * cut, cut)]
            remote(block, dst.at[bd], send.at[q], recv.at[bd], (yx * 2 + h, 2 * c + s)).wait_send()


def rows_out_got(src, dst, send, recv, band):
    it, bd, c, yx = place()
    cut = src.shape[1] // 2
    pltpu.make_async_copy(src.at[0, pl.ds(0, cut)], dst.at[band], recv.at[band]).wait()


def rows_back(src, dst, send, recv):
    it, bd, c, yx = place()
    cut = src.shape[1]
    home = bd // 2
    s = lax.rem(bd, 2)
    target = dst.at[s, pl.ds(pl.multiple_of(c * cut, cut), cut)]
    got = recv.at[2 * s + c]
    for r in range(4):
        own = (home == c) & (bd == r)

        @pl.when(own)
        def _():
            pltpu.make_async_copy(src.at[r], target, got).start()

        @pl.when(jnp.logical_not(own))
        def _():
            remote(src.at[r], target, send.at[r], got, (yx * 2 + home, r)).start()


def rows_back_sent(src, dst, send, recv):
    it, bd, c, yx = place()
    cut = src.shape[1]
    home = bd // 2
    for r in range(4):
        own = (home == c) & (bd == r)

        @pl.when(jnp.logical_not(own))
        def _():
            target = dst.at[0, pl.ds(0, cut)]
            remote(src.at[r], target, send.at[r], recv.at[0], (yx * 2 + home, r)).wait_send()


def rows_back_got(src, dst, send, recv, q):
    cut = src.shape[1]
    s, h = q // 2, q % 2
    pltpu.make_async_copy(src.at[0], dst.at[s, pl.ds(h * cut, cut)], recv.at[q]).wait()


def share_start(n, rank, peer_of, src, buf, send, recv):
    copies = []
    for o in range(1, n):
        to = peer_of(lax.rem(rank + o, n))
        copies.append(remote(src, buf.at[rank], send.at[o], recv.at[o], to))
        copies[-1].start()
    buf[rank] = src[...]
    return copies


def share_end(n, copies, buf):
    for copy in copies:
        copy.wait()
    added = buf[0]
    for i in range(1, n):
        added = added + buf[i]
    return added


def all_peers(n_items):
    it, bd, c, yx = place()
    others = []
    for o in range(1, n_items // 2):
        for k in range(2):
            others.append((lax.rem(yx + o, n_items // 2) * 2 + k, bd))
    return column_peers() + others


def gather_kernel(n_items, n_band, table, counts, vecs, tok, rows, stat, one, buf_i, part, buf_b, *sems):
    (send_t, recv_t, send_s, recv_s, send_i, recv_i, send_b, recv_b) = sems
    it, bd, c, yx = place()
    sibling = (it + 1 - 2 * c, bd)
    greet(all_peers(n_items))
    rows_out(tok, rows, send_t, recv_t)
    slots, band_rows, width = tok.shape
    at = lax.broadcasted_iota(jnp.int32, (band_rows, width), 0) + bd * band_rows
    first = jnp.zeros((1, width), f32)
    second = jnp.zeros((1, width), f32)
    for s in range(slots):
        x = jnp.where(at < counts[table[it * slots + s]], tok[s].astype(f32), 0.0)
        first = first + jnp.sum(x, 0, keepdims=True)
        second = second + jnp.sum(x * x, 0, keepdims=True)
    one[0:1, :] = first
    one[1:2, :] = second
    copies = share_start(n_items, it, lambda p: (p, bd), one, buf_i, send_i, recv_i)
    part[...] = share_end(n_items, copies, buf_i)
    copies = share_start(n_band, bd, lambda p: (it, p), part, buf_b, send_b, recv_b)
    sums = share_end(n_band, copies, buf_b) / patch_total(counts, (1, width))
    mean = sums[0:1]
    var = sums[1:2] - mean * mean
    new_var = momentum * vecs[R_VAR : R_VAR + 1, :] + momentum * var
    stat[S_MEAN : S_MEAN + 1, :] = momentum * vecs[R_MEAN : R_MEAN + 1, :] + momentum * mean
    stat[S_VAR : S_VAR + 1, :] = new_var
    stat[S_BATCH : S_BATCH + 1, :] = mean
    stat[S_INV : S_INV + 1, :] = lax.rsqrt(new_var + epsilon)
    hand = []
    for o in range(4):
        band = lax.rem(bd + o, 4)
        rows_out_got(tok, rows, send_t, recv_t, band)
        copy = remote(rows.at[band], rows.at[4 + band], send_s.at[o], recv_s.at[o], sibling)
        copy.start()
        hand.append(copy)
    for copy in hand:
        copy.wait()
    rows_out_sent(tok, rows, send_t, recv_t)


def patch_total(counts, shape):
    total = counts[0]
    for i in range(1, counts.shape[0]):
        total = total + counts[i]
    return jnp.full(shape, total, jnp.int32).astype(f32)


VMEM = pl.BlockSpec(memory_space=pltpu.VMEM)
SMEM = pl.BlockSpec(memory_space=pltpu.SMEM)
HBM = pl.BlockSpec(memory_space=pltpu.HBM)
DMA = pltpu.SemaphoreType.DMA


def gather(table, counts, vecs, tok):
    n_items, n_band = lax.axis_size("items"), lax.axis_size("band")
    slots, band_rows, width = tok.shape
    return pl.pallas_call(
        functools.partial(gather_kernel, n_items, n_band),
        name="gather",
        in_specs=[SMEM, SMEM, VMEM, VMEM],
        out_specs=[HBM, VMEM],
        out_shape=[
            jax.ShapeDtypeStruct((8, band_rows // 2, width), bf16),
            jax.ShapeDtypeStruct((4, width), f32),
        ],
        scratch_shapes=[
            pltpu.VMEM((2, width), f32),
            pltpu.VMEM((n_items, 2, width), f32),
            pltpu.VMEM((2, width), f32),
            pltpu.VMEM((n_band, 2, width), f32),
        ]
        + [DMA((4,))] * 4
        + [DMA((n_items,))] * 2
        + [DMA((n_band,))] * 2,
        compiler_params=params(collective_id=1, has_side_effects=True),
    )(table, counts, vecs, tok)


def half_lanes(ref, row, half):
    at = pl.multiple_of(lax.rem(lax.axis_index("items"), 2) * half, 128)
    return ref[row : row + 1, pl.ds(at, half)]


def project_kernel(stat, vecs, tok, wq, wk, wv, h1, q, k, v):
    half = q.shape[1]
    start = (tok[...].astype(f32) - stat[S_MEAN : S_MEAN + 1, :]) * stat[S_INV : S_INV + 1, :]
    centre = start - jnp.mean(start, -1, keepdims=True)
    spread = jnp.mean(centre * centre, -1, keepdims=True)
    h = centre * lax.rsqrt(spread + epsilon) * vecs[R_G1 : R_G1 + 1, :] + vecs[R_S1 : R_S1 + 1, :]
    h = h.astype(bf16)
    h1[...] = h
    q[...] = ((dot(h, wq[...]) + half_lanes(vecs, R_BQ, half)).astype(bf16) * score_scale).astype(bf16)
    k[...] = dot(h, wk[...]).astype(bf16)
    v[...] = (dot(h, wv[...]) + half_lanes(vecs, R_BV, half)).astype(bf16)


def project(stat, vecs, tok, wq, wk, wv, block=256):
    rows, width = tok.shape
    half = width // 2
    w = pl.BlockSpec((width, half), lambda i: (0, lax.rem(lax.axis_index("items"), 2)))
    full = pl.BlockSpec((block, width), lambda i: (i, 0))
    part = pl.BlockSpec((block, half), lambda i: (i, 0))
    return pl.pallas_call(
        project_kernel,
        name="project",
        grid=(rows // block,),
        in_specs=[VMEM, VMEM, full, w, w, w],
        out_specs=[full] + [part] * 3,
        out_shape=[jax.ShapeDtypeStruct((rows, width), bf16)]
        + [jax.ShapeDtypeStruct((rows, half), bf16)] * 3,
        compiler_params=params(),
        cost_estimate=pl.CostEstimate(
            flops=6 * rows * width * half, bytes_accessed=12 * 2**20, transcendentals=0
        ),
    )(stat, vecs, tok, wq, wk, wv)


def head_lanes(array, head, lane):
    keep = (lane >= head * HEAD_DIM) & (lane < (head + 1) * HEAD_DIM)
    return jnp.where(keep, array, jnp.zeros_like(array))


def with_spare(array, spare_value, head, lane):
    spare = (1 - head) * HEAD_DIM
    return jnp.where(lane == spare, spare_value, head_lanes(array, head, lane))


def ones_beside(array, head, lane):
    return with_spare(array, jnp.ones_like(array), head, lane)


def key_bias(table, counts, shape):
    it, bd, c, yx = place()
    cut = shape[0] // 8
    row = lax.broadcasted_iota(jnp.int32, shape, 0)
    there = row >= 4 * cut
    row = jnp.where(there, row - 4 * cut, row)
    band = row // cut
    half = jnp.where(there, 1 - c, c)
    position = band * (2 * cut) + half * cut + (row - band * cut)
    return jnp.where(position < counts[table[yx * 4 + bd]], 0.0, masked_score).astype(bf16)


def attend_kernel(qt, table, counts, q, k, v, cot, out, log_total, cot_rows, out_sib, part_sib, *sems):
    (send, recv, send_s, recv_s) = sems
    step = pl.program_id(0)
    rows, lanes = q.shape
    own = rows // 2
    it, bd, c, yx = place()
    sibling = (it + 1 - 2 * c, bd)

    @pl.when(step == 0)
    def _():
        greet(column_peers())
        rows_out(cot, cot_rows, send, recv)

    lane_k = lax.broadcasted_iota(jnp.int32, (rows, lanes), 1)
    lane_q = lax.broadcasted_iota(jnp.int32, (qt, lanes), 1)
    row_out = lax.broadcasted_iota(jnp.int32, (lanes, qt), 0)
    bias = key_bias(table, counts, (rows, lanes))
    keys = [with_spare(k[...], bias, hd, lane_k) for hd in range(2)]
    values = [ones_beside(v[...], hd, lane_k).T for hd in range(2)]
    for t in range(rows // qt):
        at = slice(t * qt, (t + 1) * qt)
        scores = [dot(keys[hd], ones_beside(q[at, :], hd, lane_q), 1, 1) for hd in range(2)]
        tops = [jnp.max(s, 0, keepdims=True) for s in scores]
        weights = [jnp.exp(s - top).astype(bf16) for s, top in zip(scores, tops)]
        parts = []
        for hd in range(2):
            part = dot(values[hd], weights[hd])
            spare = (1 - hd) * HEAD_DIM
            total = part[spare : spare + 1, :]
            log_total[0, hd : hd + 1, at] = tops[hd] + jnp.log(total)
            parts.append(part * (1.0 / total))
        both = jnp.where(row_out < HEAD_DIM, parts[0], parts[1]).T.astype(bf16)
        if t * qt < own:
            out[at, :] = both
        else:
            part_sib[step, t * qt - own : (t + 1) * qt - own, :] = both

    def hand(i):
        return remote(
            part_sib.at[i],
            out_sib.at[:, pl.ds(pl.multiple_of(i * lanes, lanes), lanes)],
            send_s.at[i],
            recv_s.at[i],
            sibling,
        )

    hand(step).start()

    @pl.when(step == pl.num_programs(0) - 1)
    def _():
        for i in range(part_sib.shape[0]):
            hand(i).wait()
        for band in range(4):
            rows_out_got(cot, cot_rows, send, recv, band)
        rows_out_sent(cot, cot_rows, send, recv)


def attend(table, counts, q, k, v, cot, qt=512):
    rows, width = q.shape
    pairs = width // 128
    blk = pl.BlockSpec((rows, 128), lambda i: (0, i))
    return pl.pallas_call(
        functools.partial(attend_kernel, qt),
        name="attend",
        grid=(pairs,),
        in_specs=[SMEM, SMEM, blk, blk, blk, HBM],
        out_specs=[
            pl.BlockSpec((rows // 2, 128), lambda i: (0, i)),
            pl.BlockSpec((1, 2, rows), lambda i: (i, 0, 0)),
            HBM,
            HBM,
        ],
        out_shape=[
            jax.ShapeDtypeStruct((rows // 2, width), bf16),
            jax.ShapeDtypeStruct((pairs, 2, rows), f32),
            jax.ShapeDtypeStruct((4, cot.shape[1] // 2, cot.shape[2]), bf16),
            jax.ShapeDtypeStruct((rows // 2, width), bf16),
        ],
        scratch_shapes=[pltpu.VMEM((pairs, rows // 2, 128), bf16)]
        + [DMA((4,))] * 2
        + [DMA((pairs,))] * 2,
        compiler_params=params(collective_id=3, has_side_effects=True),
        cost_estimate=pl.CostEstimate(
            flops=16 * rows * rows * width, bytes_accessed=5 * 2**20, transcendentals=0
        ),
    )(table, counts, q, k, v, cot)


def half_rows(ref, which, half):
    return ref[pl.ds(pl.multiple_of(which * half, 128), half), :]


def join_kernel(stat, vecs, attn_a, attn_b, wo, tok, res, h2, h2p):
    it, bd, c, yx = place()
    half = attn_a.shape[1]
    start = (tok[...].astype(f32) - stat[S_MEAN : S_MEAN + 1, :]) * stat[S_INV : S_INV + 1, :]
    r = dot(attn_a[...], half_rows(wo, c, half)) + dot(attn_b[...], half_rows(wo, 1 - c, half))
    r = start + r + vecs[R_BO : R_BO + 1, :]
    res[...] = r
    centre = r - jnp.mean(r, -1, keepdims=True)
    spread = jnp.mean(centre * centre, -1, keepdims=True)
    h = centre * lax.rsqrt(spread + epsilon) * vecs[R_G2 : R_G2 + 1, :] + vecs[R_S2 : R_S2 + 1, :]
    h = h.astype(bf16)
    h2[...] = h
    width = h.shape[1] // 8
    for x in range(4):
        first = h[:, 2 * x * width : (2 * x + 1) * width]
        second = h[:, (2 * x + 1) * width : (2 * x + 2) * width]
        h2p[:, x * width : (x + 1) * width] = jnp.where(c == 0, first, second)
        h2p[:, half + x * width : half + (x + 1) * width] = jnp.where(c == 0, second, first)


def join(stat, vecs, attn, attn_sib, w_out, tok, block=256):
    rows, half = attn.shape
    width = 2 * half
    act = pl.BlockSpec((block, half), lambda i: (i, 0))
    full = pl.BlockSpec((block, width), lambda i: (i, 0))
    return pl.pallas_call(
        join_kernel,
        name="join",
        grid=(rows // block,),
        in_specs=[VMEM, VMEM, act, act, VMEM, full],
        out_specs=[full] * 3,
        out_shape=[
            jax.ShapeDtypeStruct((rows, width), f32),
            jax.ShapeDtypeStruct((rows, width), bf16),
            jax.ShapeDtypeStruct((rows, width), bf16),
        ],
        compiler_params=params(),
        cost_estimate=pl.CostEstimate(
            flops=2 * rows * width * width, bytes_accessed=8 * 2**20, transcendentals=0
        ),
    )(stat, vecs, attn, attn_sib, w_out, tok)


def gelu_and_slope(u):
    u2 = u * u
    t = jnp.tanh(u * (0.7978845608028654 + (0.7978845608028654 * 0.044715) * u2))
    half = 0.5 + 0.5 * t
    slope = half * (
        1.0 + u * (1.0 - t) * (0.7978845608028654 + (3 * 0.7978845608028654 * 0.044715) * u2)
    )
    return u * half, slope


def mlp_kernel(vecs, h2, h2p, cot, res, *refs):
    (wu_a, wd_a, wu_b, wd_b) = refs[:4]
    (out_low, dh, dwd, dwu_a, dwu_b, dbu_a, dbu_b) = refs[4:11]
    (send_wd, send_wua, send_wub, got_wd, got_wua, got_wub, keep_a, keep_d, keep_b, out) = refs[11:21]
    (send, recv) = refs[21:]
    step = pl.program_id(0)
    steps = pl.num_programs(0) - 1
    half = h2.shape[1] // 2
    it, bd, c, yx = place()
    sibling = (it + 1 - 2 * c, bd)
    slot = lax.rem(step, 2)
    before = 1 - slot

    def copies(at, which=(0, 1, 2)):
        pairs = ((send_wd, got_wd), (send_wua, got_wua), (send_wub, got_wub))
        return [
            remote(pairs[i][0].at[at], pairs[i][1].at[at], send.at[i, at], recv.at[i, at], sibling)
            for i in which
        ]

    @pl.when(step == 0)
    def _():
        greet([sibling])
        out[...] = res[...]
        dh[...] = jnp.zeros_like(dh)

    def tile(wu, wd, dbu, which):
        lanes = pl.ds(pl.multiple_of(which * wu.shape[1], 128), wu.shape[1])
        up = dot(h2[...], wu[...]) + vecs[pl.ds(R_BU + step, 1), lanes]
        d_act = dot(cot[...], wd[...], 1, 1)
        act, slope = gelu_and_slope(up)
        act = act.astype(bf16)
        d_up32 = d_act * slope
        d_up = d_up32.astype(bf16)
        dbu[0] = jnp.sum(d_up32, 0, keepdims=True)
        d_wd = dot(cot[...], act, 0, 0).astype(bf16)
        d_wu = dot(h2p[...], d_up, 0, 0).astype(bf16)
        out[...] += dot(act, wd[...])
        dh[...] += dot(d_up, wu[...], 1, 1)
        return d_wd, d_wu

    @pl.when(step >= 2)
    def _():
        for copy in copies(slot):
            copy.wait_send()

    @pl.when(step < steps)
    def _():
        d_wd, d_wu = tile(wu_a, wd_a, dbu_a, 1 - c)
        send_wd[slot] = d_wd
        send_wua[slot] = d_wu[half:]
        keep_a[slot] = d_wu[:half]

    @pl.when(step > 0)
    def _():
        for copy in copies(before):
            copy.wait_recv()
        dwd[0] = keep_d[...] + got_wd[before]
        dwu_b[0] = keep_b[...] + got_wua[before]
        dwu_a[0] = keep_a[before] + got_wub[before]

    @pl.when(step < steps)
    def _():
        for copy in copies(slot, (0, 1)):
            copy.start()
        d_wd, d_wu = tile(wu_b, wd_b, dbu_b, c)
        send_wub[slot] = d_wu[half:]
        copies(slot, (2,))[0].start()
        keep_b[...] = d_wu[:half]
        keep_d[...] = d_wd

    @pl.when(step == steps)
    def _():
        out_low[...] = (out[...] + vecs[R_BD : R_BD + 1, :]).astype(bf16)
        for copy in copies(before):
            copy.wait_send()


def mlp(vecs, h2, h2p, cot, res, w_up, w_down):
    rows, width = h2.shape
    ff = w_up.shape[1]
    tile = ff // 8
    half = width // 2
    steps = 4
    now = lambda i: jnp.minimum(i, steps - 1)
    last = lambda i: jnp.maximum(i - 1, 0)
    at_a = lambda i: 2 * now(i) + 1 - lax.rem(lax.axis_index("items"), 2)
    at_b = lambda i: 2 * now(i) + lax.rem(lax.axis_index("items"), 2)
    w_specs = []
    for at in (at_a, at_b):
        w_specs += [
            pl.BlockSpec((width, tile), lambda i, at=at: (0, at(i))),
            pl.BlockSpec((tile, width), lambda i, at=at: (at(i), 0)),
        ]
    bias = pl.BlockSpec((1, 1, tile), lambda i: (now(i), 0, 0))
    up_grad = pl.BlockSpec((1, half, tile), lambda i: (last(i), 0, 0))
    return pl.pallas_call(
        mlp_kernel,
        name="mlp",
        grid=(steps + 1,),
        in_specs=[VMEM] * 5 + w_specs,
        out_specs=[
            VMEM,
            VMEM,
            pl.BlockSpec((1, width, tile), lambda i: (last(i), 0, 0)),
            up_grad,
            up_grad,
            bias,
            bias,
        ],
        out_shape=[jax.ShapeDtypeStruct((rows, width), bf16)]
        + [jax.ShapeDtypeStruct((rows, width), f32)]
        + [jax.ShapeDtypeStruct((steps, width, tile), bf16)]
        + [jax.ShapeDtypeStruct((steps, half, tile), bf16)] * 2
        + [jax.ShapeDtypeStruct((steps, 1, tile), f32)] * 2,
        scratch_shapes=(
            [pltpu.VMEM((2, width, tile), bf16)]
            + [pltpu.VMEM((2, half, tile), bf16)] * 2
        )
        * 2
        + [
            pltpu.VMEM((2, half, tile), bf16),
            pltpu.VMEM((width, tile), bf16),
            pltpu.VMEM((half, tile), bf16),
            pltpu.VMEM((rows, width), f32),
            DMA((3, 2)),
            DMA((3, 2)),
        ],
        compiler_params=params(collective_id=4, has_side_effects=True),
        cost_estimate=pl.CostEstimate(
            flops=2 * 6 * rows * width * ff, bytes_accessed=40 * 2**20, transcendentals=0
        ),
    )(vecs, h2, h2p, cot, res, w_up, w_down, w_up, w_down)


def norm_back(z, scale, dz):
    return scale * (dz - jnp.mean(dz, -1, keepdims=True) - z * jnp.mean(dz * z, -1, keepdims=True))


def normalize(value):
    centre = value - jnp.mean(value, -1, keepdims=True)
    scale = lax.rsqrt(jnp.mean(centre * centre, -1, keepdims=True) + epsilon)
    return centre * scale, scale


def tail_kernel(n_items, n_band, qt, *refs):
    (table, counts, stat, vecs, dbu_a, dbu_b, log_total) = refs[:7]
    (res_h, dh_h, cot_h, out_rows, attn_h, attn_sib_h, wo_h, q_h, k_h, v_h, h1_h) = refs[7:18]
    (wq_h, wk_h, wv_h, tok_h, down_h, up_a_h, up_b_h, tokens_h) = refs[18:26]
    (out_home, d_tok, total, o_down, o_up, o_wo, o_wq, o_wk, o_wv) = refs[26:35]
    (res, dh, cot, low, wo, attn, attn_sib, kd, rd1, rd2, rd3, rd4) = refs[35:47]
    (ku, ru1, ru2, ru3, ru4, q, k, v, da, da_send, dk_acc, dv_acc) = refs[47:59]
    (h1, wq, wk, wv, tok, gw, gw_core, gw1, gw2, gw3, gw4) = refs[59:70]
    (gp, gp_core, gqk1, gv1, gqk2, gv2, gp3, gp4, home) = refs[70:79]
    (small, buf_i, part, buf_b, buf_i2, part2, buf_b2) = refs[79:86]
    (send, recv, lsem, send_r, recv_r, send_g, recv_g, send_i, recv_i, send_b, recv_b) = refs[86:97]

    it, bd, c, yx = place()
    x, y = lax.rem(yx, 2), yx // 2
    bl, bh = lax.rem(bd, 2), bd // 2
    sibling = (it + 1 - 2 * c, bd)
    to_x, to_y = (it + 2 - 4 * x, bd), (it + 4 - 8 * y, bd)
    to_z1, to_z2 = (it, bd + 1 - 2 * bl), (it, lax.rem(bd + 2, 4))
    rows, width = res.shape
    half = width // 2
    fourth = width // 4
    tile = kd.shape[-1]
    sent = []

    def load(src, dst):
        copy = pltpu.make_async_copy(src, dst, lsem.at[len(loads)])
        copy.start()
        loads.append(copy)
        return copy

    def push(src, dst, to):
        i = len(sent)
        copy = remote(src, dst, send.at[i], recv.at[i], to)
        copy.start()
        sent.append(copy)
        return copy

    loads = []
    greet(all_peers(n_items))

    def down_first(yy):
        return push(down_h.at[2 * yy + 1 - x], rd1.at[yy], to_x)

    def up_first(high):
        got = []
        for low_bit in range(2):
            for i, up in enumerate((up_a_h, up_b_h)):
                src = up.at[2 * high + low_bit, pl.ds(pl.multiple_of((1 - y) * tile // 2, 128), tile // 2)]
                got.append(push(src, ru1.at[high, low_bit, i], to_y))
        return got

    d1 = [down_first(1 - y)]
    u1 = up_first(0)
    rows_back(out_rows, out_home, send_r, recv_r)

    get_res, get_dh, get_cot = load(res_h, res), load(dh_h, dh), load(cot_h, cot)
    get_wo, get_attn, get_sib = load(wo_h, wo), load(attn_h, attn), load(attn_sib_h, attn_sib)
    get_qkv = [load(src, dst) for src, dst in ((q_h, q), (k_h, k), (v_h, v))]
    get_kd = [load(down_h.at[2 * yy + x], kd.at[yy]) for yy in range(2)]
    get_ku = []
    for high in range(2):
        for low_bit in range(2):
            for i, up in enumerate((up_a_h, up_b_h)):
                src = up.at[2 * high + low_bit, pl.ds(pl.multiple_of(y * tile // 2, 128), tile // 2)]
                get_ku.append(load(src, ku.at[high, low_bit, i]))
    lanes = pl.ds(pl.multiple_of(c * half, 128), half)
    get_h1 = load(h1_h, h1)
    get_w = [load(src.at[:, lanes], dst) for src, dst in ((wq_h, wq), (wk_h, wk), (wv_h, wv))]
    get_tok = load(tok_h.at[pl.ds(0, rows)], tok)

    small[...] = jnp.zeros_like(small)
    for i in range(4):
        for src, h in ((dbu_a, 1 - c), (dbu_b, c)):
            small[4 + i : 5 + i, pl.ds(pl.multiple_of(h * half, 128), half)] = src[i]
    for copy in (get_res, get_dh, get_cot, get_wo):
        copy.wait()
    block = 256

    @pl.loop(0, rows // block)
    def _(i):
        at = pl.ds(pl.multiple_of(i * block, block), block)
        z, scale = normalize(res[at, :])
        d_h = dh[at, :]
        c32 = cot[at, :].astype(f32)
        full = c32 + norm_back(z, scale, d_h * vecs[R_G2 : R_G2 + 1, :])
        res[at, :] = full
        d_low = full.astype(bf16)
        low[at, :] = d_low
        for j, term in enumerate((d_h * z, d_h, d_low.astype(f32), c32)):
            small[j : j + 1, :] += jnp.sum(term, 0, keepdims=True)
        da[at, :] = dot(d_low, half_rows(wo, c, half), 1, 1).astype(bf16)
        da_send[at, :] = dot(d_low, half_rows(wo, 1 - c, half), 1, 1).astype(bf16)

    da_copy = push(da_send, da.at[pl.ds(rows, rows)], sibling)
    d1.append(down_first(y))
    u1 += up_first(1)

    get_attn.wait()
    get_sib.wait()
    for i, heads in enumerate((attn, attn_sib)):
        for xx in range(2):
            part_wo = dot(heads[:, xx * fourth : (xx + 1) * fourth], low[...], 0, 0).astype(bf16)
            for cc in range(2):
                gw[i, xx, cc] = part_wo[cc * fourth // 2 : (cc + 1) * fourth // 2]
    core_w = [push(gw.at[i, :, 1 - c], gw_core.at[1 - i], sibling) for i in range(2)]
    early = share_start(
        n_items, it, lambda p: (p, bd), small.at[pl.ds(0, 8)], buf_i, send_i.at[0], recv_i.at[0]
    )

    for copy in get_qkv:
        copy.wait()
    da_copy.wait_recv()
    lane_k = lax.broadcasted_iota(jnp.int32, (2 * rows, 128), 1)
    lane_q = lax.broadcasted_iota(jnp.int32, (qt, 128), 1)

    def pair(i):
        at_lanes = pl.ds(pl.multiple_of(i * 128, 128), 128)
        k_pair, v_pair = k[:, at_lanes], v[:, at_lanes]
        bias = key_bias(table, counts, k_pair.shape)
        keys = [with_spare(k_pair, bias, hd, lane_k) for hd in range(2)]
        keys_only = [head_lanes(k_pair, hd, lane_k) for hd in range(2)]
        values = [head_lanes(v_pair, hd, lane_k) for hd in range(2)]
        for t in range(2 * rows // qt):
            at = slice(t * qt, (t + 1) * qt)
            q_tile, d_tile = q[at, at_lanes], da[at, at_lanes]
            dq_both = None
            for hd in range(2):
                q_head = head_lanes(q_tile, hd, lane_q)
                d_head = head_lanes(d_tile, hd, lane_q)
                s = dot(keys[hd], ones_beside(q_tile, hd, lane_q), 1, 1)
                p = jnp.exp(s - log_total[i, hd : hd + 1, at])
                d_p = dot(values[hd], d_tile, 1, 1)
                weighted = p * d_p
                delta = jnp.sum(weighted, 0, keepdims=True)
                ds = (weighted - p * delta).astype(bf16)
                dv_part = dot(p.astype(bf16), d_head)
                dk_part = dot(ds, q_head)
                if t == 0 and hd == 0:
                    dv_acc[...] = dv_part
                    dk_acc[...] = dk_part
                else:
                    dv_acc[...] += dv_part
                    dk_acc[...] += dk_part
                term = dot(keys_only[hd], ds, 0, 0)
                dq_both = term if dq_both is None else dq_both + term
            q[at, at_lanes] = (dq_both.T * score_scale).astype(bf16)
        k[:, at_lanes] = dk_acc[...].astype(bf16)
        v[:, at_lanes] = dv_acc[...].astype(bf16)

    @pl.loop(0, 2)
    def _(i):
        pair(i)

    part[...] = share_end(n_items, early, buf_i)
    early = share_start(
        n_band, bd, lambda p: (it, p), part, buf_b, send_b.at[0], recv_b.at[0]
    )
    for copy in get_kd:
        copy.wait()
    d1[0].wait_recv()
    kd[1 - y] += rd1[1 - y]
    d2 = push(kd.at[1 - y], rd2, to_y)
    for copy in get_ku:
        copy.wait()

    def up_second(high):
        for copy in u1[4 * high : 4 * high + 4]:
            copy.wait_recv()
        ku[high] += ru1[high]
        return push(ku.at[high, :, :, pl.ds(pl.multiple_of((1 - x) * tile // 4, 128), tile // 4)], ru2.at[high], to_x)

    u2 = [up_second(0)]
    for i in range(2):
        core_w[i].wait_recv()
    for i in range(2):
        gw[i, :, c] += gw_core[i]
    rel_y = lax.rem(y + c, 2)
    w1 = push(gw.at[1 - rel_y, :, c], gw1, to_y)

    @pl.loop(2, q.shape[1] // 128)
    def _(i):
        pair(i)

    total[0:8, :] = share_end(n_band, early, buf_b)

    get_h1.wait()
    core_p = []
    for j in range(4):
        for i, d in enumerate((q, k, v)):
            part_p = dot(h1[:, j * fourth : (j + 1) * fourth], d[...], 0, 0).astype(bf16)
            for cc in range(2):
                gp[i, j, cc] = part_p[cc * fourth // 2 : (cc + 1) * fourth // 2]
        core_p.append(push(gp.at[:, j, 1 - c], gp_core.at[:, j], sibling))
    for i, d in ((0, q), (1, v)):
        row = jnp.sum(d[...].astype(f32), 0, keepdims=True)
        small[12 + i : 13 + i, pl.ds(pl.multiple_of(c * half, 128), half)] = row

    for copy in get_w:
        copy.wait()
    dh1, dh1_sib = wo, low

    @pl.loop(0, 2 * rows // block)
    def _(i):
        at = pl.ds(pl.multiple_of(lax.rem(i + rows // block, 2 * rows // block) * block, block), block)
        term = dot(q[at, :], wq[...], 1, 1) + dot(k[at, :], wk[...], 1, 1)
        dh1[at, :] = (term + dot(v[at, :], wv[...], 1, 1)).astype(bf16)

    dh_copy = push(dh1.at[pl.ds(rows, rows)], dh1_sib, sibling)
    for copy in core_p:
        copy.wait_recv()
    qk1, v1 = [], []
    for j in range(2):
        yx_x = 2 * j + 1 - x
        qk1.append(push(gp.at[pl.ds(0, 2), yx_x, c], gqk1.at[0, j], to_x))
        qk1.append(push(gp_core.at[pl.ds(0, 2), yx_x], gqk1.at[1, j], to_x))
        yx_y = 2 * (1 - y) + j
        v1.append(push(gp.at[2, yx_y, c], gv1.at[0, j], to_y))
        v1.append(push(gp_core.at[2, yx_y], gv1.at[1, j], to_y))

    get_tok.wait()
    dh_copy.wait_recv()
    g_rows = cot

    @pl.loop(0, rows // block)
    def _(i):
        at = pl.ds(pl.multiple_of(i * block, block), block)
        inv = stat[S_INV : S_INV + 1, :]
        centred = tok[at, :].astype(f32) - stat[S_MEAN : S_MEAN + 1, :]
        z, scale = normalize(centred * inv)
        d_h = dh1[at, :].astype(f32) + dh1_sib[at, :].astype(f32)
        d_start = res[at, :] + norm_back(z, scale, d_h * vecs[R_G1 : R_G1 + 1, :])
        g_rows[at, :] = (d_start * inv).astype(bf16)
        for j, term in enumerate((d_start, d_start * centred, d_h * z, d_h)):
            small[8 + j : 9 + j, :] += jnp.sum(term, 0, keepdims=True)

    late = share_start(
        n_items, it, lambda p: (p, bd), small.at[pl.ds(8, 8)], buf_i2, send_i.at[1], recv_i.at[1]
    )
    g_blocks = g_rows.reshape(4, rows // 4, width)
    rows_back(g_blocks, home, send_g, recv_g)
    part2[...] = share_end(n_items, late, buf_i2)
    late = share_start(
        n_band, bd, lambda p: (it, p), part2, buf_b2, send_b.at[1], recv_b.at[1]
    )

    d1[1].wait_recv()
    kd[y] += rd1[y]
    u2.append(up_second(1))
    sums = share_end(n_band, late, buf_b2)
    total[8:16, :] = sums

    count = patch_total(counts, (1, width))
    inv = stat[S_INV : S_INV + 1, :]
    fix = -0.5 * inv * sums[0:1, :] / count
    slope = -0.5 * inv * inv * inv * sums[1:2, :] / count
    cut = rows // 4
    position = lax.broadcasted_iota(jnp.int32, (cut, width), 0) + bd * (2 * cut)
    for i in range(4):
        s, h = i // 2, i % 2
        rows_back_got(g_blocks, home, send_g, recv_g, i)
        now = pl.ds(h * cut, cut)
        valid = position + h * cut < counts[table[it * 2 + s]]
        term = fix + slope * (tokens_h[s, now, :].astype(f32) - stat[S_BATCH : S_BATCH + 1, :])
        d_tok[s, now, :] = (home[s, now, :].astype(f32) + jnp.where(valid, term, 0.0)).astype(bf16)

    d2.wait_recv()
    kd[y] += rd2[...]
    blocks = kd.reshape(2, 2, 2, width // 4, tile)
    d3 = push(blocks.at[y, :, 1 - bl], rd3, to_z1)
    w1.wait_recv()
    gw[rel_y, :, c] += gw1[...]
    w2 = push(gw.at[rel_y, 1 - x, c], gw2, to_x)
    for copy in v1:
        copy.wait_recv()
    for j in range(2):
        gp[2, 2 * y + j, c] += gv1[0, j]
        gp_core[2, 2 * y + j] += gv1[1, j]
    v2 = [
        push(gp.at[2, 2 * y + 1 - x, c], gv2.at[0], to_x),
        push(gp_core.at[2, 2 * y + 1 - x], gv2.at[1], to_x),
    ]
    for copy in qk1:
        copy.wait_recv()
    for i in range(2):
        for j in range(2):
            gp[i, 2 * j + x, c] += gqk1[0, j, i]
            gp_core[i, 2 * j + x] += gqk1[1, j, i]
    qk2 = [
        push(gp.at[pl.ds(0, 2), 2 * (1 - y) + x, c], gqk2.at[0], to_y),
        push(gp_core.at[pl.ds(0, 2), 2 * (1 - y) + x], gqk2.at[1], to_y),
    ]
    for copy in u2:
        copy.wait_recv()
    mine = pl.ds(pl.multiple_of(x * tile // 4, 128), tile // 4)
    for high in range(2):
        ku[high, :, :, mine] += ru2[high]
    u3 = push(ku.at[:, 1 - bl, :, mine], ru3, to_z1)
    d3.wait_recv()
    for high in range(2):
        blocks[y, high, bl] += rd3[high]
    d4 = push(blocks.at[y, 1 - bh, bl], rd4, to_z2)
    w2.wait_recv()
    gw[rel_y, x, c] += gw2[...]

    def z_lanes(which):
        return pl.ds(pl.multiple_of(which * fourth, 128), fourth)

    w3 = [
        push(gw.at[rel_y, x, c, :, z_lanes(2 * high + 1 - bl)], gw3.at[high], to_z1) for high in range(2)
    ]
    for copy in v2:
        copy.wait_recv()
    here = 2 * y + x
    gp[2, here, c] += gv2[0]
    gp_core[2, here] += gv2[1]
    for copy in qk2:
        copy.wait_recv()
    for i in range(2):
        gp[i, here, c] += gqk2[0, i]
        gp_core[i, here] += gqk2[1, i]
    p3 = [
        push(gp.at[:, here, c, :, z_lanes(1 - bl)], gp3.at[0], to_z1),
        push(gp_core.at[:, here, :, z_lanes(1 - bl)], gp3.at[1], to_z1),
    ]
    u3.wait_recv()
    for high in range(2):
        ku[high, bl, :, mine] += ru3[high]
    u4 = push(ku.at[1 - bh, bl, :, mine], ru4, to_z2)
    for high in range(2):
        w3[high].wait_recv()
    w_mine = [gw[rel_y, x, c, :, z_lanes(2 * high + bl)] + gw3[high] for high in range(2)]
    gw3[0] = w_mine[0]
    gw3[1] = w_mine[1]
    w4 = push(gw3.at[1 - bh], gw4, to_z2)
    for copy in p3:
        copy.wait_recv()
    gp3[0] = gp[:, here, c, :, z_lanes(bl)] + gp3[0]
    gp3[1] = gp_core[:, here, :, z_lanes(bl)] + gp3[1]
    rel_b = lax.rem(bh + c, 2)
    p4 = push(gp3.at[1 - rel_b], gp4, to_z2)
    d4.wait_recv()
    o_down[...] = (blocks[y, bh, bl].astype(f32) + rd4[...].astype(f32)).T
    u4.wait_recv()
    up = ku[bh, bl, :, mine].astype(f32) + ru4[...].astype(f32)
    for i, h in ((0, 1 - c), (1, c)):
        o_up[:, pl.ds(pl.multiple_of(h * tile, 128), tile)] = up[i]
    w4.wait_recv()
    o_wo[...] = gw3[bh].astype(f32) + gw4[...].astype(f32)
    p4.wait_recv()
    for i, ref in enumerate((o_wq, o_wk, o_wv)):
        ref[...] = gp3[rel_b, i].astype(f32) + gp4[i].astype(f32)

    for i in range(4):
        rows_back_got(out_rows, out_home, send_r, recv_r, i)
    rows_back_sent(out_rows, out_home, send_r, recv_r)
    rows_back_sent(g_blocks, home, send_g, recv_g)
    for copy in sent:
        copy.wait_send()


def tail(table, counts, stat, vecs, dbu_a, dbu_b, log_total, res, dh, cot, out_rows, attn, attn_sib, wo, *rest, qt=512):
    (q, k, v, h1, wq, wk, wv, tok, down, up_a, up_b, tokens) = rest
    n_items, n_band = lax.axis_size("items"), lax.axis_size("band")
    rows, width = res.shape
    half, fourth, cut = width // 2, width // 4, rows // 4
    tile = down.shape[2]
    buf = lambda *shape: pltpu.VMEM(shape, bf16)
    buf32 = lambda *shape: pltpu.VMEM(shape, f32)
    out = lambda *shape: jax.ShapeDtypeStruct(shape, f32)
    e, s = fourth // 2, fourth
    return pl.pallas_call(
        functools.partial(tail_kernel, n_items, n_band, qt),
        name="tail",
        in_specs=[SMEM, SMEM] + [VMEM] * 5 + [HBM] * 18 + [VMEM],
        out_specs=[HBM] + [VMEM] * 8,
        out_shape=[
            jax.ShapeDtypeStruct(tokens.shape, bf16),
            jax.ShapeDtypeStruct(tokens.shape, bf16),
            out(16, width),
            out(tile, s),
            out(e, 2 * tile),
            out(e, s),
            out(e, s),
            out(e, s),
            out(e, s),
        ],
        scratch_shapes=[
            buf32(rows, width), buf32(rows, width), buf(rows, width), buf(rows, width),
            buf(width, width), buf(rows, half), buf(rows, half),
            buf(2, width, tile), buf(2, width, tile), buf(width, tile), buf(2, s, tile), buf(s, tile),
            buf(2, 2, 2, tile // 2, tile), buf(2, 2, 2, tile // 2, tile), buf(2, 2, 2, tile // 4, tile),
            buf(2, 2, tile // 4, tile), buf(2, tile // 4, tile),
            buf(2 * rows, half), buf(2 * rows, half), buf(2 * rows, half),
            buf(2 * rows, half), buf(rows, half), buf32(2 * rows, 128), buf32(2 * rows, 128),
            buf(2 * rows, width), buf(width, half), buf(width, half), buf(width, half), buf(rows, width),
            buf(2, 2, 2, e, width), buf(2, 2, e, width), buf(2, e, width), buf(e, width),
            buf(2, e, s), buf(e, s),
            buf(3, 4, 2, e, half), buf(3, 4, e, half), buf(2, 2, 2, e, half), buf(2, 2, e, half),
            buf(2, 2, e, half), buf(2, e, half), buf(2, 3, e, s), buf(3, e, s),
            buf(2, 2 * cut, width),
            buf32(16, width), buf32(n_items, 8, width), buf32(8, width), buf32(n_band, 8, width),
            buf32(n_items, 8, width), buf32(8, width), buf32(n_band, 8, width),
            DMA((48,)), DMA((48,)), DMA((32,)),
            DMA((4,)), DMA((4,)), DMA((4,)), DMA((4,)),
            DMA((2, n_items)), DMA((2, n_items)), DMA((2, n_band)), DMA((2, n_band)),
        ],
        compiler_params=params(collective_id=5, has_side_effects=True),
        cost_estimate=pl.CostEstimate(
            flops=60 * rows * width * width, bytes_accessed=40 * 2**20, transcendentals=0
        ),
    )(
        table, counts, stat, vecs, dbu_a, dbu_b, log_total, res, dh, cot,
        out_rows.reshape(4, cut, width), attn, attn_sib, wo, q, k, v, h1, wq, wk, wv, tok,
        down, up_a, up_b, tokens,
    )


def column_layer(
    tokens, cotangent, running_mean, running_var, slot_table, patch_counts,
    ln1_gain, ln1_bias, w_query, b_query, w_key, w_value, b_value, w_out, b_out,
    ln2_gain, ln2_bias, w_up, b_up, w_down, b_down,
):
    slots, band_rows, width = tokens.shape
    rows = slots * band_rows
    parts = (running_mean, running_var, ln1_gain, ln1_bias, b_query, b_value, b_out)
    parts += (ln2_gain, ln2_bias, b_down, b_up)
    vecs = jnp.concatenate([part.astype(f32) for part in parts]).reshape(-1, width)
    gathered, stat = gather(slot_table, patch_counts, vecs, tokens)
    tok = gathered.reshape(2 * rows, width)
    h1, q, k, v = project(stat, vecs, tok, w_query, w_key, w_value)
    attn, log_total, cot_rows, attn_sib = attend(slot_table, patch_counts, q, k, v, cotangent)
    cot_rows = cot_rows.reshape(rows, width)
    res, h2, h2p = join(stat, vecs, attn, attn_sib, w_out, tok)
    out_rows, d_h2, d_down, d_up_a, d_up_b, dbu_a, dbu_b = mlp(
        vecs, h2, h2p, cot_rows, res, w_up, w_down
    )
    output, d_tokens, small, d_w_down, d_w_up, d_w_out, d_wq, d_wk, d_wv = tail(
        slot_table, patch_counts, stat, vecs, dbu_a, dbu_b, log_total, res, d_h2, cot_rows,
        out_rows, attn, attn_sib, w_out, q, k, v, h1, w_query, w_key, w_value, tok,
        d_down, d_up_a, d_up_b, tokens,
    )
    d_gain_two, d_shift_two, d_bo, d_bdown = (small[i] for i in range(4))
    d_gain_one, d_shift_one, d_bq, d_bv = (small[i] for i in range(10, 14))
    return (
        output, d_tokens, stat[S_MEAN], stat[S_VAR], d_gain_one, d_shift_one,
        d_wq, d_bq, d_wk, d_wv, d_bv, d_w_out, d_bo, d_gain_two, d_shift_two,
        d_w_up, small[4:8].reshape(-1), d_w_down, d_bdown,
    )


def layer_norm(value, gain, shift):
    centre = value - jnp.mean(value, -1, keepdims=True)
    spread = jnp.mean(centre * centre, -1, keepdims=True)
    return centre * lax.rsqrt(spread + epsilon) * gain + shift


def gelu_tanh(value):
    return (
        0.5
        * value
        * (1.0 + jnp.tanh(0.7978845608028654 * (value + 0.044715 * value * value * value)))
    )


def head_layout():
    heads_per = 4
    return (heads_per, HEADS // heads_per, heads_per * HEAD_DIM)


def group_scores(q_part, k_part, key_mask):
    scores = (
        jnp.einsum("rhd,khd->hrk", q_part, k_part, preferred_element_type=jnp.float32) * score_scale
    )
    return jnp.where(key_mask[None, None, :], scores, masked_score)


def attend_forward(q_slot, keys_slot, values_slot, key_mask):
    heads_per, groups, group_width = head_layout()
    band_rows = q_slot.shape[0]
    seq_length = keys_slot.shape[0]

    def head_block(group_index):
        begin = group_index * group_width
        q_part = lax.dynamic_slice_in_dim(q_slot, begin, group_width, 1).reshape(
            band_rows, heads_per, HEAD_DIM
        )
        k_part = lax.dynamic_slice_in_dim(keys_slot, begin, group_width, 1).reshape(
            seq_length, heads_per, HEAD_DIM
        )
        v_part = lax.dynamic_slice_in_dim(values_slot, begin, group_width, 1).reshape(
            seq_length, heads_per, HEAD_DIM
        )
        scores = group_scores(q_part, k_part, key_mask)
        top_score = jnp.max(scores, -1, keepdims=True)
        log_total = top_score + jnp.log(jnp.sum(jnp.exp(scores - top_score), -1, keepdims=True))
        probs_low = jnp.exp(scores - log_total).astype(jnp.bfloat16)
        attended = jnp.einsum("hrk,khd->rhd", probs_low, v_part, preferred_element_type=jnp.float32)
        return (attended.reshape(band_rows, group_width), log_total[..., 0])

    attended, log_totals = lax.map(head_block, jnp.arange(groups, dtype=jnp.int32))
    return (attended.transpose(1, 0, 2).reshape(band_rows, groups * group_width), log_totals)


def attend_backward(q_slot, keys_slot, values_slot, key_mask, d_attn_slot, row_delta, log_totals):
    heads_per, groups, group_width = head_layout()
    query_rows = q_slot.shape[0]
    seq_length = keys_slot.shape[0]
    deltas = jnp.transpose(row_delta).reshape(groups, heads_per, query_rows)

    def head_block(inputs):
        group_index, log_total, delta_part = inputs
        begin = group_index * group_width
        q_part = lax.dynamic_slice_in_dim(q_slot, begin, group_width, 1).reshape(
            query_rows, heads_per, HEAD_DIM
        )
        k_part = lax.dynamic_slice_in_dim(keys_slot, begin, group_width, 1).reshape(
            seq_length, heads_per, HEAD_DIM
        )
        v_part = lax.dynamic_slice_in_dim(values_slot, begin, group_width, 1).reshape(
            seq_length, heads_per, HEAD_DIM
        )
        d_part = lax.dynamic_slice_in_dim(d_attn_slot, begin, group_width, 1).reshape(
            query_rows, heads_per, HEAD_DIM
        )
        scores = group_scores(q_part, k_part, key_mask)
        probs = jnp.exp(scores - log_total[..., None])
        d_probs = jnp.einsum("rhd,khd->hrk", d_part, v_part, preferred_element_type=jnp.float32)
        d_scores = (probs * (d_probs - delta_part[..., None])).astype(jnp.bfloat16)
        results = []
        d_q_part = (
            jnp.einsum("hrk,khd->rhd", d_scores, k_part, preferred_element_type=jnp.float32)
            * score_scale
        )
        results.append(d_q_part.reshape(query_rows, group_width))
        probs_low = probs.astype(jnp.bfloat16)
        d_k_part = (
            jnp.einsum("hrk,rhd->khd", d_scores, q_part, preferred_element_type=jnp.float32)
            * score_scale
        )
        d_v_part = jnp.einsum("hrk,rhd->khd", probs_low, d_part, preferred_element_type=jnp.float32)
        results.append(d_k_part.reshape(seq_length, group_width))
        results.append(d_v_part.reshape(seq_length, group_width))
        return tuple(results)

    mapped = lax.map(head_block, (jnp.arange(groups, dtype=jnp.int32), log_totals, deltas))
    full_width = groups * group_width
    return tuple((piece.transpose(1, 0, 2).reshape(piece.shape[1], full_width) for piece in mapped))


def local(
    tokens,
    cotangent,
    running_mean,
    running_var,
    slot_table,
    patch_counts,
    ln1_gain,
    ln1_bias,
    w_query,
    b_query,
    w_key,
    w_value,
    b_value,
    w_out,
    b_out,
    ln2_gain,
    ln2_bias,
    w_up,
    b_up,
    w_down,
    b_down,
):
    slot_count, band_rows, model_width = tokens.shape
    seq_length = band_rows * lax.axis_size("band")
    item_rank = lax.axis_index("items")
    band_rank = lax.axis_index("band")
    every_slot = jnp.arange(slot_table.shape[0], dtype=jnp.int32)
    my_slots = item_rank * slot_count + jnp.arange(slot_count, dtype=jnp.int32)
    item_ids = jnp.sum(
        jnp.where(every_slot[None, :] == my_slots[:, None], slot_table[None, :], 0), 1
    )
    lengths = jnp.sum(
        jnp.where(every_slot[None, :] == item_ids[:, None], patch_counts[None, :], 0), 1
    )
    key_mask = jnp.arange(seq_length, dtype=jnp.int32)[None, :] < lengths[:, None]
    row_mask = (band_rank * band_rows + jnp.arange(band_rows, dtype=jnp.int32))[None, :] < lengths[
        :, None
    ]
    row_keep = row_mask.astype(jnp.float32).reshape(-1, 1)
    raw_flat = tokens.astype(jnp.float32).reshape(-1, model_width)
    part_one = jnp.sum(row_keep * raw_flat, 0)
    part_two = jnp.sum(row_keep * raw_flat * raw_flat, 0)
    total_one, total_two = lax.psum((part_one, part_two), ("items", "band"))
    patch_total = jnp.sum(patch_counts).astype(jnp.float32)
    batch_mean = total_one / patch_total
    batch_var = total_two / patch_total - batch_mean * batch_mean
    new_mean = momentum * running_mean + momentum * batch_mean
    new_var = momentum * running_var + momentum * batch_var
    inverse = lax.rsqrt(new_var + epsilon)
    normed_in = (raw_flat - new_mean) * inverse
    gain_one = ln1_gain.astype(jnp.float32)
    shift_one = ln1_bias.astype(jnp.float32)
    gain_two = ln2_gain.astype(jnp.float32)
    shift_two = ln2_bias.astype(jnp.float32)
    h_one_full, norm_one_back = jax.vjp(layer_norm, normed_in, gain_one, shift_one)
    h_one = h_one_full.astype(jnp.bfloat16)
    queries = (
        jnp.dot(h_one, w_query, preferred_element_type=jnp.float32) + b_query.astype(jnp.float32)
    ).astype(jnp.bfloat16)
    key_local = (
        jnp.dot(h_one, w_key, preferred_element_type=jnp.float32)
        .astype(jnp.bfloat16)
        .reshape(slot_count, band_rows, model_width)
    )
    value_local = (
        (jnp.dot(h_one, w_value, preferred_element_type=jnp.float32) + b_value.astype(jnp.float32))
        .astype(jnp.bfloat16)
        .reshape(slot_count, band_rows, model_width)
    )
    keys_all, values_all = (
        lax.all_gather(key_local, "band", axis=1, tiled=True),
        lax.all_gather(value_local, "band", axis=1, tiled=True),
    )
    q_slots = queries.reshape(slot_count, band_rows, model_width)
    attended_list = []
    totals_list = []
    for slot_index in range(slot_count):
        attended, log_totals = attend_forward(
            q_slots[slot_index], keys_all[slot_index], values_all[slot_index], key_mask[slot_index]
        )
        attended_list.append(attended)
        totals_list.append(log_totals)
    attn_full = jnp.concatenate(attended_list, 0)
    attn_low = attn_full.astype(jnp.bfloat16)
    residual = (
        normed_in
        + jnp.dot(attn_low, w_out, preferred_element_type=jnp.float32)
        + b_out.astype(jnp.float32)
    )
    h_two_full, norm_two_back = jax.vjp(layer_norm, residual, gain_two, shift_two)
    h_two = h_two_full.astype(jnp.bfloat16)
    up_proj = jnp.dot(h_two, w_up, preferred_element_type=jnp.float32) + b_up.astype(jnp.float32)
    activated_full, gelu_back = jax.vjp(gelu_tanh, up_proj)
    activated = activated_full.astype(jnp.bfloat16)
    result = (
        residual
        + jnp.dot(activated, w_down, preferred_element_type=jnp.float32)
        + b_down.astype(jnp.float32)
    )
    output = result.astype(jnp.bfloat16).reshape(slot_count, band_rows, model_width)
    cot_low = cotangent.reshape(-1, model_width)
    cot_full = cot_low.astype(jnp.float32)
    d_w_down = jnp.einsum("tf,td->fd", activated, cot_low, preferred_element_type=jnp.float32)
    d_b_down = jnp.sum(cot_full, 0)
    d_activated = jnp.einsum("td,fd->tf", cot_low, w_down, preferred_element_type=jnp.float32)
    (d_up_full,) = gelu_back(d_activated)
    d_up = d_up_full.astype(jnp.bfloat16)
    d_w_up = jnp.einsum("td,tf->df", h_two, d_up, preferred_element_type=jnp.float32)
    d_b_up = jnp.sum(d_up, 0, dtype=jnp.float32)
    d_h_two = jnp.einsum("tf,df->td", d_up, w_up, preferred_element_type=jnp.float32)
    d_res_norm, d_gain_two, d_shift_two = norm_two_back(d_h_two)
    d_residual = cot_full + d_res_norm
    d_branch = d_residual.astype(jnp.bfloat16)
    d_w_out = jnp.einsum("td,te->de", attn_low, d_branch, preferred_element_type=jnp.float32)
    d_b_out = jnp.sum(d_branch, 0, dtype=jnp.float32)
    d_attn = jnp.einsum("te,de->td", d_branch, w_out, preferred_element_type=jnp.float32).astype(
        jnp.bfloat16
    )
    row_delta = jnp.sum(
        (d_attn.astype(jnp.float32) * attn_full).reshape(slot_count, band_rows, HEADS, HEAD_DIM), -1
    )
    d_attn_slots = d_attn.reshape(slot_count, band_rows, model_width)
    back_keys, back_values = (keys_all, values_all)
    d_q_list = []
    d_k_list = []
    d_v_list = []
    for slot_index in range(slot_count):
        d_q_slot, d_k_slot, d_v_slot = attend_backward(
            q_slots[slot_index],
            back_keys[slot_index],
            back_values[slot_index],
            key_mask[slot_index],
            d_attn_slots[slot_index],
            row_delta[slot_index],
            totals_list[slot_index],
        )
        d_q_list.append(d_q_slot)
        d_k_list.append(d_k_slot)
        d_v_list.append(d_v_slot)
    d_keys_mine, d_values_mine = (
        lax.psum_scatter(
            jnp.stack(d_k_list).astype(jnp.bfloat16), "band", scatter_dimension=1, tiled=True
        ).astype(jnp.float32),
        lax.psum_scatter(
            jnp.stack(d_v_list).astype(jnp.bfloat16), "band", scatter_dimension=1, tiled=True
        ).astype(jnp.float32),
    )
    d_queries = jnp.concatenate(d_q_list, 0).astype(jnp.bfloat16)
    d_keys = d_keys_mine.reshape(-1, model_width).astype(jnp.bfloat16)
    d_values = d_values_mine.reshape(-1, model_width).astype(jnp.bfloat16)
    d_w_query = jnp.einsum("td,te->de", h_one, d_queries, preferred_element_type=jnp.float32)
    d_b_query = jnp.sum(d_queries, 0, dtype=jnp.float32)
    d_w_key = jnp.einsum("td,te->de", h_one, d_keys, preferred_element_type=jnp.float32)
    d_w_value = jnp.einsum("td,te->de", h_one, d_values, preferred_element_type=jnp.float32)
    d_b_value = jnp.sum(d_values, 0, dtype=jnp.float32)
    d_h_one = jnp.einsum("te,de->td", d_queries, w_query, preferred_element_type=jnp.float32)
    d_h_one = d_h_one + jnp.einsum("te,de->td", d_keys, w_key, preferred_element_type=jnp.float32)
    d_h_one = d_h_one + jnp.einsum(
        "te,de->td", d_values, w_value, preferred_element_type=jnp.float32
    )
    d_start_norm, d_gain_one, d_shift_one = norm_one_back(d_h_one)
    d_start = d_residual + d_start_norm
    centred = raw_flat - new_mean
    small_sums = lax.psum(
        (
            jnp.sum(d_start, 0),
            jnp.sum(d_start * centred, 0),
            d_gain_one,
            d_shift_one,
            d_b_query,
            d_b_value,
            d_b_out,
            d_gain_two,
            d_shift_two,
            d_b_up,
            d_b_down,
        ),
        ("items", "band"),
    )
    sum_g = small_sums[0]
    sum_gx = small_sums[1]
    cube = inverse * inverse * inverse
    d_raw = d_start * inverse + row_keep * (
        -0.5 * inverse * sum_g / patch_total
        - 0.5 * cube * sum_gx * (raw_flat - batch_mean) / patch_total
    )
    d_tokens = d_raw.astype(jnp.bfloat16).reshape(slot_count, band_rows, model_width)
    weight_grads = (
        lax.psum_scatter(
            d_w_query.astype(jnp.bfloat16), "items", scatter_dimension=0, tiled=True
        ).astype(jnp.float32),
        lax.psum_scatter(
            d_w_key.astype(jnp.bfloat16), "items", scatter_dimension=0, tiled=True
        ).astype(jnp.float32),
        lax.psum_scatter(
            d_w_value.astype(jnp.bfloat16), "items", scatter_dimension=0, tiled=True
        ).astype(jnp.float32),
        lax.psum_scatter(
            d_w_out.astype(jnp.bfloat16), "items", scatter_dimension=0, tiled=True
        ).astype(jnp.float32),
        lax.psum_scatter(
            d_w_up.astype(jnp.bfloat16), "items", scatter_dimension=0, tiled=True
        ).astype(jnp.float32),
        lax.psum_scatter(
            d_w_down.astype(jnp.bfloat16), "items", scatter_dimension=0, tiled=True
        ).astype(jnp.float32),
    )
    weight_grads = (
        lax.psum_scatter(
            weight_grads[0].astype(jnp.bfloat16), "band", scatter_dimension=1, tiled=True
        ).astype(jnp.float32),
        lax.psum_scatter(
            weight_grads[1].astype(jnp.bfloat16), "band", scatter_dimension=1, tiled=True
        ).astype(jnp.float32),
        lax.psum_scatter(
            weight_grads[2].astype(jnp.bfloat16), "band", scatter_dimension=1, tiled=True
        ).astype(jnp.float32),
        lax.psum_scatter(
            weight_grads[3].astype(jnp.bfloat16), "band", scatter_dimension=1, tiled=True
        ).astype(jnp.float32),
        lax.psum_scatter(
            weight_grads[4].astype(jnp.bfloat16), "band", scatter_dimension=1, tiled=True
        ).astype(jnp.float32),
        lax.psum_scatter(
            weight_grads[5].astype(jnp.bfloat16), "band", scatter_dimension=1, tiled=True
        ).astype(jnp.float32),
    )
    return (
        output,
        d_tokens,
        new_mean,
        new_var,
        small_sums[2],
        small_sums[3],
        weight_grads[0],
        small_sums[4],
        weight_grads[1],
        weight_grads[2],
        small_sums[5],
        weight_grads[3],
        small_sums[6],
        small_sums[7],
        small_sums[8],
        weight_grads[4],
        small_sums[9],
        weight_grads[5],
        small_sums[10],
    )


def solution(mesh):
    columns = mesh.shape["items"] == 8 and mesh.shape["band"] == 4
    return jax.shard_map(
        column_layer if columns else local,
        mesh=mesh,
        in_specs=(
            P("items", "band", None),
            P("items", "band", None),
            P(),
            P(),
            P(),
            P(),
            P(),
            P(),
            P(),
            P(),
            P(),
            P(),
            P(),
            P(),
            P(),
            P(),
            P(),
            P(),
            P(),
            P(),
            P(),
        ),
        out_specs=(
            P("items", "band", None),
            P("items", "band", None),
            P(),
            P(),
            P(),
            P(),
            P("items", "band"),
            P(),
            P("items", "band"),
            P("items", "band"),
            P(),
            P("items", "band"),
            P(),
            P(),
            P(),
            P("items", "band"),
            P(),
            P("items", "band"),
            P(),
        ),
        check_vma=False,
    )
```

```python
import functools
import jax
import jax.numpy as jnp
from jax import lax
from jax.experimental import pallas as pl
from jax.experimental.pallas import tpu as pltpu
from jax.sharding import PartitionSpec as P

HEADS = 16
HEAD_DIM = 64
epsilon = 1e-05
score_scale = 0.125
masked_score = -1e30
momentum = 0.5
f32 = jnp.float32
bf16 = jnp.bfloat16
VMEM_LIMIT = 60 * 2**20
R_MEAN, R_VAR, R_G1, R_S1, R_BQ, R_BV, R_BO, R_G2, R_S2, R_BD, R_BU = range(11)
S_MEAN, S_VAR, S_BATCH, S_INV = range(4)


def dot(a, b, ca=1, cb=0):
    return lax.dot_general(a, b, (((ca,), (cb,)), ((), ())), preferred_element_type=f32)


def params(**kw):
    return pltpu.CompilerParams(vmem_limit_bytes=VMEM_LIMIT, **kw)


def place():
    it, bd = lax.axis_index("items"), lax.axis_index("band")
    return it, bd, lax.rem(it, 2), it // 2


def remote(src, dst, send, recv, to):
    return pltpu.make_async_remote_copy(
        src_ref=src,
        dst_ref=dst,
        send_sem=send,
        recv_sem=recv,
        device_id=to,
        device_id_type=pl.DeviceIdType.MESH,
    )


def greet(peers):
    barrier = pltpu.get_barrier_semaphore()
    for peer in peers:
        pl.semaphore_signal(barrier, inc=1, device_id=peer, device_id_type=pl.DeviceIdType.MESH)
    pl.semaphore_wait(barrier, len(peers))


def column_peers():
    it, bd, c, yx = place()
    peers = [(it, lax.rem(bd + o, 4)) for o in range(1, 4)]
    return peers + [(it + 1 - 2 * c, lax.rem(bd + o, 4)) for o in range(4)]


def rows_out(src, dst, send, recv):
    it, bd, c, yx = place()
    cut = src.shape[1] // 2
    for q in range(4):
        s, h = q // 2, q % 2
        block = src.at[s, pl.ds(h * cut, cut)]
        target = dst.at[bd]
        own = (c == h) & (bd == 2 * c + s)

        @pl.when(own)
        def _():
            pltpu.make_async_copy(block, target, recv.at[bd]).start()

        @pl.when(jnp.logical_not(own))
        def _():
            remote(block, target, send.at[q], recv.at[bd], (yx * 2 + h, 2 * c + s)).start()


def rows_out_sent(src, dst, send, recv):
    it, bd, c, yx = place()
    cut = src.shape[1] // 2
    for q in range(4):
        s, h = q // 2, q % 2
        own = (c == h) & (bd == 2 * c + s)

        @pl.when(jnp.logical_not(own))
        def _():
            block = src.at[s, pl.ds(h * cut, cut)]
            remote(block, dst.at[bd], send.at[q], recv.at[bd], (yx * 2 + h, 2 * c + s)).wait_send()


def rows_out_got(src, dst, send, recv, band):
    it, bd, c, yx = place()
    cut = src.shape[1] // 2
    pltpu.make_async_copy(src.at[0, pl.ds(0, cut)], dst.at[band], recv.at[band]).wait()


def rows_back(src, dst, send, recv):
    it, bd, c, yx = place()
    cut = src.shape[1]
    home = bd // 2
    s = lax.rem(bd, 2)
    target = dst.at[s, pl.ds(pl.multiple_of(c * cut, cut), cut)]
    got = recv.at[2 * s + c]
    for r in range(4):
        own = (home == c) & (bd == r)

        @pl.when(own)
        def _():
            pltpu.make_async_copy(src.at[r], target, got).start()

        @pl.when(jnp.logical_not(own))
        def _():
            remote(src.at[r], target, send.at[r], got, (yx * 2 + home, r)).start()


def rows_back_sent(src, dst, send, recv):
    it, bd, c, yx = place()
    cut = src.shape[1]
    home = bd // 2
    for r in range(4):
        own = (home == c) & (bd == r)

        @pl.when(jnp.logical_not(own))
        def _():
            target = dst.at[0, pl.ds(0, cut)]
            remote(src.at[r], target, send.at[r], recv.at[0], (yx * 2 + home, r)).wait_send()


def rows_back_got(src, dst, send, recv, q):
    cut = src.shape[1]
    s, h = q // 2, q % 2
    pltpu.make_async_copy(src.at[0], dst.at[s, pl.ds(h * cut, cut)], recv.at[q]).wait()


def share_start(n, rank, peer_of, src, buf, send, recv):
    copies = []
    for o in range(1, n):
        to = peer_of(lax.rem(rank + o, n))
        copies.append(remote(src, buf.at[rank], send.at[o], recv.at[o], to))
        copies[-1].start()
    buf[rank] = src[...]
    return copies


def share_end(n, copies, buf):
    for copy in copies:
        copy.wait()
    added = buf[0]
    for i in range(1, n):
        added = added + buf[i]
    return added


def all_peers(n_items):
    it, bd, c, yx = place()
    others = []
    for o in range(1, n_items // 2):
        for k in range(2):
            others.append((lax.rem(yx + o, n_items // 2) * 2 + k, bd))
    return column_peers() + others


def gather_kernel(n_items, n_band, table, counts, vecs, tok, rows, stat, one, buf_i, part, buf_b, *sems):
    (send_t, recv_t, send_s, recv_s, send_i, recv_i, send_b, recv_b) = sems
    it, bd, c, yx = place()
    sibling = (it + 1 - 2 * c, bd)
    greet(all_peers(n_items))
    rows_out(tok, rows, send_t, recv_t)
    slots, band_rows, width = tok.shape
    at = lax.broadcasted_iota(jnp.int32, (band_rows, width), 0) + bd * band_rows
    first = jnp.zeros((1, width), f32)
    second = jnp.zeros((1, width), f32)
    for s in range(slots):
        x = jnp.where(at < counts[table[it * slots + s]], tok[s].astype(f32), 0.0)
        first = first + jnp.sum(x, 0, keepdims=True)
        second = second + jnp.sum(x * x, 0, keepdims=True)
    one[0:1, :] = first
    one[1:2, :] = second
    copies = share_start(n_items, it, lambda p: (p, bd), one, buf_i, send_i, recv_i)
    part[...] = share_end(n_items, copies, buf_i)
    copies = share_start(n_band, bd, lambda p: (it, p), part, buf_b, send_b, recv_b)
    sums = share_end(n_band, copies, buf_b) / patch_total(counts, (1, width))
    mean = sums[0:1]
    var = sums[1:2] - mean * mean
    new_var = momentum * vecs[R_VAR : R_VAR + 1, :] + momentum * var
    stat[S_MEAN : S_MEAN + 1, :] = momentum * vecs[R_MEAN : R_MEAN + 1, :] + momentum * mean
    stat[S_VAR : S_VAR + 1, :] = new_var
    stat[S_BATCH : S_BATCH + 1, :] = mean
    stat[S_INV : S_INV + 1, :] = lax.rsqrt(new_var + epsilon)
    hand = []
    for o in range(4):
        band = lax.rem(bd + o, 4)
        rows_out_got(tok, rows, send_t, recv_t, band)
        copy = remote(rows.at[band], rows.at[4 + band], send_s.at[o], recv_s.at[o], sibling)
        copy.start()
        hand.append(copy)
    for copy in hand:
        copy.wait()
    rows_out_sent(tok, rows, send_t, recv_t)


def patch_total(counts, shape):
    total = counts[0]
    for i in range(1, counts.shape[0]):
        total = total + counts[i]
    return jnp.full(shape, total, jnp.int32).astype(f32)


VMEM = pl.BlockSpec(memory_space=pltpu.VMEM)
SMEM = pl.BlockSpec(memory_space=pltpu.SMEM)
HBM = pl.BlockSpec(memory_space=pltpu.HBM)
DMA = pltpu.SemaphoreType.DMA


def gather(table, counts, vecs, tok):
    n_items, n_band = lax.axis_size("items"), lax.axis_size("band")
    slots, band_rows, width = tok.shape
    return pl.pallas_call(
        functools.partial(gather_kernel, n_items, n_band),
        name="gather",
        in_specs=[SMEM, SMEM, VMEM, VMEM],
        out_specs=[HBM, VMEM],
        out_shape=[
            jax.ShapeDtypeStruct((8, band_rows // 2, width), bf16),
            jax.ShapeDtypeStruct((4, width), f32),
        ],
        scratch_shapes=[
            pltpu.VMEM((2, width), f32),
            pltpu.VMEM((n_items, 2, width), f32),
            pltpu.VMEM((2, width), f32),
            pltpu.VMEM((n_band, 2, width), f32),
        ]
        + [DMA((4,))] * 4
        + [DMA((n_items,))] * 2
        + [DMA((n_band,))] * 2,
        compiler_params=params(collective_id=1, has_side_effects=True),
    )(table, counts, vecs, tok)


def half_lanes(ref, row, half):
    at = pl.multiple_of(lax.rem(lax.axis_index("items"), 2) * half, 128)
    return ref[row : row + 1, pl.ds(at, half)]


def project_kernel(stat, vecs, tok, wq, wk, wv, h1, q, k, v):
    half = q.shape[1]
    start = (tok[...].astype(f32) - stat[S_MEAN : S_MEAN + 1, :]) * stat[S_INV : S_INV + 1, :]
    centre = start - jnp.mean(start, -1, keepdims=True)
    spread = jnp.mean(centre * centre, -1, keepdims=True)
    h = centre * lax.rsqrt(spread + epsilon) * vecs[R_G1 : R_G1 + 1, :] + vecs[R_S1 : R_S1 + 1, :]
    h = h.astype(bf16)
    h1[...] = h
    q[...] = ((dot(h, wq[...]) + half_lanes(vecs, R_BQ, half)).astype(bf16) * score_scale).astype(bf16)
    k[...] = dot(h, wk[...]).astype(bf16)
    v[...] = (dot(h, wv[...]) + half_lanes(vecs, R_BV, half)).astype(bf16)


def project(stat, vecs, tok, wq, wk, wv, block=256):
    rows, width = tok.shape
    half = width // 2
    w = pl.BlockSpec((width, half), lambda i: (0, lax.rem(lax.axis_index("items"), 2)))
    full = pl.BlockSpec((block, width), lambda i: (i, 0))
    part = pl.BlockSpec((block, half), lambda i: (i, 0))
    return pl.pallas_call(
        project_kernel,
        name="project",
        grid=(rows // block,),
        in_specs=[VMEM, VMEM, full, w, w, w],
        out_specs=[full] + [part] * 3,
        out_shape=[jax.ShapeDtypeStruct((rows, width), bf16)]
        + [jax.ShapeDtypeStruct((rows, half), bf16)] * 3,
        compiler_params=params(),
        cost_estimate=pl.CostEstimate(
            flops=6 * rows * width * half, bytes_accessed=12 * 2**20, transcendentals=0
        ),
    )(stat, vecs, tok, wq, wk, wv)


def head_lanes(array, head, lane):
    keep = (lane >= head * HEAD_DIM) & (lane < (head + 1) * HEAD_DIM)
    return jnp.where(keep, array, jnp.zeros_like(array))


def with_spare(array, spare_value, head, lane):
    spare = (1 - head) * HEAD_DIM
    return jnp.where(lane == spare, spare_value, head_lanes(array, head, lane))


def ones_beside(array, head, lane):
    return with_spare(array, jnp.ones_like(array), head, lane)


def key_bias(table, counts, shape):
    it, bd, c, yx = place()
    cut = shape[0] // 8
    row = lax.broadcasted_iota(jnp.int32, shape, 0)
    there = row >= 4 * cut
    row = jnp.where(there, row - 4 * cut, row)
    band = row // cut
    half = jnp.where(there, 1 - c, c)
    position = band * (2 * cut) + half * cut + (row - band * cut)
    return jnp.where(position < counts[table[yx * 4 + bd]], 0.0, masked_score).astype(bf16)


def attend_kernel(qt, table, counts, q, k, v, cot, out, log_total, cot_rows, out_sib, part_sib, *sems):
    (send, recv, send_s, recv_s) = sems
    step = pl.program_id(0)
    rows, lanes = q.shape
    own = rows // 2
    it, bd, c, yx = place()
    sibling = (it + 1 - 2 * c, bd)

    @pl.when(step == 0)
    def _():
        greet(column_peers())
        rows_out(cot, cot_rows, send, recv)

    lane_k = lax.broadcasted_iota(jnp.int32, (rows, lanes), 1)
    lane_q = lax.broadcasted_iota(jnp.int32, (qt, lanes), 1)
    row_out = lax.broadcasted_iota(jnp.int32, (lanes, qt), 0)
    bias = key_bias(table, counts, (rows, lanes))
    keys = [with_spare(k[...], bias, hd, lane_k) for hd in range(2)]
    values = [ones_beside(v[...], hd, lane_k).T for hd in range(2)]
    for t in range(rows // qt):
        at = slice(t * qt, (t + 1) * qt)
        scores = [dot(keys[hd], ones_beside(q[at, :], hd, lane_q), 1, 1) for hd in range(2)]
        tops = [jnp.max(s, 0, keepdims=True) for s in scores]
        weights = [jnp.exp(s - top).astype(bf16) for s, top in zip(scores, tops)]
        parts = []
        for hd in range(2):
            part = dot(values[hd], weights[hd])
            spare = (1 - hd) * HEAD_DIM
            total = part[spare : spare + 1, :]
            log_total[0, hd : hd + 1, at] = tops[hd] + jnp.log(total)
            parts.append(part * (1.0 / total))
        both = jnp.where(row_out < HEAD_DIM, parts[0], parts[1]).T.astype(bf16)
        if t * qt < own:
            out[at, :] = both
        else:
            part_sib[step, t * qt - own : (t + 1) * qt - own, :] = both

    def hand(i):
        return remote(
            part_sib.at[i],
            out_sib.at[:, pl.ds(pl.multiple_of(i * lanes, lanes), lanes)],
            send_s.at[i],
            recv_s.at[i],
            sibling,
        )

    hand(step).start()

    @pl.when(step == pl.num_programs(0) - 1)
    def _():
        for i in range(part_sib.shape[0]):
            hand(i).wait()
        for band in range(4):
            rows_out_got(cot, cot_rows, send, recv, band)
        rows_out_sent(cot, cot_rows, send, recv)


def attend(table, counts, q, k, v, cot, qt=512):
    rows, width = q.shape
    pairs = width // 128
    blk = pl.BlockSpec((rows, 128), lambda i: (0, i))
    return pl.pallas_call(
        functools.partial(attend_kernel, qt),
        name="attend",
        grid=(pairs,),
        in_specs=[SMEM, SMEM, blk, blk, blk, HBM],
        out_specs=[
            pl.BlockSpec((rows // 2, 128), lambda i: (0, i)),
            pl.BlockSpec((1, 2, rows), lambda i: (i, 0, 0)),
            HBM,
            HBM,
        ],
        out_shape=[
            jax.ShapeDtypeStruct((rows // 2, width), bf16),
            jax.ShapeDtypeStruct((pairs, 2, rows), f32),
            jax.ShapeDtypeStruct((4, cot.shape[1] // 2, cot.shape[2]), bf16),
            jax.ShapeDtypeStruct((rows // 2, width), bf16),
        ],
        scratch_shapes=[pltpu.VMEM((pairs, rows // 2, 128), bf16)]
        + [DMA((4,))] * 2
        + [DMA((pairs,))] * 2,
        compiler_params=params(collective_id=3, has_side_effects=True),
        cost_estimate=pl.CostEstimate(
            flops=16 * rows * rows * width, bytes_accessed=5 * 2**20, transcendentals=0
        ),
    )(table, counts, q, k, v, cot)


def half_rows(ref, which, half):
    return ref[pl.ds(pl.multiple_of(which * half, 128), half), :]


def join_kernel(stat, vecs, attn_a, attn_b, wo, tok, res, h2, h2p):
    it, bd, c, yx = place()
    half = attn_a.shape[1]
    start = (tok[...].astype(f32) - stat[S_MEAN : S_MEAN + 1, :]) * stat[S_INV : S_INV + 1, :]
    r = dot(attn_a[...], half_rows(wo, c, half)) + dot(attn_b[...], half_rows(wo, 1 - c, half))
    r = start + r + vecs[R_BO : R_BO + 1, :]
    res[...] = r
    centre = r - jnp.mean(r, -1, keepdims=True)
    spread = jnp.mean(centre * centre, -1, keepdims=True)
    h = centre * lax.rsqrt(spread + epsilon) * vecs[R_G2 : R_G2 + 1, :] + vecs[R_S2 : R_S2 + 1, :]
    h = h.astype(bf16)
    h2[...] = h
    width = h.shape[1] // 8
    for x in range(4):
        first = h[:, 2 * x * width : (2 * x + 1) * width]
        second = h[:, (2 * x + 1) * width : (2 * x + 2) * width]
        h2p[:, x * width : (x + 1) * width] = jnp.where(c == 0, first, second)
        h2p[:, half + x * width : half + (x + 1) * width] = jnp.where(c == 0, second, first)


def join(stat, vecs, attn, attn_sib, w_out, tok, block=256):
    rows, half = attn.shape
    width = 2 * half
    act = pl.BlockSpec((block, half), lambda i: (i, 0))
    full = pl.BlockSpec((block, width), lambda i: (i, 0))
    return pl.pallas_call(
        join_kernel,
        name="join",
        grid=(rows // block,),
        in_specs=[VMEM, VMEM, act, act, VMEM, full],
        out_specs=[full] * 3,
        out_shape=[
            jax.ShapeDtypeStruct((rows, width), f32),
            jax.ShapeDtypeStruct((rows, width), bf16),
            jax.ShapeDtypeStruct((rows, width), bf16),
        ],
        compiler_params=params(),
        cost_estimate=pl.CostEstimate(
            flops=2 * rows * width * width, bytes_accessed=8 * 2**20, transcendentals=0
        ),
    )(stat, vecs, attn, attn_sib, w_out, tok)


def gelu_and_slope(u):
    u2 = u * u
    t = jnp.tanh(u * (0.7978845608028654 + (0.7978845608028654 * 0.044715) * u2))
    half = 0.5 + 0.5 * t
    slope = half * (
        1.0 + u * (1.0 - t) * (0.7978845608028654 + (3 * 0.7978845608028654 * 0.044715) * u2)
    )
    return u * half, slope


def block_order(step):
    it, bd, c, yx = place()
    x = lax.rem(yx, 2)
    return 2 * lax.rem(step, 2) + jnp.where(step < 2, 1 - x, x)


def mlp_kernel(vecs, h2, h2p, cot, res, *refs):
    (wu_a, wd_a, wu_b, wd_b) = refs[:4]
    (out_low, dh, kd, rd, rest_d, ku, ru, rest_u, dbu_a, dbu_b) = refs[4:14]
    (send_wd, send_wua, send_wub, got_wd, got_wua, got_wub, keep_a, out, gd, gu) = refs[14:24]
    (send, recv, send_d, recv_d, send_u, recv_u, keep_d, sem_u, rest_sem) = refs[24:]
    step = pl.program_id(0)
    steps = pl.num_programs(0) - 1
    half = h2.shape[1] // 2
    it, bd, c, yx = place()
    x, y = lax.rem(yx, 2), yx // 2
    sibling = (it + 1 - 2 * c, bd)
    to_x, to_y = (it + 2 - 4 * x, bd), (it + 4 - 8 * y, bd)
    slot = lax.rem(step, 2)
    before = 1 - slot
    some = gd.shape[1] // 2
    part = gu.shape[2] // 2

    def copies(at, which=(0, 1, 2)):
        pairs = ((send_wd, got_wd), (send_wua, got_wua), (send_wub, got_wub))
        return [
            remote(pairs[i][0].at[at], pairs[i][1].at[at], send.at[i, at], recv.at[i, at], sibling)
            for i in which
        ]

    def down_copy(at):
        if at == 0:
            return [remote(gd.at[0], rd.at[0], send_d.at[0], recv_d.at[0], to_x)]
        if at == 1:
            first, second = pl.ds(0, some), pl.ds(some, some)
            return [
                remote(gd.at[1, first], rd.at[1, first], send_d.at[1], recv_d.at[1], to_x),
                pltpu.make_async_copy(gd.at[1, second], rest_d, rest_sem.at[2]),
            ]
        return [pltpu.make_async_copy(gd.at[at], kd.at[at - 2], keep_d.at[at - 2])]

    def up_rows(which):
        return pl.ds(pl.multiple_of(which * part, 128), part)

    def up_keep(at, i):
        return pltpu.make_async_copy(gu.at[at, i, up_rows(y)], ku.at[block_order(at), i], sem_u.at[at, i])

    def up_send(at, i):
        src, dst = gu.at[at, i, up_rows(1 - y)], ru.at[block_order(at), i]
        return remote(src, dst, send_u.at[at, i], recv_u.at[at, i], to_y)

    def up_rest(at, i):
        return pltpu.make_async_copy(gu.at[at, i, up_rows(1 - y)], rest_u.at[i], rest_sem.at[i])

    def up_ready(at, i):
        up_keep(at, i).start()

        @pl.when(at < steps - 1)
        def _():
            up_send(at, i).start()

        @pl.when(at == steps - 1)
        def _():
            up_rest(at, i).start()

    @pl.when(step == 0)
    def _():
        greet([sibling, to_x, to_y])
        out[...] = res[...]
        dh[...] = jnp.zeros_like(dh)

    def tile(wu, wd, dbu, which):
        lanes = pl.ds(pl.multiple_of(which * wu.shape[1], 128), wu.shape[1])
        up = dot(h2[...], wu[...]) + vecs[pl.ds(R_BU + block_order(step), 1), lanes]
        d_act = dot(cot[...], wd[...], 1, 1)
        act, slope = gelu_and_slope(up)
        act = act.astype(bf16)
        d_up32 = d_act * slope
        d_up = d_up32.astype(bf16)
        dbu[0] = jnp.sum(d_up32, 0, keepdims=True)
        d_wd = dot(cot[...], act, 0, 0).astype(bf16)
        d_wu = dot(h2p[...], d_up, 0, 0).astype(bf16)
        out[...] += dot(act, wd[...])
        dh[...] += dot(d_up, wu[...], 1, 1)
        return d_wd, d_wu

    @pl.when(step >= 2)
    def _():
        for copy in copies(slot):
            copy.wait_send()

    @pl.when(step < steps)
    def _():
        d_wd, d_wu = tile(wu_a, wd_a, dbu_a, 1 - c)
        send_wd[slot] = d_wd
        send_wua[slot] = d_wu[half:]
        keep_a[slot] = d_wu[:half]

    @pl.when(step > 0)
    def _():
        copies(before, (2,))[0].wait_recv()
        gu[step - 1, 0] = keep_a[before] + got_wub[before]
        up_ready(step - 1, 0)

    @pl.when(step < steps)
    def _():
        for copy in copies(slot, (0, 1)):
            copy.start()
        d_wd, d_wu = tile(wu_b, wd_b, dbu_b, c)
        send_wub[slot] = d_wu[half:]
        copies(slot, (2,))[0].start()
        for copy in copies(slot, (0, 1)):
            copy.wait_recv()
        gd[step] = d_wd + got_wd[slot]
        gu[step, 1] = d_wu[:half] + got_wua[slot]
        up_ready(step, 1)

    for at in range(4):

        @pl.when(step == at)
        def _():
            for copy in down_copy(at):
                copy.start()

    @pl.when(step == steps)
    def _():
        out_low[...] = (out[...] + vecs[R_BD : R_BD + 1, :]).astype(bf16)
        for copy in copies(before):
            copy.wait_send()
        for at in range(4):
            for copy in down_copy(at):
                copy.wait()
            for i in range(2):
                up_keep(at, i).wait()
                (up_send(at, i) if at < 3 else up_rest(at, i)).wait()


def mlp(vecs, h2, h2p, cot, res, w_up, w_down):
    rows, width = h2.shape
    ff = w_up.shape[1]
    tile = ff // 8
    half = width // 2
    steps = 4
    now = lambda i: block_order(jnp.minimum(i, steps - 1))
    at_a = lambda i: 2 * now(i) + 1 - lax.rem(lax.axis_index("items"), 2)
    at_b = lambda i: 2 * now(i) + lax.rem(lax.axis_index("items"), 2)
    w_specs = []
    for at in (at_a, at_b):
        w_specs += [
            pl.BlockSpec((width, tile), lambda i, at=at: (0, at(i))),
            pl.BlockSpec((tile, width), lambda i, at=at: (at(i), 0)),
        ]
    bias = pl.BlockSpec((1, 1, tile), lambda i: (now(i), 0, 0))
    low = lambda *shape: jax.ShapeDtypeStruct(shape, bf16)
    return pl.pallas_call(
        mlp_kernel,
        name="mlp",
        grid=(steps + 1,),
        in_specs=[VMEM] * 5 + w_specs,
        out_specs=[VMEM, VMEM] + [HBM] * 6 + [bias, bias],
        out_shape=[
            low(rows, width),
            jax.ShapeDtypeStruct((rows, width), f32),
            low(2, width, tile),
            low(2, width, tile),
            low(width // 2, tile),
            low(4, 2, half // 2, tile),
            low(4, 2, half // 2, tile),
            low(2, half // 2, tile),
        ]
        + [jax.ShapeDtypeStruct((steps, 1, tile), f32)] * 2,
        scratch_shapes=(
            [pltpu.VMEM((2, width, tile), bf16)] + [pltpu.VMEM((2, half, tile), bf16)] * 2
        )
        * 2
        + [
            pltpu.VMEM((2, half, tile), bf16),
            pltpu.VMEM((rows, width), f32),
            pltpu.VMEM((steps, width, tile), bf16),
            pltpu.VMEM((steps, 2, half, tile), bf16),
            DMA((3, 2)),
            DMA((3, 2)),
            DMA((2,)),
            DMA((2,)),
            DMA((3, 2)),
            DMA((3, 2)),
            DMA((2,)),
            DMA((4, 2)),
            DMA((3,)),
        ],
        compiler_params=params(collective_id=4, has_side_effects=True),
        cost_estimate=pl.CostEstimate(
            flops=2 * 6 * rows * width * ff, bytes_accessed=40 * 2**20, transcendentals=0
        ),
    )(vecs, h2, h2p, cot, res, w_up, w_down, w_up, w_down)


def norm_back(z, scale, dz):
    return scale * (dz - jnp.mean(dz, -1, keepdims=True) - z * jnp.mean(dz * z, -1, keepdims=True))


def normalize(value):
    centre = value - jnp.mean(value, -1, keepdims=True)
    scale = lax.rsqrt(jnp.mean(centre * centre, -1, keepdims=True) + epsilon)
    return centre * scale, scale


def tail_kernel(n_items, n_band, qt, *refs):
    (table, counts, stat, vecs, dbu_a, dbu_b, log_total) = refs[:7]
    (res_h, dh_h, cot_h, out_rows, attn_h, attn_sib_h, wo_h, q_h, k_h, v_h, h1_h) = refs[7:18]
    (wq_h, wk_h, wv_h, tok_h, kd_h, rd_h, rest_d, ku_h, ru_h, rest_u, tokens) = refs[18:29]
    (out_home, d_tok, total, o_down, o_up, o_wo, o_wq, o_wk, o_wv) = refs[29:38]
    (res, dh, cot, low, wo, attn, attn_sib, kd, rd1, rdr, rd2, rd3, rd4) = refs[38:51]
    (ku, ru1, rur, ru2, ru3, ru4, q, k, v, da, da_send, dk_acc, dv_acc) = refs[51:64]
    (h1, wq, wk, wv, tok, gw, gw_core, gw1, gw2, gw3, gw4) = refs[64:75]
    (d_pair, gp, gp_core, gp1, gp2, gp3, gp4, home) = refs[75:83]
    (small, buf_i, part, buf_b, buf_i2, part2, buf_b2) = refs[83:90]
    (send, recv, lsem, send_r, recv_r, send_g, recv_g, send_i, recv_i, send_b, recv_b) = refs[90:101]

    it, bd, c, yx = place()
    x, y = lax.rem(yx, 2), yx // 2
    bl, bh = lax.rem(bd, 2), bd // 2
    sibling = (it + 1 - 2 * c, bd)
    to_x, to_y = (it + 2 - 4 * x, bd), (it + 4 - 8 * y, bd)
    to_z1, to_z2 = (it, bd + 1 - 2 * bl), (it, lax.rem(bd + 2, 4))
    rows, width = res.shape
    half = width // 2
    fourth = width // 4
    eighth = width // 8
    tile = kd.shape[-1]
    sent = []
    loads = []

    def load(src, dst):
        copy = pltpu.make_async_copy(src, dst, lsem.at[len(loads)])
        copy.start()
        loads.append(copy)
        return copy

    def push(src, dst, to):
        i = len(sent)
        copy = remote(src, dst, send.at[i], recv.at[i], to)
        copy.start()
        sent.append(copy)
        return copy

    def some(which, size):
        return pl.ds(pl.multiple_of(which * size, 128), size)

    greet(all_peers(n_items))
    d1 = push(rest_d, rdr, to_x)
    u1 = push(rest_u, rur, to_y)
    rows_back(out_rows, out_home, send_r, recv_r)

    get_res, get_dh, get_cot = load(res_h, res), load(dh_h, dh), load(cot_h, cot)
    get_wo, get_attn, get_sib = load(wo_h, wo), load(attn_h, attn), load(attn_sib_h, attn_sib)
    get_down = [load(kd_h, kd), load(rd_h, rd1)]
    get_up = [load(ku_h, ku), load(ru_h, ru1)]
    get_qkv = [load(src, dst) for src, dst in ((q_h, q), (k_h, k), (v_h, v))]
    get_h1 = load(h1_h, h1)
    lanes = some(c, half)
    get_w = [load(src.at[:, lanes], dst) for src, dst in ((wq_h, wq), (wk_h, wk), (wv_h, wv))]
    get_tok = load(tok_h.at[pl.ds(0, rows)], tok)

    small[...] = jnp.zeros_like(small)
    for i in range(4):
        for src, h in ((dbu_a, 1 - c), (dbu_b, c)):
            small[4 + i : 5 + i, some(h, half)] = src[i]
    for copy in (get_res, get_dh, get_cot, get_wo):
        copy.wait()
    block = 256

    @pl.loop(0, rows // block)
    def _(i):
        at = some(i, block)
        z, scale = normalize(res[at, :])
        d_h = dh[at, :]
        c32 = cot[at, :].astype(f32)
        full = c32 + norm_back(z, scale, d_h * vecs[R_G2 : R_G2 + 1, :])
        res[at, :] = full
        d_low = full.astype(bf16)
        low[at, :] = d_low
        for j, term in enumerate((d_h * z, d_h, d_low.astype(f32), c32)):
            small[j : j + 1, :] += jnp.sum(term, 0, keepdims=True)
        da[at, :] = dot(d_low, half_rows(wo, c, half), 1, 1).astype(bf16)
        da_send[at, :] = dot(d_low, half_rows(wo, 1 - c, half), 1, 1).astype(bf16)

    da_copy = push(da_send, da.at[pl.ds(rows, rows)], sibling)
    early = share_start(
        n_items, it, lambda p: (p, bd), small.at[pl.ds(0, 8)], buf_i, send_i.at[0], recv_i.at[0]
    )

    get_attn.wait()
    get_sib.wait()
    for i, heads in enumerate((attn, attn_sib)):
        for xx in range(2):
            part_wo = dot(heads[:, xx * fourth : (xx + 1) * fourth], low[...], 0, 0).astype(bf16)
            for cc in range(2):
                gw[i, xx, cc] = part_wo[cc * eighth : (cc + 1) * eighth]
    core_w = [push(gw.at[i, :, 1 - c], gw_core.at[1 - i], sibling) for i in range(2)]

    for copy in get_down + get_up:
        copy.wait()
    d1.wait_recv()
    kd[0] += rd1[0]
    kd[1, 0:half] += rd1[1, 0:half]
    kd[1, half:width] += rdr[...]
    d2 = push(kd.at[1 - y], rd2, to_y)
    u1.wait_recv()
    for s in range(3):
        ku[block_order(s)] += ru1[block_order(s)]
    ku[block_order(3)] += rur[...]
    theirs, mine = some(1 - x, tile // 4), some(x, tile // 4)
    u2 = push(ku.at[:, :, theirs], ru2, to_x)

    for copy in get_qkv:
        copy.wait()
    get_h1.wait()
    da_copy.wait_recv()
    lane_k = lax.broadcasted_iota(jnp.int32, (2 * rows, 128), 1)
    lane_q = lax.broadcasted_iota(jnp.int32, (qt, 128), 1)

    def pair(i):
        at_lanes = some(i, 128)
        k_pair, v_pair = k[:, at_lanes], v[:, at_lanes]
        bias = key_bias(table, counts, k_pair.shape)
        keys = [with_spare(k_pair, bias, hd, lane_k) for hd in range(2)]
        keys_only = [head_lanes(k_pair, hd, lane_k) for hd in range(2)]
        values = [head_lanes(v_pair, hd, lane_k) for hd in range(2)]
        for t in range(2 * rows // qt):
            at = slice(t * qt, (t + 1) * qt)
            q_tile, d_tile = q[at, at_lanes], da[at, at_lanes]
            dq_both = None
            for hd in range(2):
                q_head = head_lanes(q_tile, hd, lane_q)
                d_head = head_lanes(d_tile, hd, lane_q)
                s = dot(keys[hd], ones_beside(q_tile, hd, lane_q), 1, 1)
                p = jnp.exp(s - log_total[i, hd : hd + 1, at])
                d_p = dot(values[hd], d_tile, 1, 1)
                weighted = p * d_p
                delta = jnp.sum(weighted, 0, keepdims=True)
                ds = (weighted - p * delta).astype(bf16)
                dv_part = dot(p.astype(bf16), d_head)
                dk_part = dot(ds, q_head)
                if t == 0 and hd == 0:
                    dv_acc[...] = dv_part
                    dk_acc[...] = dk_part
                else:
                    dv_acc[...] += dv_part
                    dk_acc[...] += dk_part
                term = dot(keys_only[hd], ds, 0, 0)
                dq_both = term if dq_both is None else dq_both + term
            dq = dq_both.T * score_scale
            q[at, at_lanes] = dq.astype(bf16)
            d_pair[at, 0:128] = dq.astype(bf16)
        k[:, at_lanes] = dk_acc[...].astype(bf16)
        v[:, at_lanes] = dv_acc[...].astype(bf16)
        d_pair[:, 128:256] = dk_acc[...].astype(bf16)
        d_pair[:, 256:384] = dv_acc[...].astype(bf16)
        for j in range(4):
            term = dot(h1[:, j * fourth : (j + 1) * fourth], d_pair[...], 0, 0).astype(bf16)
            for cc in range(2):
                gp[i, j, cc] = term[cc * eighth : (cc + 1) * eighth]

    def pair_core(i):
        return push(gp.at[i, :, 1 - c], gp_core.at[i], sibling)

    def chips(i, first, second):
        return 2 * second + first if i % 2 == 0 else 2 * first + second

    def first_of(i):
        return (x, y) if i % 2 == 0 else (y, x)

    def pair_first(i, core):
        core.wait_recv()
        mine_first, _ = first_of(i)
        to = to_x if i % 2 == 0 else to_y
        got = []
        for j in range(2):
            there = chips(i, 1 - mine_first, j)
            got.append(push(gp.at[i, there, c], gp1.at[i, j, 0], to))
            got.append(push(gp_core.at[i, there], gp1.at[i, j, 1], to))
        return got

    def pair_second(i, got):
        for copy in got:
            copy.wait_recv()
        mine_first, mine_second = first_of(i)
        for j in range(2):
            here = chips(i, mine_first, j)
            gp[i, here, c] += gp1[i, j, 0]
            gp_core[i, here] += gp1[i, j, 1]
        there = chips(i, mine_first, 1 - mine_second)
        to = to_y if i % 2 == 0 else to_x
        return [
            push(gp.at[i, there, c], gp2.at[i, 0], to),
            push(gp_core.at[i, there], gp2.at[i, 1], to),
        ]

    def pair_third(i, got):
        for copy in got:
            copy.wait_recv()
        gp[i, yx, c] += gp2[i, 0]
        gp_core[i, yx] += gp2[i, 1]

    pair(0)
    core_p = [pair_core(0)]
    part[...] = share_end(n_items, early, buf_i)
    early = share_start(n_band, bd, lambda p: (it, p), part, buf_b, send_b.at[0], recv_b.at[0])
    for i in range(2):
        core_w[i].wait_recv()
    for i in range(2):
        gw[i, :, c] += gw_core[i]
    rel_y = lax.rem(y + c, 2)
    w1 = push(gw.at[1 - rel_y, :, c], gw1, to_y)

    pair(1)
    core_p.append(pair_core(1))
    p1 = [pair_first(0, core_p[0])]
    total[0:8, :] = share_end(n_band, early, buf_b)

    pair(2)
    core_p.append(pair_core(2))
    p1.append(pair_first(1, core_p[1]))
    d2.wait_recv()
    kd[y] += rd2[...]
    down = kd.reshape(2, 2, 2, fourth, tile)
    d3 = push(down.at[y, :, 1 - bl], rd3, to_z1)
    u2.wait_recv()
    ku[:, :, mine] += ru2[...]
    up = ku.reshape(2, 2, 2, tile // 2, tile)
    u3 = push(up.at[:, 1 - bl, :, mine], ru3, to_z1)

    pair(3)
    core_p.append(pair_core(3))
    p1.append(pair_first(2, core_p[2]))
    for i, d in ((0, q), (1, v)):
        row = jnp.sum(d[...].astype(f32), 0, keepdims=True)
        small[12 + i : 13 + i, some(c, half)] = row
    w1.wait_recv()
    gw[rel_y, :, c] += gw1[...]
    w2 = push(gw.at[rel_y, 1 - x, c], gw2, to_x)

    for copy in get_w:
        copy.wait()
    dh1, dh1_sib = wo, low

    def first_norm_terms(i):
        at = some(i, block)
        term = dot(q[at, :], wq[...], 1, 1) + dot(k[at, :], wk[...], 1, 1)
        dh1[at, :] = (term + dot(v[at, :], wv[...], 1, 1)).astype(bf16)

    @pl.loop(rows // block, 2 * rows // block)
    def _(i):
        first_norm_terms(i)

    dh_copy = push(dh1.at[pl.ds(rows, rows)], dh1_sib, sibling)
    p1.append(pair_first(3, core_p[3]))
    p2 = [pair_second(0, p1[0])]

    @pl.loop(0, rows // block)
    def _(i):
        first_norm_terms(i)

    get_tok.wait()
    dh_copy.wait_recv()
    g_rows = cot

    @pl.loop(0, rows // block)
    def _(i):
        at = some(i, block)
        inv = stat[S_INV : S_INV + 1, :]
        centred = tok[at, :].astype(f32) - stat[S_MEAN : S_MEAN + 1, :]
        z, scale = normalize(centred * inv)
        d_h = dh1[at, :].astype(f32) + dh1_sib[at, :].astype(f32)
        d_start = res[at, :] + norm_back(z, scale, d_h * vecs[R_G1 : R_G1 + 1, :])
        g_rows[at, :] = (d_start * inv).astype(bf16)
        for j, term in enumerate((d_start, d_start * centred, d_h * z, d_h)):
            small[8 + j : 9 + j, :] += jnp.sum(term, 0, keepdims=True)

    late = share_start(
        n_items, it, lambda p: (p, bd), small.at[pl.ds(8, 8)], buf_i2, send_i.at[1], recv_i.at[1]
    )
    g_blocks = g_rows.reshape(4, rows // 4, width)
    rows_back(g_blocks, home, send_g, recv_g)
    p2.append(pair_second(1, p1[1]))
    part2[...] = share_end(n_items, late, buf_i2)
    late = share_start(n_band, bd, lambda p: (it, p), part2, buf_b2, send_b.at[1], recv_b.at[1])

    d3.wait_recv()
    for high in range(2):
        down[y, high, bl] += rd3[high]
    d4 = push(down.at[y, 1 - bh, bl], rd4, to_z2)
    u3.wait_recv()
    for high in range(2):
        up[high, bl, :, mine] += ru3[high]
    u4 = push(up.at[1 - bh, bl, :, mine], ru4, to_z2)
    p2.append(pair_second(2, p1[2]))
    w2.wait_recv()
    gw[rel_y, x, c] += gw2[...]

    def z_lanes(which):
        return some(which, fourth)

    w3 = [
        push(gw.at[rel_y, x, c, :, z_lanes(2 * high + 1 - bl)], gw3.at[high], to_z1) for high in range(2)
    ]
    p2.append(pair_second(3, p1[3]))
    sums = share_end(n_band, late, buf_b2)
    total[8:16, :] = sums

    for i in range(4):
        pair_third(i, p2[i])
    p3 = []
    for i in range(2):
        there = 2 * (1 - bl) + i
        p3.append(push(gp.at[there, yx, c], gp3.at[i, 0], to_z1))
        p3.append(push(gp_core.at[there, yx], gp3.at[i, 1], to_z1))

    for high in range(2):
        w3[high].wait_recv()
    for high in range(2):
        gw3[high] = gw[rel_y, x, c, :, z_lanes(2 * high + bl)] + gw3[high]
    w4 = push(gw3.at[1 - bh], gw4, to_z2)
    for copy in p3:
        copy.wait_recv()
    for i in range(2):
        here = 2 * bl + i
        gp3[i, 0] = gp[here, yx, c] + gp3[i, 0]
        gp3[i, 1] = gp_core[here, yx] + gp3[i, 1]
    rel_b = lax.rem(bh + c, 2)
    p4 = push(gp3.at[:, 1 - rel_b], gp4, to_z2)

    count = patch_total(counts, (1, width))
    inv = stat[S_INV : S_INV + 1, :]
    fix = -0.5 * inv * sums[0:1, :] / count
    slope = -0.5 * inv * inv * inv * sums[1:2, :] / count
    cut = rows // 4
    position = lax.broadcasted_iota(jnp.int32, (cut, width), 0) + bd * (2 * cut)
    for i in range(4):
        s, h = i // 2, i % 2
        rows_back_got(g_blocks, home, send_g, recv_g, i)
        now = pl.ds(h * cut, cut)
        valid = position + h * cut < counts[table[it * 2 + s]]
        term = fix + slope * (tokens[s, now, :].astype(f32) - stat[S_BATCH : S_BATCH + 1, :])
        d_tok[s, now, :] = (home[s, now, :].astype(f32) + jnp.where(valid, term, 0.0)).astype(bf16)

    d4.wait_recv()
    o_down[...] = (down[y, bh, bl].astype(f32) + rd4[...].astype(f32)).T
    u4.wait_recv()
    up_sum = up[bh, bl, :, mine].astype(f32) + ru4[...].astype(f32)
    for i, h in ((0, 1 - c), (1, c)):
        o_up[:, some(h, tile)] = up_sum[i]
    w4.wait_recv()
    o_wo[...] = gw3[bh].astype(f32) + gw4[...].astype(f32)
    p4.wait_recv()
    for i in range(2):
        all_three = gp3[i, rel_b].astype(f32) + gp4[i].astype(f32)
        for j, ref in enumerate((o_wq, o_wk, o_wv)):
            ref[:, i * 128 : (i + 1) * 128] = all_three[:, j * 128 : (j + 1) * 128]

    for i in range(4):
        rows_back_got(out_rows, out_home, send_r, recv_r, i)
    rows_back_sent(out_rows, out_home, send_r, recv_r)
    rows_back_sent(g_blocks, home, send_g, recv_g)
    for copy in sent:
        copy.wait_send()


def tail(table, counts, stat, vecs, dbu_a, dbu_b, log_total, res, dh, cot, out_rows, *rest, qt=512):
    attn, attn_sib, wo, q, k, v, h1, wq, wk, wv, tok, kd, rd, rest_d, ku, ru, rest_u, tokens = rest
    n_items, n_band = lax.axis_size("items"), lax.axis_size("band")
    rows, width = res.shape
    half, fourth, cut = width // 2, width // 4, rows // 4
    tile = kd.shape[2]
    buf = lambda *shape: pltpu.VMEM(shape, bf16)
    buf32 = lambda *shape: pltpu.VMEM(shape, f32)
    out = lambda *shape: jax.ShapeDtypeStruct(shape, f32)
    e, s = fourth // 2, fourth
    return pl.pallas_call(
        functools.partial(tail_kernel, n_items, n_band, qt),
        name="tail",
        in_specs=[SMEM, SMEM] + [VMEM] * 5 + [HBM] * 21 + [VMEM],
        out_specs=[HBM] + [VMEM] * 8,
        out_shape=[
            jax.ShapeDtypeStruct(tokens.shape, bf16),
            jax.ShapeDtypeStruct(tokens.shape, bf16),
            out(16, width),
            out(tile, s),
            out(e, 2 * tile),
            out(e, s),
            out(e, s),
            out(e, s),
            out(e, s),
        ],
        scratch_shapes=[
            buf32(rows, width), buf32(rows, width), buf(rows, width), buf(rows, width),
            buf(width, width), buf(rows, half), buf(rows, half),
            buf(2, width, tile), buf(2, width, tile), buf(half, tile), buf(width, tile), buf(2, s, tile),
            buf(s, tile),
            buf(4, 2, tile // 2, tile), buf(4, 2, tile // 2, tile), buf(2, tile // 2, tile),
            buf(4, 2, tile // 4, tile), buf(2, 2, tile // 4, tile), buf(2, tile // 4, tile),
            buf(2 * rows, half), buf(2 * rows, half), buf(2 * rows, half),
            buf(2 * rows, half), buf(rows, half), buf32(2 * rows, 128), buf32(2 * rows, 128),
            buf(2 * rows, width), buf(width, half), buf(width, half), buf(width, half), buf(rows, width),
            buf(2, 2, 2, e, width), buf(2, 2, e, width), buf(2, e, width), buf(e, width),
            buf(2, e, s), buf(e, s),
            buf(2 * rows, 384), buf(4, 4, 2, e, 384), buf(4, 4, e, 384), buf(4, 2, 2, e, 384),
            buf(4, 2, e, 384), buf(2, 2, e, 384), buf(2, e, 384),
            buf(2, 2 * cut, width),
            buf32(16, width), buf32(n_items, 8, width), buf32(8, width), buf32(n_band, 8, width),
            buf32(n_items, 8, width), buf32(8, width), buf32(n_band, 8, width),
            DMA((64,)), DMA((64,)), DMA((24,)),
            DMA((4,)), DMA((4,)), DMA((4,)), DMA((4,)),
            DMA((2, n_items)), DMA((2, n_items)), DMA((2, n_band)), DMA((2, n_band)),
        ],
        compiler_params=params(collective_id=5, has_side_effects=True),
        cost_estimate=pl.CostEstimate(
            flops=60 * rows * width * width, bytes_accessed=40 * 2**20, transcendentals=0
        ),
    )(
        table, counts, stat, vecs, dbu_a, dbu_b, log_total, res, dh, cot,
        out_rows.reshape(4, cut, width), attn, attn_sib, wo, q, k, v, h1, wq, wk, wv, tok,
        kd, rd, rest_d, ku, ru, rest_u, tokens,
    )


def column_layer(
    tokens, cotangent, running_mean, running_var, slot_table, patch_counts,
    ln1_gain, ln1_bias, w_query, b_query, w_key, w_value, b_value, w_out, b_out,
    ln2_gain, ln2_bias, w_up, b_up, w_down, b_down,
):
    slots, band_rows, width = tokens.shape
    rows = slots * band_rows
    parts = (running_mean, running_var, ln1_gain, ln1_bias, b_query, b_value, b_out)
    parts += (ln2_gain, ln2_bias, b_down, b_up)
    vecs = jnp.concatenate([part.astype(f32) for part in parts]).reshape(-1, width)
    gathered, stat = gather(slot_table, patch_counts, vecs, tokens)
    tok = gathered.reshape(2 * rows, width)
    h1, q, k, v = project(stat, vecs, tok, w_query, w_key, w_value)
    attn, log_total, cot_rows, attn_sib = attend(slot_table, patch_counts, q, k, v, cotangent)
    cot_rows = cot_rows.reshape(rows, width)
    res, h2, h2p = join(stat, vecs, attn, attn_sib, w_out, tok)
    out_rows, d_h2, kd, rd, rest_d, ku, ru, rest_u, dbu_a, dbu_b = mlp(
        vecs, h2, h2p, cot_rows, res, w_up, w_down
    )
    output, d_tokens, small, d_w_down, d_w_up, d_w_out, d_wq, d_wk, d_wv = tail(
        slot_table, patch_counts, stat, vecs, dbu_a, dbu_b, log_total, res, d_h2, cot_rows,
        out_rows, attn, attn_sib, w_out, q, k, v, h1, w_query, w_key, w_value, tok,
        kd, rd, rest_d, ku, ru, rest_u, tokens,
    )
    d_gain_two, d_shift_two, d_bo, d_bdown = (small[i] for i in range(4))
    d_gain_one, d_shift_one, d_bq, d_bv = (small[i] for i in range(10, 14))
    return (
        output, d_tokens, stat[S_MEAN], stat[S_VAR], d_gain_one, d_shift_one,
        d_wq, d_bq, d_wk, d_wv, d_bv, d_w_out, d_bo, d_gain_two, d_shift_two,
        d_w_up, small[4:8].reshape(-1), d_w_down, d_bdown,
    )


def layer_norm(value, gain, shift):
    centre = value - jnp.mean(value, -1, keepdims=True)
    spread = jnp.mean(centre * centre, -1, keepdims=True)
    return centre * lax.rsqrt(spread + epsilon) * gain + shift


def gelu_tanh(value):
    return (
        0.5
        * value
        * (1.0 + jnp.tanh(0.7978845608028654 * (value + 0.044715 * value * value * value)))
    )


def head_layout():
    heads_per = 4
    return (heads_per, HEADS // heads_per, heads_per * HEAD_DIM)


def group_scores(q_part, k_part, key_mask):
    scores = (
        jnp.einsum("rhd,khd->hrk", q_part, k_part, preferred_element_type=jnp.float32) * score_scale
    )
    return jnp.where(key_mask[None, None, :], scores, masked_score)


def attend_forward(q_slot, keys_slot, values_slot, key_mask):
    heads_per, groups, group_width = head_layout()
    band_rows = q_slot.shape[0]
    seq_length = keys_slot.shape[0]

    def head_block(group_index):
        begin = group_index * group_width
        q_part = lax.dynamic_slice_in_dim(q_slot, begin, group_width, 1).reshape(
            band_rows, heads_per, HEAD_DIM
        )
        k_part = lax.dynamic_slice_in_dim(keys_slot, begin, group_width, 1).reshape(
            seq_length, heads_per, HEAD_DIM
        )
        v_part = lax.dynamic_slice_in_dim(values_slot, begin, group_width, 1).reshape(
            seq_length, heads_per, HEAD_DIM
        )
        scores = group_scores(q_part, k_part, key_mask)
        top_score = jnp.max(scores, -1, keepdims=True)
        log_total = top_score + jnp.log(jnp.sum(jnp.exp(scores - top_score), -1, keepdims=True))
        probs_low = jnp.exp(scores - log_total).astype(jnp.bfloat16)
        attended = jnp.einsum("hrk,khd->rhd", probs_low, v_part, preferred_element_type=jnp.float32)
        return (attended.reshape(band_rows, group_width), log_total[..., 0])

    attended, log_totals = lax.map(head_block, jnp.arange(groups, dtype=jnp.int32))
    return (attended.transpose(1, 0, 2).reshape(band_rows, groups * group_width), log_totals)


def attend_backward(q_slot, keys_slot, values_slot, key_mask, d_attn_slot, row_delta, log_totals):
    heads_per, groups, group_width = head_layout()
    query_rows = q_slot.shape[0]
    seq_length = keys_slot.shape[0]
    deltas = jnp.transpose(row_delta).reshape(groups, heads_per, query_rows)

    def head_block(inputs):
        group_index, log_total, delta_part = inputs
        begin = group_index * group_width
        q_part = lax.dynamic_slice_in_dim(q_slot, begin, group_width, 1).reshape(
            query_rows, heads_per, HEAD_DIM
        )
        k_part = lax.dynamic_slice_in_dim(keys_slot, begin, group_width, 1).reshape(
            seq_length, heads_per, HEAD_DIM
        )
        v_part = lax.dynamic_slice_in_dim(values_slot, begin, group_width, 1).reshape(
            seq_length, heads_per, HEAD_DIM
        )
        d_part = lax.dynamic_slice_in_dim(d_attn_slot, begin, group_width, 1).reshape(
            query_rows, heads_per, HEAD_DIM
        )
        scores = group_scores(q_part, k_part, key_mask)
        probs = jnp.exp(scores - log_total[..., None])
        d_probs = jnp.einsum("rhd,khd->hrk", d_part, v_part, preferred_element_type=jnp.float32)
        d_scores = (probs * (d_probs - delta_part[..., None])).astype(jnp.bfloat16)
        results = []
        d_q_part = (
            jnp.einsum("hrk,khd->rhd", d_scores, k_part, preferred_element_type=jnp.float32)
            * score_scale
        )
        results.append(d_q_part.reshape(query_rows, group_width))
        probs_low = probs.astype(jnp.bfloat16)
        d_k_part = (
            jnp.einsum("hrk,rhd->khd", d_scores, q_part, preferred_element_type=jnp.float32)
            * score_scale
        )
        d_v_part = jnp.einsum("hrk,rhd->khd", probs_low, d_part, preferred_element_type=jnp.float32)
        results.append(d_k_part.reshape(seq_length, group_width))
        results.append(d_v_part.reshape(seq_length, group_width))
        return tuple(results)

    mapped = lax.map(head_block, (jnp.arange(groups, dtype=jnp.int32), log_totals, deltas))
    full_width = groups * group_width
    return tuple((piece.transpose(1, 0, 2).reshape(piece.shape[1], full_width) for piece in mapped))


def local(
    tokens,
    cotangent,
    running_mean,
    running_var,
    slot_table,
    patch_counts,
    ln1_gain,
    ln1_bias,
    w_query,
    b_query,
    w_key,
    w_value,
    b_value,
    w_out,
    b_out,
    ln2_gain,
    ln2_bias,
    w_up,
    b_up,
    w_down,
    b_down,
):
    slot_count, band_rows, model_width = tokens.shape
    seq_length = band_rows * lax.axis_size("band")
    item_rank = lax.axis_index("items")
    band_rank = lax.axis_index("band")
    every_slot = jnp.arange(slot_table.shape[0], dtype=jnp.int32)
    my_slots = item_rank * slot_count + jnp.arange(slot_count, dtype=jnp.int32)
    item_ids = jnp.sum(
        jnp.where(every_slot[None, :] == my_slots[:, None], slot_table[None, :], 0), 1
    )
    lengths = jnp.sum(
        jnp.where(every_slot[None, :] == item_ids[:, None], patch_counts[None, :], 0), 1
    )
    key_mask = jnp.arange(seq_length, dtype=jnp.int32)[None, :] < lengths[:, None]
    row_mask = (band_rank * band_rows + jnp.arange(band_rows, dtype=jnp.int32))[None, :] < lengths[
        :, None
    ]
    row_keep = row_mask.astype(jnp.float32).reshape(-1, 1)
    raw_flat = tokens.astype(jnp.float32).reshape(-1, model_width)
    part_one = jnp.sum(row_keep * raw_flat, 0)
    part_two = jnp.sum(row_keep * raw_flat * raw_flat, 0)
    total_one, total_two = lax.psum((part_one, part_two), ("items", "band"))
    patch_total = jnp.sum(patch_counts).astype(jnp.float32)
    batch_mean = total_one / patch_total
    batch_var = total_two / patch_total - batch_mean * batch_mean
    new_mean = momentum * running_mean + momentum * batch_mean
    new_var = momentum * running_var + momentum * batch_var
    inverse = lax.rsqrt(new_var + epsilon)
    normed_in = (raw_flat - new_mean) * inverse
    gain_one = ln1_gain.astype(jnp.float32)
    shift_one = ln1_bias.astype(jnp.float32)
    gain_two = ln2_gain.astype(jnp.float32)
    shift_two = ln2_bias.astype(jnp.float32)
    h_one_full, norm_one_back = jax.vjp(layer_norm, normed_in, gain_one, shift_one)
    h_one = h_one_full.astype(jnp.bfloat16)
    queries = (
        jnp.dot(h_one, w_query, preferred_element_type=jnp.float32) + b_query.astype(jnp.float32)
    ).astype(jnp.bfloat16)
    key_local = (
        jnp.dot(h_one, w_key, preferred_element_type=jnp.float32)
        .astype(jnp.bfloat16)
        .reshape(slot_count, band_rows, model_width)
    )
    value_local = (
        (jnp.dot(h_one, w_value, preferred_element_type=jnp.float32) + b_value.astype(jnp.float32))
        .astype(jnp.bfloat16)
        .reshape(slot_count, band_rows, model_width)
    )
    keys_all, values_all = (
        lax.all_gather(key_local, "band", axis=1, tiled=True),
        lax.all_gather(value_local, "band", axis=1, tiled=True),
    )
    q_slots = queries.reshape(slot_count, band_rows, model_width)
    attended_list = []
    totals_list = []
    for slot_index in range(slot_count):
        attended, log_totals = attend_forward(
            q_slots[slot_index], keys_all[slot_index], values_all[slot_index], key_mask[slot_index]
        )
        attended_list.append(attended)
        totals_list.append(log_totals)
    attn_full = jnp.concatenate(attended_list, 0)
    attn_low = attn_full.astype(jnp.bfloat16)
    residual = (
        normed_in
        + jnp.dot(attn_low, w_out, preferred_element_type=jnp.float32)
        + b_out.astype(jnp.float32)
    )
    h_two_full, norm_two_back = jax.vjp(layer_norm, residual, gain_two, shift_two)
    h_two = h_two_full.astype(jnp.bfloat16)
    up_proj = jnp.dot(h_two, w_up, preferred_element_type=jnp.float32) + b_up.astype(jnp.float32)
    activated_full, gelu_back = jax.vjp(gelu_tanh, up_proj)
    activated = activated_full.astype(jnp.bfloat16)
    result = (
        residual
        + jnp.dot(activated, w_down, preferred_element_type=jnp.float32)
        + b_down.astype(jnp.float32)
    )
    output = result.astype(jnp.bfloat16).reshape(slot_count, band_rows, model_width)
    cot_low = cotangent.reshape(-1, model_width)
    cot_full = cot_low.astype(jnp.float32)
    d_w_down = jnp.einsum("tf,td->fd", activated, cot_low, preferred_element_type=jnp.float32)
    d_b_down = jnp.sum(cot_full, 0)
    d_activated = jnp.einsum("td,fd->tf", cot_low, w_down, preferred_element_type=jnp.float32)
    (d_up_full,) = gelu_back(d_activated)
    d_up = d_up_full.astype(jnp.bfloat16)
    d_w_up = jnp.einsum("td,tf->df", h_two, d_up, preferred_element_type=jnp.float32)
    d_b_up = jnp.sum(d_up, 0, dtype=jnp.float32)
    d_h_two = jnp.einsum("tf,df->td", d_up, w_up, preferred_element_type=jnp.float32)
    d_res_norm, d_gain_two, d_shift_two = norm_two_back(d_h_two)
    d_residual = cot_full + d_res_norm
    d_branch = d_residual.astype(jnp.bfloat16)
    d_w_out = jnp.einsum("td,te->de", attn_low, d_branch, preferred_element_type=jnp.float32)
    d_b_out = jnp.sum(d_branch, 0, dtype=jnp.float32)
    d_attn = jnp.einsum("te,de->td", d_branch, w_out, preferred_element_type=jnp.float32).astype(
        jnp.bfloat16
    )
    row_delta = jnp.sum(
        (d_attn.astype(jnp.float32) * attn_full).reshape(slot_count, band_rows, HEADS, HEAD_DIM), -1
    )
    d_attn_slots = d_attn.reshape(slot_count, band_rows, model_width)
    back_keys, back_values = (keys_all, values_all)
    d_q_list = []
    d_k_list = []
    d_v_list = []
    for slot_index in range(slot_count):
        d_q_slot, d_k_slot, d_v_slot = attend_backward(
            q_slots[slot_index],
            back_keys[slot_index],
            back_values[slot_index],
            key_mask[slot_index],
            d_attn_slots[slot_index],
            row_delta[slot_index],
            totals_list[slot_index],
        )
        d_q_list.append(d_q_slot)
        d_k_list.append(d_k_slot)
        d_v_list.append(d_v_slot)
    d_keys_mine, d_values_mine = (
        lax.psum_scatter(
            jnp.stack(d_k_list).astype(jnp.bfloat16), "band", scatter_dimension=1, tiled=True
        ).astype(jnp.float32),
        lax.psum_scatter(
            jnp.stack(d_v_list).astype(jnp.bfloat16), "band", scatter_dimension=1, tiled=True
        ).astype(jnp.float32),
    )
    d_queries = jnp.concatenate(d_q_list, 0).astype(jnp.bfloat16)
    d_keys = d_keys_mine.reshape(-1, model_width).astype(jnp.bfloat16)
    d_values = d_values_mine.reshape(-1, model_width).astype(jnp.bfloat16)
    d_w_query = jnp.einsum("td,te->de", h_one, d_queries, preferred_element_type=jnp.float32)
    d_b_query = jnp.sum(d_queries, 0, dtype=jnp.float32)
    d_w_key = jnp.einsum("td,te->de", h_one, d_keys, preferred_element_type=jnp.float32)
    d_w_value = jnp.einsum("td,te->de", h_one, d_values, preferred_element_type=jnp.float32)
    d_b_value = jnp.sum(d_values, 0, dtype=jnp.float32)
    d_h_one = jnp.einsum("te,de->td", d_queries, w_query, preferred_element_type=jnp.float32)
    d_h_one = d_h_one + jnp.einsum("te,de->td", d_keys, w_key, preferred_element_type=jnp.float32)
    d_h_one = d_h_one + jnp.einsum(
        "te,de->td", d_values, w_value, preferred_element_type=jnp.float32
    )
    d_start_norm, d_gain_one, d_shift_one = norm_one_back(d_h_one)
    d_start = d_residual + d_start_norm
    centred = raw_flat - new_mean
    small_sums = lax.psum(
        (
            jnp.sum(d_start, 0),
            jnp.sum(d_start * centred, 0),
            d_gain_one,
            d_shift_one,
            d_b_query,
            d_b_value,
            d_b_out,
            d_gain_two,
            d_shift_two,
            d_b_up,
            d_b_down,
        ),
        ("items", "band"),
    )
    sum_g = small_sums[0]
    sum_gx = small_sums[1]
    cube = inverse * inverse * inverse
    d_raw = d_start * inverse + row_keep * (
        -0.5 * inverse * sum_g / patch_total
        - 0.5 * cube * sum_gx * (raw_flat - batch_mean) / patch_total
    )
    d_tokens = d_raw.astype(jnp.bfloat16).reshape(slot_count, band_rows, model_width)
    weight_grads = (
        lax.psum_scatter(
            d_w_query.astype(jnp.bfloat16), "items", scatter_dimension=0, tiled=True
        ).astype(jnp.float32),
        lax.psum_scatter(
            d_w_key.astype(jnp.bfloat16), "items", scatter_dimension=0, tiled=True
        ).astype(jnp.float32),
        lax.psum_scatter(
            d_w_value.astype(jnp.bfloat16), "items", scatter_dimension=0, tiled=True
        ).astype(jnp.float32),
        lax.psum_scatter(
            d_w_out.astype(jnp.bfloat16), "items", scatter_dimension=0, tiled=True
        ).astype(jnp.float32),
        lax.psum_scatter(
            d_w_up.astype(jnp.bfloat16), "items", scatter_dimension=0, tiled=True
        ).astype(jnp.float32),
        lax.psum_scatter(
            d_w_down.astype(jnp.bfloat16), "items", scatter_dimension=0, tiled=True
        ).astype(jnp.float32),
    )
    weight_grads = (
        lax.psum_scatter(
            weight_grads[0].astype(jnp.bfloat16), "band", scatter_dimension=1, tiled=True
        ).astype(jnp.float32),
        lax.psum_scatter(
            weight_grads[1].astype(jnp.bfloat16), "band", scatter_dimension=1, tiled=True
        ).astype(jnp.float32),
        lax.psum_scatter(
            weight_grads[2].astype(jnp.bfloat16), "band", scatter_dimension=1, tiled=True
        ).astype(jnp.float32),
        lax.psum_scatter(
            weight_grads[3].astype(jnp.bfloat16), "band", scatter_dimension=1, tiled=True
        ).astype(jnp.float32),
        lax.psum_scatter(
            weight_grads[4].astype(jnp.bfloat16), "band", scatter_dimension=1, tiled=True
        ).astype(jnp.float32),
        lax.psum_scatter(
            weight_grads[5].astype(jnp.bfloat16), "band", scatter_dimension=1, tiled=True
        ).astype(jnp.float32),
    )
    return (
        output,
        d_tokens,
        new_mean,
        new_var,
        small_sums[2],
        small_sums[3],
        weight_grads[0],
        small_sums[4],
        weight_grads[1],
        weight_grads[2],
        small_sums[5],
        weight_grads[3],
        small_sums[6],
        small_sums[7],
        small_sums[8],
        weight_grads[4],
        small_sums[9],
        weight_grads[5],
        small_sums[10],
    )


def solution(mesh):
    columns = mesh.shape["items"] == 8 and mesh.shape["band"] == 4
    return jax.shard_map(
        column_layer if columns else local,
        mesh=mesh,
        in_specs=(
            P("items", "band", None),
            P("items", "band", None),
            P(),
            P(),
            P(),
            P(),
            P(),
            P(),
            P(),
            P(),
            P(),
            P(),
            P(),
            P(),
            P(),
            P(),
            P(),
            P(),
            P(),
            P(),
            P(),
        ),
        out_specs=(
            P("items", "band", None),
            P("items", "band", None),
            P(),
            P(),
            P(),
            P(),
            P("items", "band"),
            P(),
            P("items", "band"),
            P("items", "band"),
            P(),
            P("items", "band"),
            P(),
            P(),
            P(),
            P("items", "band"),
            P(),
            P("items", "band"),
            P(),
        ),
        check_vma=False,
    )
```

```python
import functools
import jax
import jax.numpy as jnp
from jax import lax
from jax.experimental import pallas as pl
from jax.experimental.pallas import tpu as pltpu
from jax.sharding import PartitionSpec as P

HEADS = 16
HEAD_DIM = 64
epsilon = 1e-05
score_scale = 0.125
masked_score = -1e30
momentum = 0.5
f32 = jnp.float32
bf16 = jnp.bfloat16
VMEM_LIMIT = 60 * 2**20
R_MEAN, R_VAR, R_G1, R_S1, R_BQ, R_BV, R_BO, R_G2, R_S2, R_BD, R_BU = range(11)
S_MEAN, S_VAR, S_BATCH, S_INV = range(4)


def dot(a, b, ca=1, cb=0):
    return lax.dot_general(a, b, (((ca,), (cb,)), ((), ())), preferred_element_type=f32)


def params(**kw):
    return pltpu.CompilerParams(vmem_limit_bytes=VMEM_LIMIT, **kw)


def place():
    it, bd = lax.axis_index("items"), lax.axis_index("band")
    return it, bd, lax.rem(it, 2), it // 2


def remote(src, dst, send, recv, to):
    return pltpu.make_async_remote_copy(
        src_ref=src,
        dst_ref=dst,
        send_sem=send,
        recv_sem=recv,
        device_id=to,
        device_id_type=pl.DeviceIdType.MESH,
    )


def greet(peers):
    barrier = pltpu.get_barrier_semaphore()
    for peer in peers:
        pl.semaphore_signal(barrier, inc=1, device_id=peer, device_id_type=pl.DeviceIdType.MESH)
    pl.semaphore_wait(barrier, len(peers))


def column_peers():
    it, bd, c, yx = place()
    peers = [(it, lax.rem(bd + o, 4)) for o in range(1, 4)]
    return peers + [(it + 1 - 2 * c, lax.rem(bd + o, 4)) for o in range(4)]


def rows_out(src, dst, send, recv):
    it, bd, c, yx = place()
    cut = src.shape[1] // 2
    for q in range(4):
        s, h = q // 2, q % 2
        block = src.at[s, pl.ds(h * cut, cut)]
        target = dst.at[bd]
        own = (c == h) & (bd == 2 * c + s)

        @pl.when(own)
        def _():
            pltpu.make_async_copy(block, target, recv.at[bd]).start()

        @pl.when(jnp.logical_not(own))
        def _():
            remote(block, target, send.at[q], recv.at[bd], (yx * 2 + h, 2 * c + s)).start()


def rows_out_sent(src, dst, send, recv):
    it, bd, c, yx = place()
    cut = src.shape[1] // 2
    for q in range(4):
        s, h = q // 2, q % 2
        own = (c == h) & (bd == 2 * c + s)

        @pl.when(jnp.logical_not(own))
        def _():
            block = src.at[s, pl.ds(h * cut, cut)]
            remote(block, dst.at[bd], send.at[q], recv.at[bd], (yx * 2 + h, 2 * c + s)).wait_send()


def rows_out_got(src, dst, send, recv, band):
    it, bd, c, yx = place()
    cut = src.shape[1] // 2
    pltpu.make_async_copy(src.at[0, pl.ds(0, cut)], dst.at[band], recv.at[band]).wait()


def rows_back(src, dst, send, recv):
    it, bd, c, yx = place()
    cut = src.shape[1]
    home = bd // 2
    s = lax.rem(bd, 2)
    target = dst.at[s, pl.ds(pl.multiple_of(c * cut, cut), cut)]
    got = recv.at[2 * s + c]
    for r in range(4):
        own = (home == c) & (bd == r)

        @pl.when(own)
        def _():
            pltpu.make_async_copy(src.at[r], target, got).start()

        @pl.when(jnp.logical_not(own))
        def _():
            remote(src.at[r], target, send.at[r], got, (yx * 2 + home, r)).start()


def rows_back_sent(src, dst, send, recv):
    it, bd, c, yx = place()
    cut = src.shape[1]
    home = bd // 2
    for r in range(4):
        own = (home == c) & (bd == r)

        @pl.when(jnp.logical_not(own))
        def _():
            target = dst.at[0, pl.ds(0, cut)]
            remote(src.at[r], target, send.at[r], recv.at[0], (yx * 2 + home, r)).wait_send()


def rows_back_got(src, dst, send, recv, q):
    cut = src.shape[1]
    s, h = q // 2, q % 2
    pltpu.make_async_copy(src.at[0], dst.at[s, pl.ds(h * cut, cut)], recv.at[q]).wait()


def share_start(n, rank, peer_of, src, buf, send, recv):
    copies = []
    for o in range(1, n):
        to = peer_of(lax.rem(rank + o, n))
        copies.append(remote(src, buf.at[rank], send.at[o], recv.at[o], to))
        copies[-1].start()
    buf[rank] = src[...]
    return copies


def share_end(n, copies, buf):
    for copy in copies:
        copy.wait()
    added = buf[0]
    for i in range(1, n):
        added = added + buf[i]
    return added


def all_peers(n_items):
    it, bd, c, yx = place()
    others = []
    for o in range(1, n_items // 2):
        for k in range(2):
            others.append((lax.rem(yx + o, n_items // 2) * 2 + k, bd))
    return column_peers() + others


def patch_total(counts, shape):
    total = counts[0]
    for i in range(1, counts.shape[0]):
        total = total + counts[i]
    return jnp.full(shape, total, jnp.int32).astype(f32)


VMEM = pl.BlockSpec(memory_space=pltpu.VMEM)
SMEM = pl.BlockSpec(memory_space=pltpu.SMEM)
HBM = pl.BlockSpec(memory_space=pltpu.HBM)
DMA = pltpu.SemaphoreType.DMA


def half_lanes(ref, row, half):
    at = pl.multiple_of(lax.rem(lax.axis_index("items"), 2) * half, 128)
    return ref[row : row + 1, pl.ds(at, half)]


def half_rows(ref, which, half):
    return ref[pl.ds(pl.multiple_of(which * half, 128), half), :]


def head_lanes(array, head, lane):
    keep = (lane >= head * HEAD_DIM) & (lane < (head + 1) * HEAD_DIM)
    return jnp.where(keep, array, jnp.zeros_like(array))


def with_spare(array, spare_value, head, lane):
    spare = (1 - head) * HEAD_DIM
    return jnp.where(lane == spare, spare_value, head_lanes(array, head, lane))


def ones_beside(array, head, lane):
    return with_spare(array, jnp.ones_like(array), head, lane)


def key_bias(table, counts, shape):
    it, bd, c, yx = place()
    cut = shape[0] // 8
    row = lax.broadcasted_iota(jnp.int32, shape, 0)
    there = row >= 4 * cut
    row = jnp.where(there, row - 4 * cut, row)
    band = row // cut
    half = jnp.where(there, 1 - c, c)
    position = band * (2 * cut) + half * cut + (row - band * cut)
    return jnp.where(position < counts[table[yx * 4 + bd]], 0.0, masked_score).astype(bf16)


def normalize(value):
    centre = value - jnp.mean(value, -1, keepdims=True)
    scale = lax.rsqrt(jnp.mean(centre * centre, -1, keepdims=True) + epsilon)
    return centre * scale, scale


def front_kernel(n_items, n_band, qt, table, counts, *refs):
    singles = refs[:10]
    (b_up, tok, cot, wq_h, wk_h, wv_h, wo_h) = refs[10:17]
    (vecs, stat, rows_h, cot_rows, h1_h, q_h, k_h, v_h, log_total, attn_h, attn_sib_h) = refs[17:28]
    (res, h2, h2p) = refs[28:31]
    (rows, wq, wk, wv, wo, h1, q, k, v, attn, attn_sib, part_sib) = refs[31:43]
    (one, buf_i, part, buf_b) = refs[43:47]
    (send_t, recv_t, send_c, recv_c, send_s, recv_s, send_a, recv_a) = refs[47:55]
    (send_i, recv_i, send_b, recv_b, lsem) = refs[55:60]
    it, bd, c, yx = place()
    sibling = (it + 1 - 2 * c, bd)
    slots, band_rows, width = tok.shape
    cut = band_rows // 2
    half = width // 2
    own = 4 * cut
    local = []

    def move(src, dst):
        copy = pltpu.make_async_copy(src, dst, lsem.at[len(local)])
        copy.start()
        local.append(copy)
        return copy

    greet(all_peers(n_items))
    rows_out(tok, rows, send_t, recv_t)
    lanes = pl.ds(pl.multiple_of(c * half, 128), half)
    get_w = [move(src.at[:, lanes], dst) for src, dst in ((wq_h, wq), (wk_h, wk), (wv_h, wv))]
    get_wo = move(wo_h, wo)
    for i, ref in enumerate(singles):
        vecs[i : i + 1, :] = ref[...].astype(f32).reshape(1, width)
    for i in range(b_up.shape[0] // width):
        vecs[R_BU + i : R_BU + i + 1, :] = b_up[pl.ds(i * width, width)].astype(f32).reshape(1, width)

    at = lax.broadcasted_iota(jnp.int32, (band_rows, width), 0) + bd * band_rows
    first = jnp.zeros((1, width), f32)
    second = jnp.zeros((1, width), f32)
    for s in range(slots):
        x = jnp.where(at < counts[table[it * slots + s]], tok[s].astype(f32), 0.0)
        first = first + jnp.sum(x, 0, keepdims=True)
        second = second + jnp.sum(x * x, 0, keepdims=True)
    one[0:1, :] = first
    one[1:2, :] = second
    copies = share_start(n_items, it, lambda p: (p, bd), one, buf_i, send_i, recv_i)
    part[...] = share_end(n_items, copies, buf_i)
    copies = share_start(n_band, bd, lambda p: (it, p), part, buf_b, send_b, recv_b)
    sums = share_end(n_band, copies, buf_b) / patch_total(counts, (1, width))
    mean = sums[0:1]
    var = sums[1:2] - mean * mean
    new_var = momentum * vecs[R_VAR : R_VAR + 1, :] + momentum * var
    stat[S_MEAN : S_MEAN + 1, :] = momentum * vecs[R_MEAN : R_MEAN + 1, :] + momentum * mean
    stat[S_VAR : S_VAR + 1, :] = new_var
    stat[S_BATCH : S_BATCH + 1, :] = mean
    stat[S_INV : S_INV + 1, :] = lax.rsqrt(new_var + epsilon)
    for copy in get_w:
        copy.wait()

    def hand(o):
        band = jnp.bitwise_xor(bd, o)
        return remote(rows.at[band], rows.at[4 + band], send_s.at[o], recv_s.at[o], sibling)

    def project(o, base):
        bands = [jnp.bitwise_xor(bd, o), jnp.bitwise_xor(bd, o + 1)]
        x = jnp.concatenate([rows[base + band] for band in bands]).astype(f32)
        start = (x - stat[S_MEAN : S_MEAN + 1, :]) * stat[S_INV : S_INV + 1, :]
        z, _ = normalize(start)
        h = (z * vecs[R_G1 : R_G1 + 1, :] + vecs[R_S1 : R_S1 + 1, :]).astype(bf16)
        q_new = ((dot(h, wq[...]) + half_lanes(vecs, R_BQ, half)).astype(bf16) * score_scale).astype(bf16)
        k_new = dot(h, wk[...]).astype(bf16)
        v_new = (dot(h, wv[...]) + half_lanes(vecs, R_BV, half)).astype(bf16)
        for i, band in enumerate(bands):
            to = pl.ds(pl.multiple_of((base + band) * cut, 128), cut)
            for ref, new in ((h1, h), (q, q_new), (k, k_new), (v, v_new)):
                ref[to, :] = new[i * cut : (i + 1) * cut]

    for o in (0, 2):
        for i in (o, o + 1):
            rows_out_got(tok, rows, send_t, recv_t, jnp.bitwise_xor(bd, i))
            hand(i).start()
        if o == 2:
            rows_out(cot, cot_rows, send_c, recv_c)
        project(o, 0)
        for i in (o, o + 1):
            hand(i).wait_recv()
        project(o, 4)
    move(rows.at[pl.ds(0, 4)], rows_h)
    for src, dst in ((h1, h1_h), (q, q_h), (k, k_h), (v, v_h)):
        move(src, dst)

    lane_k = lax.broadcasted_iota(jnp.int32, (2 * own, 128), 1)
    lane_q = lax.broadcasted_iota(jnp.int32, (qt, 128), 1)
    row_out = lax.broadcasted_iota(jnp.int32, (128, qt), 0)

    def hand_attn(i):
        to = attn_sib.at[:, pl.ds(pl.multiple_of(i * 128, 128), 128)]
        return remote(part_sib.at[i], to, send_a.at[i], recv_a.at[i], sibling)

    @pl.loop(0, half // 128)
    def _(i):
        at_lanes = pl.ds(pl.multiple_of(i * 128, 128), 128)
        k_pair, v_pair = k[:, at_lanes], v[:, at_lanes]
        bias = key_bias(table, counts, k_pair.shape)
        keys = [with_spare(k_pair, bias, hd, lane_k) for hd in range(2)]
        values = [ones_beside(v_pair, hd, lane_k).T for hd in range(2)]
        for t in range(2 * own // qt):
            at = slice(t * qt, (t + 1) * qt)
            q_tile = q[at, at_lanes]
            scores = [dot(keys[hd], ones_beside(q_tile, hd, lane_q), 1, 1) for hd in range(2)]
            tops = [jnp.max(s, 0, keepdims=True) for s in scores]
            weights = [jnp.exp(s - top).astype(bf16) for s, top in zip(scores, tops)]
            parts = []
            for hd in range(2):
                both = dot(values[hd], weights[hd])
                spare = (1 - hd) * HEAD_DIM
                total = both[spare : spare + 1, :]
                log_total[i, hd : hd + 1, at] = tops[hd] + jnp.log(total)
                parts.append(both * (1.0 / total))
            both = jnp.where(row_out < HEAD_DIM, parts[0], parts[1]).T.astype(bf16)
            if t * qt < own:
                attn[at, at_lanes] = both
            else:
                part_sib[i, t * qt - own : (t + 1) * qt - own, :] = both
        hand_attn(i).start()

    move(attn, attn_h)
    get_wo.wait()
    for i in range(half // 128):
        hand_attn(i).wait_recv()
    move(attn_sib, attn_sib_h)

    block = 256

    @pl.loop(0, own // block)
    def _(i):
        at = pl.ds(pl.multiple_of(i * block, block), block)
        x = rows[pl.ds(i * (block // cut), block // cut)].reshape(block, width).astype(f32)
        start = (x - stat[S_MEAN : S_MEAN + 1, :]) * stat[S_INV : S_INV + 1, :]
        r = dot(attn[at, :], half_rows(wo, c, half)) + dot(attn_sib[at, :], half_rows(wo, 1 - c, half))
        r = start + r + vecs[R_BO : R_BO + 1, :]
        res[at, :] = r
        z, _ = normalize(r)
        h = (z * vecs[R_G2 : R_G2 + 1, :] + vecs[R_S2 : R_S2 + 1, :]).astype(bf16)
        h2[at, :] = h
        e = width // 8
        for j in range(4):
            even = h[:, 2 * j * e : (2 * j + 1) * e]
            odd = h[:, (2 * j + 1) * e : (2 * j + 2) * e]
            h2p[at, j * e : (j + 1) * e] = jnp.where(c == 0, even, odd)
            h2p[at, half + j * e : half + (j + 1) * e] = jnp.where(c == 0, odd, even)

    for band in range(4):
        rows_out_got(cot, cot_rows, send_c, recv_c, band)
        hand(band).wait_send()
    rows_out_sent(tok, rows, send_t, recv_t)
    rows_out_sent(cot, cot_rows, send_c, recv_c)
    for i in range(half // 128):
        hand_attn(i).wait_send()
    for copy in local[4:]:
        copy.wait()


def front(table, counts, singles, b_up, tok, cot, wq, wk, wv, wo, qt=512):
    n_items, n_band = lax.axis_size("items"), lax.axis_size("band")
    slots, band_rows, width = tok.shape
    cut, half = band_rows // 2, width // 2
    own = 4 * cut
    pairs = half // 128
    low = lambda *shape: jax.ShapeDtypeStruct(shape, bf16)
    wide = lambda *shape: jax.ShapeDtypeStruct(shape, f32)
    buf = lambda *shape: pltpu.VMEM(shape, bf16)
    return pl.pallas_call(
        functools.partial(front_kernel, n_items, n_band, qt),
        name="front",
        in_specs=[SMEM, SMEM] + [VMEM] * 13 + [HBM] * 4,
        out_specs=[VMEM, VMEM] + [HBM] * 6 + [VMEM] + [HBM] * 2 + [VMEM] * 3,
        out_shape=[
            wide(16, width),
            wide(4, width),
            low(4, cut, width),
            low(4, cut, width),
            low(2 * own, width),
            low(2 * own, half),
            low(2 * own, half),
            low(2 * own, half),
            wide(pairs, 2, 2 * own),
            low(own, half),
            low(own, half),
            wide(own, width),
            low(own, width),
            low(own, width),
        ],
        scratch_shapes=[
            buf(8, cut, width),
            buf(width, half),
            buf(width, half),
            buf(width, half),
            buf(width, width),
            buf(2 * own, width),
            buf(2 * own, half),
            buf(2 * own, half),
            buf(2 * own, half),
            buf(own, half),
            buf(own, half),
            buf(pairs, own, 128),
            pltpu.VMEM((2, width), f32),
            pltpu.VMEM((n_items, 2, width), f32),
            pltpu.VMEM((2, width), f32),
            pltpu.VMEM((n_band, 2, width), f32),
        ]
        + [DMA((4,))] * 6
        + [DMA((pairs,))] * 2
        + [DMA((n_items,))] * 2
        + [DMA((n_band,))] * 2
        + [DMA((12,))],
        compiler_params=params(collective_id=1, has_side_effects=True),
        cost_estimate=pl.CostEstimate(
            flops=16 * own * own * width, bytes_accessed=30 * 2**20, transcendentals=0
        ),
    )(table, counts, *singles, b_up, tok, cot, wq, wk, wv, wo)


def gelu_and_slope(u):
    u2 = u * u
    t = jnp.tanh(u * (0.7978845608028654 + (0.7978845608028654 * 0.044715) * u2))
    half = 0.5 + 0.5 * t
    slope = half * (
        1.0 + u * (1.0 - t) * (0.7978845608028654 + (3 * 0.7978845608028654 * 0.044715) * u2)
    )
    return u * half, slope


def block_order(step):
    it, bd, c, yx = place()
    x = lax.rem(yx, 2)
    return 2 * lax.rem(step, 2) + jnp.where(step < 2, 1 - x, x)


def mlp_kernel(vecs, h2, h2p, cot, res, *refs):
    (wu_a, wd_a, wu_b, wd_b) = refs[:4]
    (out_low, dh, kd, rd, rest_d, ku, ru, rest_u, dbu_a, dbu_b) = refs[4:14]
    (send_wd, send_wua, send_wub, got_wd, got_wua, got_wub, keep_a, out, gd, gu) = refs[14:24]
    (send, recv, send_d, recv_d, send_u, recv_u, keep_d, sem_u, rest_sem) = refs[24:]
    step = pl.program_id(0)
    steps = pl.num_programs(0) - 1
    half = h2.shape[1] // 2
    it, bd, c, yx = place()
    x, y = lax.rem(yx, 2), yx // 2
    sibling = (it + 1 - 2 * c, bd)
    to_x, to_y = (it + 2 - 4 * x, bd), (it + 4 - 8 * y, bd)
    slot = lax.rem(step, 2)
    before = 1 - slot
    some = gd.shape[1] // 2
    part = gu.shape[2] // 2

    def copies(at, which=(0, 1, 2)):
        pairs = ((send_wd, got_wd), (send_wua, got_wua), (send_wub, got_wub))
        return [
            remote(pairs[i][0].at[at], pairs[i][1].at[at], send.at[i, at], recv.at[i, at], sibling)
            for i in which
        ]

    def down_copy(at):
        if at == 0:
            return [remote(gd.at[0], rd.at[0], send_d.at[0], recv_d.at[0], to_x)]
        if at == 1:
            first, second = pl.ds(0, some), pl.ds(some, some)
            return [
                remote(gd.at[1, first], rd.at[1, first], send_d.at[1], recv_d.at[1], to_x),
                pltpu.make_async_copy(gd.at[1, second], rest_d, rest_sem.at[2]),
            ]
        return [pltpu.make_async_copy(gd.at[at], kd.at[at - 2], keep_d.at[at - 2])]

    def up_rows(which):
        return pl.ds(pl.multiple_of(which * part, 128), part)

    def up_keep(at, i):
        return pltpu.make_async_copy(gu.at[at, i, up_rows(y)], ku.at[block_order(at), i], sem_u.at[at, i])

    def up_send(at, i):
        src, dst = gu.at[at, i, up_rows(1 - y)], ru.at[block_order(at), i]
        return remote(src, dst, send_u.at[at, i], recv_u.at[at, i], to_y)

    def up_rest(at, i):
        return pltpu.make_async_copy(gu.at[at, i, up_rows(1 - y)], rest_u.at[i], rest_sem.at[i])

    def up_ready(at, i):
        up_keep(at, i).start()

        @pl.when(at < steps - 1)
        def _():
            up_send(at, i).start()

        @pl.when(at == steps - 1)
        def _():
            up_rest(at, i).start()

    @pl.when(step == 0)
    def _():
        greet([sibling, to_x, to_y])
        out[...] = res[...]
        dh[...] = jnp.zeros_like(dh)

    def tile(wu, wd, dbu, which):
        lanes = pl.ds(pl.multiple_of(which * wu.shape[1], 128), wu.shape[1])
        up = dot(h2[...], wu[...]) + vecs[pl.ds(R_BU + block_order(step), 1), lanes]
        d_act = dot(cot[...], wd[...], 1, 1)
        act, slope = gelu_and_slope(up)
        act = act.astype(bf16)
        d_up32 = d_act * slope
        d_up = d_up32.astype(bf16)
        dbu[0] = jnp.sum(d_up32, 0, keepdims=True)
        d_wd = dot(cot[...], act, 0, 0).astype(bf16)
        d_wu = dot(h2p[...], d_up, 0, 0).astype(bf16)
        out[...] += dot(act, wd[...])
        dh[...] += dot(d_up, wu[...], 1, 1)
        return d_wd, d_wu

    @pl.when(step >= 2)
    def _():
        for copy in copies(slot):
            copy.wait_send()

    @pl.when(step < steps)
    def _():
        d_wd, d_wu = tile(wu_a, wd_a, dbu_a, 1 - c)
        send_wd[slot] = d_wd
        send_wua[slot] = d_wu[half:]
        keep_a[slot] = d_wu[:half]

    @pl.when(step > 0)
    def _():
        copies(before, (2,))[0].wait_recv()
        gu[step - 1, 0] = keep_a[before] + got_wub[before]
        up_ready(step - 1, 0)

    @pl.when(step < steps)
    def _():
        for copy in copies(slot, (0, 1)):
            copy.start()
        d_wd, d_wu = tile(wu_b, wd_b, dbu_b, c)
        send_wub[slot] = d_wu[half:]
        copies(slot, (2,))[0].start()
        for copy in copies(slot, (0, 1)):
            copy.wait_recv()
        gd[step] = d_wd + got_wd[slot]
        gu[step, 1] = d_wu[:half] + got_wua[slot]
        up_ready(step, 1)

    for at in range(4):

        @pl.when(step == at)
        def _():
            for copy in down_copy(at):
                copy.start()

    @pl.when(step == steps)
    def _():
        out_low[...] = (out[...] + vecs[R_BD : R_BD + 1, :]).astype(bf16)
        for copy in copies(before):
            copy.wait_send()
        for at in range(4):
            for copy in down_copy(at):
                copy.wait()
            for i in range(2):
                up_keep(at, i).wait()
                (up_send(at, i) if at < 3 else up_rest(at, i)).wait()


def mlp(vecs, h2, h2p, cot, res, w_up, w_down):
    rows, width = h2.shape
    ff = w_up.shape[1]
    tile = ff // 8
    half = width // 2
    steps = 4
    now = lambda i: block_order(jnp.minimum(i, steps - 1))
    at_a = lambda i: 2 * now(i) + 1 - lax.rem(lax.axis_index("items"), 2)
    at_b = lambda i: 2 * now(i) + lax.rem(lax.axis_index("items"), 2)
    w_specs = []
    for at in (at_a, at_b):
        w_specs += [
            pl.BlockSpec((width, tile), lambda i, at=at: (0, at(i))),
            pl.BlockSpec((tile, width), lambda i, at=at: (at(i), 0)),
        ]
    bias = pl.BlockSpec((1, 1, tile), lambda i: (now(i), 0, 0))
    low = lambda *shape: jax.ShapeDtypeStruct(shape, bf16)
    return pl.pallas_call(
        mlp_kernel,
        name="mlp",
        grid=(steps + 1,),
        in_specs=[VMEM] * 5 + w_specs,
        out_specs=[VMEM, VMEM] + [HBM] * 6 + [bias, bias],
        out_shape=[
            low(rows, width),
            jax.ShapeDtypeStruct((rows, width), f32),
            low(2, width, tile),
            low(2, width, tile),
            low(width // 2, tile),
            low(4, 2, half // 2, tile),
            low(4, 2, half // 2, tile),
            low(2, half // 2, tile),
        ]
        + [jax.ShapeDtypeStruct((steps, 1, tile), f32)] * 2,
        scratch_shapes=(
            [pltpu.VMEM((2, width, tile), bf16)] + [pltpu.VMEM((2, half, tile), bf16)] * 2
        )
        * 2
        + [
            pltpu.VMEM((2, half, tile), bf16),
            pltpu.VMEM((rows, width), f32),
            pltpu.VMEM((steps, width, tile), bf16),
            pltpu.VMEM((steps, 2, half, tile), bf16),
            DMA((3, 2)),
            DMA((3, 2)),
            DMA((2,)),
            DMA((2,)),
            DMA((3, 2)),
            DMA((3, 2)),
            DMA((2,)),
            DMA((4, 2)),
            DMA((3,)),
        ],
        compiler_params=params(collective_id=4, has_side_effects=True),
        cost_estimate=pl.CostEstimate(
            flops=2 * 6 * rows * width * ff, bytes_accessed=40 * 2**20, transcendentals=0
        ),
    )(vecs, h2, h2p, cot, res, w_up, w_down, w_up, w_down)


def norm_back(z, scale, dz):
    return scale * (dz - jnp.mean(dz, -1, keepdims=True) - z * jnp.mean(dz * z, -1, keepdims=True))


def tail_kernel(n_items, n_band, qt, *refs):
    (table, counts, stat, vecs, dbu_a, dbu_b, log_total) = refs[:7]
    (res_h, dh_h, cot_h, out_rows, attn_h, attn_sib_h, wo_h, q_h, k_h, v_h, h1_h) = refs[7:18]
    (wq_h, wk_h, wv_h, tok_h, kd_h, rd_h, rest_d, ku_h, ru_h, rest_u, tokens) = refs[18:29]
    (out_home, d_tok, total, o_down, o_up, o_wo, o_wq, o_wk, o_wv) = refs[29:38]
    (res, dh, cot, low, wo, attn, attn_sib, kd, rd1, rdr, rd2, rd3, rd4) = refs[38:51]
    (ku, ru1, rur, ru2, ru3, ru4, q, k, v, da, da_send, dk_acc, dv_acc) = refs[51:64]
    (h1, wq, wk, wv, tok, gw, gw_core, gw1, gw2, gw3, gw4) = refs[64:75]
    (d_pair, gp, gp_core, gp1, gp2, gp3, gp4, home) = refs[75:83]
    (small, buf_i, part, buf_b, buf_i2, part2, buf_b2) = refs[83:90]
    (send, recv, lsem, send_r, recv_r, send_g, recv_g, send_i, recv_i, send_b, recv_b) = refs[90:101]

    it, bd, c, yx = place()
    x, y = lax.rem(yx, 2), yx // 2
    bl, bh = lax.rem(bd, 2), bd // 2
    sibling = (it + 1 - 2 * c, bd)
    to_x, to_y = (it + 2 - 4 * x, bd), (it + 4 - 8 * y, bd)
    to_z1, to_z2 = (it, bd + 1 - 2 * bl), (it, lax.rem(bd + 2, 4))
    rows, width = res.shape
    half = width // 2
    fourth = width // 4
    eighth = width // 8
    tile = kd.shape[-1]
    sent = []
    loads = []

    def load(src, dst):
        copy = pltpu.make_async_copy(src, dst, lsem.at[len(loads)])
        copy.start()
        loads.append(copy)
        return copy

    def push(src, dst, to):
        i = len(sent)
        copy = remote(src, dst, send.at[i], recv.at[i], to)
        copy.start()
        sent.append(copy)
        return copy

    def some(which, size):
        return pl.ds(pl.multiple_of(which * size, 128), size)

    greet(all_peers(n_items))
    d1 = push(rest_d, rdr, to_x)
    u1 = push(rest_u, rur, to_y)
    load(out_rows, tok).wait()
    out_blocks = tok.reshape(4, rows // 4, width)
    rows_back(out_blocks, out_home, send_r, recv_r)

    get_res, get_dh, get_cot = load(res_h, res), load(dh_h, dh), load(cot_h, cot)
    get_wo, get_attn, get_sib = load(wo_h, wo), load(attn_h, attn), load(attn_sib_h, attn_sib)
    get_down = [load(kd_h, kd), load(rd_h, rd1)]
    get_up = [load(ku_h, ku), load(ru_h, ru1)]
    get_qkv = [load(src, dst) for src, dst in ((q_h, q), (k_h, k), (v_h, v))]
    get_h1 = load(h1_h, h1)
    lanes = some(c, half)
    get_w = [load(src.at[:, lanes], dst) for src, dst in ((wq_h, wq), (wk_h, wk), (wv_h, wv))]

    small[...] = jnp.zeros_like(small)
    for i in range(4):
        for src, h in ((dbu_a, 1 - c), (dbu_b, c)):
            small[4 + i : 5 + i, some(h, half)] = src[i]
    for copy in (get_res, get_dh, get_cot, get_wo):
        copy.wait()
    block = 256

    @pl.loop(0, rows // block)
    def _(i):
        at = some(i, block)
        z, scale = normalize(res[at, :])
        d_h = dh[at, :]
        c32 = cot[at, :].astype(f32)
        full = c32 + norm_back(z, scale, d_h * vecs[R_G2 : R_G2 + 1, :])
        res[at, :] = full
        d_low = full.astype(bf16)
        low[at, :] = d_low
        for j, term in enumerate((d_h * z, d_h, d_low.astype(f32), c32)):
            small[j : j + 1, :] += jnp.sum(term, 0, keepdims=True)
        da[at, :] = dot(d_low, half_rows(wo, c, half), 1, 1).astype(bf16)
        da_send[at, :] = dot(d_low, half_rows(wo, 1 - c, half), 1, 1).astype(bf16)

    da_copy = push(da_send, da.at[pl.ds(rows, rows)], sibling)
    early = share_start(
        n_items, it, lambda p: (p, bd), small.at[pl.ds(0, 8)], buf_i, send_i.at[0], recv_i.at[0]
    )

    get_attn.wait()
    get_sib.wait()
    for i, heads in enumerate((attn, attn_sib)):
        for xx in range(2):
            part_wo = dot(heads[:, xx * fourth : (xx + 1) * fourth], low[...], 0, 0).astype(bf16)
            for cc in range(2):
                gw[i, xx, cc] = part_wo[cc * eighth : (cc + 1) * eighth]
    core_w = [push(gw.at[i, :, 1 - c], gw_core.at[1 - i], sibling) for i in range(2)]

    for copy in get_down + get_up:
        copy.wait()
    d1.wait_recv()
    kd[0] += rd1[0]
    kd[1, 0:half] += rd1[1, 0:half]
    kd[1, half:width] += rdr[...]
    d2 = push(kd.at[1 - y], rd2, to_y)
    u1.wait_recv()
    for s in range(3):
        ku[block_order(s)] += ru1[block_order(s)]
    ku[block_order(3)] += rur[...]
    theirs, mine = some(1 - x, tile // 4), some(x, tile // 4)
    u2 = push(ku.at[:, :, theirs], ru2, to_x)

    for copy in get_qkv:
        copy.wait()
    get_h1.wait()
    da_copy.wait_recv()
    lane_k = lax.broadcasted_iota(jnp.int32, (2 * rows, 128), 1)
    lane_q = lax.broadcasted_iota(jnp.int32, (qt, 128), 1)

    def pair(i):
        at_lanes = some(i, 128)
        k_pair, v_pair = k[:, at_lanes], v[:, at_lanes]
        bias = key_bias(table, counts, k_pair.shape)
        keys = [with_spare(k_pair, bias, hd, lane_k) for hd in range(2)]
        keys_only = [head_lanes(k_pair, hd, lane_k) for hd in range(2)]
        values = [head_lanes(v_pair, hd, lane_k) for hd in range(2)]
        for t in range(2 * rows // qt):
            at = slice(t * qt, (t + 1) * qt)
            q_tile, d_tile = q[at, at_lanes], da[at, at_lanes]
            dq_both = None
            for hd in range(2):
                q_head = head_lanes(q_tile, hd, lane_q)
                d_head = head_lanes(d_tile, hd, lane_q)
                s = dot(keys[hd], ones_beside(q_tile, hd, lane_q), 1, 1)
                p = jnp.exp(s - log_total[i, hd : hd + 1, at])
                d_p = dot(values[hd], d_tile, 1, 1)
                weighted = p * d_p
                delta = jnp.sum(weighted, 0, keepdims=True)
                ds = (weighted - p * delta).astype(bf16)
                dv_part = dot(p.astype(bf16), d_head)
                dk_part = dot(ds, q_head)
                if t == 0 and hd == 0:
                    dv_acc[...] = dv_part
                    dk_acc[...] = dk_part
                else:
                    dv_acc[...] += dv_part
                    dk_acc[...] += dk_part
                term = dot(keys_only[hd], ds, 0, 0)
                dq_both = term if dq_both is None else dq_both + term
            dq = dq_both.T * score_scale
            q[at, at_lanes] = dq.astype(bf16)
            d_pair[at, 0:128] = dq.astype(bf16)
        k[:, at_lanes] = dk_acc[...].astype(bf16)
        v[:, at_lanes] = dv_acc[...].astype(bf16)
        d_pair[:, 128:256] = dk_acc[...].astype(bf16)
        d_pair[:, 256:384] = dv_acc[...].astype(bf16)
        for j in range(4):
            term = dot(h1[:, j * fourth : (j + 1) * fourth], d_pair[...], 0, 0).astype(bf16)
            for cc in range(2):
                gp[i, j, cc] = term[cc * eighth : (cc + 1) * eighth]

    def pair_core(i):
        return push(gp.at[i, :, 1 - c], gp_core.at[i], sibling)

    def chips(i, first, second):
        return 2 * second + first if i % 2 == 0 else 2 * first + second

    def first_of(i):
        return (x, y) if i % 2 == 0 else (y, x)

    def pair_first(i, core):
        core.wait_recv()
        mine_first, _ = first_of(i)
        to = to_x if i % 2 == 0 else to_y
        got = []
        for j in range(2):
            there = chips(i, 1 - mine_first, j)
            got.append(push(gp.at[i, there, c], gp1.at[i, j, 0], to))
            got.append(push(gp_core.at[i, there], gp1.at[i, j, 1], to))
        return got

    def pair_second(i, got):
        for copy in got:
            copy.wait_recv()
        mine_first, mine_second = first_of(i)
        for j in range(2):
            here = chips(i, mine_first, j)
            gp[i, here, c] += gp1[i, j, 0]
            gp_core[i, here] += gp1[i, j, 1]
        there = chips(i, mine_first, 1 - mine_second)
        to = to_y if i % 2 == 0 else to_x
        return [
            push(gp.at[i, there, c], gp2.at[i, 0], to),
            push(gp_core.at[i, there], gp2.at[i, 1], to),
        ]

    def pair_third(i, got):
        for copy in got:
            copy.wait_recv()
        gp[i, yx, c] += gp2[i, 0]
        gp_core[i, yx] += gp2[i, 1]

    pair(0)
    core_p = [pair_core(0)]
    part[...] = share_end(n_items, early, buf_i)
    early = share_start(n_band, bd, lambda p: (it, p), part, buf_b, send_b.at[0], recv_b.at[0])
    for i in range(2):
        core_w[i].wait_recv()
    for i in range(2):
        gw[i, :, c] += gw_core[i]
    rel_y = lax.rem(y + c, 2)
    w1 = push(gw.at[1 - rel_y, :, c], gw1, to_y)

    pair(1)
    core_p.append(pair_core(1))
    p1 = [pair_first(0, core_p[0])]
    total[0:8, :] = share_end(n_band, early, buf_b)

    pair(2)
    core_p.append(pair_core(2))
    p1.append(pair_first(1, core_p[1]))
    d2.wait_recv()
    kd[y] += rd2[...]
    down = kd.reshape(2, 2, 2, fourth, tile)
    d3 = push(down.at[y, :, 1 - bl], rd3, to_z1)
    u2.wait_recv()
    ku[:, :, mine] += ru2[...]
    up = ku.reshape(2, 2, 2, tile // 2, tile)
    u3 = push(up.at[:, 1 - bl, :, mine], ru3, to_z1)

    pair(3)
    core_p.append(pair_core(3))
    p1.append(pair_first(2, core_p[2]))
    for i, d in ((0, q), (1, v)):
        row = jnp.sum(d[...].astype(f32), 0, keepdims=True)
        small[12 + i : 13 + i, some(c, half)] = row
    w1.wait_recv()
    gw[rel_y, :, c] += gw1[...]
    w2 = push(gw.at[rel_y, 1 - x, c], gw2, to_x)

    for copy in get_w:
        copy.wait()
    dh1, dh1_sib = wo, low

    def first_norm_terms(i):
        at = some(i, block)
        term = dot(q[at, :], wq[...], 1, 1) + dot(k[at, :], wk[...], 1, 1)
        dh1[at, :] = (term + dot(v[at, :], wv[...], 1, 1)).astype(bf16)

    @pl.loop(rows // block, 2 * rows // block)
    def _(i):
        first_norm_terms(i)

    dh_copy = push(dh1.at[pl.ds(rows, rows)], dh1_sib, sibling)
    for i in range(4):
        rows_back_got(out_blocks, out_home, send_r, recv_r, i)
    rows_back_sent(out_blocks, out_home, send_r, recv_r)
    get_tok = load(tok_h, tok)
    p1.append(pair_first(3, core_p[3]))
    p2 = [pair_second(0, p1[0])]

    @pl.loop(0, rows // block)
    def _(i):
        first_norm_terms(i)

    get_tok.wait()
    dh_copy.wait_recv()
    g_rows = cot

    @pl.loop(0, rows // block)
    def _(i):
        at = some(i, block)
        inv = stat[S_INV : S_INV + 1, :]
        centred = tok[at, :].astype(f32) - stat[S_MEAN : S_MEAN + 1, :]
        z, scale = normalize(centred * inv)
        d_h = dh1[at, :].astype(f32) + dh1_sib[at, :].astype(f32)
        d_start = res[at, :] + norm_back(z, scale, d_h * vecs[R_G1 : R_G1 + 1, :])
        g_rows[at, :] = (d_start * inv).astype(bf16)
        for j, term in enumerate((d_start, d_start * centred, d_h * z, d_h)):
            small[8 + j : 9 + j, :] += jnp.sum(term, 0, keepdims=True)

    late = share_start(
        n_items, it, lambda p: (p, bd), small.at[pl.ds(8, 8)], buf_i2, send_i.at[1], recv_i.at[1]
    )
    g_blocks = g_rows.reshape(4, rows // 4, width)
    rows_back(g_blocks, home, send_g, recv_g)
    p2.append(pair_second(1, p1[1]))
    part2[...] = share_end(n_items, late, buf_i2)
    late = share_start(n_band, bd, lambda p: (it, p), part2, buf_b2, send_b.at[1], recv_b.at[1])

    d3.wait_recv()
    for high in range(2):
        down[y, high, bl] += rd3[high]
    d4 = push(down.at[y, 1 - bh, bl], rd4, to_z2)
    u3.wait_recv()
    for high in range(2):
        up[high, bl, :, mine] += ru3[high]
    u4 = push(up.at[1 - bh, bl, :, mine], ru4, to_z2)
    p2.append(pair_second(2, p1[2]))
    w2.wait_recv()
    gw[rel_y, x, c] += gw2[...]

    def z_lanes(which):
        return some(which, fourth)

    w3 = [
        push(gw.at[rel_y, x, c, :, z_lanes(2 * high + 1 - bl)], gw3.at[high], to_z1) for high in range(2)
    ]
    p2.append(pair_second(3, p1[3]))
    sums = share_end(n_band, late, buf_b2)
    total[8:16, :] = sums

    for i in range(4):
        pair_third(i, p2[i])
    p3 = []
    for i in range(2):
        there = 2 * (1 - bl) + i
        p3.append(push(gp.at[there, yx, c], gp3.at[i, 0], to_z1))
        p3.append(push(gp_core.at[there, yx], gp3.at[i, 1], to_z1))

    for high in range(2):
        w3[high].wait_recv()
    for high in range(2):
        gw3[high] = gw[rel_y, x, c, :, z_lanes(2 * high + bl)] + gw3[high]
    w4 = push(gw3.at[1 - bh], gw4, to_z2)
    for copy in p3:
        copy.wait_recv()
    for i in range(2):
        here = 2 * bl + i
        gp3[i, 0] = gp[here, yx, c] + gp3[i, 0]
        gp3[i, 1] = gp_core[here, yx] + gp3[i, 1]
    rel_b = lax.rem(bh + c, 2)
    p4 = push(gp3.at[:, 1 - rel_b], gp4, to_z2)

    count = patch_total(counts, (1, width))
    inv = stat[S_INV : S_INV + 1, :]
    fix = -0.5 * inv * sums[0:1, :] / count
    slope = -0.5 * inv * inv * inv * sums[1:2, :] / count
    cut = rows // 4
    position = lax.broadcasted_iota(jnp.int32, (cut, width), 0) + bd * (2 * cut)
    for i in range(4):
        s, h = i // 2, i % 2
        rows_back_got(g_blocks, home, send_g, recv_g, i)
        now = pl.ds(h * cut, cut)
        valid = position + h * cut < counts[table[it * 2 + s]]
        term = fix + slope * (tokens[s, now, :].astype(f32) - stat[S_BATCH : S_BATCH + 1, :])
        d_tok[s, now, :] = (home[s, now, :].astype(f32) + jnp.where(valid, term, 0.0)).astype(bf16)

    d4.wait_recv()
    o_down[...] = (down[y, bh, bl].astype(f32) + rd4[...].astype(f32)).T
    u4.wait_recv()
    up_sum = up[bh, bl, :, mine].astype(f32) + ru4[...].astype(f32)
    for i, h in ((0, 1 - c), (1, c)):
        o_up[:, some(h, tile)] = up_sum[i]
    w4.wait_recv()
    o_wo[...] = gw3[bh].astype(f32) + gw4[...].astype(f32)
    p4.wait_recv()
    for i in range(2):
        all_three = gp3[i, rel_b].astype(f32) + gp4[i].astype(f32)
        for j, ref in enumerate((o_wq, o_wk, o_wv)):
            ref[:, i * 128 : (i + 1) * 128] = all_three[:, j * 128 : (j + 1) * 128]

    rows_back_sent(g_blocks, home, send_g, recv_g)
    for copy in sent:
        copy.wait_send()


def tail(table, counts, stat, vecs, dbu_a, dbu_b, log_total, res, dh, cot, out_rows, *rest, qt=512):
    attn, attn_sib, wo, q, k, v, h1, wq, wk, wv, tok, kd, rd, rest_d, ku, ru, rest_u, tokens = rest
    n_items, n_band = lax.axis_size("items"), lax.axis_size("band")
    rows, width = res.shape
    half, fourth, cut = width // 2, width // 4, rows // 4
    tile = kd.shape[2]
    buf = lambda *shape: pltpu.VMEM(shape, bf16)
    buf32 = lambda *shape: pltpu.VMEM(shape, f32)
    out = lambda *shape: jax.ShapeDtypeStruct(shape, f32)
    e, s = fourth // 2, fourth
    return pl.pallas_call(
        functools.partial(tail_kernel, n_items, n_band, qt),
        name="tail",
        in_specs=[SMEM, SMEM] + [VMEM] * 5 + [HBM] * 21 + [VMEM],
        out_specs=[HBM] + [VMEM] * 8,
        out_shape=[
            jax.ShapeDtypeStruct(tokens.shape, bf16),
            jax.ShapeDtypeStruct(tokens.shape, bf16),
            out(16, width),
            out(tile, s),
            out(e, 2 * tile),
            out(e, s),
            out(e, s),
            out(e, s),
            out(e, s),
        ],
        scratch_shapes=[
            buf32(rows, width), buf32(rows, width), buf(rows, width), buf(rows, width),
            buf(width, width), buf(rows, half), buf(rows, half),
            buf(2, width, tile), buf(2, width, tile), buf(half, tile), buf(width, tile), buf(2, s, tile),
            buf(s, tile),
            buf(4, 2, tile // 2, tile), buf(4, 2, tile // 2, tile), buf(2, tile // 2, tile),
            buf(4, 2, tile // 4, tile), buf(2, 2, tile // 4, tile), buf(2, tile // 4, tile),
            buf(2 * rows, half), buf(2 * rows, half), buf(2 * rows, half),
            buf(2 * rows, half), buf(rows, half), buf32(2 * rows, 128), buf32(2 * rows, 128),
            buf(2 * rows, width), buf(width, half), buf(width, half), buf(width, half), buf(rows, width),
            buf(2, 2, 2, e, width), buf(2, 2, e, width), buf(2, e, width), buf(e, width),
            buf(2, e, s), buf(e, s),
            buf(2 * rows, 384), buf(4, 4, 2, e, 384), buf(4, 4, e, 384), buf(4, 2, 2, e, 384),
            buf(4, 2, e, 384), buf(2, 2, e, 384), buf(2, e, 384),
            buf(2, 2 * cut, width),
            buf32(16, width), buf32(n_items, 8, width), buf32(8, width), buf32(n_band, 8, width),
            buf32(n_items, 8, width), buf32(8, width), buf32(n_band, 8, width),
            DMA((64,)), DMA((64,)), DMA((24,)),
            DMA((4,)), DMA((4,)), DMA((4,)), DMA((4,)),
            DMA((2, n_items)), DMA((2, n_items)), DMA((2, n_band)), DMA((2, n_band)),
        ],
        compiler_params=params(collective_id=5, has_side_effects=True),
        cost_estimate=pl.CostEstimate(
            flops=60 * rows * width * width, bytes_accessed=40 * 2**20, transcendentals=0
        ),
    )(
        table, counts, stat, vecs, dbu_a, dbu_b, log_total, res, dh, cot,
        out_rows, attn, attn_sib, wo, q, k, v, h1, wq, wk, wv, tok,
        kd, rd, rest_d, ku, ru, rest_u, tokens,
    )


def emit_kernel(stat, small, *refs):
    n = (len(refs) - 11) // 2
    sources, singles, targets = refs[:n], refs[n : n + 11], refs[n + 11 :]
    for source, target in zip(sources, targets):
        target[...] = source[...]
    singles[0][...] = stat[S_MEAN, :]
    singles[1][...] = stat[S_VAR, :]
    for ref, row in zip(singles[2:10], (10, 11, 12, 13, 2, 0, 1, 3)):
        ref[...] = small[row, :]
    singles[10][...] = small[4:8, :].reshape(4 * small.shape[1])


def emit(stat, small, arrays):
    width = stat.shape[1]
    return pl.pallas_call(
        emit_kernel,
        name="emit",
        in_specs=[VMEM] * (2 + len(arrays)),
        out_specs=[VMEM] * (11 + len(arrays)),
        out_shape=[jax.ShapeDtypeStruct((width,), f32)] * 10
        + [jax.ShapeDtypeStruct((4 * width,), f32)]
        + [jax.ShapeDtypeStruct(a.shape, a.dtype) for a in arrays],
        compiler_params=params(),
    )(stat, small, *arrays)


def column_layer(
    tokens, cotangent, running_mean, running_var, slot_table, patch_counts,
    ln1_gain, ln1_bias, w_query, b_query, w_key, w_value, b_value, w_out, b_out,
    ln2_gain, ln2_bias, w_up, b_up, w_down, b_down,
):
    slots, band_rows, width = tokens.shape
    rows = slots * band_rows
    singles = (running_mean, running_var, ln1_gain, ln1_bias, b_query, b_value, b_out)
    singles += (ln2_gain, ln2_bias, b_down)
    vecs, stat, tok, cot_rows, h1, q, k, v, log_total, attn, attn_sib, res, h2, h2p = front(
        slot_table, patch_counts, singles, b_up, tokens, cotangent, w_query, w_key, w_value, w_out
    )
    tok, cot_rows = tok.reshape(rows, width), cot_rows.reshape(rows, width)
    out_rows, d_h2, kd, rd, rest_d, ku, ru, rest_u, dbu_a, dbu_b = mlp(
        vecs, h2, h2p, cot_rows, res, w_up, w_down
    )
    output, d_tokens, small, d_w_down, d_w_up, d_w_out, d_wq, d_wk, d_wv = tail(
        slot_table, patch_counts, stat, vecs, dbu_a, dbu_b, log_total, res, d_h2, cot_rows,
        out_rows, attn, attn_sib, w_out, q, k, v, h1, w_query, w_key, w_value, tok,
        kd, rd, rest_d, ku, ru, rest_u, tokens,
    )
    singles = emit(
        stat, small, (output, d_tokens, d_wq, d_wk, d_wv, d_w_out, d_w_up, d_w_down)
    )
    (new_mean, new_var, d_g1, d_s1, d_bq, d_bv, d_bo, d_g2, d_s2, d_bd, d_bu) = singles[:11]
    output, d_tokens, d_wq, d_wk, d_wv, d_w_out, d_w_up, d_w_down = singles[11:]
    return (
        output, d_tokens, new_mean, new_var, d_g1, d_s1, d_wq, d_bq, d_wk, d_wv, d_bv,
        d_w_out, d_bo, d_g2, d_s2, d_w_up, d_bu, d_w_down, d_bd,
    )


def layer_norm(value, gain, shift):
    centre = value - jnp.mean(value, -1, keepdims=True)
    spread = jnp.mean(centre * centre, -1, keepdims=True)
    return centre * lax.rsqrt(spread + epsilon) * gain + shift


def gelu_tanh(value):
    return (
        0.5
        * value
        * (1.0 + jnp.tanh(0.7978845608028654 * (value + 0.044715 * value * value * value)))
    )


def head_layout():
    heads_per = 4
    return (heads_per, HEADS // heads_per, heads_per * HEAD_DIM)


def group_scores(q_part, k_part, key_mask):
    scores = (
        jnp.einsum("rhd,khd->hrk", q_part, k_part, preferred_element_type=jnp.float32) * score_scale
    )
    return jnp.where(key_mask[None, None, :], scores, masked_score)


def attend_forward(q_slot, keys_slot, values_slot, key_mask):
    heads_per, groups, group_width = head_layout()
    band_rows = q_slot.shape[0]
    seq_length = keys_slot.shape[0]

    def head_block(group_index):
        begin = group_index * group_width
        q_part = lax.dynamic_slice_in_dim(q_slot, begin, group_width, 1).reshape(
            band_rows, heads_per, HEAD_DIM
        )
        k_part = lax.dynamic_slice_in_dim(keys_slot, begin, group_width, 1).reshape(
            seq_length, heads_per, HEAD_DIM
        )
        v_part = lax.dynamic_slice_in_dim(values_slot, begin, group_width, 1).reshape(
            seq_length, heads_per, HEAD_DIM
        )
        scores = group_scores(q_part, k_part, key_mask)
        top_score = jnp.max(scores, -1, keepdims=True)
        log_total = top_score + jnp.log(jnp.sum(jnp.exp(scores - top_score), -1, keepdims=True))
        probs_low = jnp.exp(scores - log_total).astype(jnp.bfloat16)
        attended = jnp.einsum("hrk,khd->rhd", probs_low, v_part, preferred_element_type=jnp.float32)
        return (attended.reshape(band_rows, group_width), log_total[..., 0])

    attended, log_totals = lax.map(head_block, jnp.arange(groups, dtype=jnp.int32))
    return (attended.transpose(1, 0, 2).reshape(band_rows, groups * group_width), log_totals)


def attend_backward(q_slot, keys_slot, values_slot, key_mask, d_attn_slot, row_delta, log_totals):
    heads_per, groups, group_width = head_layout()
    query_rows = q_slot.shape[0]
    seq_length = keys_slot.shape[0]
    deltas = jnp.transpose(row_delta).reshape(groups, heads_per, query_rows)

    def head_block(inputs):
        group_index, log_total, delta_part = inputs
        begin = group_index * group_width
        q_part = lax.dynamic_slice_in_dim(q_slot, begin, group_width, 1).reshape(
            query_rows, heads_per, HEAD_DIM
        )
        k_part = lax.dynamic_slice_in_dim(keys_slot, begin, group_width, 1).reshape(
            seq_length, heads_per, HEAD_DIM
        )
        v_part = lax.dynamic_slice_in_dim(values_slot, begin, group_width, 1).reshape(
            seq_length, heads_per, HEAD_DIM
        )
        d_part = lax.dynamic_slice_in_dim(d_attn_slot, begin, group_width, 1).reshape(
            query_rows, heads_per, HEAD_DIM
        )
        scores = group_scores(q_part, k_part, key_mask)
        probs = jnp.exp(scores - log_total[..., None])
        d_probs = jnp.einsum("rhd,khd->hrk", d_part, v_part, preferred_element_type=jnp.float32)
        d_scores = (probs * (d_probs - delta_part[..., None])).astype(jnp.bfloat16)
        results = []
        d_q_part = (
            jnp.einsum("hrk,khd->rhd", d_scores, k_part, preferred_element_type=jnp.float32)
            * score_scale
        )
        results.append(d_q_part.reshape(query_rows, group_width))
        probs_low = probs.astype(jnp.bfloat16)
        d_k_part = (
            jnp.einsum("hrk,rhd->khd", d_scores, q_part, preferred_element_type=jnp.float32)
            * score_scale
        )
        d_v_part = jnp.einsum("hrk,rhd->khd", probs_low, d_part, preferred_element_type=jnp.float32)
        results.append(d_k_part.reshape(seq_length, group_width))
        results.append(d_v_part.reshape(seq_length, group_width))
        return tuple(results)

    mapped = lax.map(head_block, (jnp.arange(groups, dtype=jnp.int32), log_totals, deltas))
    full_width = groups * group_width
    return tuple((piece.transpose(1, 0, 2).reshape(piece.shape[1], full_width) for piece in mapped))


def local(
    tokens,
    cotangent,
    running_mean,
    running_var,
    slot_table,
    patch_counts,
    ln1_gain,
    ln1_bias,
    w_query,
    b_query,
    w_key,
    w_value,
    b_value,
    w_out,
    b_out,
    ln2_gain,
    ln2_bias,
    w_up,
    b_up,
    w_down,
    b_down,
):
    slot_count, band_rows, model_width = tokens.shape
    seq_length = band_rows * lax.axis_size("band")
    item_rank = lax.axis_index("items")
    band_rank = lax.axis_index("band")
    every_slot = jnp.arange(slot_table.shape[0], dtype=jnp.int32)
    my_slots = item_rank * slot_count + jnp.arange(slot_count, dtype=jnp.int32)
    item_ids = jnp.sum(
        jnp.where(every_slot[None, :] == my_slots[:, None], slot_table[None, :], 0), 1
    )
    lengths = jnp.sum(
        jnp.where(every_slot[None, :] == item_ids[:, None], patch_counts[None, :], 0), 1
    )
    key_mask = jnp.arange(seq_length, dtype=jnp.int32)[None, :] < lengths[:, None]
    row_mask = (band_rank * band_rows + jnp.arange(band_rows, dtype=jnp.int32))[None, :] < lengths[
        :, None
    ]
    row_keep = row_mask.astype(jnp.float32).reshape(-1, 1)
    raw_flat = tokens.astype(jnp.float32).reshape(-1, model_width)
    part_one = jnp.sum(row_keep * raw_flat, 0)
    part_two = jnp.sum(row_keep * raw_flat * raw_flat, 0)
    total_one, total_two = lax.psum((part_one, part_two), ("items", "band"))
    patch_total = jnp.sum(patch_counts).astype(jnp.float32)
    batch_mean = total_one / patch_total
    batch_var = total_two / patch_total - batch_mean * batch_mean
    new_mean = momentum * running_mean + momentum * batch_mean
    new_var = momentum * running_var + momentum * batch_var
    inverse = lax.rsqrt(new_var + epsilon)
    normed_in = (raw_flat - new_mean) * inverse
    gain_one = ln1_gain.astype(jnp.float32)
    shift_one = ln1_bias.astype(jnp.float32)
    gain_two = ln2_gain.astype(jnp.float32)
    shift_two = ln2_bias.astype(jnp.float32)
    h_one_full, norm_one_back = jax.vjp(layer_norm, normed_in, gain_one, shift_one)
    h_one = h_one_full.astype(jnp.bfloat16)
    queries = (
        jnp.dot(h_one, w_query, preferred_element_type=jnp.float32) + b_query.astype(jnp.float32)
    ).astype(jnp.bfloat16)
    key_local = (
        jnp.dot(h_one, w_key, preferred_element_type=jnp.float32)
        .astype(jnp.bfloat16)
        .reshape(slot_count, band_rows, model_width)
    )
    value_local = (
        (jnp.dot(h_one, w_value, preferred_element_type=jnp.float32) + b_value.astype(jnp.float32))
        .astype(jnp.bfloat16)
        .reshape(slot_count, band_rows, model_width)
    )
    keys_all, values_all = (
        lax.all_gather(key_local, "band", axis=1, tiled=True),
        lax.all_gather(value_local, "band", axis=1, tiled=True),
    )
    q_slots = queries.reshape(slot_count, band_rows, model_width)
    attended_list = []
    totals_list = []
    for slot_index in range(slot_count):
        attended, log_totals = attend_forward(
            q_slots[slot_index], keys_all[slot_index], values_all[slot_index], key_mask[slot_index]
        )
        attended_list.append(attended)
        totals_list.append(log_totals)
    attn_full = jnp.concatenate(attended_list, 0)
    attn_low = attn_full.astype(jnp.bfloat16)
    residual = (
        normed_in
        + jnp.dot(attn_low, w_out, preferred_element_type=jnp.float32)
        + b_out.astype(jnp.float32)
    )
    h_two_full, norm_two_back = jax.vjp(layer_norm, residual, gain_two, shift_two)
    h_two = h_two_full.astype(jnp.bfloat16)
    up_proj = jnp.dot(h_two, w_up, preferred_element_type=jnp.float32) + b_up.astype(jnp.float32)
    activated_full, gelu_back = jax.vjp(gelu_tanh, up_proj)
    activated = activated_full.astype(jnp.bfloat16)
    result = (
        residual
        + jnp.dot(activated, w_down, preferred_element_type=jnp.float32)
        + b_down.astype(jnp.float32)
    )
    output = result.astype(jnp.bfloat16).reshape(slot_count, band_rows, model_width)
    cot_low = cotangent.reshape(-1, model_width)
    cot_full = cot_low.astype(jnp.float32)
    d_w_down = jnp.einsum("tf,td->fd", activated, cot_low, preferred_element_type=jnp.float32)
    d_b_down = jnp.sum(cot_full, 0)
    d_activated = jnp.einsum("td,fd->tf", cot_low, w_down, preferred_element_type=jnp.float32)
    (d_up_full,) = gelu_back(d_activated)
    d_up = d_up_full.astype(jnp.bfloat16)
    d_w_up = jnp.einsum("td,tf->df", h_two, d_up, preferred_element_type=jnp.float32)
    d_b_up = jnp.sum(d_up, 0, dtype=jnp.float32)
    d_h_two = jnp.einsum("tf,df->td", d_up, w_up, preferred_element_type=jnp.float32)
    d_res_norm, d_gain_two, d_shift_two = norm_two_back(d_h_two)
    d_residual = cot_full + d_res_norm
    d_branch = d_residual.astype(jnp.bfloat16)
    d_w_out = jnp.einsum("td,te->de", attn_low, d_branch, preferred_element_type=jnp.float32)
    d_b_out = jnp.sum(d_branch, 0, dtype=jnp.float32)
    d_attn = jnp.einsum("te,de->td", d_branch, w_out, preferred_element_type=jnp.float32).astype(
        jnp.bfloat16
    )
    row_delta = jnp.sum(
        (d_attn.astype(jnp.float32) * attn_full).reshape(slot_count, band_rows, HEADS, HEAD_DIM), -1
    )
    d_attn_slots = d_attn.reshape(slot_count, band_rows, model_width)
    back_keys, back_values = (keys_all, values_all)
    d_q_list = []
    d_k_list = []
    d_v_list = []
    for slot_index in range(slot_count):
        d_q_slot, d_k_slot, d_v_slot = attend_backward(
            q_slots[slot_index],
            back_keys[slot_index],
            back_values[slot_index],
            key_mask[slot_index],
            d_attn_slots[slot_index],
            row_delta[slot_index],
            totals_list[slot_index],
        )
        d_q_list.append(d_q_slot)
        d_k_list.append(d_k_slot)
        d_v_list.append(d_v_slot)
    d_keys_mine, d_values_mine = (
        lax.psum_scatter(
            jnp.stack(d_k_list).astype(jnp.bfloat16), "band", scatter_dimension=1, tiled=True
        ).astype(jnp.float32),
        lax.psum_scatter(
            jnp.stack(d_v_list).astype(jnp.bfloat16), "band", scatter_dimension=1, tiled=True
        ).astype(jnp.float32),
    )
    d_queries = jnp.concatenate(d_q_list, 0).astype(jnp.bfloat16)
    d_keys = d_keys_mine.reshape(-1, model_width).astype(jnp.bfloat16)
    d_values = d_values_mine.reshape(-1, model_width).astype(jnp.bfloat16)
    d_w_query = jnp.einsum("td,te->de", h_one, d_queries, preferred_element_type=jnp.float32)
    d_b_query = jnp.sum(d_queries, 0, dtype=jnp.float32)
    d_w_key = jnp.einsum("td,te->de", h_one, d_keys, preferred_element_type=jnp.float32)
    d_w_value = jnp.einsum("td,te->de", h_one, d_values, preferred_element_type=jnp.float32)
    d_b_value = jnp.sum(d_values, 0, dtype=jnp.float32)
    d_h_one = jnp.einsum("te,de->td", d_queries, w_query, preferred_element_type=jnp.float32)
    d_h_one = d_h_one + jnp.einsum("te,de->td", d_keys, w_key, preferred_element_type=jnp.float32)
    d_h_one = d_h_one + jnp.einsum(
        "te,de->td", d_values, w_value, preferred_element_type=jnp.float32
    )
    d_start_norm, d_gain_one, d_shift_one = norm_one_back(d_h_one)
    d_start = d_residual + d_start_norm
    centred = raw_flat - new_mean
    small_sums = lax.psum(
        (
            jnp.sum(d_start, 0),
            jnp.sum(d_start * centred, 0),
            d_gain_one,
            d_shift_one,
            d_b_query,
            d_b_value,
            d_b_out,
            d_gain_two,
            d_shift_two,
            d_b_up,
            d_b_down,
        ),
        ("items", "band"),
    )
    sum_g = small_sums[0]
    sum_gx = small_sums[1]
    cube = inverse * inverse * inverse
    d_raw = d_start * inverse + row_keep * (
        -0.5 * inverse * sum_g / patch_total
        - 0.5 * cube * sum_gx * (raw_flat - batch_mean) / patch_total
    )
    d_tokens = d_raw.astype(jnp.bfloat16).reshape(slot_count, band_rows, model_width)
    weight_grads = (
        lax.psum_scatter(
            d_w_query.astype(jnp.bfloat16), "items", scatter_dimension=0, tiled=True
        ).astype(jnp.float32),
        lax.psum_scatter(
            d_w_key.astype(jnp.bfloat16), "items", scatter_dimension=0, tiled=True
        ).astype(jnp.float32),
        lax.psum_scatter(
            d_w_value.astype(jnp.bfloat16), "items", scatter_dimension=0, tiled=True
        ).astype(jnp.float32),
        lax.psum_scatter(
            d_w_out.astype(jnp.bfloat16), "items", scatter_dimension=0, tiled=True
        ).astype(jnp.float32),
        lax.psum_scatter(
            d_w_up.astype(jnp.bfloat16), "items", scatter_dimension=0, tiled=True
        ).astype(jnp.float32),
        lax.psum_scatter(
            d_w_down.astype(jnp.bfloat16), "items", scatter_dimension=0, tiled=True
        ).astype(jnp.float32),
    )
    weight_grads = (
        lax.psum_scatter(
            weight_grads[0].astype(jnp.bfloat16), "band", scatter_dimension=1, tiled=True
        ).astype(jnp.float32),
        lax.psum_scatter(
            weight_grads[1].astype(jnp.bfloat16), "band", scatter_dimension=1, tiled=True
        ).astype(jnp.float32),
        lax.psum_scatter(
            weight_grads[2].astype(jnp.bfloat16), "band", scatter_dimension=1, tiled=True
        ).astype(jnp.float32),
        lax.psum_scatter(
            weight_grads[3].astype(jnp.bfloat16), "band", scatter_dimension=1, tiled=True
        ).astype(jnp.float32),
        lax.psum_scatter(
            weight_grads[4].astype(jnp.bfloat16), "band", scatter_dimension=1, tiled=True
        ).astype(jnp.float32),
        lax.psum_scatter(
            weight_grads[5].astype(jnp.bfloat16), "band", scatter_dimension=1, tiled=True
        ).astype(jnp.float32),
    )
    return (
        output,
        d_tokens,
        new_mean,
        new_var,
        small_sums[2],
        small_sums[3],
        weight_grads[0],
        small_sums[4],
        weight_grads[1],
        weight_grads[2],
        small_sums[5],
        weight_grads[3],
        small_sums[6],
        small_sums[7],
        small_sums[8],
        weight_grads[4],
        small_sums[9],
        weight_grads[5],
        small_sums[10],
    )


def solution(mesh):
    columns = mesh.shape["items"] == 8 and mesh.shape["band"] == 4
    return jax.shard_map(
        column_layer if columns else local,
        mesh=mesh,
        in_specs=(
            P("items", "band", None),
            P("items", "band", None),
            P(),
            P(),
            P(),
            P(),
            P(),
            P(),
            P(),
            P(),
            P(),
            P(),
            P(),
            P(),
            P(),
            P(),
            P(),
            P(),
            P(),
            P(),
            P(),
        ),
        out_specs=(
            P("items", "band", None),
            P("items", "band", None),
            P(),
            P(),
            P(),
            P(),
            P("items", "band"),
            P(),
            P("items", "band"),
            P("items", "band"),
            P(),
            P("items", "band"),
            P(),
            P(),
            P(),
            P("items", "band"),
            P(),
            P("items", "band"),
            P(),
        ),
        check_vma=False,
    )
```

```python
import functools
import jax
import jax.numpy as jnp
from jax import lax
from jax.experimental import pallas as pl
from jax.experimental.pallas import tpu as pltpu
from jax.sharding import PartitionSpec as P

HEADS = 16
HEAD_DIM = 64
epsilon = 1e-05
score_scale = 0.125
masked_score = -1e30
momentum = 0.5
f32 = jnp.float32
bf16 = jnp.bfloat16
VMEM_LIMIT = 60 * 2**20
R_MEAN, R_VAR, R_G1, R_S1, R_BQ, R_BV, R_BO, R_G2, R_S2, R_BD, R_BU = range(11)
S_MEAN, S_VAR, S_BATCH, S_INV = range(4)


def dot(a, b, ca=1, cb=0):
    return lax.dot_general(a, b, (((ca,), (cb,)), ((), ())), preferred_element_type=f32)


def params(**kw):
    return pltpu.CompilerParams(vmem_limit_bytes=VMEM_LIMIT, **kw)


def place():
    it, bd = lax.axis_index("items"), lax.axis_index("band")
    return it, bd, lax.rem(it, 2), it // 2


def remote(src, dst, send, recv, to):
    return pltpu.make_async_remote_copy(
        src_ref=src,
        dst_ref=dst,
        send_sem=send,
        recv_sem=recv,
        device_id=to,
        device_id_type=pl.DeviceIdType.MESH,
    )


def greet(peers):
    barrier = pltpu.get_barrier_semaphore()
    for peer in peers:
        pl.semaphore_signal(barrier, inc=1, device_id=peer, device_id_type=pl.DeviceIdType.MESH)
    pl.semaphore_wait(barrier, len(peers))


def column_peers():
    it, bd, c, yx = place()
    peers = [(it, lax.rem(bd + o, 4)) for o in range(1, 4)]
    return peers + [(it + 1 - 2 * c, lax.rem(bd + o, 4)) for o in range(4)]


def rows_out(src, dst, send, recv):
    it, bd, c, yx = place()
    cut = src.shape[1] // 2
    for q in range(4):
        s, h = q // 2, q % 2
        block = src.at[s, pl.ds(h * cut, cut)]
        target = dst.at[bd]
        own = (c == h) & (bd == 2 * c + s)

        @pl.when(own)
        def _():
            pltpu.make_async_copy(block, target, recv.at[bd]).start()

        @pl.when(jnp.logical_not(own))
        def _():
            remote(block, target, send.at[q], recv.at[bd], (yx * 2 + h, 2 * c + s)).start()


def rows_out_sent(src, dst, send, recv):
    it, bd, c, yx = place()
    cut = src.shape[1] // 2
    for q in range(4):
        s, h = q // 2, q % 2
        own = (c == h) & (bd == 2 * c + s)

        @pl.when(jnp.logical_not(own))
        def _():
            block = src.at[s, pl.ds(h * cut, cut)]
            remote(block, dst.at[bd], send.at[q], recv.at[bd], (yx * 2 + h, 2 * c + s)).wait_send()


def rows_out_got(src, dst, send, recv, band):
    it, bd, c, yx = place()
    cut = src.shape[1] // 2
    pltpu.make_async_copy(src.at[0, pl.ds(0, cut)], dst.at[band], recv.at[band]).wait()


def rows_back(src, dst, send, recv, which=range(4)):
    it, bd, c, yx = place()
    cut = src.shape[1]
    home = bd // 2
    s = lax.rem(bd, 2)
    target = dst.at[s, pl.ds(pl.multiple_of(c * cut, cut), cut)]
    got = recv.at[2 * s + c]
    for r in which:
        own = (home == c) & (bd == r)

        @pl.when(own)
        def _():
            pltpu.make_async_copy(src.at[r], target, got).start()

        @pl.when(jnp.logical_not(own))
        def _():
            remote(src.at[r], target, send.at[r], got, (yx * 2 + home, r)).start()


def rows_back_sent(src, dst, send, recv):
    it, bd, c, yx = place()
    cut = src.shape[1]
    home = bd // 2
    for r in range(4):
        own = (home == c) & (bd == r)

        @pl.when(jnp.logical_not(own))
        def _():
            target = dst.at[0, pl.ds(0, cut)]
            remote(src.at[r], target, send.at[r], recv.at[0], (yx * 2 + home, r)).wait_send()


def rows_back_got(src, dst, send, recv, q):
    cut = src.shape[1]
    s, h = q // 2, q % 2
    pltpu.make_async_copy(src.at[0], dst.at[s, pl.ds(h * cut, cut)], recv.at[q]).wait()


def share_start(n, rank, peer_of, src, buf, send, recv):
    copies = []
    for o in range(1, n):
        to = peer_of(lax.rem(rank + o, n))
        copies.append(remote(src, buf.at[rank], send.at[o], recv.at[o], to))
        copies[-1].start()
    buf[rank] = src[...]
    return copies


def share_end(n, copies, buf):
    for copy in copies:
        copy.wait()
    added = buf[0]
    for i in range(1, n):
        added = added + buf[i]
    return added


def all_peers(n_items):
    it, bd, c, yx = place()
    others = []
    for o in range(1, n_items // 2):
        for k in range(2):
            others.append((lax.rem(yx + o, n_items // 2) * 2 + k, bd))
    return column_peers() + others


def patch_total(counts, shape):
    total = counts[0]
    for i in range(1, counts.shape[0]):
        total = total + counts[i]
    return jnp.full(shape, total, jnp.int32).astype(f32)


VMEM = pl.BlockSpec(memory_space=pltpu.VMEM)
SMEM = pl.BlockSpec(memory_space=pltpu.SMEM)
HBM = pl.BlockSpec(memory_space=pltpu.HBM)
DMA = pltpu.SemaphoreType.DMA


def half_lanes(ref, row, half):
    at = pl.multiple_of(lax.rem(lax.axis_index("items"), 2) * half, 128)
    return ref[row : row + 1, pl.ds(at, half)]


def half_rows(ref, which, half):
    return ref[pl.ds(pl.multiple_of(which * half, 128), half), :]


def head_lanes(array, head, lane):
    keep = (lane >= head * HEAD_DIM) & (lane < (head + 1) * HEAD_DIM)
    return jnp.where(keep, array, jnp.zeros_like(array))


def with_spare(array, spare_value, head, lane):
    spare = (1 - head) * HEAD_DIM
    return jnp.where(lane == spare, spare_value, head_lanes(array, head, lane))


def ones_beside(array, head, lane):
    return with_spare(array, jnp.ones_like(array), head, lane)


def key_bias(table, counts, shape):
    it, bd, c, yx = place()
    cut = shape[0] // 8
    row = lax.broadcasted_iota(jnp.int32, shape, 0)
    there = row >= 4 * cut
    row = jnp.where(there, row - 4 * cut, row)
    band = row // cut
    half = jnp.where(there, 1 - c, c)
    position = band * (2 * cut) + half * cut + (row - band * cut)
    return jnp.where(position < counts[table[yx * 4 + bd]], 0.0, masked_score).astype(bf16)


def normalize(value):
    centre = value - jnp.mean(value, -1, keepdims=True)
    scale = lax.rsqrt(jnp.mean(centre * centre, -1, keepdims=True) + epsilon)
    return centre * scale, scale


def front_kernel(n_items, n_band, qt, table, counts, *refs):
    singles = refs[:10]
    (b_up, tok, cot, wq_h, wk_h, wv_h, wo_h) = refs[10:17]
    (vecs, stat, rows_h, cot_rows, h1_h, q_h, k_h, v_h, log_total, attn_h, attn_sib_h) = refs[17:28]
    (res, h2, h2p) = refs[28:31]
    (rows, wq, wk, wv, wo, h1, q, k, v, attn, attn_sib, part_sib) = refs[31:43]
    (one, buf_i, part, buf_b) = refs[43:47]
    (send_t, recv_t, send_c, recv_c, send_s, recv_s, send_a, recv_a) = refs[47:55]
    (send_i, recv_i, send_b, recv_b, lsem) = refs[55:60]
    it, bd, c, yx = place()
    sibling = (it + 1 - 2 * c, bd)
    slots, band_rows, width = tok.shape
    cut = band_rows // 2
    half = width // 2
    own = 4 * cut
    local = []

    def move(src, dst):
        copy = pltpu.make_async_copy(src, dst, lsem.at[len(local)])
        copy.start()
        local.append(copy)
        return copy

    greet(all_peers(n_items))
    rows_out(tok, rows, send_t, recv_t)
    lanes = pl.ds(pl.multiple_of(c * half, 128), half)
    get_w = [move(src.at[:, lanes], dst) for src, dst in ((wq_h, wq), (wk_h, wk), (wv_h, wv))]
    get_wo = move(wo_h, wo)
    for i, ref in enumerate(singles):
        vecs[i : i + 1, :] = ref[...].astype(f32).reshape(1, width)
    for i in range(b_up.shape[0] // width):
        vecs[R_BU + i : R_BU + i + 1, :] = b_up[pl.ds(i * width, width)].astype(f32).reshape(1, width)

    at = lax.broadcasted_iota(jnp.int32, (band_rows, width), 0) + bd * band_rows
    first = jnp.zeros((1, width), f32)
    second = jnp.zeros((1, width), f32)
    for s in range(slots):
        x = jnp.where(at < counts[table[it * slots + s]], tok[s].astype(f32), 0.0)
        first = first + jnp.sum(x, 0, keepdims=True)
        second = second + jnp.sum(x * x, 0, keepdims=True)
    one[0:1, :] = first
    one[1:2, :] = second
    copies = share_start(n_items, it, lambda p: (p, bd), one, buf_i, send_i, recv_i)
    part[...] = share_end(n_items, copies, buf_i)
    copies = share_start(n_band, bd, lambda p: (it, p), part, buf_b, send_b, recv_b)
    sums = share_end(n_band, copies, buf_b) / patch_total(counts, (1, width))
    mean = sums[0:1]
    var = sums[1:2] - mean * mean
    new_var = momentum * vecs[R_VAR : R_VAR + 1, :] + momentum * var
    stat[S_MEAN : S_MEAN + 1, :] = momentum * vecs[R_MEAN : R_MEAN + 1, :] + momentum * mean
    stat[S_VAR : S_VAR + 1, :] = new_var
    stat[S_BATCH : S_BATCH + 1, :] = mean
    stat[S_INV : S_INV + 1, :] = lax.rsqrt(new_var + epsilon)
    for copy in get_w:
        copy.wait()

    def hand(o):
        band = jnp.bitwise_xor(bd, o)
        return remote(rows.at[band], rows.at[4 + band], send_s.at[o], recv_s.at[o], sibling)

    def project(o, base):
        bands = [jnp.bitwise_xor(bd, o), jnp.bitwise_xor(bd, o + 1)]
        x = jnp.concatenate([rows[base + band] for band in bands]).astype(f32)
        start = (x - stat[S_MEAN : S_MEAN + 1, :]) * stat[S_INV : S_INV + 1, :]
        z, _ = normalize(start)
        h = (z * vecs[R_G1 : R_G1 + 1, :] + vecs[R_S1 : R_S1 + 1, :]).astype(bf16)
        q_new = ((dot(h, wq[...]) + half_lanes(vecs, R_BQ, half)).astype(bf16) * score_scale).astype(bf16)
        k_new = dot(h, wk[...]).astype(bf16)
        v_new = (dot(h, wv[...]) + half_lanes(vecs, R_BV, half)).astype(bf16)
        for i, band in enumerate(bands):
            to = pl.ds(pl.multiple_of((base + band) * cut, 128), cut)
            for ref, new in ((h1, h), (q, q_new), (k, k_new), (v, v_new)):
                ref[to, :] = new[i * cut : (i + 1) * cut]

    for o in (0, 2):
        for i in (o, o + 1):
            rows_out_got(tok, rows, send_t, recv_t, jnp.bitwise_xor(bd, i))
            hand(i).start()
        if o == 2:
            rows_out(cot, cot_rows, send_c, recv_c)
        project(o, 0)
        for i in (o, o + 1):
            hand(i).wait_recv()
        project(o, 4)
    move(rows.at[pl.ds(0, 4)], rows_h)
    for src, dst in ((h1, h1_h), (q, q_h), (k, k_h), (v, v_h)):
        move(src, dst)

    lane_k = lax.broadcasted_iota(jnp.int32, (2 * own, 128), 1)
    lane_q = lax.broadcasted_iota(jnp.int32, (qt, 128), 1)
    row_out = lax.broadcasted_iota(jnp.int32, (128, qt), 0)

    def hand_attn(i):
        to = attn_sib.at[:, pl.ds(pl.multiple_of(i * 128, 128), 128)]
        return remote(part_sib.at[i], to, send_a.at[i], recv_a.at[i], sibling)

    @pl.loop(0, half // 128)
    def _(i):
        at_lanes = pl.ds(pl.multiple_of(i * 128, 128), 128)
        k_pair, v_pair = k[:, at_lanes], v[:, at_lanes]
        bias = key_bias(table, counts, k_pair.shape)
        keys = [with_spare(k_pair, bias, hd, lane_k) for hd in range(2)]
        values = [ones_beside(v_pair, hd, lane_k).T for hd in range(2)]
        units = [(slice(t * qt, (t + 1) * qt), hd) for t in range(2 * own // qt) for hd in range(2)]
        scores = [dot(keys[hd], ones_beside(q[at, at_lanes], hd, lane_q), 1, 1) for at, hd in units]
        tops = [jnp.max(s, 0, keepdims=True) for s in scores]
        weights = [jnp.exp(s - top).astype(bf16) for s, top in zip(scores, tops)]
        parts = []
        for (at, hd), top, weight in zip(units, tops, weights):
            both = dot(values[hd], weight)
            spare = (1 - hd) * HEAD_DIM
            total = both[spare : spare + 1, :]
            log_total[i, hd : hd + 1, at] = top + jnp.log(total)
            parts.append(both * (1.0 / total))
        for t in range(2 * own // qt):
            both = jnp.where(row_out < HEAD_DIM, parts[2 * t], parts[2 * t + 1]).T.astype(bf16)
            if t * qt < own:
                attn[t * qt : (t + 1) * qt, at_lanes] = both
            else:
                part_sib[i, t * qt - own : (t + 1) * qt - own, :] = both
        hand_attn(i).start()

    move(attn, attn_h)
    get_wo.wait()
    for i in range(half // 128):
        hand_attn(i).wait_recv()
    move(attn_sib, attn_sib_h)

    block = 256

    @pl.loop(0, own // block)
    def _(i):
        at = pl.ds(pl.multiple_of(i * block, block), block)
        x = rows[pl.ds(i * (block // cut), block // cut)].reshape(block, width).astype(f32)
        start = (x - stat[S_MEAN : S_MEAN + 1, :]) * stat[S_INV : S_INV + 1, :]
        r = dot(attn[at, :], half_rows(wo, c, half)) + dot(attn_sib[at, :], half_rows(wo, 1 - c, half))
        r = start + r + vecs[R_BO : R_BO + 1, :]
        res[at, :] = r
        z, _ = normalize(r)
        h = (z * vecs[R_G2 : R_G2 + 1, :] + vecs[R_S2 : R_S2 + 1, :]).astype(bf16)
        h2[at, :] = h
        e = width // 8
        for j in range(4):
            even = h[:, 2 * j * e : (2 * j + 1) * e]
            odd = h[:, (2 * j + 1) * e : (2 * j + 2) * e]
            h2p[at, j * e : (j + 1) * e] = jnp.where(c == 0, even, odd)
            h2p[at, half + j * e : half + (j + 1) * e] = jnp.where(c == 0, odd, even)

    for band in range(4):
        rows_out_got(cot, cot_rows, send_c, recv_c, band)
        hand(band).wait_send()
    rows_out_sent(tok, rows, send_t, recv_t)
    rows_out_sent(cot, cot_rows, send_c, recv_c)
    for i in range(half // 128):
        hand_attn(i).wait_send()
    for copy in local[4:]:
        copy.wait()


def front(table, counts, singles, b_up, tok, cot, wq, wk, wv, wo, qt=512):
    n_items, n_band = lax.axis_size("items"), lax.axis_size("band")
    slots, band_rows, width = tok.shape
    cut, half = band_rows // 2, width // 2
    own = 4 * cut
    pairs = half // 128
    low = lambda *shape: jax.ShapeDtypeStruct(shape, bf16)
    wide = lambda *shape: jax.ShapeDtypeStruct(shape, f32)
    buf = lambda *shape: pltpu.VMEM(shape, bf16)
    return pl.pallas_call(
        functools.partial(front_kernel, n_items, n_band, qt),
        name="front",
        in_specs=[SMEM, SMEM] + [VMEM] * 13 + [HBM] * 4,
        out_specs=[VMEM, VMEM] + [HBM] * 6 + [VMEM] + [HBM] * 2 + [VMEM] * 3,
        out_shape=[
            wide(16, width),
            wide(4, width),
            low(4, cut, width),
            low(4, cut, width),
            low(2 * own, width),
            low(2 * own, half),
            low(2 * own, half),
            low(2 * own, half),
            wide(pairs, 2, 2 * own),
            low(own, half),
            low(own, half),
            wide(own, width),
            low(own, width),
            low(own, width),
        ],
        scratch_shapes=[
            buf(8, cut, width),
            buf(width, half),
            buf(width, half),
            buf(width, half),
            buf(width, width),
            buf(2 * own, width),
            buf(2 * own, half),
            buf(2 * own, half),
            buf(2 * own, half),
            buf(own, half),
            buf(own, half),
            buf(pairs, own, 128),
            pltpu.VMEM((2, width), f32),
            pltpu.VMEM((n_items, 2, width), f32),
            pltpu.VMEM((2, width), f32),
            pltpu.VMEM((n_band, 2, width), f32),
        ]
        + [DMA((4,))] * 6
        + [DMA((pairs,))] * 2
        + [DMA((n_items,))] * 2
        + [DMA((n_band,))] * 2
        + [DMA((12,))],
        compiler_params=params(collective_id=1, has_side_effects=True),
        cost_estimate=pl.CostEstimate(
            flops=16 * own * own * width, bytes_accessed=30 * 2**20, transcendentals=0
        ),
    )(table, counts, *singles, b_up, tok, cot, wq, wk, wv, wo)


def gelu_and_slope(u):
    u2 = u * u
    t = jnp.tanh(u * (0.7978845608028654 + (0.7978845608028654 * 0.044715) * u2))
    half = 0.5 + 0.5 * t
    slope = half * (
        1.0 + u * (1.0 - t) * (0.7978845608028654 + (3 * 0.7978845608028654 * 0.044715) * u2)
    )
    return u * half, slope


def block_order(step):
    it, bd, c, yx = place()
    x = lax.rem(yx, 2)
    return 2 * lax.rem(step, 2) + jnp.where(step < 2, 1 - x, x)


def mlp_kernel(vecs, h2, h2p, cot, res, *refs):
    (wu_a, wd_a, wu_b, wd_b) = refs[:4]
    (out_low, dh, kd, rd, rest_d, ku, ru, rest_u, dbu_a, dbu_b) = refs[4:14]
    (send_wd, send_wua, send_wub, got_wd, got_wua, got_wub, keep_a, out, gd, gu) = refs[14:24]
    (send, recv, send_d, recv_d, send_u, recv_u, keep_d, sem_u, rest_sem) = refs[24:]
    step = pl.program_id(0)
    steps = pl.num_programs(0) - 1
    half = h2.shape[1] // 2
    it, bd, c, yx = place()
    x, y = lax.rem(yx, 2), yx // 2
    sibling = (it + 1 - 2 * c, bd)
    to_x, to_y = (it + 2 - 4 * x, bd), (it + 4 - 8 * y, bd)
    slot = lax.rem(step, 2)
    before = 1 - slot
    some = gd.shape[2] // 2
    part = gu.shape[2] // 2

    def copies(at, which=(0, 1, 2)):
        pairs = ((send_wd, got_wd), (send_wua, got_wua), (send_wub, got_wub))
        return [
            remote(pairs[i][0].at[at], pairs[i][1].at[at], send.at[i, at], recv.at[i, at], sibling)
            for i in which
        ]

    def down_copy(at):
        if at == 0:
            return [remote(gd.at[0], rd.at[0], send_d.at[0], recv_d.at[0], to_x)]
        if at == 1:
            first, second = pl.ds(0, some), pl.ds(some, some)
            return [
                remote(gd.at[1, :, first], rd.at[1, :, first], send_d.at[1], recv_d.at[1], to_x),
                pltpu.make_async_copy(gd.at[1, :, second], rest_d, rest_sem.at[2]),
            ]
        return [pltpu.make_async_copy(gd.at[at], kd.at[at - 2], keep_d.at[at - 2])]

    def up_rows(which):
        return pl.ds(pl.multiple_of(which * part, 128), part)

    def up_keep(at, i):
        return pltpu.make_async_copy(gu.at[at, i, up_rows(y)], ku.at[block_order(at), i], sem_u.at[at, i])

    def up_send(at, i):
        src, dst = gu.at[at, i, up_rows(1 - y)], ru.at[block_order(at), i]
        return remote(src, dst, send_u.at[at, i], recv_u.at[at, i], to_y)

    def up_rest(at, i):
        return pltpu.make_async_copy(gu.at[at, i, up_rows(1 - y)], rest_u.at[i], rest_sem.at[i])

    def up_ready(at, i):
        up_keep(at, i).start()

        @pl.when(at < steps - 1)
        def _():
            up_send(at, i).start()

        @pl.when(at == steps - 1)
        def _():
            up_rest(at, i).start()

    @pl.when(step == 0)
    def _():
        greet([sibling, to_x, to_y])
        out[...] = res[...]
        dh[...] = jnp.zeros_like(dh)

    def tile(wu, wd, dbu, which):
        lanes = pl.ds(pl.multiple_of(which * wu.shape[1], 128), wu.shape[1])
        up = dot(h2[...], wu[...]) + vecs[pl.ds(R_BU + block_order(step), 1), lanes]
        d_act = dot(cot[...], wd[...], 1, 1)
        act, slope = gelu_and_slope(up)
        act = act.astype(bf16)
        d_up32 = d_act * slope
        d_up = d_up32.astype(bf16)
        dbu[0] = jnp.sum(d_up32, 0, keepdims=True)
        d_wd = dot(cot[...], act, 0, 0).astype(bf16)
        d_wu = dot(h2p[...], d_up, 0, 0).astype(bf16)
        out[...] += dot(act, wd[...])
        dh[...] += dot(d_up, wu[...], 1, 1)
        return d_wd, d_wu

    @pl.when(step >= 2)
    def _():
        for copy in copies(slot):
            copy.wait_send()

    @pl.when(step < steps)
    def _():
        d_wd, d_wu = tile(wu_a, wd_a, dbu_a, 1 - c)
        send_wd[slot] = d_wd
        send_wua[slot] = d_wu[half:]
        keep_a[slot] = d_wu[:half]

    @pl.when(step > 0)
    def _():
        copies(before, (2,))[0].wait_recv()
        gu[step - 1, 0] = keep_a[before] + got_wub[before]
        up_ready(step - 1, 0)

    @pl.when(step < steps)
    def _():
        for copy in copies(slot, (0, 1)):
            copy.start()
        d_wd, d_wu = tile(wu_b, wd_b, dbu_b, c)
        send_wub[slot] = d_wu[half:]
        copies(slot, (2,))[0].start()
        for copy in copies(slot, (0, 1)):
            copy.wait_recv()
        gd[step] = (d_wd + got_wd[slot]).reshape(gd.shape[1:])
        gu[step, 1] = d_wu[:half] + got_wua[slot]
        up_ready(step, 1)

    for at in range(4):

        @pl.when(step == at)
        def _():
            for copy in down_copy(at):
                copy.start()

    @pl.when(step == steps)
    def _():
        out_low[...] = (out[...] + vecs[R_BD : R_BD + 1, :]).astype(bf16)
        for copy in copies(before):
            copy.wait_send()
        for at in range(4):
            for copy in down_copy(at):
                copy.wait()
            for i in range(2):
                up_keep(at, i).wait()
                (up_send(at, i) if at < 3 else up_rest(at, i)).wait()


def mlp(vecs, h2, h2p, cot, res, w_up, w_down):
    rows, width = h2.shape
    ff = w_up.shape[1]
    tile = ff // 8
    half = width // 2
    steps = 4
    now = lambda i: block_order(jnp.minimum(i, steps - 1))
    at_a = lambda i: 2 * now(i) + 1 - lax.rem(lax.axis_index("items"), 2)
    at_b = lambda i: 2 * now(i) + lax.rem(lax.axis_index("items"), 2)
    w_specs = []
    for at in (at_a, at_b):
        w_specs += [
            pl.BlockSpec((width, tile), lambda i, at=at: (0, at(i))),
            pl.BlockSpec((tile, width), lambda i, at=at: (at(i), 0)),
        ]
    bias = pl.BlockSpec((1, 1, tile), lambda i: (now(i), 0, 0))
    low = lambda *shape: jax.ShapeDtypeStruct(shape, bf16)
    return pl.pallas_call(
        mlp_kernel,
        name="mlp",
        grid=(steps + 1,),
        in_specs=[VMEM] * 5 + w_specs,
        out_specs=[VMEM, VMEM] + [HBM] * 6 + [bias, bias],
        out_shape=[
            low(rows, width),
            jax.ShapeDtypeStruct((rows, width), f32),
            low(2, 4, width // 4, tile),
            low(2, 4, width // 4, tile),
            low(4, width // 8, tile),
            low(4, 2, half // 2, tile),
            low(4, 2, half // 2, tile),
            low(2, half // 2, tile),
        ]
        + [jax.ShapeDtypeStruct((steps, 1, tile), f32)] * 2,
        scratch_shapes=(
            [pltpu.VMEM((2, width, tile), bf16)] + [pltpu.VMEM((2, half, tile), bf16)] * 2
        )
        * 2
        + [
            pltpu.VMEM((2, half, tile), bf16),
            pltpu.VMEM((rows, width), f32),
            pltpu.VMEM((steps, 4, width // 4, tile), bf16),
            pltpu.VMEM((steps, 2, half, tile), bf16),
            DMA((3, 2)),
            DMA((3, 2)),
            DMA((2,)),
            DMA((2,)),
            DMA((3, 2)),
            DMA((3, 2)),
            DMA((2,)),
            DMA((4, 2)),
            DMA((3,)),
        ],
        compiler_params=params(collective_id=4, has_side_effects=True),
        cost_estimate=pl.CostEstimate(
            flops=2 * 6 * rows * width * ff, bytes_accessed=40 * 2**20, transcendentals=0
        ),
    )(vecs, h2, h2p, cot, res, w_up, w_down, w_up, w_down)


def norm_back(z, scale, dz):
    return scale * (dz - jnp.mean(dz, -1, keepdims=True) - z * jnp.mean(dz * z, -1, keepdims=True))


def tail_kernel(n_items, n_band, qt, *refs):
    (table, counts, stat, vecs, dbu_a, dbu_b, log_total) = refs[:7]
    (res_h, dh_h, cot_h, out_rows, attn_h, attn_sib_h, wo_h, q_h, k_h, v_h, h1_h) = refs[7:18]
    (wq_h, wk_h, wv_h, tok_h, kd_h, rd_h, rest_d, ku_h, ru_h, rest_u, tokens) = refs[18:29]
    (out_home, d_tok, total, o_down, o_up, o_wo, o_wq, o_wk, o_wv) = refs[29:38]
    (res, dh, cot, low, wo, attn, attn_sib, kd, rd1, rdr, rd2, rd3, rd4) = refs[38:51]
    (ku, ru1, rur, ru2, ru3, ru4, q, k, v, da, da_send, dk_acc, dv_acc) = refs[51:64]
    (h1, wq, wk, wv, tok, gw, gw_core, gw1, gw2, gw3, gw4) = refs[64:75]
    (d_pair, gp, gp_core, gp1, gp2, gp3, gp4, home) = refs[75:83]
    (small, buf_i, part, buf_b, buf_i2, part2, buf_b2) = refs[83:90]
    (send, recv, lsem, send_r, recv_r, send_g, recv_g, send_i, recv_i, send_b, recv_b) = refs[90:101]

    it, bd, c, yx = place()
    x, y = lax.rem(yx, 2), yx // 2
    bl, bh = lax.rem(bd, 2), bd // 2
    sibling = (it + 1 - 2 * c, bd)
    to_x, to_y = (it + 2 - 4 * x, bd), (it + 4 - 8 * y, bd)
    to_z1, to_z2 = (it, bd + 1 - 2 * bl), (it, lax.rem(bd + 2, 4))
    rows, width = res.shape
    half = width // 2
    fourth = width // 4
    eighth = width // 8
    tile = kd.shape[-1]
    sent = []
    loads = []

    def load(src, dst):
        copy = pltpu.make_async_copy(src, dst, lsem.at[len(loads)])
        copy.start()
        loads.append(copy)
        return copy

    def push(src, dst, to, start=True):
        i = len(sent)
        copy = remote(src, dst, send.at[i], recv.at[i], to)
        if start:
            copy.start()
        sent.append(copy)
        return copy

    def some(which, size):
        return pl.ds(pl.multiple_of(which * size, 128), size)

    greet(all_peers(n_items))
    d1 = push(rest_d, rdr, to_x)
    u1 = push(rest_u, rur, to_y)
    load(out_rows, tok).wait()
    out_blocks = tok.reshape(4, rows // 4, width)
    rows_back(out_blocks, out_home, send_r, recv_r)

    get_res, get_dh, get_cot = load(res_h, res), load(dh_h, dh), load(cot_h, cot)
    get_wo, get_attn, get_sib = load(wo_h, wo), load(attn_h, attn), load(attn_sib_h, attn_sib)
    get_down = [load(kd_h, kd), load(rd_h, rd1)]
    get_up = [load(ku_h, ku), load(ru_h, ru1)]
    get_qkv = [load(src, dst) for src, dst in ((q_h, q), (k_h, k), (v_h, v))]
    get_h1 = load(h1_h, h1)
    lanes = some(c, half)
    get_w = [load(src.at[:, lanes], dst) for src, dst in ((wq_h, wq), (wk_h, wk), (wv_h, wv))]

    small[...] = jnp.zeros_like(small)
    for i in range(4):
        for src, h in ((dbu_a, 1 - c), (dbu_b, c)):
            small[4 + i : 5 + i, some(h, half)] = src[i]
    for copy in (get_res, get_dh, get_cot, get_wo):
        copy.wait()
    block = 256

    def second_norm(i):
        at = some(i, block)
        z, scale = normalize(res[at, :])
        d_h = dh[at, :]
        c32 = cot[at, :].astype(f32)
        full = c32 + norm_back(z, scale, d_h * vecs[R_G2 : R_G2 + 1, :])
        res[at, :] = full
        d_low = full.astype(bf16)
        low[at, :] = d_low
        for j, term in enumerate((d_h * z, d_h, d_low.astype(f32), c32)):
            small[j : j + 1, :] += jnp.sum(term, 0, keepdims=True)
        da[at, :] = dot(d_low, half_rows(wo, c, half), 1, 1).astype(bf16)
        da_send[at, :] = dot(d_low, half_rows(wo, 1 - c, half), 1, 1).astype(bf16)

    theirs, mine = some(1 - x, tile // 4), some(x, tile // 4)
    cuts = [some(0, eighth), some(1, eighth)]
    down, up = kd.reshape(2, 2, 2, fourth, tile), ku.reshape(2, 2, 2, tile // 2, tile)

    def down_second(i):
        return push(kd.at[1 - y, :, cuts[i]], rd2.at[:, cuts[i]], to_y)

    def up_second(s, i):
        b = block_order(s)
        ku[b, i] += ru1[b, i] if s < 3 else rur[i]
        return push(ku.at[b, i, theirs], ru2.at[b, i], to_x)

    def down_third(i):
        d2[i].wait_recv()
        kd[y, :, cuts[i]] += rd2[:, cuts[i]]
        return push(down.at[y, :, 1 - bl, cuts[i]], rd3.at[:, cuts[i]], to_z1)

    def up_third(i):
        for copy in u2[i]:
            copy.wait_recv()
        ku[:, i, mine] += ru2[:, i]
        return push(up.at[:, 1 - bl, i, mine], ru3.at[:, i], to_z1)

    def down_fourth(i):
        d3[i].wait_recv()
        for high in range(2):
            down[y, high, bl, cuts[i]] += rd3[high, cuts[i]]
        return push(down.at[y, 1 - bh, bl, cuts[i]], rd4.at[cuts[i]], to_z2)

    def up_fourth(i):
        u3[i].wait_recv()
        for high in range(2):
            up[high, bl, i, mine] += ru3[high, i]
        return push(up.at[1 - bh, bl, i, mine], ru4.at[i], to_z2)

    second_norm(0)
    for copy in get_down + get_up:
        copy.wait()
    for yy in range(2):
        kd[yy, :, cuts[0]] += rd1[yy, :, cuts[0]]
    d2 = [down_second(0)]
    u2 = [[up_second(s, 0) for s in range(3)], []]
    second_norm(1)

    da_copy = push(da_send, da.at[pl.ds(rows, rows)], sibling)
    early = share_start(
        n_items, it, lambda p: (p, bd), small.at[pl.ds(0, 8)], buf_i, send_i.at[0], recv_i.at[0]
    )

    get_attn.wait()
    get_sib.wait()
    for i, heads in enumerate((attn, attn_sib)):
        for xx in range(2):
            part_wo = dot(heads[:, xx * fourth : (xx + 1) * fourth], low[...], 0, 0).astype(bf16)
            for cc in range(2):
                gw[i, xx, cc] = part_wo[cc * eighth : (cc + 1) * eighth]
    core_w = [push(gw.at[i, :, 1 - c], gw_core.at[1 - i], sibling) for i in range(2)]

    d1.wait_recv()
    kd[0, :, cuts[1]] += rd1[0, :, cuts[1]]
    kd[1, :, cuts[1]] += rdr[...]
    d2.append(down_second(1))
    u1.wait_recv()
    u2[0].append(up_second(3, 0))
    u2[1] = [up_second(s, 1) for s in range(4)]

    for copy in get_qkv:
        copy.wait()
    get_h1.wait()
    da_copy.wait_recv()
    lane_k = lax.broadcasted_iota(jnp.int32, (2 * rows, 128), 1)
    lane_q = lax.broadcasted_iota(jnp.int32, (qt, 128), 1)

    def pair(i):
        at_lanes = some(i, 128)
        k_pair, v_pair = k[:, at_lanes], v[:, at_lanes]
        bias = key_bias(table, counts, k_pair.shape)
        keys = [with_spare(k_pair, bias, hd, lane_k) for hd in range(2)]
        keys_only = [head_lanes(k_pair, hd, lane_k) for hd in range(2)]
        values = [head_lanes(v_pair, hd, lane_k) for hd in range(2)]
        for t in range(2 * rows // qt):
            at = slice(t * qt, (t + 1) * qt)
            q_tile, d_tile = q[at, at_lanes], da[at, at_lanes]
            dq_both = None
            for hd in range(2):
                q_head = head_lanes(q_tile, hd, lane_q)
                d_head = head_lanes(d_tile, hd, lane_q)
                s = dot(keys[hd], ones_beside(q_tile, hd, lane_q), 1, 1)
                p = jnp.exp(s - log_total[i, hd : hd + 1, at])
                d_p = dot(values[hd], d_tile, 1, 1)
                weighted = p * d_p
                delta = jnp.sum(weighted, 0, keepdims=True)
                ds = (weighted - p * delta).astype(bf16)
                dv_part = dot(p.astype(bf16), d_head)
                dk_part = dot(ds, q_head)
                if t == 0 and hd == 0:
                    dv_acc[...] = dv_part
                    dk_acc[...] = dk_part
                else:
                    dv_acc[...] += dv_part
                    dk_acc[...] += dk_part
                term = dot(keys_only[hd], ds, 0, 0)
                dq_both = term if dq_both is None else dq_both + term
            dq = dq_both.T * score_scale
            q[at, at_lanes] = dq.astype(bf16)
            d_pair[at, 0:128] = dq.astype(bf16)
        k[:, at_lanes] = dk_acc[...].astype(bf16)
        v[:, at_lanes] = dv_acc[...].astype(bf16)
        d_pair[:, 128:256] = dk_acc[...].astype(bf16)
        d_pair[:, 256:384] = dv_acc[...].astype(bf16)
        for j in range(4):
            term = dot(h1[:, j * fourth : (j + 1) * fourth], d_pair[...], 0, 0).astype(bf16)
            for cc in range(2):
                gp[i, j, cc] = term[cc * eighth : (cc + 1) * eighth]

    def pair_core(i):
        return push(gp.at[i, :, 1 - c], gp_core.at[i], sibling)

    def chips(i, first, second):
        return 2 * second + first if i % 2 == 0 else 2 * first + second

    def first_of(i):
        return (x, y) if i % 2 == 0 else (y, x)

    def pair_first(i, core):
        core.wait_recv()
        mine_first, _ = first_of(i)
        to = to_x if i % 2 == 0 else to_y
        got = []
        for j in range(2):
            there = chips(i, 1 - mine_first, j)
            got.append(push(gp.at[i, there, c], gp1.at[i, j, 0], to))
            got.append(push(gp_core.at[i, there], gp1.at[i, j, 1], to))
        return got

    def pair_second(i, got):
        for copy in got:
            copy.wait_recv()
        mine_first, mine_second = first_of(i)
        for j in range(2):
            here = chips(i, mine_first, j)
            gp[i, here, c] += gp1[i, j, 0]
            gp_core[i, here] += gp1[i, j, 1]
        there = chips(i, mine_first, 1 - mine_second)
        to = to_y if i % 2 == 0 else to_x
        return [
            push(gp.at[i, there, c], gp2.at[i, 0], to),
            push(gp_core.at[i, there], gp2.at[i, 1], to),
        ]

    def pair_third(i, got):
        for copy in got:
            copy.wait_recv()
        gp[i, yx, c] += gp2[i, 0]
        gp_core[i, yx] += gp2[i, 1]

    pair(0)
    core_p = [pair_core(0)]
    part[...] = share_end(n_items, early, buf_i)
    early = share_start(n_band, bd, lambda p: (it, p), part, buf_b, send_b.at[0], recv_b.at[0])
    for i in range(2):
        core_w[i].wait_recv()
    for i in range(2):
        gw[i, :, c] += gw_core[i]
    rel_y = lax.rem(y + c, 2)
    w1 = push(gw.at[1 - rel_y, :, c], gw1, to_y)
    d3 = [down_third(0)]
    u3 = [up_third(0)]

    pair(1)
    core_p.append(pair_core(1))
    p1 = [pair_first(0, core_p[0])]
    total[0:8, :] = share_end(n_band, early, buf_b)

    pair(2)
    core_p.append(pair_core(2))
    d4 = [down_fourth(0)]
    u4 = [up_fourth(0)]
    d3.append(down_third(1))
    u3.append(up_third(1))
    p1.append(pair_first(1, core_p[1]))

    pair(3)
    core_p.append(pair_core(3))
    p1.append(pair_first(2, core_p[2]))
    for i, d in ((0, q), (1, v)):
        row = jnp.sum(d[...].astype(f32), 0, keepdims=True)
        small[12 + i : 13 + i, some(c, half)] = row
    w1.wait_recv()
    gw[rel_y, :, c] += gw1[...]
    w2 = push(gw.at[rel_y, 1 - x, c], gw2, to_x)

    for copy in get_w:
        copy.wait()
    dh1, dh1_sib = wo, low

    def first_norm_terms(i):
        at = some(i, block)
        term = dot(q[at, :], wq[...], 1, 1) + dot(k[at, :], wk[...], 1, 1)
        dh1[at, :] = (term + dot(v[at, :], wv[...], 1, 1)).astype(bf16)

    @pl.loop(rows // block, 2 * rows // block)
    def _(i):
        first_norm_terms(i)

    dh_copy = push(dh1.at[pl.ds(rows, rows)], dh1_sib, sibling)
    p1.append(pair_first(3, core_p[3]))
    for i in range(4):
        rows_back_got(out_blocks, out_home, send_r, recv_r, i)
    rows_back_sent(out_blocks, out_home, send_r, recv_r)
    get_tok = load(tok_h, tok)
    d4.append(down_fourth(1))
    u4.append(up_fourth(1))
    p2 = [pair_second(0, p1[0]), pair_second(1, p1[1])]

    g_rows = cot
    g_blocks = g_rows.reshape(4, rows // 4, width)

    def first_norm(i):
        first_norm_terms(i)
        at = some(i, block)
        inv = stat[S_INV : S_INV + 1, :]
        centred = tok[at, :].astype(f32) - stat[S_MEAN : S_MEAN + 1, :]
        z, scale = normalize(centred * inv)
        d_h = dh1[at, :].astype(f32) + dh1_sib[at, :].astype(f32)
        d_start = res[at, :] + norm_back(z, scale, d_h * vecs[R_G1 : R_G1 + 1, :])
        g_rows[at, :] = (d_start * inv).astype(bf16)
        for j, term in enumerate((d_start, d_start * centred, d_h * z, d_h)):
            small[8 + j : 9 + j, :] += jnp.sum(term, 0, keepdims=True)

    get_tok.wait()
    dh_copy.wait_recv()
    first_norm(0)
    rows_back(g_blocks, home, send_g, recv_g, (0, 1))
    first_norm(1)
    rows_back(g_blocks, home, send_g, recv_g, (2, 3))
    late = share_start(
        n_items, it, lambda p: (p, bd), small.at[pl.ds(8, 8)], buf_i2, send_i.at[1], recv_i.at[1]
    )
    p2.append(pair_second(2, p1[2]))
    part2[...] = share_end(n_items, late, buf_i2)
    late = share_start(n_band, bd, lambda p: (it, p), part2, buf_b2, send_b.at[1], recv_b.at[1])

    pair_third(0, p2[0])
    pair_third(1, p2[1])
    p3 = []
    for i in range(2):
        there = 2 * (1 - bl) + i
        p3.append(push(gp.at[there, yx, c], gp3.at[i, 0], to_z1, False))
        p3.append(push(gp_core.at[there, yx], gp3.at[i, 1], to_z1, False))

    @pl.when(bl == 1)
    def _():
        for copy in p3:
            copy.start()

    p2.append(pair_second(3, p1[3]))
    w2.wait_recv()
    gw[rel_y, x, c] += gw2[...]

    def z_lanes(which):
        return some(which, fourth)

    w3 = [
        push(gw.at[rel_y, x, c, :, z_lanes(2 * high + 1 - bl)], gw3.at[high], to_z1) for high in range(2)
    ]
    pair_third(2, p2[2])
    pair_third(3, p2[3])

    @pl.when(bl == 0)
    def _():
        for copy in p3:
            copy.start()

    sums = share_end(n_band, late, buf_b2)
    total[8:16, :] = sums
    for high in range(2):
        w3[high].wait_recv()
    for high in range(2):
        gw3[high] = gw[rel_y, x, c, :, z_lanes(2 * high + bl)] + gw3[high]
    w4 = push(gw3.at[1 - bh], gw4, to_z2)
    for copy in p3:
        copy.wait_recv()
    for i in range(2):
        here = 2 * bl + i
        gp3[i, 0] = gp[here, yx, c] + gp3[i, 0]
        gp3[i, 1] = gp_core[here, yx] + gp3[i, 1]
    rel_b = lax.rem(bh + c, 2)
    p4 = push(gp3.at[:, 1 - rel_b], gp4, to_z2)

    count = patch_total(counts, (1, width))
    inv = stat[S_INV : S_INV + 1, :]
    fix = -0.5 * inv * sums[0:1, :] / count
    slope = -0.5 * inv * inv * inv * sums[1:2, :] / count
    cut = rows // 4
    position = lax.broadcasted_iota(jnp.int32, (cut, width), 0) + bd * (2 * cut)
    for i in range(4):
        s, h = i // 2, i % 2
        rows_back_got(g_blocks, home, send_g, recv_g, i)
        now = pl.ds(h * cut, cut)
        valid = position + h * cut < counts[table[it * 2 + s]]
        term = fix + slope * (tokens[s, now, :].astype(f32) - stat[S_BATCH : S_BATCH + 1, :])
        d_tok[s, now, :] = (home[s, now, :].astype(f32) + jnp.where(valid, term, 0.0)).astype(bf16)

    for copy in d4 + u4:
        copy.wait_recv()
    o_down[...] = (down[y, bh, bl].astype(f32) + rd4[...].astype(f32)).T
    up_sum = up[bh, bl, :, mine].astype(f32) + ru4[...].astype(f32)
    for i, h in ((0, 1 - c), (1, c)):
        o_up[:, some(h, tile)] = up_sum[i]
    w4.wait_recv()
    o_wo[...] = gw3[bh].astype(f32) + gw4[...].astype(f32)
    p4.wait_recv()
    for i in range(2):
        all_three = gp3[i, rel_b].astype(f32) + gp4[i].astype(f32)
        for j, ref in enumerate((o_wq, o_wk, o_wv)):
            ref[:, i * 128 : (i + 1) * 128] = all_three[:, j * 128 : (j + 1) * 128]

    rows_back_sent(g_blocks, home, send_g, recv_g)
    for copy in sent:
        copy.wait_send()


def tail(table, counts, stat, vecs, dbu_a, dbu_b, log_total, res, dh, cot, out_rows, *rest, qt=512):
    attn, attn_sib, wo, q, k, v, h1, wq, wk, wv, tok, kd, rd, rest_d, ku, ru, rest_u, tokens = rest
    n_items, n_band = lax.axis_size("items"), lax.axis_size("band")
    rows, width = res.shape
    half, fourth, cut = width // 2, width // 4, rows // 4
    tile = kd.shape[3]
    buf = lambda *shape: pltpu.VMEM(shape, bf16)
    buf32 = lambda *shape: pltpu.VMEM(shape, f32)
    out = lambda *shape: jax.ShapeDtypeStruct(shape, f32)
    e, s = fourth // 2, fourth
    return pl.pallas_call(
        functools.partial(tail_kernel, n_items, n_band, qt),
        name="tail",
        in_specs=[SMEM, SMEM] + [VMEM] * 5 + [HBM] * 21 + [VMEM],
        out_specs=[HBM] + [VMEM] * 8,
        out_shape=[
            jax.ShapeDtypeStruct(tokens.shape, bf16),
            jax.ShapeDtypeStruct(tokens.shape, bf16),
            out(16, width),
            out(tile, s),
            out(e, 2 * tile),
            out(e, s),
            out(e, s),
            out(e, s),
            out(e, s),
        ],
        scratch_shapes=[
            buf32(rows, width), buf32(rows, width), buf(rows, width), buf(rows, width),
            buf(width, width), buf(rows, half), buf(rows, half),
            buf(2, 4, s, tile), buf(2, 4, s, tile), buf(4, e, tile), buf(4, s, tile), buf(2, s, tile),
            buf(s, tile),
            buf(4, 2, tile // 2, tile), buf(4, 2, tile // 2, tile), buf(2, tile // 2, tile),
            buf(4, 2, tile // 4, tile), buf(2, 2, tile // 4, tile), buf(2, tile // 4, tile),
            buf(2 * rows, half), buf(2 * rows, half), buf(2 * rows, half),
            buf(2 * rows, half), buf(rows, half), buf32(2 * rows, 128), buf32(2 * rows, 128),
            buf(2 * rows, width), buf(width, half), buf(width, half), buf(width, half), buf(rows, width),
            buf(2, 2, 2, e, width), buf(2, 2, e, width), buf(2, e, width), buf(e, width),
            buf(2, e, s), buf(e, s),
            buf(2 * rows, 384), buf(4, 4, 2, e, 384), buf(4, 4, e, 384), buf(4, 2, 2, e, 384),
            buf(4, 2, e, 384), buf(2, 2, e, 384), buf(2, e, 384),
            buf(2, 2 * cut, width),
            buf32(16, width), buf32(n_items, 8, width), buf32(8, width), buf32(n_band, 8, width),
            buf32(n_items, 8, width), buf32(8, width), buf32(n_band, 8, width),
            DMA((80,)), DMA((80,)), DMA((24,)),
            DMA((4,)), DMA((4,)), DMA((4,)), DMA((4,)),
            DMA((2, n_items)), DMA((2, n_items)), DMA((2, n_band)), DMA((2, n_band)),
        ],
        compiler_params=params(collective_id=5, has_side_effects=True),
        cost_estimate=pl.CostEstimate(
            flops=60 * rows * width * width, bytes_accessed=40 * 2**20, transcendentals=0
        ),
    )(
        table, counts, stat, vecs, dbu_a, dbu_b, log_total, res, dh, cot,
        out_rows, attn, attn_sib, wo, q, k, v, h1, wq, wk, wv, tok,
        kd, rd, rest_d, ku, ru, rest_u, tokens,
    )


def emit_kernel(stat, small, *refs):
    n = (len(refs) - 11) // 2
    sources, singles, targets = refs[:n], refs[n : n + 11], refs[n + 11 :]
    for source, target in zip(sources, targets):
        target[...] = source[...]
    singles[0][...] = stat[S_MEAN, :]
    singles[1][...] = stat[S_VAR, :]
    for ref, row in zip(singles[2:10], (10, 11, 12, 13, 2, 0, 1, 3)):
        ref[...] = small[row, :]
    singles[10][...] = small[4:8, :].reshape(4 * small.shape[1])


def emit(stat, small, arrays):
    width = stat.shape[1]
    return pl.pallas_call(
        emit_kernel,
        name="emit",
        in_specs=[VMEM] * (2 + len(arrays)),
        out_specs=[VMEM] * (11 + len(arrays)),
        out_shape=[jax.ShapeDtypeStruct((width,), f32)] * 10
        + [jax.ShapeDtypeStruct((4 * width,), f32)]
        + [jax.ShapeDtypeStruct(a.shape, a.dtype) for a in arrays],
        compiler_params=params(),
    )(stat, small, *arrays)


def column_layer(
    tokens, cotangent, running_mean, running_var, slot_table, patch_counts,
    ln1_gain, ln1_bias, w_query, b_query, w_key, w_value, b_value, w_out, b_out,
    ln2_gain, ln2_bias, w_up, b_up, w_down, b_down,
):
    slots, band_rows, width = tokens.shape
    rows = slots * band_rows
    singles = (running_mean, running_var, ln1_gain, ln1_bias, b_query, b_value, b_out)
    singles += (ln2_gain, ln2_bias, b_down)
    vecs, stat, tok, cot_rows, h1, q, k, v, log_total, attn, attn_sib, res, h2, h2p = front(
        slot_table, patch_counts, singles, b_up, tokens, cotangent, w_query, w_key, w_value, w_out
    )
    tok, cot_rows = tok.reshape(rows, width), cot_rows.reshape(rows, width)
    out_rows, d_h2, kd, rd, rest_d, ku, ru, rest_u, dbu_a, dbu_b = mlp(
        vecs, h2, h2p, cot_rows, res, w_up, w_down
    )
    output, d_tokens, small, d_w_down, d_w_up, d_w_out, d_wq, d_wk, d_wv = tail(
        slot_table, patch_counts, stat, vecs, dbu_a, dbu_b, log_total, res, d_h2, cot_rows,
        out_rows, attn, attn_sib, w_out, q, k, v, h1, w_query, w_key, w_value, tok,
        kd, rd, rest_d, ku, ru, rest_u, tokens,
    )
    singles = emit(
        stat, small, (output, d_tokens, d_wq, d_wk, d_wv, d_w_out, d_w_up, d_w_down)
    )
    (new_mean, new_var, d_g1, d_s1, d_bq, d_bv, d_bo, d_g2, d_s2, d_bd, d_bu) = singles[:11]
    output, d_tokens, d_wq, d_wk, d_wv, d_w_out, d_w_up, d_w_down = singles[11:]
    return (
        output, d_tokens, new_mean, new_var, d_g1, d_s1, d_wq, d_bq, d_wk, d_wv, d_bv,
        d_w_out, d_bo, d_g2, d_s2, d_w_up, d_bu, d_w_down, d_bd,
    )


def layer_norm(value, gain, shift):
    centre = value - jnp.mean(value, -1, keepdims=True)
    spread = jnp.mean(centre * centre, -1, keepdims=True)
    return centre * lax.rsqrt(spread + epsilon) * gain + shift


def gelu_tanh(value):
    return (
        0.5
        * value
        * (1.0 + jnp.tanh(0.7978845608028654 * (value + 0.044715 * value * value * value)))
    )


def head_layout():
    heads_per = 4
    return (heads_per, HEADS // heads_per, heads_per * HEAD_DIM)


def group_scores(q_part, k_part, key_mask):
    scores = (
        jnp.einsum("rhd,khd->hrk", q_part, k_part, preferred_element_type=jnp.float32) * score_scale
    )
    return jnp.where(key_mask[None, None, :], scores, masked_score)


def attend_forward(q_slot, keys_slot, values_slot, key_mask):
    heads_per, groups, group_width = head_layout()
    band_rows = q_slot.shape[0]
    seq_length = keys_slot.shape[0]

    def head_block(group_index):
        begin = group_index * group_width
        q_part = lax.dynamic_slice_in_dim(q_slot, begin, group_width, 1).reshape(
            band_rows, heads_per, HEAD_DIM
        )
        k_part = lax.dynamic_slice_in_dim(keys_slot, begin, group_width, 1).reshape(
            seq_length, heads_per, HEAD_DIM
        )
        v_part = lax.dynamic_slice_in_dim(values_slot, begin, group_width, 1).reshape(
            seq_length, heads_per, HEAD_DIM
        )
        scores = group_scores(q_part, k_part, key_mask)
        top_score = jnp.max(scores, -1, keepdims=True)
        log_total = top_score + jnp.log(jnp.sum(jnp.exp(scores - top_score), -1, keepdims=True))
        probs_low = jnp.exp(scores - log_total).astype(jnp.bfloat16)
        attended = jnp.einsum("hrk,khd->rhd", probs_low, v_part, preferred_element_type=jnp.float32)
        return (attended.reshape(band_rows, group_width), log_total[..., 0])

    attended, log_totals = lax.map(head_block, jnp.arange(groups, dtype=jnp.int32))
    return (attended.transpose(1, 0, 2).reshape(band_rows, groups * group_width), log_totals)


def attend_backward(q_slot, keys_slot, values_slot, key_mask, d_attn_slot, row_delta, log_totals):
    heads_per, groups, group_width = head_layout()
    query_rows = q_slot.shape[0]
    seq_length = keys_slot.shape[0]
    deltas = jnp.transpose(row_delta).reshape(groups, heads_per, query_rows)

    def head_block(inputs):
        group_index, log_total, delta_part = inputs
        begin = group_index * group_width
        q_part = lax.dynamic_slice_in_dim(q_slot, begin, group_width, 1).reshape(
            query_rows, heads_per, HEAD_DIM
        )
        k_part = lax.dynamic_slice_in_dim(keys_slot, begin, group_width, 1).reshape(
            seq_length, heads_per, HEAD_DIM
        )
        v_part = lax.dynamic_slice_in_dim(values_slot, begin, group_width, 1).reshape(
            seq_length, heads_per, HEAD_DIM
        )
        d_part = lax.dynamic_slice_in_dim(d_attn_slot, begin, group_width, 1).reshape(
            query_rows, heads_per, HEAD_DIM
        )
        scores = group_scores(q_part, k_part, key_mask)
        probs = jnp.exp(scores - log_total[..., None])
        d_probs = jnp.einsum("rhd,khd->hrk", d_part, v_part, preferred_element_type=jnp.float32)
        d_scores = (probs * (d_probs - delta_part[..., None])).astype(jnp.bfloat16)
        results = []
        d_q_part = (
            jnp.einsum("hrk,khd->rhd", d_scores, k_part, preferred_element_type=jnp.float32)
            * score_scale
        )
        results.append(d_q_part.reshape(query_rows, group_width))
        probs_low = probs.astype(jnp.bfloat16)
        d_k_part = (
            jnp.einsum("hrk,rhd->khd", d_scores, q_part, preferred_element_type=jnp.float32)
            * score_scale
        )
        d_v_part = jnp.einsum("hrk,rhd->khd", probs_low, d_part, preferred_element_type=jnp.float32)
        results.append(d_k_part.reshape(seq_length, group_width))
        results.append(d_v_part.reshape(seq_length, group_width))
        return tuple(results)

    mapped = lax.map(head_block, (jnp.arange(groups, dtype=jnp.int32), log_totals, deltas))
    full_width = groups * group_width
    return tuple((piece.transpose(1, 0, 2).reshape(piece.shape[1], full_width) for piece in mapped))


def local(
    tokens,
    cotangent,
    running_mean,
    running_var,
    slot_table,
    patch_counts,
    ln1_gain,
    ln1_bias,
    w_query,
    b_query,
    w_key,
    w_value,
    b_value,
    w_out,
    b_out,
    ln2_gain,
    ln2_bias,
    w_up,
    b_up,
    w_down,
    b_down,
):
    slot_count, band_rows, model_width = tokens.shape
    seq_length = band_rows * lax.axis_size("band")
    item_rank = lax.axis_index("items")
    band_rank = lax.axis_index("band")
    every_slot = jnp.arange(slot_table.shape[0], dtype=jnp.int32)
    my_slots = item_rank * slot_count + jnp.arange(slot_count, dtype=jnp.int32)
    item_ids = jnp.sum(
        jnp.where(every_slot[None, :] == my_slots[:, None], slot_table[None, :], 0), 1
    )
    lengths = jnp.sum(
        jnp.where(every_slot[None, :] == item_ids[:, None], patch_counts[None, :], 0), 1
    )
    key_mask = jnp.arange(seq_length, dtype=jnp.int32)[None, :] < lengths[:, None]
    row_mask = (band_rank * band_rows + jnp.arange(band_rows, dtype=jnp.int32))[None, :] < lengths[
        :, None
    ]
    row_keep = row_mask.astype(jnp.float32).reshape(-1, 1)
    raw_flat = tokens.astype(jnp.float32).reshape(-1, model_width)
    part_one = jnp.sum(row_keep * raw_flat, 0)
    part_two = jnp.sum(row_keep * raw_flat * raw_flat, 0)
    total_one, total_two = lax.psum((part_one, part_two), ("items", "band"))
    patch_total = jnp.sum(patch_counts).astype(jnp.float32)
    batch_mean = total_one / patch_total
    batch_var = total_two / patch_total - batch_mean * batch_mean
    new_mean = momentum * running_mean + momentum * batch_mean
    new_var = momentum * running_var + momentum * batch_var
    inverse = lax.rsqrt(new_var + epsilon)
    normed_in = (raw_flat - new_mean) * inverse
    gain_one = ln1_gain.astype(jnp.float32)
    shift_one = ln1_bias.astype(jnp.float32)
    gain_two = ln2_gain.astype(jnp.float32)
    shift_two = ln2_bias.astype(jnp.float32)
    h_one_full, norm_one_back = jax.vjp(layer_norm, normed_in, gain_one, shift_one)
    h_one = h_one_full.astype(jnp.bfloat16)
    queries = (
        jnp.dot(h_one, w_query, preferred_element_type=jnp.float32) + b_query.astype(jnp.float32)
    ).astype(jnp.bfloat16)
    key_local = (
        jnp.dot(h_one, w_key, preferred_element_type=jnp.float32)
        .astype(jnp.bfloat16)
        .reshape(slot_count, band_rows, model_width)
    )
    value_local = (
        (jnp.dot(h_one, w_value, preferred_element_type=jnp.float32) + b_value.astype(jnp.float32))
        .astype(jnp.bfloat16)
        .reshape(slot_count, band_rows, model_width)
    )
    keys_all, values_all = (
        lax.all_gather(key_local, "band", axis=1, tiled=True),
        lax.all_gather(value_local, "band", axis=1, tiled=True),
    )
    q_slots = queries.reshape(slot_count, band_rows, model_width)
    attended_list = []
    totals_list = []
    for slot_index in range(slot_count):
        attended, log_totals = attend_forward(
            q_slots[slot_index], keys_all[slot_index], values_all[slot_index], key_mask[slot_index]
        )
        attended_list.append(attended)
        totals_list.append(log_totals)
    attn_full = jnp.concatenate(attended_list, 0)
    attn_low = attn_full.astype(jnp.bfloat16)
    residual = (
        normed_in
        + jnp.dot(attn_low, w_out, preferred_element_type=jnp.float32)
        + b_out.astype(jnp.float32)
    )
    h_two_full, norm_two_back = jax.vjp(layer_norm, residual, gain_two, shift_two)
    h_two = h_two_full.astype(jnp.bfloat16)
    up_proj = jnp.dot(h_two, w_up, preferred_element_type=jnp.float32) + b_up.astype(jnp.float32)
    activated_full, gelu_back = jax.vjp(gelu_tanh, up_proj)
    activated = activated_full.astype(jnp.bfloat16)
    result = (
        residual
        + jnp.dot(activated, w_down, preferred_element_type=jnp.float32)
        + b_down.astype(jnp.float32)
    )
    output = result.astype(jnp.bfloat16).reshape(slot_count, band_rows, model_width)
    cot_low = cotangent.reshape(-1, model_width)
    cot_full = cot_low.astype(jnp.float32)
    d_w_down = jnp.einsum("tf,td->fd", activated, cot_low, preferred_element_type=jnp.float32)
    d_b_down = jnp.sum(cot_full, 0)
    d_activated = jnp.einsum("td,fd->tf", cot_low, w_down, preferred_element_type=jnp.float32)
    (d_up_full,) = gelu_back(d_activated)
    d_up = d_up_full.astype(jnp.bfloat16)
    d_w_up = jnp.einsum("td,tf->df", h_two, d_up, preferred_element_type=jnp.float32)
    d_b_up = jnp.sum(d_up, 0, dtype=jnp.float32)
    d_h_two = jnp.einsum("tf,df->td", d_up, w_up, preferred_element_type=jnp.float32)
    d_res_norm, d_gain_two, d_shift_two = norm_two_back(d_h_two)
    d_residual = cot_full + d_res_norm
    d_branch = d_residual.astype(jnp.bfloat16)
    d_w_out = jnp.einsum("td,te->de", attn_low, d_branch, preferred_element_type=jnp.float32)
    d_b_out = jnp.sum(d_branch, 0, dtype=jnp.float32)
    d_attn = jnp.einsum("te,de->td", d_branch, w_out, preferred_element_type=jnp.float32).astype(
        jnp.bfloat16
    )
    row_delta = jnp.sum(
        (d_attn.astype(jnp.float32) * attn_full).reshape(slot_count, band_rows, HEADS, HEAD_DIM), -1
    )
    d_attn_slots = d_attn.reshape(slot_count, band_rows, model_width)
    back_keys, back_values = (keys_all, values_all)
    d_q_list = []
    d_k_list = []
    d_v_list = []
    for slot_index in range(slot_count):
        d_q_slot, d_k_slot, d_v_slot = attend_backward(
            q_slots[slot_index],
            back_keys[slot_index],
            back_values[slot_index],
            key_mask[slot_index],
            d_attn_slots[slot_index],
            row_delta[slot_index],
            totals_list[slot_index],
        )
        d_q_list.append(d_q_slot)
        d_k_list.append(d_k_slot)
        d_v_list.append(d_v_slot)
    d_keys_mine, d_values_mine = (
        lax.psum_scatter(
            jnp.stack(d_k_list).astype(jnp.bfloat16), "band", scatter_dimension=1, tiled=True
        ).astype(jnp.float32),
        lax.psum_scatter(
            jnp.stack(d_v_list).astype(jnp.bfloat16), "band", scatter_dimension=1, tiled=True
        ).astype(jnp.float32),
    )
    d_queries = jnp.concatenate(d_q_list, 0).astype(jnp.bfloat16)
    d_keys = d_keys_mine.reshape(-1, model_width).astype(jnp.bfloat16)
    d_values = d_values_mine.reshape(-1, model_width).astype(jnp.bfloat16)
    d_w_query = jnp.einsum("td,te->de", h_one, d_queries, preferred_element_type=jnp.float32)
    d_b_query = jnp.sum(d_queries, 0, dtype=jnp.float32)
    d_w_key = jnp.einsum("td,te->de", h_one, d_keys, preferred_element_type=jnp.float32)
    d_w_value = jnp.einsum("td,te->de", h_one, d_values, preferred_element_type=jnp.float32)
    d_b_value = jnp.sum(d_values, 0, dtype=jnp.float32)
    d_h_one = jnp.einsum("te,de->td", d_queries, w_query, preferred_element_type=jnp.float32)
    d_h_one = d_h_one + jnp.einsum("te,de->td", d_keys, w_key, preferred_element_type=jnp.float32)
    d_h_one = d_h_one + jnp.einsum(
        "te,de->td", d_values, w_value, preferred_element_type=jnp.float32
    )
    d_start_norm, d_gain_one, d_shift_one = norm_one_back(d_h_one)
    d_start = d_residual + d_start_norm
    centred = raw_flat - new_mean
    small_sums = lax.psum(
        (
            jnp.sum(d_start, 0),
            jnp.sum(d_start * centred, 0),
            d_gain_one,
            d_shift_one,
            d_b_query,
            d_b_value,
            d_b_out,
            d_gain_two,
            d_shift_two,
            d_b_up,
            d_b_down,
        ),
        ("items", "band"),
    )
    sum_g = small_sums[0]
    sum_gx = small_sums[1]
    cube = inverse * inverse * inverse
    d_raw = d_start * inverse + row_keep * (
        -0.5 * inverse * sum_g / patch_total
        - 0.5 * cube * sum_gx * (raw_flat - batch_mean) / patch_total
    )
    d_tokens = d_raw.astype(jnp.bfloat16).reshape(slot_count, band_rows, model_width)
    weight_grads = (
        lax.psum_scatter(
            d_w_query.astype(jnp.bfloat16), "items", scatter_dimension=0, tiled=True
        ).astype(jnp.float32),
        lax.psum_scatter(
            d_w_key.astype(jnp.bfloat16), "items", scatter_dimension=0, tiled=True
        ).astype(jnp.float32),
        lax.psum_scatter(
            d_w_value.astype(jnp.bfloat16), "items", scatter_dimension=0, tiled=True
        ).astype(jnp.float32),
        lax.psum_scatter(
            d_w_out.astype(jnp.bfloat16), "items", scatter_dimension=0, tiled=True
        ).astype(jnp.float32),
        lax.psum_scatter(
            d_w_up.astype(jnp.bfloat16), "items", scatter_dimension=0, tiled=True
        ).astype(jnp.float32),
        lax.psum_scatter(
            d_w_down.astype(jnp.bfloat16), "items", scatter_dimension=0, tiled=True
        ).astype(jnp.float32),
    )
    weight_grads = (
        lax.psum_scatter(
            weight_grads[0].astype(jnp.bfloat16), "band", scatter_dimension=1, tiled=True
        ).astype(jnp.float32),
        lax.psum_scatter(
            weight_grads[1].astype(jnp.bfloat16), "band", scatter_dimension=1, tiled=True
        ).astype(jnp.float32),
        lax.psum_scatter(
            weight_grads[2].astype(jnp.bfloat16), "band", scatter_dimension=1, tiled=True
        ).astype(jnp.float32),
        lax.psum_scatter(
            weight_grads[3].astype(jnp.bfloat16), "band", scatter_dimension=1, tiled=True
        ).astype(jnp.float32),
        lax.psum_scatter(
            weight_grads[4].astype(jnp.bfloat16), "band", scatter_dimension=1, tiled=True
        ).astype(jnp.float32),
        lax.psum_scatter(
            weight_grads[5].astype(jnp.bfloat16), "band", scatter_dimension=1, tiled=True
        ).astype(jnp.float32),
    )
    return (
        output,
        d_tokens,
        new_mean,
        new_var,
        small_sums[2],
        small_sums[3],
        weight_grads[0],
        small_sums[4],
        weight_grads[1],
        weight_grads[2],
        small_sums[5],
        weight_grads[3],
        small_sums[6],
        small_sums[7],
        small_sums[8],
        weight_grads[4],
        small_sums[9],
        weight_grads[5],
        small_sums[10],
    )


def solution(mesh):
    columns = mesh.shape["items"] == 8 and mesh.shape["band"] == 4
    return jax.shard_map(
        column_layer if columns else local,
        mesh=mesh,
        in_specs=(
            P("items", "band", None),
            P("items", "band", None),
            P(),
            P(),
            P(),
            P(),
            P(),
            P(),
            P(),
            P(),
            P(),
            P(),
            P(),
            P(),
            P(),
            P(),
            P(),
            P(),
            P(),
            P(),
            P(),
        ),
        out_specs=(
            P("items", "band", None),
            P("items", "band", None),
            P(),
            P(),
            P(),
            P(),
            P("items", "band"),
            P(),
            P("items", "band"),
            P("items", "band"),
            P(),
            P("items", "band"),
            P(),
            P(),
            P(),
            P("items", "band"),
            P(),
            P("items", "band"),
            P(),
        ),
        check_vma=False,
    )
```

```python
import functools
import jax
import jax.numpy as jnp
from jax import lax
from jax.experimental import pallas as pl
from jax.experimental.pallas import tpu as pltpu
from jax.sharding import PartitionSpec as P

HEADS = 16
HEAD_DIM = 64
epsilon = 1e-05
score_scale = 0.125
masked_score = -1e30
momentum = 0.5
f32 = jnp.float32
bf16 = jnp.bfloat16
VMEM_LIMIT = 60 * 2**20
R_MEAN, R_VAR, R_G1, R_S1, R_BQ, R_BV, R_BO, R_G2, R_S2, R_BD, R_BU = range(11)
S_MEAN, S_VAR, S_BATCH, S_INV = range(4)


def dot(a, b, ca=1, cb=0):
    return lax.dot_general(a, b, (((ca,), (cb,)), ((), ())), preferred_element_type=f32)


def params(**kw):
    return pltpu.CompilerParams(vmem_limit_bytes=VMEM_LIMIT, **kw)


def place():
    it, bd = lax.axis_index("items"), lax.axis_index("band")
    return it, bd, lax.rem(it, 2), it // 2


def remote(src, dst, send, recv, to):
    return pltpu.make_async_remote_copy(
        src_ref=src,
        dst_ref=dst,
        send_sem=send,
        recv_sem=recv,
        device_id=to,
        device_id_type=pl.DeviceIdType.MESH,
    )


def greet(peers):
    barrier = pltpu.get_barrier_semaphore()
    for peer in peers:
        pl.semaphore_signal(barrier, inc=1, device_id=peer, device_id_type=pl.DeviceIdType.MESH)
    pl.semaphore_wait(barrier, len(peers))


def column_peers():
    it, bd, c, yx = place()
    peers = [(it, lax.rem(bd + o, 4)) for o in range(1, 4)]
    return peers + [(it + 1 - 2 * c, lax.rem(bd + o, 4)) for o in range(4)]


def rows_out(src, dst, send, recv):
    it, bd, c, yx = place()
    cut = src.shape[1] // 2
    for q in range(4):
        s, h = q // 2, q % 2
        block = src.at[s, pl.ds(h * cut, cut)]
        target = dst.at[bd]
        own = (c == h) & (bd == 2 * c + s)

        @pl.when(own)
        def _():
            pltpu.make_async_copy(block, target, recv.at[bd]).start()

        @pl.when(jnp.logical_not(own))
        def _():
            remote(block, target, send.at[q], recv.at[bd], (yx * 2 + h, 2 * c + s)).start()


def rows_out_sent(src, dst, send, recv):
    it, bd, c, yx = place()
    cut = src.shape[1] // 2
    for q in range(4):
        s, h = q // 2, q % 2
        own = (c == h) & (bd == 2 * c + s)

        @pl.when(jnp.logical_not(own))
        def _():
            block = src.at[s, pl.ds(h * cut, cut)]
            remote(block, dst.at[bd], send.at[q], recv.at[bd], (yx * 2 + h, 2 * c + s)).wait_send()


def rows_out_got(src, dst, send, recv, band):
    it, bd, c, yx = place()
    cut = src.shape[1] // 2
    pltpu.make_async_copy(src.at[0, pl.ds(0, cut)], dst.at[band], recv.at[band]).wait()


def rows_back(src, dst, send, recv, which=range(4)):
    it, bd, c, yx = place()
    cut = src.shape[1]
    home = bd // 2
    s = lax.rem(bd, 2)
    target = dst.at[s, pl.ds(pl.multiple_of(c * cut, cut), cut)]
    got = recv.at[2 * s + c]
    for r in which:
        own = (home == c) & (bd == r)

        @pl.when(own)
        def _():
            pltpu.make_async_copy(src.at[r], target, got).start()

        @pl.when(jnp.logical_not(own))
        def _():
            remote(src.at[r], target, send.at[r], got, (yx * 2 + home, r)).start()


def rows_back_sent(src, dst, send, recv):
    it, bd, c, yx = place()
    cut = src.shape[1]
    home = bd // 2
    for r in range(4):
        own = (home == c) & (bd == r)

        @pl.when(jnp.logical_not(own))
        def _():
            target = dst.at[0, pl.ds(0, cut)]
            remote(src.at[r], target, send.at[r], recv.at[0], (yx * 2 + home, r)).wait_send()


def rows_back_got(src, dst, send, recv, q):
    cut = src.shape[1]
    s, h = q // 2, q % 2
    pltpu.make_async_copy(src.at[0], dst.at[s, pl.ds(h * cut, cut)], recv.at[q]).wait()


def share_start(n, rank, peer_of, src, buf, send, recv):
    copies = []
    for o in range(1, n):
        to = peer_of(lax.rem(rank + o, n))
        copies.append(remote(src, buf.at[rank], send.at[o], recv.at[o], to))
        copies[-1].start()
    buf[rank] = src[...]
    return copies


def share_end(n, copies, buf):
    for copy in copies:
        copy.wait()
    added = buf[0]
    for i in range(1, n):
        added = added + buf[i]
    return added


def all_peers(n_items):
    it, bd, c, yx = place()
    others = []
    for o in range(1, n_items // 2):
        for k in range(2):
            others.append((lax.rem(yx + o, n_items // 2) * 2 + k, bd))
    return column_peers() + others


def patch_total(counts, shape):
    total = counts[0]
    for i in range(1, counts.shape[0]):
        total = total + counts[i]
    return jnp.full(shape, total, jnp.int32).astype(f32)


VMEM = pl.BlockSpec(memory_space=pltpu.VMEM)
SMEM = pl.BlockSpec(memory_space=pltpu.SMEM)
HBM = pl.BlockSpec(memory_space=pltpu.HBM)
DMA = pltpu.SemaphoreType.DMA


def half_lanes(ref, row, half):
    at = pl.multiple_of(lax.rem(lax.axis_index("items"), 2) * half, 128)
    return ref[row : row + 1, pl.ds(at, half)]


def half_rows(ref, which, half):
    return ref[pl.ds(pl.multiple_of(which * half, 128), half), :]


def head_lanes(array, head, lane):
    keep = (lane >= head * HEAD_DIM) & (lane < (head + 1) * HEAD_DIM)
    return jnp.where(keep, array, jnp.zeros_like(array))


def with_spare(array, spare_value, head, lane):
    spare = (1 - head) * HEAD_DIM
    return jnp.where(lane == spare, spare_value, head_lanes(array, head, lane))


def ones_beside(array, head, lane):
    return with_spare(array, jnp.ones_like(array), head, lane)


def key_bias(table, counts, shape):
    it, bd, c, yx = place()
    cut = shape[0] // 8
    row = lax.broadcasted_iota(jnp.int32, shape, 0)
    there = row >= 4 * cut
    row = jnp.where(there, row - 4 * cut, row)
    band = row // cut
    half = jnp.where(there, 1 - c, c)
    position = band * (2 * cut) + half * cut + (row - band * cut)
    return jnp.where(position < counts[table[yx * 4 + bd]], 0.0, masked_score).astype(bf16)


def normalize(value):
    centre = value - jnp.mean(value, -1, keepdims=True)
    scale = lax.rsqrt(jnp.mean(centre * centre, -1, keepdims=True) + epsilon)
    return centre * scale, scale


def front_kernel(n_items, n_band, qt, table, counts, *refs):
    singles = refs[:10]
    (b_up, tok, cot, wq_h, wk_h, wv_h, wo_h) = refs[10:17]
    (vecs, stat, rows_h, cot_rows, h1_h, q_h, k_h, v_h, log_total, attn_h, attn_sib_h) = refs[17:28]
    (res, h2, h2p) = refs[28:31]
    (rows, wq, wk, wv, wo, h1, q, k, v, attn, attn_sib, part_sib) = refs[31:43]
    (one, buf_i, part, buf_b) = refs[43:47]
    (send_t, recv_t, send_c, recv_c, send_s, recv_s, send_a, recv_a) = refs[47:55]
    (send_i, recv_i, send_b, recv_b, lsem) = refs[55:60]
    it, bd, c, yx = place()
    sibling = (it + 1 - 2 * c, bd)
    slots, band_rows, width = tok.shape
    cut = band_rows // 2
    half = width // 2
    own = 4 * cut
    local = []

    def move(src, dst):
        copy = pltpu.make_async_copy(src, dst, lsem.at[len(local)])
        copy.start()
        local.append(copy)
        return copy

    greet(all_peers(n_items))
    rows_out(tok, rows, send_t, recv_t)
    lanes = pl.ds(pl.multiple_of(c * half, 128), half)
    get_w = [move(src.at[:, lanes], dst) for src, dst in ((wq_h, wq), (wk_h, wk), (wv_h, wv))]
    get_wo = move(wo_h, wo)
    for i, ref in enumerate(singles):
        vecs[i : i + 1, :] = ref[...].astype(f32).reshape(1, width)
    for i in range(b_up.shape[0] // width):
        vecs[R_BU + i : R_BU + i + 1, :] = b_up[pl.ds(i * width, width)].astype(f32).reshape(1, width)

    at = lax.broadcasted_iota(jnp.int32, (band_rows, width), 0) + bd * band_rows
    first = jnp.zeros((1, width), f32)
    second = jnp.zeros((1, width), f32)
    for s in range(slots):
        x = jnp.where(at < counts[table[it * slots + s]], tok[s].astype(f32), 0.0)
        first = first + jnp.sum(x, 0, keepdims=True)
        second = second + jnp.sum(x * x, 0, keepdims=True)
    one[0:1, :] = first
    one[1:2, :] = second
    copies = share_start(n_items, it, lambda p: (p, bd), one, buf_i, send_i, recv_i)
    part[...] = share_end(n_items, copies, buf_i)
    copies = share_start(n_band, bd, lambda p: (it, p), part, buf_b, send_b, recv_b)
    sums = share_end(n_band, copies, buf_b) / patch_total(counts, (1, width))
    mean = sums[0:1]
    var = sums[1:2] - mean * mean
    new_var = momentum * vecs[R_VAR : R_VAR + 1, :] + momentum * var
    stat[S_MEAN : S_MEAN + 1, :] = momentum * vecs[R_MEAN : R_MEAN + 1, :] + momentum * mean
    stat[S_VAR : S_VAR + 1, :] = new_var
    stat[S_BATCH : S_BATCH + 1, :] = mean
    stat[S_INV : S_INV + 1, :] = lax.rsqrt(new_var + epsilon)
    for copy in get_w:
        copy.wait()

    def hand(o):
        band = jnp.bitwise_xor(bd, o)
        return remote(rows.at[band], rows.at[4 + band], send_s.at[o], recv_s.at[o], sibling)

    def project(o, base):
        bands = [jnp.bitwise_xor(bd, o), jnp.bitwise_xor(bd, o + 1)]
        x = jnp.concatenate([rows[base + band] for band in bands]).astype(f32)
        start = (x - stat[S_MEAN : S_MEAN + 1, :]) * stat[S_INV : S_INV + 1, :]
        z, _ = normalize(start)
        h = (z * vecs[R_G1 : R_G1 + 1, :] + vecs[R_S1 : R_S1 + 1, :]).astype(bf16)
        q_new = ((dot(h, wq[...]) + half_lanes(vecs, R_BQ, half)).astype(bf16) * score_scale).astype(bf16)
        k_new = dot(h, wk[...]).astype(bf16)
        v_new = (dot(h, wv[...]) + half_lanes(vecs, R_BV, half)).astype(bf16)
        for i, band in enumerate(bands):
            to = pl.ds(pl.multiple_of((base + band) * cut, 128), cut)
            for ref, new in ((h1, h), (q, q_new), (k, k_new), (v, v_new)):
                ref[to, :] = new[i * cut : (i + 1) * cut]

    for o in (0, 2):
        for i in (o, o + 1):
            rows_out_got(tok, rows, send_t, recv_t, jnp.bitwise_xor(bd, i))
            hand(i).start()
        if o == 2:
            rows_out(cot, cot_rows, send_c, recv_c)
        project(o, 0)
        for i in (o, o + 1):
            hand(i).wait_recv()
        project(o, 4)
    move(rows.at[pl.ds(0, 4)], rows_h)
    for src, dst in ((h1, h1_h), (q, q_h), (k, k_h), (v, v_h)):
        move(src, dst)

    lane_k = lax.broadcasted_iota(jnp.int32, (2 * own, 128), 1)
    lane_q = lax.broadcasted_iota(jnp.int32, (qt, 128), 1)
    row_out = lax.broadcasted_iota(jnp.int32, (128, qt), 0)

    def hand_attn(i):
        to = attn_sib.at[:, pl.ds(pl.multiple_of(i * 128, 128), 128)]
        return remote(part_sib.at[i], to, send_a.at[i], recv_a.at[i], sibling)

    @pl.loop(0, half // 128)
    def _(i):
        at_lanes = pl.ds(pl.multiple_of(i * 128, 128), 128)
        k_pair, v_pair = k[:, at_lanes], v[:, at_lanes]
        bias = key_bias(table, counts, k_pair.shape)
        keys = [with_spare(k_pair, bias, hd, lane_k) for hd in range(2)]
        values = [ones_beside(v_pair, hd, lane_k).T for hd in range(2)]
        units = [(slice(t * qt, (t + 1) * qt), hd) for t in range(2 * own // qt) for hd in range(2)]
        scores = [dot(keys[hd], ones_beside(q[at, at_lanes], hd, lane_q), 1, 1) for at, hd in units]
        tops = [jnp.max(s, 0, keepdims=True) for s in scores]
        weights = [jnp.exp(s - top).astype(bf16) for s, top in zip(scores, tops)]
        parts = []
        for (at, hd), top, weight in zip(units, tops, weights):
            both = dot(values[hd], weight)
            spare = (1 - hd) * HEAD_DIM
            total = both[spare : spare + 1, :]
            log_total[i, hd : hd + 1, at] = top + jnp.log(total)
            parts.append(both * (1.0 / total))
        for t in range(2 * own // qt):
            both = jnp.where(row_out < HEAD_DIM, parts[2 * t], parts[2 * t + 1]).T.astype(bf16)
            if t * qt < own:
                attn[t * qt : (t + 1) * qt, at_lanes] = both
            else:
                part_sib[i, t * qt - own : (t + 1) * qt - own, :] = both
        hand_attn(i).start()

    move(attn, attn_h)
    get_wo.wait()
    for i in range(half // 128):
        hand_attn(i).wait_recv()
    move(attn_sib, attn_sib_h)

    block = 256

    @pl.loop(0, own // block)
    def _(i):
        at = pl.ds(pl.multiple_of(i * block, block), block)
        x = rows[pl.ds(i * (block // cut), block // cut)].reshape(block, width).astype(f32)
        start = (x - stat[S_MEAN : S_MEAN + 1, :]) * stat[S_INV : S_INV + 1, :]
        r = dot(attn[at, :], half_rows(wo, c, half)) + dot(attn_sib[at, :], half_rows(wo, 1 - c, half))
        r = start + r + vecs[R_BO : R_BO + 1, :]
        res[at, :] = r
        z, _ = normalize(r)
        h = (z * vecs[R_G2 : R_G2 + 1, :] + vecs[R_S2 : R_S2 + 1, :]).astype(bf16)
        h2[at, :] = h
        e = width // 8
        for j in range(4):
            even = h[:, 2 * j * e : (2 * j + 1) * e]
            odd = h[:, (2 * j + 1) * e : (2 * j + 2) * e]
            h2p[at, j * e : (j + 1) * e] = jnp.where(c == 0, even, odd)
            h2p[at, half + j * e : half + (j + 1) * e] = jnp.where(c == 0, odd, even)

    for band in range(4):
        rows_out_got(cot, cot_rows, send_c, recv_c, band)
        hand(band).wait_send()
    rows_out_sent(tok, rows, send_t, recv_t)
    rows_out_sent(cot, cot_rows, send_c, recv_c)
    for i in range(half // 128):
        hand_attn(i).wait_send()
    for copy in local[4:]:
        copy.wait()


def front(table, counts, singles, b_up, tok, cot, wq, wk, wv, wo, qt=512):
    n_items, n_band = lax.axis_size("items"), lax.axis_size("band")
    slots, band_rows, width = tok.shape
    cut, half = band_rows // 2, width // 2
    own = 4 * cut
    pairs = half // 128
    low = lambda *shape: jax.ShapeDtypeStruct(shape, bf16)
    wide = lambda *shape: jax.ShapeDtypeStruct(shape, f32)
    buf = lambda *shape: pltpu.VMEM(shape, bf16)
    return pl.pallas_call(
        functools.partial(front_kernel, n_items, n_band, qt),
        name="front",
        in_specs=[SMEM, SMEM] + [VMEM] * 13 + [HBM] * 4,
        out_specs=[VMEM, VMEM] + [HBM] * 6 + [VMEM] + [HBM] * 2 + [VMEM] * 3,
        out_shape=[
            wide(16, width),
            wide(4, width),
            low(4, cut, width),
            low(4, cut, width),
            low(2 * own, width),
            low(2 * own, half),
            low(2 * own, half),
            low(2 * own, half),
            wide(pairs, 2, 2 * own),
            low(own, half),
            low(own, half),
            wide(own, width),
            low(own, width),
            low(own, width),
        ],
        scratch_shapes=[
            buf(8, cut, width),
            buf(width, half),
            buf(width, half),
            buf(width, half),
            buf(width, width),
            buf(2 * own, width),
            buf(2 * own, half),
            buf(2 * own, half),
            buf(2 * own, half),
            buf(own, half),
            buf(own, half),
            buf(pairs, own, 128),
            pltpu.VMEM((2, width), f32),
            pltpu.VMEM((n_items, 2, width), f32),
            pltpu.VMEM((2, width), f32),
            pltpu.VMEM((n_band, 2, width), f32),
        ]
        + [DMA((4,))] * 6
        + [DMA((pairs,))] * 2
        + [DMA((n_items,))] * 2
        + [DMA((n_band,))] * 2
        + [DMA((12,))],
        compiler_params=params(collective_id=1, has_side_effects=True),
        cost_estimate=pl.CostEstimate(
            flops=16 * own * own * width, bytes_accessed=30 * 2**20, transcendentals=0
        ),
    )(table, counts, *singles, b_up, tok, cot, wq, wk, wv, wo)


def gelu_and_slope(u):
    u2 = u * u
    t = jnp.tanh(u * (0.7978845608028654 + (0.7978845608028654 * 0.044715) * u2))
    half = 0.5 + 0.5 * t
    slope = half * (
        1.0 + u * (1.0 - t) * (0.7978845608028654 + (3 * 0.7978845608028654 * 0.044715) * u2)
    )
    return u * half, slope


def block_order(step):
    it, bd, c, yx = place()
    x = lax.rem(yx, 2)
    return 2 * lax.rem(step, 2) + jnp.where(step < 2, 1 - x, x)


def mlp_kernel(vecs, h2, h2p, cot, res, *refs):
    (wu_a, wd_a, wu_b, wd_b) = refs[:4]
    (out_low, dh, kd, rd, rest_d, ku, ru, rest_u, dbu_a, dbu_b) = refs[4:14]
    (send_wd, send_wua, send_wub, got_wd, got_wua, got_wub, keep_a, out, gd, gu) = refs[14:24]
    (send, recv, send_d, recv_d, send_u, recv_u, keep_d, sem_u, rest_sem) = refs[24:]
    step = pl.program_id(0)
    steps = pl.num_programs(0) - 1
    half = h2.shape[1] // 2
    it, bd, c, yx = place()
    x, y = lax.rem(yx, 2), yx // 2
    sibling = (it + 1 - 2 * c, bd)
    to_x, to_y = (it + 2 - 4 * x, bd), (it + 4 - 8 * y, bd)
    slot = lax.rem(step, 2)
    before = 1 - slot
    some = gd.shape[2] // 2
    part = gu.shape[2] // 2

    def copies(at, which=(0, 1, 2)):
        pairs = ((send_wd, got_wd), (send_wua, got_wua), (send_wub, got_wub))
        return [
            remote(pairs[i][0].at[at], pairs[i][1].at[at], send.at[i, at], recv.at[i, at], sibling)
            for i in which
        ]

    def down_copy(at):
        if at == 0:
            return [remote(gd.at[0], rd.at[0], send_d.at[0], recv_d.at[0], to_x)]
        if at == 1:
            first, second = pl.ds(0, some), pl.ds(some, some)
            return [
                remote(gd.at[1, :, first], rd.at[1, :, first], send_d.at[1], recv_d.at[1], to_x),
                pltpu.make_async_copy(gd.at[1, :, second], rest_d, rest_sem.at[2]),
            ]
        return [pltpu.make_async_copy(gd.at[at], kd.at[at - 2], keep_d.at[at - 2])]

    def up_rows(which):
        return pl.ds(pl.multiple_of(which * part, 128), part)

    def up_keep(at, i):
        return pltpu.make_async_copy(gu.at[at, i, up_rows(y)], ku.at[block_order(at), i], sem_u.at[at, i])

    def up_send(at, i):
        src, dst = gu.at[at, i, up_rows(1 - y)], ru.at[block_order(at), i]
        return remote(src, dst, send_u.at[at, i], recv_u.at[at, i], to_y)

    def up_rest(at, i):
        return pltpu.make_async_copy(gu.at[at, i, up_rows(1 - y)], rest_u.at[i], rest_sem.at[i])

    def up_ready(at, i):
        up_keep(at, i).start()

        @pl.when(at < steps - 1)
        def _():
            up_send(at, i).start()

        @pl.when(at == steps - 1)
        def _():
            up_rest(at, i).start()

    @pl.when(step == 0)
    def _():
        greet([sibling, to_x, to_y])
        out[...] = res[...]
        dh[...] = jnp.zeros_like(dh)

    def tile(wu, wd, dbu, which):
        lanes = pl.ds(pl.multiple_of(which * wu.shape[1], 128), wu.shape[1])
        up = dot(h2[...], wu[...]) + vecs[pl.ds(R_BU + block_order(step), 1), lanes]
        d_act = dot(cot[...], wd[...], 1, 1)
        act, slope = gelu_and_slope(up)
        act = act.astype(bf16)
        d_up32 = d_act * slope
        d_up = d_up32.astype(bf16)
        dbu[0] = jnp.sum(d_up32, 0, keepdims=True)
        d_wd = dot(cot[...], act, 0, 0).astype(bf16)
        d_wu = dot(h2p[...], d_up, 0, 0).astype(bf16)
        out[...] += dot(act, wd[...])
        dh[...] += dot(d_up, wu[...], 1, 1)
        return d_wd, d_wu

    @pl.when(step >= 2)
    def _():
        for copy in copies(slot):
            copy.wait_send()

    @pl.when(step < steps)
    def _():
        d_wd, d_wu = tile(wu_a, wd_a, dbu_a, 1 - c)
        send_wd[slot] = d_wd
        send_wua[slot] = d_wu[half:]
        keep_a[slot] = d_wu[:half]

    @pl.when(step > 0)
    def _():
        copies(before, (2,))[0].wait_recv()
        gu[step - 1, 0] = keep_a[before] + got_wub[before]
        up_ready(step - 1, 0)

    @pl.when(step < steps)
    def _():
        for copy in copies(slot, (0, 1)):
            copy.start()
        d_wd, d_wu = tile(wu_b, wd_b, dbu_b, c)
        send_wub[slot] = d_wu[half:]
        copies(slot, (2,))[0].start()
        for copy in copies(slot, (0, 1)):
            copy.wait_recv()
        gd[step] = (d_wd + got_wd[slot]).reshape(gd.shape[1:])
        gu[step, 1] = d_wu[:half] + got_wua[slot]
        up_ready(step, 1)

    for at in range(4):

        @pl.when(step == at)
        def _():
            for copy in down_copy(at):
                copy.start()

    @pl.when(step == steps)
    def _():
        out_low[...] = (out[...] + vecs[R_BD : R_BD + 1, :]).astype(bf16)
        for copy in copies(before):
            copy.wait_send()
        for at in range(4):
            for copy in down_copy(at):
                copy.wait()
            for i in range(2):
                up_keep(at, i).wait()
                (up_send(at, i) if at < 3 else up_rest(at, i)).wait()


def mlp(vecs, h2, h2p, cot, res, w_up, w_down):
    rows, width = h2.shape
    ff = w_up.shape[1]
    tile = ff // 8
    half = width // 2
    steps = 4
    now = lambda i: block_order(jnp.minimum(i, steps - 1))
    at_a = lambda i: 2 * now(i) + 1 - lax.rem(lax.axis_index("items"), 2)
    at_b = lambda i: 2 * now(i) + lax.rem(lax.axis_index("items"), 2)
    w_specs = []
    for at in (at_a, at_b):
        w_specs += [
            pl.BlockSpec((width, tile), lambda i, at=at: (0, at(i))),
            pl.BlockSpec((tile, width), lambda i, at=at: (at(i), 0)),
        ]
    bias = pl.BlockSpec((1, 1, tile), lambda i: (now(i), 0, 0))
    low = lambda *shape: jax.ShapeDtypeStruct(shape, bf16)
    return pl.pallas_call(
        mlp_kernel,
        name="mlp",
        grid=(steps + 1,),
        in_specs=[VMEM] * 5 + w_specs,
        out_specs=[VMEM, VMEM] + [HBM] * 6 + [bias, bias],
        out_shape=[
            low(rows, width),
            jax.ShapeDtypeStruct((rows, width), f32),
            low(2, 4, width // 4, tile),
            low(2, 4, width // 4, tile),
            low(4, width // 8, tile),
            low(4, 2, half // 2, tile),
            low(4, 2, half // 2, tile),
            low(2, half // 2, tile),
        ]
        + [jax.ShapeDtypeStruct((steps, 1, tile), f32)] * 2,
        scratch_shapes=(
            [pltpu.VMEM((2, width, tile), bf16)] + [pltpu.VMEM((2, half, tile), bf16)] * 2
        )
        * 2
        + [
            pltpu.VMEM((2, half, tile), bf16),
            pltpu.VMEM((rows, width), f32),
            pltpu.VMEM((steps, 4, width // 4, tile), bf16),
            pltpu.VMEM((steps, 2, half, tile), bf16),
            DMA((3, 2)),
            DMA((3, 2)),
            DMA((2,)),
            DMA((2,)),
            DMA((3, 2)),
            DMA((3, 2)),
            DMA((2,)),
            DMA((4, 2)),
            DMA((3,)),
        ],
        compiler_params=params(collective_id=4, has_side_effects=True),
        cost_estimate=pl.CostEstimate(
            flops=2 * 6 * rows * width * ff, bytes_accessed=40 * 2**20, transcendentals=0
        ),
    )(vecs, h2, h2p, cot, res, w_up, w_down, w_up, w_down)


def norm_back(z, scale, dz):
    return scale * (dz - jnp.mean(dz, -1, keepdims=True) - z * jnp.mean(dz * z, -1, keepdims=True))


def tail_kernel(n_items, n_band, qt, *refs):
    (table, counts, stat, vecs, dbu_a, dbu_b, log_total) = refs[:7]
    (res_h, dh_h, cot_h, out_rows, attn_h, attn_sib_h, wo_h, q_h, k_h, v_h, h1_h) = refs[7:18]
    (wq_h, wk_h, wv_h, tok_h, kd_h, rd_h, rest_d, ku_h, ru_h, rest_u, tokens) = refs[18:29]
    (out_home, d_tok, total, o_down, o_up, o_wo, o_wq, o_wk, o_wv) = refs[29:38]
    (res, dh, cot, low, wo, attn, attn_sib, kd, rd1, rdr, rd2, rd3, rd4) = refs[38:51]
    (ku, ru1, rur, ru2, ru3, ru4, q, k, v, da, da_send, dk_acc, dv_acc) = refs[51:64]
    (h1, wq, wk, wv, tok, gw, gw_core, gw1, gw2, gw3, gw4) = refs[64:75]
    (d_pair, gp, gp_core, gp1, gp2, gp3, gp4, home) = refs[75:83]
    (small, buf_i, part, buf_b, buf_i2, part2, buf_b2) = refs[83:90]
    (send, recv, lsem, send_r, recv_r, send_g, recv_g, send_i, recv_i, send_b, recv_b) = refs[90:101]

    it, bd, c, yx = place()
    x, y = lax.rem(yx, 2), yx // 2
    bl, bh = lax.rem(bd, 2), bd // 2
    sibling = (it + 1 - 2 * c, bd)
    to_x, to_y = (it + 2 - 4 * x, bd), (it + 4 - 8 * y, bd)
    to_z1, to_z2 = (it, bd + 1 - 2 * bl), (it, lax.rem(bd + 2, 4))
    rows, width = res.shape
    half = width // 2
    fourth = width // 4
    eighth = width // 8
    tile = kd.shape[-1]
    sent = []
    loads = []

    def load(src, dst):
        copy = pltpu.make_async_copy(src, dst, lsem.at[len(loads)])
        copy.start()
        loads.append(copy)
        return copy

    def push(src, dst, to, start=True):
        i = len(sent)
        copy = remote(src, dst, send.at[i], recv.at[i], to)
        if start:
            copy.start()
        sent.append(copy)
        return copy

    def some(which, size):
        return pl.ds(pl.multiple_of(which * size, 128), size)

    greet(all_peers(n_items))
    d1 = push(rest_d, rdr, to_x)
    u1 = push(rest_u, rur, to_y)
    load(out_rows, tok).wait()
    out_blocks = tok.reshape(4, rows // 4, width)
    rows_back(out_blocks, out_home, send_r, recv_r)

    get_res, get_dh, get_cot = load(res_h, res), load(dh_h, dh), load(cot_h, cot)
    get_wo, get_attn, get_sib = load(wo_h, wo), load(attn_h, attn), load(attn_sib_h, attn_sib)
    get_down = [load(kd_h, kd), load(rd_h, rd1)]
    get_up = [load(ku_h, ku), load(ru_h, ru1)]
    get_qkv = [load(src, dst) for src, dst in ((q_h, q), (k_h, k), (v_h, v))]
    get_h1 = load(h1_h, h1)
    lanes = some(c, half)
    get_w = [load(src.at[:, lanes], dst) for src, dst in ((wq_h, wq), (wk_h, wk), (wv_h, wv))]

    small[...] = jnp.zeros_like(small)
    for i in range(4):
        for src, h in ((dbu_a, 1 - c), (dbu_b, c)):
            small[4 + i : 5 + i, some(h, half)] = src[i]
    for copy in (get_res, get_dh, get_cot, get_wo):
        copy.wait()
    block = 256

    def second_norm(i):
        at = some(i, block)
        z, scale = normalize(res[at, :])
        d_h = dh[at, :]
        c32 = cot[at, :].astype(f32)
        full = c32 + norm_back(z, scale, d_h * vecs[R_G2 : R_G2 + 1, :])
        res[at, :] = full
        d_low = full.astype(bf16)
        low[at, :] = d_low
        for j, term in enumerate((d_h * z, d_h, d_low.astype(f32), c32)):
            small[j : j + 1, :] += jnp.sum(term, 0, keepdims=True)
        da[at, :] = dot(d_low, half_rows(wo, c, half), 1, 1).astype(bf16)
        da_send[at, :] = dot(d_low, half_rows(wo, 1 - c, half), 1, 1).astype(bf16)

    theirs, mine = some(1 - x, tile // 4), some(x, tile // 4)
    cuts = [some(0, eighth), some(1, eighth)]
    down, up = kd.reshape(2, 2, 2, fourth, tile), ku.reshape(2, 2, 2, tile // 2, tile)

    def down_second(i):
        return push(kd.at[1 - y, :, cuts[i]], rd2.at[:, cuts[i]], to_y)

    def up_second(s, i):
        b = block_order(s)
        ku[b, i] += ru1[b, i] if s < 3 else rur[i]
        return push(ku.at[b, i, theirs], ru2.at[b, i], to_x)

    def down_third(i):
        d2[i].wait_recv()
        kd[y, :, cuts[i]] += rd2[:, cuts[i]]
        return push(down.at[y, :, 1 - bl, cuts[i]], rd3.at[:, cuts[i]], to_z1)

    def up_third(i):
        for copy in u2[i]:
            copy.wait_recv()
        ku[:, i, mine] += ru2[:, i]
        return push(up.at[:, 1 - bl, i, mine], ru3.at[:, i], to_z1)

    def down_fourth(i):
        d3[i].wait_recv()
        for high in range(2):
            down[y, high, bl, cuts[i]] += rd3[high, cuts[i]]
        return push(down.at[y, 1 - bh, bl, cuts[i]], rd4.at[cuts[i]], to_z2)

    def up_fourth(i):
        u3[i].wait_recv()
        for high in range(2):
            up[high, bl, i, mine] += ru3[high, i]
        return push(up.at[1 - bh, bl, i, mine], ru4.at[i], to_z2)

    second_norm(0)
    for copy in get_down + get_up:
        copy.wait()
    for yy in range(2):
        kd[yy, :, cuts[0]] += rd1[yy, :, cuts[0]]
    d2 = [down_second(0)]
    u2 = [[up_second(s, 0) for s in range(3)], []]
    second_norm(1)

    da_copy = push(da_send, da.at[pl.ds(rows, rows)], sibling)
    early = share_start(
        n_items, it, lambda p: (p, bd), small.at[pl.ds(0, 8)], buf_i, send_i.at[0], recv_i.at[0]
    )

    get_attn.wait()
    get_sib.wait()
    for i, heads in enumerate((attn, attn_sib)):
        for xx in range(2):
            part_wo = dot(heads[:, xx * fourth : (xx + 1) * fourth], low[...], 0, 0).astype(bf16)
            for cc in range(2):
                gw[i, xx, cc] = part_wo[cc * eighth : (cc + 1) * eighth]
    core_w = [push(gw.at[i, :, 1 - c], gw_core.at[1 - i], sibling) for i in range(2)]

    d1.wait_recv()
    kd[0, :, cuts[1]] += rd1[0, :, cuts[1]]
    kd[1, :, cuts[1]] += rdr[...]
    u1.wait_recv()
    u2[0].append(up_second(3, 0))

    for copy in get_qkv:
        copy.wait()
    get_h1.wait()
    da_copy.wait_recv()
    lane_k = lax.broadcasted_iota(jnp.int32, (2 * rows, 128), 1)
    lane_q = lax.broadcasted_iota(jnp.int32, (qt, 128), 1)

    def pair(i):
        at_lanes = some(i, 128)
        k_pair, v_pair = k[:, at_lanes], v[:, at_lanes]
        bias = key_bias(table, counts, k_pair.shape)
        keys = [with_spare(k_pair, bias, hd, lane_k) for hd in range(2)]
        keys_only = [head_lanes(k_pair, hd, lane_k) for hd in range(2)]
        values = [head_lanes(v_pair, hd, lane_k) for hd in range(2)]
        for t in range(2 * rows // qt):
            at = slice(t * qt, (t + 1) * qt)
            q_tile, d_tile = q[at, at_lanes], da[at, at_lanes]
            dq_both = None
            for hd in range(2):
                q_head = head_lanes(q_tile, hd, lane_q)
                d_head = head_lanes(d_tile, hd, lane_q)
                s = dot(keys[hd], ones_beside(q_tile, hd, lane_q), 1, 1)
                p = jnp.exp(s - log_total[i, hd : hd + 1, at])
                d_p = dot(values[hd], d_tile, 1, 1)
                weighted = p * d_p
                delta = jnp.sum(weighted, 0, keepdims=True)
                ds = (weighted - p * delta).astype(bf16)
                dv_part = dot(p.astype(bf16), d_head)
                dk_part = dot(ds, q_head)
                if t == 0 and hd == 0:
                    dv_acc[...] = dv_part
                    dk_acc[...] = dk_part
                else:
                    dv_acc[...] += dv_part
                    dk_acc[...] += dk_part
                term = dot(keys_only[hd], ds, 0, 0)
                dq_both = term if dq_both is None else dq_both + term
            dq = dq_both.T * score_scale
            q[at, at_lanes] = dq.astype(bf16)
            d_pair[at, 0:128] = dq.astype(bf16)
        k[:, at_lanes] = dk_acc[...].astype(bf16)
        v[:, at_lanes] = dv_acc[...].astype(bf16)
        d_pair[:, 128:256] = dk_acc[...].astype(bf16)
        d_pair[:, 256:384] = dv_acc[...].astype(bf16)
        for j in range(4):
            term = dot(h1[:, j * fourth : (j + 1) * fourth], d_pair[...], 0, 0).astype(bf16)
            for cc in range(2):
                gp[i, j, cc] = term[cc * eighth : (cc + 1) * eighth]

    def pair_core(i):
        return push(gp.at[i, :, 1 - c], gp_core.at[i], sibling)

    def chips(i, first, second):
        return 2 * second + first if i % 2 == 0 else 2 * first + second

    def first_of(i):
        return (x, y) if i % 2 == 0 else (y, x)

    def pair_first(i, core):
        core.wait_recv()
        mine_first, _ = first_of(i)
        to = to_x if i % 2 == 0 else to_y
        got = []
        for j in range(2):
            there = chips(i, 1 - mine_first, j)
            got.append(push(gp.at[i, there, c], gp1.at[i, j, 0], to))
            got.append(push(gp_core.at[i, there], gp1.at[i, j, 1], to))
        return got

    def pair_second(i, got):
        for copy in got:
            copy.wait_recv()
        mine_first, mine_second = first_of(i)
        for j in range(2):
            here = chips(i, mine_first, j)
            gp[i, here, c] += gp1[i, j, 0]
            gp_core[i, here] += gp1[i, j, 1]
        there = chips(i, mine_first, 1 - mine_second)
        to = to_y if i % 2 == 0 else to_x
        return [
            push(gp.at[i, there, c], gp2.at[i, 0], to),
            push(gp_core.at[i, there], gp2.at[i, 1], to),
        ]

    def pair_third(i, got):
        for copy in got:
            copy.wait_recv()
        gp[i, yx, c] += gp2[i, 0]
        gp_core[i, yx] += gp2[i, 1]

    pair(0)
    core_p = [pair_core(0)]
    part[...] = share_end(n_items, early, buf_i)
    early = share_start(n_band, bd, lambda p: (it, p), part, buf_b, send_b.at[0], recv_b.at[0])
    for i in range(2):
        core_w[i].wait_recv()
    for i in range(2):
        gw[i, :, c] += gw_core[i]
    rel_y = lax.rem(y + c, 2)
    d3 = [down_third(0)]
    d2.append(down_second(1))
    u3 = [up_third(0)]
    u2[1] = [up_second(s, 1) for s in range(4)]

    pair(1)
    core_p.append(pair_core(1))
    p1 = [pair_first(0, core_p[0])]
    w1 = push(gw.at[1 - rel_y, :, c], gw1, to_y)
    total[0:8, :] = share_end(n_band, early, buf_b)

    pair(2)
    core_p.append(pair_core(2))
    d4 = [down_fourth(0)]
    u4 = [up_fourth(0)]
    d3.append(down_third(1))
    u3.append(up_third(1))
    p1.append(pair_first(1, core_p[1]))

    pair(3)
    core_p.append(pair_core(3))
    p1.append(pair_first(2, core_p[2]))
    for i, d in ((0, q), (1, v)):
        row = jnp.sum(d[...].astype(f32), 0, keepdims=True)
        small[12 + i : 13 + i, some(c, half)] = row
    w1.wait_recv()
    gw[rel_y, :, c] += gw1[...]
    w2 = push(gw.at[rel_y, 1 - x, c], gw2, to_x)

    for copy in get_w:
        copy.wait()
    dh1, dh1_sib = wo, low

    def first_norm_terms(i):
        at = some(i, block)
        term = dot(q[at, :], wq[...], 1, 1) + dot(k[at, :], wk[...], 1, 1)
        dh1[at, :] = (term + dot(v[at, :], wv[...], 1, 1)).astype(bf16)

    @pl.loop(rows // block, 2 * rows // block)
    def _(i):
        first_norm_terms(i)

    dh_copy = push(dh1.at[pl.ds(rows, rows)], dh1_sib, sibling)
    p1.append(pair_first(3, core_p[3]))
    for i in range(4):
        rows_back_got(out_blocks, out_home, send_r, recv_r, i)
    rows_back_sent(out_blocks, out_home, send_r, recv_r)
    get_tok = load(tok_h, tok)
    d4.append(down_fourth(1))
    u4.append(up_fourth(1))
    p2 = [pair_second(0, p1[0]), pair_second(1, p1[1])]

    g_rows = cot
    g_blocks = g_rows.reshape(4, rows // 4, width)

    def first_norm(i):
        first_norm_terms(i)
        at = some(i, block)
        inv = stat[S_INV : S_INV + 1, :]
        centred = tok[at, :].astype(f32) - stat[S_MEAN : S_MEAN + 1, :]
        z, scale = normalize(centred * inv)
        d_h = dh1[at, :].astype(f32) + dh1_sib[at, :].astype(f32)
        d_start = res[at, :] + norm_back(z, scale, d_h * vecs[R_G1 : R_G1 + 1, :])
        g_rows[at, :] = (d_start * inv).astype(bf16)
        for j, term in enumerate((d_start, d_start * centred, d_h * z, d_h)):
            small[8 + j : 9 + j, :] += jnp.sum(term, 0, keepdims=True)

    get_tok.wait()
    dh_copy.wait_recv()
    first_norm(0)
    rows_back(g_blocks, home, send_g, recv_g, (0, 1))
    first_norm(1)
    rows_back(g_blocks, home, send_g, recv_g, (2, 3))
    late = share_start(
        n_items, it, lambda p: (p, bd), small.at[pl.ds(8, 8)], buf_i2, send_i.at[1], recv_i.at[1]
    )
    p2.append(pair_second(2, p1[2]))
    part2[...] = share_end(n_items, late, buf_i2)
    late = share_start(n_band, bd, lambda p: (it, p), part2, buf_b2, send_b.at[1], recv_b.at[1])

    pair_third(0, p2[0])
    pair_third(1, p2[1])
    p3 = []
    for i in range(2):
        there = 2 * (1 - bl) + i
        p3.append(push(gp.at[there, yx, c], gp3.at[i, 0], to_z1, False))
        p3.append(push(gp_core.at[there, yx], gp3.at[i, 1], to_z1, False))

    @pl.when(bl == 1)
    def _():
        for copy in p3:
            copy.start()

    p2.append(pair_second(3, p1[3]))
    w2.wait_recv()
    gw[rel_y, x, c] += gw2[...]

    def z_lanes(which):
        return some(which, fourth)

    w3 = [
        push(gw.at[rel_y, x, c, :, z_lanes(2 * high + 1 - bl)], gw3.at[high], to_z1) for high in range(2)
    ]
    pair_third(2, p2[2])
    pair_third(3, p2[3])

    @pl.when(bl == 0)
    def _():
        for copy in p3:
            copy.start()

    sums = share_end(n_band, late, buf_b2)
    total[8:16, :] = sums
    for high in range(2):
        w3[high].wait_recv()
    for high in range(2):
        gw3[high] = gw[rel_y, x, c, :, z_lanes(2 * high + bl)] + gw3[high]
    w4 = push(gw3.at[1 - bh], gw4, to_z2)
    for copy in p3:
        copy.wait_recv()
    for i in range(2):
        here = 2 * bl + i
        gp3[i, 0] = gp[here, yx, c] + gp3[i, 0]
        gp3[i, 1] = gp_core[here, yx] + gp3[i, 1]
    rel_b = lax.rem(bh + c, 2)
    p4 = push(gp3.at[:, 1 - rel_b], gp4, to_z2)

    count = patch_total(counts, (1, width))
    inv = stat[S_INV : S_INV + 1, :]
    fix = -0.5 * inv * sums[0:1, :] / count
    slope = -0.5 * inv * inv * inv * sums[1:2, :] / count
    cut = rows // 4
    position = lax.broadcasted_iota(jnp.int32, (cut, width), 0) + bd * (2 * cut)
    for i in range(4):
        s, h = i // 2, i % 2
        rows_back_got(g_blocks, home, send_g, recv_g, i)
        now = pl.ds(h * cut, cut)
        valid = position + h * cut < counts[table[it * 2 + s]]
        term = fix + slope * (tokens[s, now, :].astype(f32) - stat[S_BATCH : S_BATCH + 1, :])
        d_tok[s, now, :] = (home[s, now, :].astype(f32) + jnp.where(valid, term, 0.0)).astype(bf16)

    for copy in d4 + u4:
        copy.wait_recv()
    o_down[...] = (down[y, bh, bl].astype(f32) + rd4[...].astype(f32)).T
    up_sum = up[bh, bl, :, mine].astype(f32) + ru4[...].astype(f32)
    for i, h in ((0, 1 - c), (1, c)):
        o_up[:, some(h, tile)] = up_sum[i]
    w4.wait_recv()
    o_wo[...] = gw3[bh].astype(f32) + gw4[...].astype(f32)
    p4.wait_recv()
    for i in range(2):
        all_three = gp3[i, rel_b].astype(f32) + gp4[i].astype(f32)
        for j, ref in enumerate((o_wq, o_wk, o_wv)):
            ref[:, i * 128 : (i + 1) * 128] = all_three[:, j * 128 : (j + 1) * 128]

    rows_back_sent(g_blocks, home, send_g, recv_g)
    for copy in sent:
        copy.wait_send()


def tail(table, counts, stat, vecs, dbu_a, dbu_b, log_total, res, dh, cot, out_rows, *rest, qt=512):
    attn, attn_sib, wo, q, k, v, h1, wq, wk, wv, tok, kd, rd, rest_d, ku, ru, rest_u, tokens = rest
    n_items, n_band = lax.axis_size("items"), lax.axis_size("band")
    rows, width = res.shape
    half, fourth, cut = width // 2, width // 4, rows // 4
    tile = kd.shape[3]
    buf = lambda *shape: pltpu.VMEM(shape, bf16)
    buf32 = lambda *shape: pltpu.VMEM(shape, f32)
    out = lambda *shape: jax.ShapeDtypeStruct(shape, f32)
    e, s = fourth // 2, fourth
    return pl.pallas_call(
        functools.partial(tail_kernel, n_items, n_band, qt),
        name="tail",
        in_specs=[SMEM, SMEM] + [VMEM] * 5 + [HBM] * 21 + [VMEM],
        out_specs=[HBM] + [VMEM] * 8,
        out_shape=[
            jax.ShapeDtypeStruct(tokens.shape, bf16),
            jax.ShapeDtypeStruct(tokens.shape, bf16),
            out(16, width),
            out(tile, s),
            out(e, 2 * tile),
            out(e, s),
            out(e, s),
            out(e, s),
            out(e, s),
        ],
        scratch_shapes=[
            buf32(rows, width), buf32(rows, width), buf(rows, width), buf(rows, width),
            buf(width, width), buf(rows, half), buf(rows, half),
            buf(2, 4, s, tile), buf(2, 4, s, tile), buf(4, e, tile), buf(4, s, tile), buf(2, s, tile),
            buf(s, tile),
            buf(4, 2, tile // 2, tile), buf(4, 2, tile // 2, tile), buf(2, tile // 2, tile),
            buf(4, 2, tile // 4, tile), buf(2, 2, tile // 4, tile), buf(2, tile // 4, tile),
            buf(2 * rows, half), buf(2 * rows, half), buf(2 * rows, half),
            buf(2 * rows, half), buf(rows, half), buf32(2 * rows, 128), buf32(2 * rows, 128),
            buf(2 * rows, width), buf(width, half), buf(width, half), buf(width, half), buf(rows, width),
            buf(2, 2, 2, e, width), buf(2, 2, e, width), buf(2, e, width), buf(e, width),
            buf(2, e, s), buf(e, s),
            buf(2 * rows, 384), buf(4, 4, 2, e, 384), buf(4, 4, e, 384), buf(4, 2, 2, e, 384),
            buf(4, 2, e, 384), buf(2, 2, e, 384), buf(2, e, 384),
            buf(2, 2 * cut, width),
            buf32(16, width), buf32(n_items, 8, width), buf32(8, width), buf32(n_band, 8, width),
            buf32(n_items, 8, width), buf32(8, width), buf32(n_band, 8, width),
            DMA((80,)), DMA((80,)), DMA((24,)),
            DMA((4,)), DMA((4,)), DMA((4,)), DMA((4,)),
            DMA((2, n_items)), DMA((2, n_items)), DMA((2, n_band)), DMA((2, n_band)),
        ],
        compiler_params=params(collective_id=5, has_side_effects=True),
        cost_estimate=pl.CostEstimate(
            flops=60 * rows * width * width, bytes_accessed=40 * 2**20, transcendentals=0
        ),
    )(
        table, counts, stat, vecs, dbu_a, dbu_b, log_total, res, dh, cot,
        out_rows, attn, attn_sib, wo, q, k, v, h1, wq, wk, wv, tok,
        kd, rd, rest_d, ku, ru, rest_u, tokens,
    )


def emit_kernel(stat, small, *refs):
    n = (len(refs) - 11) // 2
    sources, singles, targets = refs[:n], refs[n : n + 11], refs[n + 11 :]
    for source, target in zip(sources, targets):
        target[...] = source[...]
    singles[0][...] = stat[S_MEAN, :]
    singles[1][...] = stat[S_VAR, :]
    for ref, row in zip(singles[2:10], (10, 11, 12, 13, 2, 0, 1, 3)):
        ref[...] = small[row, :]
    singles[10][...] = small[4:8, :].reshape(4 * small.shape[1])


def emit(stat, small, arrays):
    width = stat.shape[1]
    return pl.pallas_call(
        emit_kernel,
        name="emit",
        in_specs=[VMEM] * (2 + len(arrays)),
        out_specs=[VMEM] * (11 + len(arrays)),
        out_shape=[jax.ShapeDtypeStruct((width,), f32)] * 10
        + [jax.ShapeDtypeStruct((4 * width,), f32)]
        + [jax.ShapeDtypeStruct(a.shape, a.dtype) for a in arrays],
        compiler_params=params(),
    )(stat, small, *arrays)


def column_layer(
    tokens, cotangent, running_mean, running_var, slot_table, patch_counts,
    ln1_gain, ln1_bias, w_query, b_query, w_key, w_value, b_value, w_out, b_out,
    ln2_gain, ln2_bias, w_up, b_up, w_down, b_down,
):
    slots, band_rows, width = tokens.shape
    rows = slots * band_rows
    singles = (running_mean, running_var, ln1_gain, ln1_bias, b_query, b_value, b_out)
    singles += (ln2_gain, ln2_bias, b_down)
    vecs, stat, tok, cot_rows, h1, q, k, v, log_total, attn, attn_sib, res, h2, h2p = front(
        slot_table, patch_counts, singles, b_up, tokens, cotangent, w_query, w_key, w_value, w_out
    )
    tok, cot_rows = tok.reshape(rows, width), cot_rows.reshape(rows, width)
    out_rows, d_h2, kd, rd, rest_d, ku, ru, rest_u, dbu_a, dbu_b = mlp(
        vecs, h2, h2p, cot_rows, res, w_up, w_down
    )
    output, d_tokens, small, d_w_down, d_w_up, d_w_out, d_wq, d_wk, d_wv = tail(
        slot_table, patch_counts, stat, vecs, dbu_a, dbu_b, log_total, res, d_h2, cot_rows,
        out_rows, attn, attn_sib, w_out, q, k, v, h1, w_query, w_key, w_value, tok,
        kd, rd, rest_d, ku, ru, rest_u, tokens,
    )
    singles = emit(
        stat, small, (output, d_tokens, d_wq, d_wk, d_wv, d_w_out, d_w_up, d_w_down)
    )
    (new_mean, new_var, d_g1, d_s1, d_bq, d_bv, d_bo, d_g2, d_s2, d_bd, d_bu) = singles[:11]
    output, d_tokens, d_wq, d_wk, d_wv, d_w_out, d_w_up, d_w_down = singles[11:]
    return (
        output, d_tokens, new_mean, new_var, d_g1, d_s1, d_wq, d_bq, d_wk, d_wv, d_bv,
        d_w_out, d_bo, d_g2, d_s2, d_w_up, d_bu, d_w_down, d_bd,
    )


def layer_norm(value, gain, shift):
    centre = value - jnp.mean(value, -1, keepdims=True)
    spread = jnp.mean(centre * centre, -1, keepdims=True)
    return centre * lax.rsqrt(spread + epsilon) * gain + shift


def gelu_tanh(value):
    return (
        0.5
        * value
        * (1.0 + jnp.tanh(0.7978845608028654 * (value + 0.044715 * value * value * value)))
    )


def head_layout():
    heads_per = 4
    return (heads_per, HEADS // heads_per, heads_per * HEAD_DIM)


def group_scores(q_part, k_part, key_mask):
    scores = (
        jnp.einsum("rhd,khd->hrk", q_part, k_part, preferred_element_type=jnp.float32) * score_scale
    )
    return jnp.where(key_mask[None, None, :], scores, masked_score)


def attend_forward(q_slot, keys_slot, values_slot, key_mask):
    heads_per, groups, group_width = head_layout()
    band_rows = q_slot.shape[0]
    seq_length = keys_slot.shape[0]

    def head_block(group_index):
        begin = group_index * group_width
        q_part = lax.dynamic_slice_in_dim(q_slot, begin, group_width, 1).reshape(
            band_rows, heads_per, HEAD_DIM
        )
        k_part = lax.dynamic_slice_in_dim(keys_slot, begin, group_width, 1).reshape(
            seq_length, heads_per, HEAD_DIM
        )
        v_part = lax.dynamic_slice_in_dim(values_slot, begin, group_width, 1).reshape(
            seq_length, heads_per, HEAD_DIM
        )
        scores = group_scores(q_part, k_part, key_mask)
        top_score = jnp.max(scores, -1, keepdims=True)
        log_total = top_score + jnp.log(jnp.sum(jnp.exp(scores - top_score), -1, keepdims=True))
        probs_low = jnp.exp(scores - log_total).astype(jnp.bfloat16)
        attended = jnp.einsum("hrk,khd->rhd", probs_low, v_part, preferred_element_type=jnp.float32)
        return (attended.reshape(band_rows, group_width), log_total[..., 0])

    attended, log_totals = lax.map(head_block, jnp.arange(groups, dtype=jnp.int32))
    return (attended.transpose(1, 0, 2).reshape(band_rows, groups * group_width), log_totals)


def attend_backward(q_slot, keys_slot, values_slot, key_mask, d_attn_slot, row_delta, log_totals):
    heads_per, groups, group_width = head_layout()
    query_rows = q_slot.shape[0]
    seq_length = keys_slot.shape[0]
    deltas = jnp.transpose(row_delta).reshape(groups, heads_per, query_rows)

    def head_block(inputs):
        group_index, log_total, delta_part = inputs
        begin = group_index * group_width
        q_part = lax.dynamic_slice_in_dim(q_slot, begin, group_width, 1).reshape(
            query_rows, heads_per, HEAD_DIM
        )
        k_part = lax.dynamic_slice_in_dim(keys_slot, begin, group_width, 1).reshape(
            seq_length, heads_per, HEAD_DIM
        )
        v_part = lax.dynamic_slice_in_dim(values_slot, begin, group_width, 1).reshape(
            seq_length, heads_per, HEAD_DIM
        )
        d_part = lax.dynamic_slice_in_dim(d_attn_slot, begin, group_width, 1).reshape(
            query_rows, heads_per, HEAD_DIM
        )
        scores = group_scores(q_part, k_part, key_mask)
        probs = jnp.exp(scores - log_total[..., None])
        d_probs = jnp.einsum("rhd,khd->hrk", d_part, v_part, preferred_element_type=jnp.float32)
        d_scores = (probs * (d_probs - delta_part[..., None])).astype(jnp.bfloat16)
        results = []
        d_q_part = (
            jnp.einsum("hrk,khd->rhd", d_scores, k_part, preferred_element_type=jnp.float32)
            * score_scale
        )
        results.append(d_q_part.reshape(query_rows, group_width))
        probs_low = probs.astype(jnp.bfloat16)
        d_k_part = (
            jnp.einsum("hrk,rhd->khd", d_scores, q_part, preferred_element_type=jnp.float32)
            * score_scale
        )
        d_v_part = jnp.einsum("hrk,rhd->khd", probs_low, d_part, preferred_element_type=jnp.float32)
        results.append(d_k_part.reshape(seq_length, group_width))
        results.append(d_v_part.reshape(seq_length, group_width))
        return tuple(results)

    mapped = lax.map(head_block, (jnp.arange(groups, dtype=jnp.int32), log_totals, deltas))
    full_width = groups * group_width
    return tuple((piece.transpose(1, 0, 2).reshape(piece.shape[1], full_width) for piece in mapped))


def local(
    tokens,
    cotangent,
    running_mean,
    running_var,
    slot_table,
    patch_counts,
    ln1_gain,
    ln1_bias,
    w_query,
    b_query,
    w_key,
    w_value,
    b_value,
    w_out,
    b_out,
    ln2_gain,
    ln2_bias,
    w_up,
    b_up,
    w_down,
    b_down,
):
    slot_count, band_rows, model_width = tokens.shape
    seq_length = band_rows * lax.axis_size("band")
    item_rank = lax.axis_index("items")
    band_rank = lax.axis_index("band")
    every_slot = jnp.arange(slot_table.shape[0], dtype=jnp.int32)
    my_slots = item_rank * slot_count + jnp.arange(slot_count, dtype=jnp.int32)
    item_ids = jnp.sum(
        jnp.where(every_slot[None, :] == my_slots[:, None], slot_table[None, :], 0), 1
    )
    lengths = jnp.sum(
        jnp.where(every_slot[None, :] == item_ids[:, None], patch_counts[None, :], 0), 1
    )
    key_mask = jnp.arange(seq_length, dtype=jnp.int32)[None, :] < lengths[:, None]
    row_mask = (band_rank * band_rows + jnp.arange(band_rows, dtype=jnp.int32))[None, :] < lengths[
        :, None
    ]
    row_keep = row_mask.astype(jnp.float32).reshape(-1, 1)
    raw_flat = tokens.astype(jnp.float32).reshape(-1, model_width)
    part_one = jnp.sum(row_keep * raw_flat, 0)
    part_two = jnp.sum(row_keep * raw_flat * raw_flat, 0)
    total_one, total_two = lax.psum((part_one, part_two), ("items", "band"))
    patch_total = jnp.sum(patch_counts).astype(jnp.float32)
    batch_mean = total_one / patch_total
    batch_var = total_two / patch_total - batch_mean * batch_mean
    new_mean = momentum * running_mean + momentum * batch_mean
    new_var = momentum * running_var + momentum * batch_var
    inverse = lax.rsqrt(new_var + epsilon)
    normed_in = (raw_flat - new_mean) * inverse
    gain_one = ln1_gain.astype(jnp.float32)
    shift_one = ln1_bias.astype(jnp.float32)
    gain_two = ln2_gain.astype(jnp.float32)
    shift_two = ln2_bias.astype(jnp.float32)
    h_one_full, norm_one_back = jax.vjp(layer_norm, normed_in, gain_one, shift_one)
    h_one = h_one_full.astype(jnp.bfloat16)
    queries = (
        jnp.dot(h_one, w_query, preferred_element_type=jnp.float32) + b_query.astype(jnp.float32)
    ).astype(jnp.bfloat16)
    key_local = (
        jnp.dot(h_one, w_key, preferred_element_type=jnp.float32)
        .astype(jnp.bfloat16)
        .reshape(slot_count, band_rows, model_width)
    )
    value_local = (
        (jnp.dot(h_one, w_value, preferred_element_type=jnp.float32) + b_value.astype(jnp.float32))
        .astype(jnp.bfloat16)
        .reshape(slot_count, band_rows, model_width)
    )
    keys_all, values_all = (
        lax.all_gather(key_local, "band", axis=1, tiled=True),
        lax.all_gather(value_local, "band", axis=1, tiled=True),
    )
    q_slots = queries.reshape(slot_count, band_rows, model_width)
    attended_list = []
    totals_list = []
    for slot_index in range(slot_count):
        attended, log_totals = attend_forward(
            q_slots[slot_index], keys_all[slot_index], values_all[slot_index], key_mask[slot_index]
        )
        attended_list.append(attended)
        totals_list.append(log_totals)
    attn_full = jnp.concatenate(attended_list, 0)
    attn_low = attn_full.astype(jnp.bfloat16)
    residual = (
        normed_in
        + jnp.dot(attn_low, w_out, preferred_element_type=jnp.float32)
        + b_out.astype(jnp.float32)
    )
    h_two_full, norm_two_back = jax.vjp(layer_norm, residual, gain_two, shift_two)
    h_two = h_two_full.astype(jnp.bfloat16)
    up_proj = jnp.dot(h_two, w_up, preferred_element_type=jnp.float32) + b_up.astype(jnp.float32)
    activated_full, gelu_back = jax.vjp(gelu_tanh, up_proj)
    activated = activated_full.astype(jnp.bfloat16)
    result = (
        residual
        + jnp.dot(activated, w_down, preferred_element_type=jnp.float32)
        + b_down.astype(jnp.float32)
    )
    output = result.astype(jnp.bfloat16).reshape(slot_count, band_rows, model_width)
    cot_low = cotangent.reshape(-1, model_width)
    cot_full = cot_low.astype(jnp.float32)
    d_w_down = jnp.einsum("tf,td->fd", activated, cot_low, preferred_element_type=jnp.float32)
    d_b_down = jnp.sum(cot_full, 0)
    d_activated = jnp.einsum("td,fd->tf", cot_low, w_down, preferred_element_type=jnp.float32)
    (d_up_full,) = gelu_back(d_activated)
    d_up = d_up_full.astype(jnp.bfloat16)
    d_w_up = jnp.einsum("td,tf->df", h_two, d_up, preferred_element_type=jnp.float32)
    d_b_up = jnp.sum(d_up, 0, dtype=jnp.float32)
    d_h_two = jnp.einsum("tf,df->td", d_up, w_up, preferred_element_type=jnp.float32)
    d_res_norm, d_gain_two, d_shift_two = norm_two_back(d_h_two)
    d_residual = cot_full + d_res_norm
    d_branch = d_residual.astype(jnp.bfloat16)
    d_w_out = jnp.einsum("td,te->de", attn_low, d_branch, preferred_element_type=jnp.float32)
    d_b_out = jnp.sum(d_branch, 0, dtype=jnp.float32)
    d_attn = jnp.einsum("te,de->td", d_branch, w_out, preferred_element_type=jnp.float32).astype(
        jnp.bfloat16
    )
    row_delta = jnp.sum(
        (d_attn.astype(jnp.float32) * attn_full).reshape(slot_count, band_rows, HEADS, HEAD_DIM), -1
    )
    d_attn_slots = d_attn.reshape(slot_count, band_rows, model_width)
    back_keys, back_values = (keys_all, values_all)
    d_q_list = []
    d_k_list = []
    d_v_list = []
    for slot_index in range(slot_count):
        d_q_slot, d_k_slot, d_v_slot = attend_backward(
            q_slots[slot_index],
            back_keys[slot_index],
            back_values[slot_index],
            key_mask[slot_index],
            d_attn_slots[slot_index],
            row_delta[slot_index],
            totals_list[slot_index],
        )
        d_q_list.append(d_q_slot)
        d_k_list.append(d_k_slot)
        d_v_list.append(d_v_slot)
    d_keys_mine, d_values_mine = (
        lax.psum_scatter(
            jnp.stack(d_k_list).astype(jnp.bfloat16), "band", scatter_dimension=1, tiled=True
        ).astype(jnp.float32),
        lax.psum_scatter(
            jnp.stack(d_v_list).astype(jnp.bfloat16), "band", scatter_dimension=1, tiled=True
        ).astype(jnp.float32),
    )
    d_queries = jnp.concatenate(d_q_list, 0).astype(jnp.bfloat16)
    d_keys = d_keys_mine.reshape(-1, model_width).astype(jnp.bfloat16)
    d_values = d_values_mine.reshape(-1, model_width).astype(jnp.bfloat16)
    d_w_query = jnp.einsum("td,te->de", h_one, d_queries, preferred_element_type=jnp.float32)
    d_b_query = jnp.sum(d_queries, 0, dtype=jnp.float32)
    d_w_key = jnp.einsum("td,te->de", h_one, d_keys, preferred_element_type=jnp.float32)
    d_w_value = jnp.einsum("td,te->de", h_one, d_values, preferred_element_type=jnp.float32)
    d_b_value = jnp.sum(d_values, 0, dtype=jnp.float32)
    d_h_one = jnp.einsum("te,de->td", d_queries, w_query, preferred_element_type=jnp.float32)
    d_h_one = d_h_one + jnp.einsum("te,de->td", d_keys, w_key, preferred_element_type=jnp.float32)
    d_h_one = d_h_one + jnp.einsum(
        "te,de->td", d_values, w_value, preferred_element_type=jnp.float32
    )
    d_start_norm, d_gain_one, d_shift_one = norm_one_back(d_h_one)
    d_start = d_residual + d_start_norm
    centred = raw_flat - new_mean
    small_sums = lax.psum(
        (
            jnp.sum(d_start, 0),
            jnp.sum(d_start * centred, 0),
            d_gain_one,
            d_shift_one,
            d_b_query,
            d_b_value,
            d_b_out,
            d_gain_two,
            d_shift_two,
            d_b_up,
            d_b_down,
        ),
        ("items", "band"),
    )
    sum_g = small_sums[0]
    sum_gx = small_sums[1]
    cube = inverse * inverse * inverse
    d_raw = d_start * inverse + row_keep * (
        -0.5 * inverse * sum_g / patch_total
        - 0.5 * cube * sum_gx * (raw_flat - batch_mean) / patch_total
    )
    d_tokens = d_raw.astype(jnp.bfloat16).reshape(slot_count, band_rows, model_width)
    weight_grads = (
        lax.psum_scatter(
            d_w_query.astype(jnp.bfloat16), "items", scatter_dimension=0, tiled=True
        ).astype(jnp.float32),
        lax.psum_scatter(
            d_w_key.astype(jnp.bfloat16), "items", scatter_dimension=0, tiled=True
        ).astype(jnp.float32),
        lax.psum_scatter(
            d_w_value.astype(jnp.bfloat16), "items", scatter_dimension=0, tiled=True
        ).astype(jnp.float32),
        lax.psum_scatter(
            d_w_out.astype(jnp.bfloat16), "items", scatter_dimension=0, tiled=True
        ).astype(jnp.float32),
        lax.psum_scatter(
            d_w_up.astype(jnp.bfloat16), "items", scatter_dimension=0, tiled=True
        ).astype(jnp.float32),
        lax.psum_scatter(
            d_w_down.astype(jnp.bfloat16), "items", scatter_dimension=0, tiled=True
        ).astype(jnp.float32),
    )
    weight_grads = (
        lax.psum_scatter(
            weight_grads[0].astype(jnp.bfloat16), "band", scatter_dimension=1, tiled=True
        ).astype(jnp.float32),
        lax.psum_scatter(
            weight_grads[1].astype(jnp.bfloat16), "band", scatter_dimension=1, tiled=True
        ).astype(jnp.float32),
        lax.psum_scatter(
            weight_grads[2].astype(jnp.bfloat16), "band", scatter_dimension=1, tiled=True
        ).astype(jnp.float32),
        lax.psum_scatter(
            weight_grads[3].astype(jnp.bfloat16), "band", scatter_dimension=1, tiled=True
        ).astype(jnp.float32),
        lax.psum_scatter(
            weight_grads[4].astype(jnp.bfloat16), "band", scatter_dimension=1, tiled=True
        ).astype(jnp.float32),
        lax.psum_scatter(
            weight_grads[5].astype(jnp.bfloat16), "band", scatter_dimension=1, tiled=True
        ).astype(jnp.float32),
    )
    return (
        output,
        d_tokens,
        new_mean,
        new_var,
        small_sums[2],
        small_sums[3],
        weight_grads[0],
        small_sums[4],
        weight_grads[1],
        weight_grads[2],
        small_sums[5],
        weight_grads[3],
        small_sums[6],
        small_sums[7],
        small_sums[8],
        weight_grads[4],
        small_sums[9],
        weight_grads[5],
        small_sums[10],
    )


def solution(mesh):
    columns = mesh.shape["items"] == 8 and mesh.shape["band"] == 4
    return jax.shard_map(
        column_layer if columns else local,
        mesh=mesh,
        in_specs=(
            P("items", "band", None),
            P("items", "band", None),
            P(),
            P(),
            P(),
            P(),
            P(),
            P(),
            P(),
            P(),
            P(),
            P(),
            P(),
            P(),
            P(),
            P(),
            P(),
            P(),
            P(),
            P(),
            P(),
        ),
        out_specs=(
            P("items", "band", None),
            P("items", "band", None),
            P(),
            P(),
            P(),
            P(),
            P("items", "band"),
            P(),
            P("items", "band"),
            P("items", "band"),
            P(),
            P("items", "band"),
            P(),
            P(),
            P(),
            P("items", "band"),
            P(),
            P("items", "band"),
            P(),
        ),
        check_vma=False,
    )
```

```python
import functools
import jax
import jax.numpy as jnp
from jax import lax
from jax.experimental import pallas as pl
from jax.experimental.pallas import tpu as pltpu
from jax.sharding import PartitionSpec as P

HEADS = 16
HEAD_DIM = 64
epsilon = 1e-05
score_scale = 0.125
masked_score = -1e30
momentum = 0.5
f32 = jnp.float32
bf16 = jnp.bfloat16
VMEM_LIMIT = 60 * 2**20
R_MEAN, R_VAR, R_G1, R_S1, R_BQ, R_BV, R_BO, R_G2, R_S2, R_BD, R_BU = range(11)
S_MEAN, S_VAR, S_BATCH, S_INV = range(4)


def dot(a, b, ca=1, cb=0):
    return lax.dot_general(a, b, (((ca,), (cb,)), ((), ())), preferred_element_type=f32)


def params(**kw):
    return pltpu.CompilerParams(vmem_limit_bytes=VMEM_LIMIT, **kw)


def place():
    it, bd = lax.axis_index("items"), lax.axis_index("band")
    return it, bd, lax.rem(it, 2), it // 2


def remote(src, dst, send, recv, to):
    return pltpu.make_async_remote_copy(
        src_ref=src,
        dst_ref=dst,
        send_sem=send,
        recv_sem=recv,
        device_id=to,
        device_id_type=pl.DeviceIdType.MESH,
    )


def greet(peers):
    barrier = pltpu.get_barrier_semaphore()
    for peer in peers:
        pl.semaphore_signal(barrier, inc=1, device_id=peer, device_id_type=pl.DeviceIdType.MESH)
    pl.semaphore_wait(barrier, len(peers))


def column_peers():
    it, bd, c, yx = place()
    peers = [(it, lax.rem(bd + o, 4)) for o in range(1, 4)]
    return peers + [(it + 1 - 2 * c, lax.rem(bd + o, 4)) for o in range(4)]


def rows_out(src, dst, send, recv):
    it, bd, c, yx = place()
    cut = src.shape[1] // 2
    for q in range(4):
        s, h = q // 2, q % 2
        block = src.at[s, pl.ds(h * cut, cut)]
        target = dst.at[bd]
        own = (c == h) & (bd == 2 * c + s)

        @pl.when(own)
        def _():
            pltpu.make_async_copy(block, target, recv.at[bd]).start()

        @pl.when(jnp.logical_not(own))
        def _():
            remote(block, target, send.at[q], recv.at[bd], (yx * 2 + h, 2 * c + s)).start()


def rows_out_sent(src, dst, send, recv):
    it, bd, c, yx = place()
    cut = src.shape[1] // 2
    for q in range(4):
        s, h = q // 2, q % 2
        own = (c == h) & (bd == 2 * c + s)

        @pl.when(jnp.logical_not(own))
        def _():
            block = src.at[s, pl.ds(h * cut, cut)]
            remote(block, dst.at[bd], send.at[q], recv.at[bd], (yx * 2 + h, 2 * c + s)).wait_send()


def rows_out_got(src, dst, send, recv, band):
    it, bd, c, yx = place()
    cut = src.shape[1] // 2
    pltpu.make_async_copy(src.at[0, pl.ds(0, cut)], dst.at[band], recv.at[band]).wait()


def rows_back(src, dst, send, recv, which=range(4)):
    it, bd, c, yx = place()
    cut = src.shape[1]
    home = bd // 2
    s = lax.rem(bd, 2)
    target = dst.at[s, pl.ds(pl.multiple_of(c * cut, cut), cut)]
    got = recv.at[2 * s + c]
    for r in which:
        own = (home == c) & (bd == r)

        @pl.when(own)
        def _():
            pltpu.make_async_copy(src.at[r], target, got).start()

        @pl.when(jnp.logical_not(own))
        def _():
            remote(src.at[r], target, send.at[r], got, (yx * 2 + home, r)).start()


def rows_back_sent(src, dst, send, recv):
    it, bd, c, yx = place()
    cut = src.shape[1]
    home = bd // 2
    for r in range(4):
        own = (home == c) & (bd == r)

        @pl.when(jnp.logical_not(own))
        def _():
            target = dst.at[0, pl.ds(0, cut)]
            remote(src.at[r], target, send.at[r], recv.at[0], (yx * 2 + home, r)).wait_send()


def rows_back_got(src, dst, send, recv, q):
    cut = src.shape[1]
    s, h = q // 2, q % 2
    pltpu.make_async_copy(src.at[0], dst.at[s, pl.ds(h * cut, cut)], recv.at[q]).wait()


def share_start(n, rank, peer_of, src, buf, send, recv):
    copies = []
    for o in range(1, n):
        to = peer_of(lax.rem(rank + o, n))
        copies.append(remote(src, buf.at[rank], send.at[o], recv.at[o], to))
        copies[-1].start()
    buf[rank] = src[...]
    return copies


def share_end(n, copies, buf):
    for copy in copies:
        copy.wait()
    added = buf[0]
    for i in range(1, n):
        added = added + buf[i]
    return added


def all_peers(n_items):
    it, bd, c, yx = place()
    others = []
    for o in range(1, n_items // 2):
        for k in range(2):
            others.append((lax.rem(yx + o, n_items // 2) * 2 + k, bd))
    return column_peers() + others


def patch_total(counts, shape):
    total = counts[0]
    for i in range(1, counts.shape[0]):
        total = total + counts[i]
    return jnp.full(shape, total, jnp.int32).astype(f32)


VMEM = pl.BlockSpec(memory_space=pltpu.VMEM)
SMEM = pl.BlockSpec(memory_space=pltpu.SMEM)
HBM = pl.BlockSpec(memory_space=pltpu.HBM)
DMA = pltpu.SemaphoreType.DMA


def half_lanes(ref, row, half):
    at = pl.multiple_of(lax.rem(lax.axis_index("items"), 2) * half, 128)
    return ref[row : row + 1, pl.ds(at, half)]


def half_rows(ref, which, half):
    return ref[pl.ds(pl.multiple_of(which * half, 128), half), :]


def head_lanes(array, head, lane):
    keep = (lane >= head * HEAD_DIM) & (lane < (head + 1) * HEAD_DIM)
    return jnp.where(keep, array, jnp.zeros_like(array))


def with_spare(array, spare_value, head, lane):
    spare = (1 - head) * HEAD_DIM
    return jnp.where(lane == spare, spare_value, head_lanes(array, head, lane))


def ones_beside(array, head, lane):
    return with_spare(array, jnp.ones_like(array), head, lane)


def key_bias(table, counts, shape):
    it, bd, c, yx = place()
    cut = shape[0] // 8
    row = lax.broadcasted_iota(jnp.int32, shape, 0)
    there = row >= 4 * cut
    row = jnp.where(there, row - 4 * cut, row)
    band = row // cut
    half = jnp.where(there, 1 - c, c)
    position = band * (2 * cut) + half * cut + (row - band * cut)
    return jnp.where(position < counts[table[yx * 4 + bd]], 0.0, masked_score).astype(bf16)


def normalize(value):
    centre = value - jnp.mean(value, -1, keepdims=True)
    scale = lax.rsqrt(jnp.mean(centre * centre, -1, keepdims=True) + epsilon)
    return centre * scale, scale


def front_kernel(n_items, n_band, qt, table, counts, *refs):
    singles = refs[:10]
    (b_up, tok, cot, wq_h, wk_h, wv_h, wo_h) = refs[10:17]
    (vecs, stat, rows_h, cot_rows, h1_h, q_h, k_h, v_h, log_total, attn_h, attn_sib_h) = refs[17:28]
    (res, h2, h2p) = refs[28:31]
    (rows, wq, wk, wv, wo, h1, q, k, v, attn, attn_sib, part_sib) = refs[31:43]
    (one, buf_i, part, buf_b) = refs[43:47]
    (send_t, recv_t, send_c, recv_c, send_s, recv_s, send_a, recv_a) = refs[47:55]
    (send_i, recv_i, send_b, recv_b, lsem) = refs[55:60]
    it, bd, c, yx = place()
    sibling = (it + 1 - 2 * c, bd)
    slots, band_rows, width = tok.shape
    cut = band_rows // 2
    half = width // 2
    own = 4 * cut
    local = []

    def move(src, dst):
        copy = pltpu.make_async_copy(src, dst, lsem.at[len(local)])
        copy.start()
        local.append(copy)
        return copy

    greet(all_peers(n_items))
    rows_out(tok, rows, send_t, recv_t)
    lanes = pl.ds(pl.multiple_of(c * half, 128), half)
    get_w = [move(src.at[:, lanes], dst) for src, dst in ((wq_h, wq), (wk_h, wk), (wv_h, wv))]
    get_wo = move(wo_h, wo)
    for i, ref in enumerate(singles):
        vecs[i : i + 1, :] = ref[...].astype(f32).reshape(1, width)
    for i in range(b_up.shape[0] // width):
        vecs[R_BU + i : R_BU + i + 1, :] = b_up[pl.ds(i * width, width)].astype(f32).reshape(1, width)

    at = lax.broadcasted_iota(jnp.int32, (band_rows, width), 0) + bd * band_rows
    first = jnp.zeros((1, width), f32)
    second = jnp.zeros((1, width), f32)
    for s in range(slots):
        x = jnp.where(at < counts[table[it * slots + s]], tok[s].astype(f32), 0.0)
        first = first + jnp.sum(x, 0, keepdims=True)
        second = second + jnp.sum(x * x, 0, keepdims=True)
    one[0:1, :] = first
    one[1:2, :] = second
    copies = share_start(n_items, it, lambda p: (p, bd), one, buf_i, send_i, recv_i)
    part[...] = share_end(n_items, copies, buf_i)
    copies = share_start(n_band, bd, lambda p: (it, p), part, buf_b, send_b, recv_b)
    sums = share_end(n_band, copies, buf_b) / patch_total(counts, (1, width))
    mean = sums[0:1]
    var = sums[1:2] - mean * mean
    new_var = momentum * vecs[R_VAR : R_VAR + 1, :] + momentum * var
    stat[S_MEAN : S_MEAN + 1, :] = momentum * vecs[R_MEAN : R_MEAN + 1, :] + momentum * mean
    stat[S_VAR : S_VAR + 1, :] = new_var
    stat[S_BATCH : S_BATCH + 1, :] = mean
    stat[S_INV : S_INV + 1, :] = lax.rsqrt(new_var + epsilon)
    for copy in get_w:
        copy.wait()

    def hand(o):
        band = jnp.bitwise_xor(bd, o)
        return remote(rows.at[band], rows.at[4 + band], send_s.at[o], recv_s.at[o], sibling)

    def project(o, base):
        bands = [jnp.bitwise_xor(bd, o), jnp.bitwise_xor(bd, o + 1)]
        x = jnp.concatenate([rows[base + band] for band in bands]).astype(f32)
        start = (x - stat[S_MEAN : S_MEAN + 1, :]) * stat[S_INV : S_INV + 1, :]
        z, _ = normalize(start)
        h = (z * vecs[R_G1 : R_G1 + 1, :] + vecs[R_S1 : R_S1 + 1, :]).astype(bf16)
        q_new = ((dot(h, wq[...]) + half_lanes(vecs, R_BQ, half)).astype(bf16) * score_scale).astype(bf16)
        k_new = dot(h, wk[...]).astype(bf16)
        v_new = (dot(h, wv[...]) + half_lanes(vecs, R_BV, half)).astype(bf16)
        for i, band in enumerate(bands):
            to = pl.ds(pl.multiple_of((base + band) * cut, 128), cut)
            for ref, new in ((h1, h), (q, q_new), (k, k_new), (v, v_new)):
                ref[to, :] = new[i * cut : (i + 1) * cut]

    for o in (0, 2):
        for i in (o, o + 1):
            rows_out_got(tok, rows, send_t, recv_t, jnp.bitwise_xor(bd, i))
            hand(i).start()
        if o == 2:
            rows_out(cot, cot_rows, send_c, recv_c)
        project(o, 0)
        for i in (o, o + 1):
            hand(i).wait_recv()
        project(o, 4)
    move(rows.at[pl.ds(0, 4)], rows_h)
    for src, dst in ((h1, h1_h), (q, q_h), (k, k_h), (v, v_h)):
        move(src, dst)

    lane_k = lax.broadcasted_iota(jnp.int32, (2 * own, 128), 1)
    lane_q = lax.broadcasted_iota(jnp.int32, (qt, 128), 1)
    row_out = lax.broadcasted_iota(jnp.int32, (128, qt), 0)

    def hand_attn(i):
        to = attn_sib.at[:, pl.ds(pl.multiple_of(i * 128, 128), 128)]
        return remote(part_sib.at[i], to, send_a.at[i], recv_a.at[i], sibling)

    @pl.loop(0, half // 128)
    def _(i):
        at_lanes = pl.ds(pl.multiple_of(i * 128, 128), 128)
        k_pair, v_pair = k[:, at_lanes], v[:, at_lanes]
        bias = key_bias(table, counts, k_pair.shape)
        keys = [with_spare(k_pair, bias, hd, lane_k) for hd in range(2)]
        values = [ones_beside(v_pair, hd, lane_k).T for hd in range(2)]
        units = [(slice(t * qt, (t + 1) * qt), hd) for t in range(2 * own // qt) for hd in range(2)]
        scores = [dot(keys[hd], ones_beside(q[at, at_lanes], hd, lane_q), 1, 1) for at, hd in units]
        tops = [jnp.max(s, 0, keepdims=True) for s in scores]
        weights = [jnp.exp(s - top).astype(bf16) for s, top in zip(scores, tops)]
        parts = []
        for (at, hd), top, weight in zip(units, tops, weights):
            both = dot(values[hd], weight)
            spare = (1 - hd) * HEAD_DIM
            total = both[spare : spare + 1, :]
            log_total[i, hd : hd + 1, at] = top + jnp.log(total)
            parts.append(both * (1.0 / total))
        for t in range(2 * own // qt):
            both = jnp.where(row_out < HEAD_DIM, parts[2 * t], parts[2 * t + 1]).T.astype(bf16)
            if t * qt < own:
                attn[t * qt : (t + 1) * qt, at_lanes] = both
            else:
                part_sib[i, t * qt - own : (t + 1) * qt - own, :] = both
        hand_attn(i).start()

    move(attn, attn_h)
    get_wo.wait()
    for i in range(half // 128):
        hand_attn(i).wait_recv()
    move(attn_sib, attn_sib_h)

    block = 256

    @pl.loop(0, own // block)
    def _(i):
        at = pl.ds(pl.multiple_of(i * block, block), block)
        x = rows[pl.ds(i * (block // cut), block // cut)].reshape(block, width).astype(f32)
        start = (x - stat[S_MEAN : S_MEAN + 1, :]) * stat[S_INV : S_INV + 1, :]
        r = dot(attn[at, :], half_rows(wo, c, half)) + dot(attn_sib[at, :], half_rows(wo, 1 - c, half))
        r = start + r + vecs[R_BO : R_BO + 1, :]
        res[at, :] = r
        z, _ = normalize(r)
        h = (z * vecs[R_G2 : R_G2 + 1, :] + vecs[R_S2 : R_S2 + 1, :]).astype(bf16)
        h2[at, :] = h
        e = width // 8
        for j in range(4):
            even = h[:, 2 * j * e : (2 * j + 1) * e]
            odd = h[:, (2 * j + 1) * e : (2 * j + 2) * e]
            h2p[at, j * e : (j + 1) * e] = jnp.where(c == 0, even, odd)
            h2p[at, half + j * e : half + (j + 1) * e] = jnp.where(c == 0, odd, even)

    for band in range(4):
        rows_out_got(cot, cot_rows, send_c, recv_c, band)
        hand(band).wait_send()
    rows_out_sent(tok, rows, send_t, recv_t)
    rows_out_sent(cot, cot_rows, send_c, recv_c)
    for i in range(half // 128):
        hand_attn(i).wait_send()
    for copy in local[4:]:
        copy.wait()


def front(table, counts, singles, b_up, tok, cot, wq, wk, wv, wo, qt=512):
    n_items, n_band = lax.axis_size("items"), lax.axis_size("band")
    slots, band_rows, width = tok.shape
    cut, half = band_rows // 2, width // 2
    own = 4 * cut
    pairs = half // 128
    low = lambda *shape: jax.ShapeDtypeStruct(shape, bf16)
    wide = lambda *shape: jax.ShapeDtypeStruct(shape, f32)
    buf = lambda *shape: pltpu.VMEM(shape, bf16)
    return pl.pallas_call(
        functools.partial(front_kernel, n_items, n_band, qt),
        name="front",
        in_specs=[SMEM, SMEM] + [VMEM] * 13 + [HBM] * 4,
        out_specs=[VMEM, VMEM] + [HBM] * 6 + [VMEM] + [HBM] * 2 + [VMEM] * 3,
        out_shape=[
            wide(16, width),
            wide(4, width),
            low(4, cut, width),
            low(4, cut, width),
            low(2 * own, width),
            low(2 * own, half),
            low(2 * own, half),
            low(2 * own, half),
            wide(pairs, 2, 2 * own),
            low(own, half),
            low(own, half),
            wide(own, width),
            low(own, width),
            low(own, width),
        ],
        scratch_shapes=[
            buf(8, cut, width),
            buf(width, half),
            buf(width, half),
            buf(width, half),
            buf(width, width),
            buf(2 * own, width),
            buf(2 * own, half),
            buf(2 * own, half),
            buf(2 * own, half),
            buf(own, half),
            buf(own, half),
            buf(pairs, own, 128),
            pltpu.VMEM((2, width), f32),
            pltpu.VMEM((n_items, 2, width), f32),
            pltpu.VMEM((2, width), f32),
            pltpu.VMEM((n_band, 2, width), f32),
        ]
        + [DMA((4,))] * 6
        + [DMA((pairs,))] * 2
        + [DMA((n_items,))] * 2
        + [DMA((n_band,))] * 2
        + [DMA((12,))],
        compiler_params=params(collective_id=1, has_side_effects=True),
        cost_estimate=pl.CostEstimate(
            flops=16 * own * own * width, bytes_accessed=30 * 2**20, transcendentals=0
        ),
    )(table, counts, *singles, b_up, tok, cot, wq, wk, wv, wo)


def gelu_and_slope(u):
    u2 = u * u
    t = jnp.tanh(u * (0.7978845608028654 + (0.7978845608028654 * 0.044715) * u2))
    half = 0.5 + 0.5 * t
    slope = half * (
        1.0 + u * (1.0 - t) * (0.7978845608028654 + (3 * 0.7978845608028654 * 0.044715) * u2)
    )
    return u * half, slope


def block_order(step):
    it, bd, c, yx = place()
    x = lax.rem(yx, 2)
    return 2 * lax.rem(step, 2) + jnp.where(step < 2, 1 - x, x)


def mlp_kernel(vecs, h2, h2p, cot, res, *refs):
    (wu_a, wd_a, wu_b, wd_b) = refs[:4]
    (out_low, dh, kd, rd, rest_d, ku, ru, rest_u, dbu_a, dbu_b) = refs[4:14]
    (send_wd, send_wua, send_wub, got_wd, got_wua, got_wub, keep_a, out, gd, gu) = refs[14:24]
    (send, recv, send_d, recv_d, send_u, recv_u, keep_d, sem_u, rest_sem) = refs[24:]
    step = pl.program_id(0)
    steps = pl.num_programs(0) - 1
    half = h2.shape[1] // 2
    it, bd, c, yx = place()
    x, y = lax.rem(yx, 2), yx // 2
    sibling = (it + 1 - 2 * c, bd)
    to_x, to_y = (it + 2 - 4 * x, bd), (it + 4 - 8 * y, bd)
    slot = lax.rem(step, 2)
    before = 1 - slot
    some = gd.shape[2] // 2
    part = gu.shape[2] // 2

    def copies(at, which=(0, 1, 2)):
        pairs = ((send_wd, got_wd), (send_wua, got_wua), (send_wub, got_wub))
        return [
            remote(pairs[i][0].at[at], pairs[i][1].at[at], send.at[i, at], recv.at[i, at], sibling)
            for i in which
        ]

    def down_copy(at):
        if at == 0:
            return [remote(gd.at[0], rd.at[0], send_d.at[0], recv_d.at[0], to_x)]
        if at == 1:
            first, second = pl.ds(0, some), pl.ds(some, some)
            return [
                remote(gd.at[1, :, first], rd.at[1, :, first], send_d.at[1], recv_d.at[1], to_x),
                pltpu.make_async_copy(gd.at[1, :, second], rest_d, rest_sem.at[2]),
            ]
        return [pltpu.make_async_copy(gd.at[at], kd.at[at - 2], keep_d.at[at - 2])]

    def up_rows(which):
        return pl.ds(pl.multiple_of(which * part, 128), part)

    def up_keep(at, i):
        return pltpu.make_async_copy(gu.at[at, i, up_rows(y)], ku.at[block_order(at), i], sem_u.at[at, i])

    def up_send(at, i):
        src, dst = gu.at[at, i, up_rows(1 - y)], ru.at[block_order(at), i]
        return remote(src, dst, send_u.at[at, i], recv_u.at[at, i], to_y)

    def up_rest(at, i):
        return pltpu.make_async_copy(gu.at[at, i, up_rows(1 - y)], rest_u.at[i], rest_sem.at[i])

    def up_ready(at, i):
        up_keep(at, i).start()

        @pl.when(at < steps - 1)
        def _():
            up_send(at, i).start()

        @pl.when(at == steps - 1)
        def _():
            up_rest(at, i).start()

    @pl.when(step == 0)
    def _():
        greet([sibling, to_x, to_y])
        out[...] = res[...]
        dh[...] = jnp.zeros_like(dh)

    def tile(wu, wd, dbu, which):
        lanes = pl.ds(pl.multiple_of(which * wu.shape[1], 128), wu.shape[1])
        up = dot(h2[...], wu[...]) + vecs[pl.ds(R_BU + block_order(step), 1), lanes]
        d_act = dot(cot[...], wd[...], 1, 1)
        act, slope = gelu_and_slope(up)
        act = act.astype(bf16)
        d_up32 = d_act * slope
        d_up = d_up32.astype(bf16)
        dbu[0] = jnp.sum(d_up32, 0, keepdims=True)
        d_wd = dot(cot[...], act, 0, 0).astype(bf16)
        d_wu = dot(h2p[...], d_up, 0, 0).astype(bf16)
        out[...] += dot(act, wd[...])
        dh[...] += dot(d_up, wu[...], 1, 1)
        return d_wd, d_wu

    @pl.when(step >= 2)
    def _():
        for copy in copies(slot):
            copy.wait_send()

    @pl.when(step < steps)
    def _():
        d_wd, d_wu = tile(wu_a, wd_a, dbu_a, 1 - c)
        send_wd[slot] = d_wd
        send_wua[slot] = d_wu[half:]
        keep_a[slot] = d_wu[:half]

    @pl.when(step > 0)
    def _():
        copies(before, (2,))[0].wait_recv()
        gu[step - 1, 0] = keep_a[before] + got_wub[before]
        up_ready(step - 1, 0)

    @pl.when(step < steps)
    def _():
        for copy in copies(slot, (0, 1)):
            copy.start()
        d_wd, d_wu = tile(wu_b, wd_b, dbu_b, c)
        send_wub[slot] = d_wu[half:]
        copies(slot, (2,))[0].start()
        for copy in copies(slot, (0, 1)):
            copy.wait_recv()
        gd[step] = (d_wd + got_wd[slot]).reshape(gd.shape[1:])
        gu[step, 1] = d_wu[:half] + got_wua[slot]
        up_ready(step, 1)

    for at in range(4):

        @pl.when(step == at)
        def _():
            for copy in down_copy(at):
                copy.start()

    @pl.when(step == steps)
    def _():
        out_low[...] = (out[...] + vecs[R_BD : R_BD + 1, :]).astype(bf16)
        for copy in copies(before):
            copy.wait_send()
        for at in range(4):
            for copy in down_copy(at):
                copy.wait()
            for i in range(2):
                up_keep(at, i).wait()
                (up_send(at, i) if at < 3 else up_rest(at, i)).wait()


def mlp(vecs, h2, h2p, cot, res, w_up, w_down):
    rows, width = h2.shape
    ff = w_up.shape[1]
    tile = ff // 8
    half = width // 2
    steps = 4
    now = lambda i: block_order(jnp.minimum(i, steps - 1))
    at_a = lambda i: 2 * now(i) + 1 - lax.rem(lax.axis_index("items"), 2)
    at_b = lambda i: 2 * now(i) + lax.rem(lax.axis_index("items"), 2)
    w_specs = []
    for at in (at_a, at_b):
        w_specs += [
            pl.BlockSpec((width, tile), lambda i, at=at: (0, at(i))),
            pl.BlockSpec((tile, width), lambda i, at=at: (at(i), 0)),
        ]
    bias = pl.BlockSpec((1, 1, tile), lambda i: (now(i), 0, 0))
    low = lambda *shape: jax.ShapeDtypeStruct(shape, bf16)
    return pl.pallas_call(
        mlp_kernel,
        name="mlp",
        grid=(steps + 1,),
        in_specs=[VMEM] * 5 + w_specs,
        out_specs=[VMEM, VMEM] + [HBM] * 6 + [bias, bias],
        out_shape=[
            low(rows, width),
            jax.ShapeDtypeStruct((rows, width), f32),
            low(2, 4, width // 4, tile),
            low(2, 4, width // 4, tile),
            low(4, width // 8, tile),
            low(4, 2, half // 2, tile),
            low(4, 2, half // 2, tile),
            low(2, half // 2, tile),
        ]
        + [jax.ShapeDtypeStruct((steps, 1, tile), f32)] * 2,
        scratch_shapes=(
            [pltpu.VMEM((2, width, tile), bf16)] + [pltpu.VMEM((2, half, tile), bf16)] * 2
        )
        * 2
        + [
            pltpu.VMEM((2, half, tile), bf16),
            pltpu.VMEM((rows, width), f32),
            pltpu.VMEM((steps, 4, width // 4, tile), bf16),
            pltpu.VMEM((steps, 2, half, tile), bf16),
            DMA((3, 2)),
            DMA((3, 2)),
            DMA((2,)),
            DMA((2,)),
            DMA((3, 2)),
            DMA((3, 2)),
            DMA((2,)),
            DMA((4, 2)),
            DMA((3,)),
        ],
        compiler_params=params(collective_id=4, has_side_effects=True),
        cost_estimate=pl.CostEstimate(
            flops=2 * 6 * rows * width * ff, bytes_accessed=40 * 2**20, transcendentals=0
        ),
    )(vecs, h2, h2p, cot, res, w_up, w_down, w_up, w_down)


def norm_back(z, scale, dz):
    return scale * (dz - jnp.mean(dz, -1, keepdims=True) - z * jnp.mean(dz * z, -1, keepdims=True))


def tail_kernel(n_items, n_band, qt, *refs):
    (table, counts, stat, vecs, dbu_a, dbu_b, log_total) = refs[:7]
    (res_h, dh_h, cot_h, out_rows, attn_h, attn_sib_h, wo_h, q_h, k_h, v_h, h1_h) = refs[7:18]
    (wq_h, wk_h, wv_h, tok_h, kd_h, rd_h, rest_d, ku_h, ru_h, rest_u, tokens) = refs[18:29]
    (out_home, d_tok, total, o_down, o_up, o_wo, o_wq, o_wk, o_wv) = refs[29:38]
    (res, dh, cot, low, wo, attn, attn_sib, kd, rd1, rdr, rd2, rd3, rd4) = refs[38:51]
    (ku, ru1, rur, ru2, ru3, ru4, q, k, v, da, da_send, dk_acc, dv_acc) = refs[51:64]
    (h1, wq, wk, wv, tok, gw, gw_core, gw1, gw2, gw3, gw4) = refs[64:75]
    (d_pair, gp, gp_core, gp1, gp2, gp3, gp4, home) = refs[75:83]
    (small, buf_i, part, buf_b, buf_i2, part2, buf_b2) = refs[83:90]
    (send, recv, lsem, send_r, recv_r, send_g, recv_g, send_i, recv_i, send_b, recv_b) = refs[90:101]

    it, bd, c, yx = place()
    x, y = lax.rem(yx, 2), yx // 2
    bl, bh = lax.rem(bd, 2), bd // 2
    sibling = (it + 1 - 2 * c, bd)
    to_x, to_y = (it + 2 - 4 * x, bd), (it + 4 - 8 * y, bd)
    to_z1, to_z2 = (it, bd + 1 - 2 * bl), (it, lax.rem(bd + 2, 4))
    rows, width = res.shape
    half = width // 2
    fourth = width // 4
    eighth = width // 8
    tile = kd.shape[-1]
    sent = []
    loads = []

    def load(src, dst):
        copy = pltpu.make_async_copy(src, dst, lsem.at[len(loads)])
        copy.start()
        loads.append(copy)
        return copy

    def push(src, dst, to, start=True):
        i = len(sent)
        copy = remote(src, dst, send.at[i], recv.at[i], to)
        if start:
            copy.start()
        sent.append(copy)
        return copy

    def some(which, size):
        return pl.ds(pl.multiple_of(which * size, 128), size)

    greet(all_peers(n_items))
    d1 = push(rest_d, rdr, to_x)
    u1 = push(rest_u, rur, to_y)
    load(out_rows, tok).wait()
    out_blocks = tok.reshape(4, rows // 4, width)
    rows_back(out_blocks, out_home, send_r, recv_r)

    get_res, get_dh, get_cot = load(res_h, res), load(dh_h, dh), load(cot_h, cot)
    get_wo, get_attn, get_sib = load(wo_h, wo), load(attn_h, attn), load(attn_sib_h, attn_sib)
    get_down = [load(kd_h, kd), load(rd_h, rd1)]
    get_up = [load(ku_h, ku), load(ru_h, ru1)]
    get_qkv = [load(src, dst) for src, dst in ((q_h, q), (k_h, k), (v_h, v))]
    get_h1 = load(h1_h, h1)
    lanes = some(c, half)
    get_w = [load(src.at[:, lanes], dst) for src, dst in ((wq_h, wq), (wk_h, wk), (wv_h, wv))]

    small[...] = jnp.zeros_like(small)
    for i in range(4):
        for src, h in ((dbu_a, 1 - c), (dbu_b, c)):
            small[4 + i : 5 + i, some(h, half)] = src[i]
    for copy in (get_res, get_dh, get_cot, get_wo):
        copy.wait()
    block = 256

    def second_norm(i):
        at = some(i, block)
        z, scale = normalize(res[at, :])
        d_h = dh[at, :]
        c32 = cot[at, :].astype(f32)
        full = c32 + norm_back(z, scale, d_h * vecs[R_G2 : R_G2 + 1, :])
        res[at, :] = full
        d_low = full.astype(bf16)
        low[at, :] = d_low
        for j, term in enumerate((d_h * z, d_h, d_low.astype(f32), c32)):
            small[j : j + 1, :] += jnp.sum(term, 0, keepdims=True)
        da[at, :] = dot(d_low, half_rows(wo, c, half), 1, 1).astype(bf16)
        da_send[at, :] = dot(d_low, half_rows(wo, 1 - c, half), 1, 1).astype(bf16)

    theirs, mine = some(1 - x, tile // 4), some(x, tile // 4)
    cuts = [some(0, eighth), some(1, eighth)]
    down, up = kd.reshape(2, 2, 2, fourth, tile), ku.reshape(2, 2, 2, tile // 2, tile)

    def down_second(i):
        return push(kd.at[1 - y, :, cuts[i]], rd2.at[:, cuts[i]], to_y)

    def up_second(s, i):
        b = block_order(s)
        ku[b, i] += ru1[b, i] if s < 3 else rur[i]
        return push(ku.at[b, i, theirs], ru2.at[b, i], to_x)

    def down_third(i):
        d2[i].wait_recv()
        kd[y, :, cuts[i]] += rd2[:, cuts[i]]
        return push(down.at[y, :, 1 - bl, cuts[i]], rd3.at[:, cuts[i]], to_z1)

    def up_third(i):
        for copy in u2[i]:
            copy.wait_recv()
        ku[:, i, mine] += ru2[:, i]
        return push(up.at[:, 1 - bl, i, mine], ru3.at[:, i], to_z1)

    def down_fourth(i):
        d3[i].wait_recv()
        for high in range(2):
            down[y, high, bl, cuts[i]] += rd3[high, cuts[i]]
        return push(down.at[y, 1 - bh, bl, cuts[i]], rd4.at[cuts[i]], to_z2)

    def up_fourth(i):
        u3[i].wait_recv()
        for high in range(2):
            up[high, bl, i, mine] += ru3[high, i]
        return push(up.at[1 - bh, bl, i, mine], ru4.at[i], to_z2)

    second_norm(0)
    for copy in get_down + get_up:
        copy.wait()
    for yy in range(2):
        kd[yy, :, cuts[0]] += rd1[yy, :, cuts[0]]
    d2 = [down_second(0)]
    u2 = [[up_second(s, 0) for s in range(3)], []]
    second_norm(1)

    da_copy = push(da_send, da.at[pl.ds(rows, rows)], sibling)
    early = share_start(
        n_items, it, lambda p: (p, bd), small.at[pl.ds(0, 8)], buf_i, send_i.at[0], recv_i.at[0]
    )

    get_attn.wait()
    get_sib.wait()
    for i, heads in enumerate((attn, attn_sib)):
        for xx in range(2):
            part_wo = dot(heads[:, xx * fourth : (xx + 1) * fourth], low[...], 0, 0).astype(bf16)
            for cc in range(2):
                gw[i, xx, cc] = part_wo[cc * eighth : (cc + 1) * eighth]
    core_w = [push(gw.at[i, :, 1 - c], gw_core.at[1 - i], sibling) for i in range(2)]

    d1.wait_recv()
    kd[0, :, cuts[1]] += rd1[0, :, cuts[1]]
    kd[1, :, cuts[1]] += rdr[...]
    u1.wait_recv()
    u2[0].append(up_second(3, 0))

    for copy in get_qkv:
        copy.wait()
    get_h1.wait()
    da_copy.wait_recv()
    lane_k = lax.broadcasted_iota(jnp.int32, (2 * rows, 128), 1)
    lane_q = lax.broadcasted_iota(jnp.int32, (qt, 128), 1)

    def pair(i):
        at_lanes = some(i, 128)
        k_pair, v_pair = k[:, at_lanes], v[:, at_lanes]
        bias = key_bias(table, counts, k_pair.shape)
        keys = [with_spare(k_pair, bias, hd, lane_k) for hd in range(2)]
        keys_only = [head_lanes(k_pair, hd, lane_k) for hd in range(2)]
        values = [head_lanes(v_pair, hd, lane_k) for hd in range(2)]
        for t in range(2 * rows // qt):
            at = slice(t * qt, (t + 1) * qt)
            q_tile, d_tile = q[at, at_lanes], da[at, at_lanes]
            dq_both = None
            for hd in range(2):
                q_head = head_lanes(q_tile, hd, lane_q)
                d_head = head_lanes(d_tile, hd, lane_q)
                s = dot(keys[hd], ones_beside(q_tile, hd, lane_q), 1, 1)
                p = jnp.exp(s - log_total[i, hd : hd + 1, at])
                d_p = dot(values[hd], d_tile, 1, 1)
                weighted = p * d_p
                delta = jnp.sum(weighted, 0, keepdims=True)
                ds = (weighted - p * delta).astype(bf16)
                dv_part = dot(p.astype(bf16), d_head)
                dk_part = dot(ds, q_head)
                if t == 0 and hd == 0:
                    dv_acc[...] = dv_part
                    dk_acc[...] = dk_part
                else:
                    dv_acc[...] += dv_part
                    dk_acc[...] += dk_part
                term = dot(keys_only[hd], ds, 0, 0)
                dq_both = term if dq_both is None else dq_both + term
            dq = dq_both.T * score_scale
            q[at, at_lanes] = dq.astype(bf16)
            d_pair[at, 0:128] = dq.astype(bf16)
        k[:, at_lanes] = dk_acc[...].astype(bf16)
        v[:, at_lanes] = dv_acc[...].astype(bf16)
        d_pair[:, 128:256] = dk_acc[...].astype(bf16)
        d_pair[:, 256:384] = dv_acc[...].astype(bf16)
        for j in range(4):
            term = dot(h1[:, j * fourth : (j + 1) * fourth], d_pair[...], 0, 0).astype(bf16)
            for cc in range(2):
                gp[i, j, cc] = term[cc * eighth : (cc + 1) * eighth]

    def pair_core(i):
        return push(gp.at[i, :, 1 - c], gp_core.at[i], sibling)

    def chips(i, first, second):
        return 2 * second + first if i % 2 == 0 else 2 * first + second

    def first_of(i):
        return (x, y) if i % 2 == 0 else (y, x)

    def pair_first(i, core):
        core.wait_recv()
        mine_first, _ = first_of(i)
        to = to_x if i % 2 == 0 else to_y
        got = []
        for j in range(2):
            there = chips(i, 1 - mine_first, j)
            got.append(push(gp.at[i, there, c], gp1.at[i, j, 0], to))
            got.append(push(gp_core.at[i, there], gp1.at[i, j, 1], to))
        return got

    def pair_second(i, got):
        for copy in got:
            copy.wait_recv()
        mine_first, mine_second = first_of(i)
        for j in range(2):
            here = chips(i, mine_first, j)
            gp[i, here, c] += gp1[i, j, 0]
            gp_core[i, here] += gp1[i, j, 1]
        there = chips(i, mine_first, 1 - mine_second)
        to = to_y if i % 2 == 0 else to_x
        return [
            push(gp.at[i, there, c], gp2.at[i, 0], to),
            push(gp_core.at[i, there], gp2.at[i, 1], to),
        ]

    def pair_third(i, got):
        for copy in got:
            copy.wait_recv()
        gp[i, yx, c] += gp2[i, 0]
        gp_core[i, yx] += gp2[i, 1]

    pair(0)
    core_p = [pair_core(0)]
    part[...] = share_end(n_items, early, buf_i)
    early = share_start(n_band, bd, lambda p: (it, p), part, buf_b, send_b.at[0], recv_b.at[0])
    for i in range(2):
        core_w[i].wait_recv()
    for i in range(2):
        gw[i, :, c] += gw_core[i]
    rel_y = lax.rem(y + c, 2)
    d3 = [down_third(0)]
    d2.append(down_second(1))
    u3 = [up_third(0)]
    u2[1] = [up_second(s, 1) for s in range(4)]

    pair(1)
    core_p.append(pair_core(1))
    p1 = [pair_first(0, core_p[0])]
    w1 = push(gw.at[1 - rel_y, :, c], gw1, to_y)
    total[0:8, :] = share_end(n_band, early, buf_b)

    pair(2)
    core_p.append(pair_core(2))
    d4 = [down_fourth(0)]
    u4 = [up_fourth(0)]
    d3.append(down_third(1))
    u3.append(up_third(1))
    p1.append(pair_first(1, core_p[1]))

    pair(3)
    core_p.append(pair_core(3))
    p1.append(pair_first(2, core_p[2]))
    for i, d in ((0, q), (1, v)):
        row = jnp.sum(d[...].astype(f32), 0, keepdims=True)
        small[12 + i : 13 + i, some(c, half)] = row
    w1.wait_recv()
    gw[rel_y, :, c] += gw1[...]
    w2 = push(gw.at[rel_y, 1 - x, c], gw2, to_x)

    for copy in get_w:
        copy.wait()
    dh1, dh1_sib = wo, low

    def first_norm_terms(i):
        at = some(i, block)
        term = dot(q[at, :], wq[...], 1, 1) + dot(k[at, :], wk[...], 1, 1)
        dh1[at, :] = (term + dot(v[at, :], wv[...], 1, 1)).astype(bf16)

    @pl.loop(rows // block, 2 * rows // block)
    def _(i):
        first_norm_terms(i)

    dh_copy = push(dh1.at[pl.ds(rows, rows)], dh1_sib, sibling)
    p1.append(pair_first(3, core_p[3]))
    for i in range(4):
        rows_back_got(out_blocks, out_home, send_r, recv_r, i)
    rows_back_sent(out_blocks, out_home, send_r, recv_r)
    get_tok = load(tok_h, tok)
    d4.append(down_fourth(1))
    u4.append(up_fourth(1))
    p2 = [pair_second(0, p1[0]), pair_second(1, p1[1])]

    g_rows = cot
    g_blocks = g_rows.reshape(4, rows // 4, width)

    def first_norm(i):
        first_norm_terms(i)
        at = some(i, block)
        inv = stat[S_INV : S_INV + 1, :]
        centred = tok[at, :].astype(f32) - stat[S_MEAN : S_MEAN + 1, :]
        z, scale = normalize(centred * inv)
        d_h = dh1[at, :].astype(f32) + dh1_sib[at, :].astype(f32)
        d_start = res[at, :] + norm_back(z, scale, d_h * vecs[R_G1 : R_G1 + 1, :])
        g_rows[at, :] = (d_start * inv).astype(bf16)
        for j, term in enumerate((d_start, d_start * centred, d_h * z, d_h)):
            small[8 + j : 9 + j, :] += jnp.sum(term, 0, keepdims=True)

    get_tok.wait()
    dh_copy.wait_recv()
    first_norm(0)
    rows_back(g_blocks, home, send_g, recv_g, (0, 1))
    first_norm(1)
    rows_back(g_blocks, home, send_g, recv_g, (2, 3))
    late = share_start(
        n_items, it, lambda p: (p, bd), small.at[pl.ds(8, 8)], buf_i2, send_i.at[1], recv_i.at[1]
    )
    p2.append(pair_second(2, p1[2]))
    part2[...] = share_end(n_items, late, buf_i2)
    late = share_start(n_band, bd, lambda p: (it, p), part2, buf_b2, send_b.at[1], recv_b.at[1])

    pair_third(0, p2[0])
    pair_third(1, p2[1])
    p3 = []
    for i in range(2):
        there = 2 * (1 - bl) + i
        p3.append(push(gp.at[there, yx, c], gp3.at[i, 0], to_z1, False))
        p3.append(push(gp_core.at[there, yx], gp3.at[i, 1], to_z1, False))

    @pl.when(bl == 1)
    def _():
        for copy in p3:
            copy.start()

    p2.append(pair_second(3, p1[3]))
    w2.wait_recv()
    gw[rel_y, x, c] += gw2[...]

    def z_lanes(which):
        return some(which, fourth)

    w3 = [
        push(gw.at[rel_y, x, c, :, z_lanes(2 * high + 1 - bl)], gw3.at[high], to_z1) for high in range(2)
    ]
    pair_third(2, p2[2])
    pair_third(3, p2[3])

    @pl.when(bl == 0)
    def _():
        for copy in p3:
            copy.start()

    sums = share_end(n_band, late, buf_b2)
    total[8:16, :] = sums
    for high in range(2):
        w3[high].wait_recv()
    for high in range(2):
        gw3[high] = gw[rel_y, x, c, :, z_lanes(2 * high + bl)] + gw3[high]
    w4 = push(gw3.at[1 - bh], gw4, to_z2)
    for copy in p3:
        copy.wait_recv()
    for i in range(2):
        here = 2 * bl + i
        gp3[i, 0] = gp[here, yx, c] + gp3[i, 0]
        gp3[i, 1] = gp_core[here, yx] + gp3[i, 1]
    rel_b = lax.rem(bh + c, 2)
    p4 = push(gp3.at[:, 1 - rel_b], gp4, to_z2)

    count = patch_total(counts, (1, width))
    inv = stat[S_INV : S_INV + 1, :]
    fix = -0.5 * inv * sums[0:1, :] / count
    slope = -0.5 * inv * inv * inv * sums[1:2, :] / count
    cut = rows // 4
    position = lax.broadcasted_iota(jnp.int32, (cut, width), 0) + bd * (2 * cut)
    for i in range(4):
        s, h = i // 2, i % 2
        rows_back_got(g_blocks, home, send_g, recv_g, i)
        now = pl.ds(h * cut, cut)
        valid = position + h * cut < counts[table[it * 2 + s]]
        term = fix + slope * (tokens[s, now, :].astype(f32) - stat[S_BATCH : S_BATCH + 1, :])
        d_tok[s, now, :] = (home[s, now, :].astype(f32) + jnp.where(valid, term, 0.0)).astype(bf16)

    for copy in d4 + u4:
        copy.wait_recv()
    o_down[...] = (down[y, bh, bl].astype(f32) + rd4[...].astype(f32)).T
    up_sum = up[bh, bl, :, mine].astype(f32) + ru4[...].astype(f32)
    for i, h in ((0, 1 - c), (1, c)):
        o_up[:, some(h, tile)] = up_sum[i]
    w4.wait_recv()
    o_wo[...] = gw3[bh].astype(f32) + gw4[...].astype(f32)
    p4.wait_recv()
    for i in range(2):
        all_three = gp3[i, rel_b].astype(f32) + gp4[i].astype(f32)
        for j, ref in enumerate((o_wq, o_wk, o_wv)):
            ref[:, i * 128 : (i + 1) * 128] = all_three[:, j * 128 : (j + 1) * 128]

    rows_back_sent(g_blocks, home, send_g, recv_g)
    for copy in sent:
        copy.wait_send()


def tail(table, counts, stat, vecs, dbu_a, dbu_b, log_total, res, dh, cot, out_rows, *rest, qt=512):
    attn, attn_sib, wo, q, k, v, h1, wq, wk, wv, tok, kd, rd, rest_d, ku, ru, rest_u, tokens = rest
    n_items, n_band = lax.axis_size("items"), lax.axis_size("band")
    rows, width = res.shape
    half, fourth, cut = width // 2, width // 4, rows // 4
    tile = kd.shape[3]
    buf = lambda *shape: pltpu.VMEM(shape, bf16)
    buf32 = lambda *shape: pltpu.VMEM(shape, f32)
    out = lambda *shape: jax.ShapeDtypeStruct(shape, f32)
    e, s = fourth // 2, fourth
    return pl.pallas_call(
        functools.partial(tail_kernel, n_items, n_band, qt),
        name="tail",
        in_specs=[SMEM, SMEM] + [VMEM] * 5 + [HBM] * 21 + [VMEM],
        out_specs=[HBM] + [VMEM] * 8,
        out_shape=[
            jax.ShapeDtypeStruct(tokens.shape, bf16),
            jax.ShapeDtypeStruct(tokens.shape, bf16),
            out(16, width),
            out(tile, s),
            out(e, 2 * tile),
            out(e, s),
            out(e, s),
            out(e, s),
            out(e, s),
        ],
        scratch_shapes=[
            buf32(rows, width), buf32(rows, width), buf(rows, width), buf(rows, width),
            buf(width, width), buf(rows, half), buf(rows, half),
            buf(2, 4, s, tile), buf(2, 4, s, tile), buf(4, e, tile), buf(4, s, tile), buf(2, s, tile),
            buf(s, tile),
            buf(4, 2, tile // 2, tile), buf(4, 2, tile // 2, tile), buf(2, tile // 2, tile),
            buf(4, 2, tile // 4, tile), buf(2, 2, tile // 4, tile), buf(2, tile // 4, tile),
            buf(2 * rows, half), buf(2 * rows, half), buf(2 * rows, half),
            buf(2 * rows, half), buf(rows, half), buf32(2 * rows, 128), buf32(2 * rows, 128),
            buf(2 * rows, width), buf(width, half), buf(width, half), buf(width, half), buf(rows, width),
            buf(2, 2, 2, e, width), buf(2, 2, e, width), buf(2, e, width), buf(e, width),
            buf(2, e, s), buf(e, s),
            buf(2 * rows, 384), buf(4, 4, 2, e, 384), buf(4, 4, e, 384), buf(4, 2, 2, e, 384),
            buf(4, 2, e, 384), buf(2, 2, e, 384), buf(2, e, 384),
            buf(2, 2 * cut, width),
            buf32(16, width), buf32(n_items, 8, width), buf32(8, width), buf32(n_band, 8, width),
            buf32(n_items, 8, width), buf32(8, width), buf32(n_band, 8, width),
            DMA((80,)), DMA((80,)), DMA((24,)),
            DMA((4,)), DMA((4,)), DMA((4,)), DMA((4,)),
            DMA((2, n_items)), DMA((2, n_items)), DMA((2, n_band)), DMA((2, n_band)),
        ],
        compiler_params=params(collective_id=5, has_side_effects=True),
        cost_estimate=pl.CostEstimate(
            flops=60 * rows * width * width, bytes_accessed=40 * 2**20, transcendentals=0
        ),
    )(
        table, counts, stat, vecs, dbu_a, dbu_b, log_total, res, dh, cot,
        out_rows, attn, attn_sib, wo, q, k, v, h1, wq, wk, wv, tok,
        kd, rd, rest_d, ku, ru, rest_u, tokens,
    )


def emit_kernel(stat, small, *refs):
    n = (len(refs) - 11) // 2
    sources, singles, targets = refs[:n], refs[n : n + 11], refs[n + 11 :]
    for source, target in zip(sources, targets):
        target[...] = source[...]
    singles[0][...] = stat[S_MEAN, :]
    singles[1][...] = stat[S_VAR, :]
    for ref, row in zip(singles[2:10], (10, 11, 12, 13, 2, 0, 1, 3)):
        ref[...] = small[row, :]
    singles[10][...] = small[4:8, :].reshape(4 * small.shape[1])


def quarter(array):
    lead = array.shape[:-2]
    block = lead + (array.shape[-2] // 4, array.shape[-1])
    return pl.BlockSpec(block, lambda i: (0,) * len(lead) + (i, 0))


def emit(stat, small, arrays):
    width = stat.shape[1]
    return pl.pallas_call(
        emit_kernel,
        name="emit",
        grid=(4,),
        in_specs=[VMEM] * 2 + [quarter(a) for a in arrays],
        out_specs=[VMEM] * 11 + [quarter(a) for a in arrays],
        out_shape=[jax.ShapeDtypeStruct((width,), f32)] * 10
        + [jax.ShapeDtypeStruct((4 * width,), f32)]
        + [jax.ShapeDtypeStruct(a.shape, a.dtype) for a in arrays],
        compiler_params=params(),
    )(stat, small, *arrays)


def column_layer(
    tokens, cotangent, running_mean, running_var, slot_table, patch_counts,
    ln1_gain, ln1_bias, w_query, b_query, w_key, w_value, b_value, w_out, b_out,
    ln2_gain, ln2_bias, w_up, b_up, w_down, b_down,
):
    slots, band_rows, width = tokens.shape
    rows = slots * band_rows
    singles = (running_mean, running_var, ln1_gain, ln1_bias, b_query, b_value, b_out)
    singles += (ln2_gain, ln2_bias, b_down)
    vecs, stat, tok, cot_rows, h1, q, k, v, log_total, attn, attn_sib, res, h2, h2p = front(
        slot_table, patch_counts, singles, b_up, tokens, cotangent, w_query, w_key, w_value, w_out
    )
    tok, cot_rows = tok.reshape(rows, width), cot_rows.reshape(rows, width)
    out_rows, d_h2, kd, rd, rest_d, ku, ru, rest_u, dbu_a, dbu_b = mlp(
        vecs, h2, h2p, cot_rows, res, w_up, w_down
    )
    output, d_tokens, small, d_w_down, d_w_up, d_w_out, d_wq, d_wk, d_wv = tail(
        slot_table, patch_counts, stat, vecs, dbu_a, dbu_b, log_total, res, d_h2, cot_rows,
        out_rows, attn, attn_sib, w_out, q, k, v, h1, w_query, w_key, w_value, tok,
        kd, rd, rest_d, ku, ru, rest_u, tokens,
    )
    singles = emit(
        stat, small, (output, d_tokens, d_wq, d_wk, d_wv, d_w_out, d_w_up, d_w_down)
    )
    (new_mean, new_var, d_g1, d_s1, d_bq, d_bv, d_bo, d_g2, d_s2, d_bd, d_bu) = singles[:11]
    output, d_tokens, d_wq, d_wk, d_wv, d_w_out, d_w_up, d_w_down = singles[11:]
    return (
        output, d_tokens, new_mean, new_var, d_g1, d_s1, d_wq, d_bq, d_wk, d_wv, d_bv,
        d_w_out, d_bo, d_g2, d_s2, d_w_up, d_bu, d_w_down, d_bd,
    )


def layer_norm(value, gain, shift):
    centre = value - jnp.mean(value, -1, keepdims=True)
    spread = jnp.mean(centre * centre, -1, keepdims=True)
    return centre * lax.rsqrt(spread + epsilon) * gain + shift


def gelu_tanh(value):
    return (
        0.5
        * value
        * (1.0 + jnp.tanh(0.7978845608028654 * (value + 0.044715 * value * value * value)))
    )


def head_layout():
    heads_per = 4
    return (heads_per, HEADS // heads_per, heads_per * HEAD_DIM)


def group_scores(q_part, k_part, key_mask):
    scores = (
        jnp.einsum("rhd,khd->hrk", q_part, k_part, preferred_element_type=jnp.float32) * score_scale
    )
    return jnp.where(key_mask[None, None, :], scores, masked_score)


def attend_forward(q_slot, keys_slot, values_slot, key_mask):
    heads_per, groups, group_width = head_layout()
    band_rows = q_slot.shape[0]
    seq_length = keys_slot.shape[0]

    def head_block(group_index):
        begin = group_index * group_width
        q_part = lax.dynamic_slice_in_dim(q_slot, begin, group_width, 1).reshape(
            band_rows, heads_per, HEAD_DIM
        )
        k_part = lax.dynamic_slice_in_dim(keys_slot, begin, group_width, 1).reshape(
            seq_length, heads_per, HEAD_DIM
        )
        v_part = lax.dynamic_slice_in_dim(values_slot, begin, group_width, 1).reshape(
            seq_length, heads_per, HEAD_DIM
        )
        scores = group_scores(q_part, k_part, key_mask)
        top_score = jnp.max(scores, -1, keepdims=True)
        log_total = top_score + jnp.log(jnp.sum(jnp.exp(scores - top_score), -1, keepdims=True))
        probs_low = jnp.exp(scores - log_total).astype(jnp.bfloat16)
        attended = jnp.einsum("hrk,khd->rhd", probs_low, v_part, preferred_element_type=jnp.float32)
        return (attended.reshape(band_rows, group_width), log_total[..., 0])

    attended, log_totals = lax.map(head_block, jnp.arange(groups, dtype=jnp.int32))
    return (attended.transpose(1, 0, 2).reshape(band_rows, groups * group_width), log_totals)


def attend_backward(q_slot, keys_slot, values_slot, key_mask, d_attn_slot, row_delta, log_totals):
    heads_per, groups, group_width = head_layout()
    query_rows = q_slot.shape[0]
    seq_length = keys_slot.shape[0]
    deltas = jnp.transpose(row_delta).reshape(groups, heads_per, query_rows)

    def head_block(inputs):
        group_index, log_total, delta_part = inputs
        begin = group_index * group_width
        q_part = lax.dynamic_slice_in_dim(q_slot, begin, group_width, 1).reshape(
            query_rows, heads_per, HEAD_DIM
        )
        k_part = lax.dynamic_slice_in_dim(keys_slot, begin, group_width, 1).reshape(
            seq_length, heads_per, HEAD_DIM
        )
        v_part = lax.dynamic_slice_in_dim(values_slot, begin, group_width, 1).reshape(
            seq_length, heads_per, HEAD_DIM
        )
        d_part = lax.dynamic_slice_in_dim(d_attn_slot, begin, group_width, 1).reshape(
            query_rows, heads_per, HEAD_DIM
        )
        scores = group_scores(q_part, k_part, key_mask)
        probs = jnp.exp(scores - log_total[..., None])
        d_probs = jnp.einsum("rhd,khd->hrk", d_part, v_part, preferred_element_type=jnp.float32)
        d_scores = (probs * (d_probs - delta_part[..., None])).astype(jnp.bfloat16)
        results = []
        d_q_part = (
            jnp.einsum("hrk,khd->rhd", d_scores, k_part, preferred_element_type=jnp.float32)
            * score_scale
        )
        results.append(d_q_part.reshape(query_rows, group_width))
        probs_low = probs.astype(jnp.bfloat16)
        d_k_part = (
            jnp.einsum("hrk,rhd->khd", d_scores, q_part, preferred_element_type=jnp.float32)
            * score_scale
        )
        d_v_part = jnp.einsum("hrk,rhd->khd", probs_low, d_part, preferred_element_type=jnp.float32)
        results.append(d_k_part.reshape(seq_length, group_width))
        results.append(d_v_part.reshape(seq_length, group_width))
        return tuple(results)

    mapped = lax.map(head_block, (jnp.arange(groups, dtype=jnp.int32), log_totals, deltas))
    full_width = groups * group_width
    return tuple((piece.transpose(1, 0, 2).reshape(piece.shape[1], full_width) for piece in mapped))


def local(
    tokens,
    cotangent,
    running_mean,
    running_var,
    slot_table,
    patch_counts,
    ln1_gain,
    ln1_bias,
    w_query,
    b_query,
    w_key,
    w_value,
    b_value,
    w_out,
    b_out,
    ln2_gain,
    ln2_bias,
    w_up,
    b_up,
    w_down,
    b_down,
):
    slot_count, band_rows, model_width = tokens.shape
    seq_length = band_rows * lax.axis_size("band")
    item_rank = lax.axis_index("items")
    band_rank = lax.axis_index("band")
    every_slot = jnp.arange(slot_table.shape[0], dtype=jnp.int32)
    my_slots = item_rank * slot_count + jnp.arange(slot_count, dtype=jnp.int32)
    item_ids = jnp.sum(
        jnp.where(every_slot[None, :] == my_slots[:, None], slot_table[None, :], 0), 1
    )
    lengths = jnp.sum(
        jnp.where(every_slot[None, :] == item_ids[:, None], patch_counts[None, :], 0), 1
    )
    key_mask = jnp.arange(seq_length, dtype=jnp.int32)[None, :] < lengths[:, None]
    row_mask = (band_rank * band_rows + jnp.arange(band_rows, dtype=jnp.int32))[None, :] < lengths[
        :, None
    ]
    row_keep = row_mask.astype(jnp.float32).reshape(-1, 1)
    raw_flat = tokens.astype(jnp.float32).reshape(-1, model_width)
    part_one = jnp.sum(row_keep * raw_flat, 0)
    part_two = jnp.sum(row_keep * raw_flat * raw_flat, 0)
    total_one, total_two = lax.psum((part_one, part_two), ("items", "band"))
    patch_total = jnp.sum(patch_counts).astype(jnp.float32)
    batch_mean = total_one / patch_total
    batch_var = total_two / patch_total - batch_mean * batch_mean
    new_mean = momentum * running_mean + momentum * batch_mean
    new_var = momentum * running_var + momentum * batch_var
    inverse = lax.rsqrt(new_var + epsilon)
    normed_in = (raw_flat - new_mean) * inverse
    gain_one = ln1_gain.astype(jnp.float32)
    shift_one = ln1_bias.astype(jnp.float32)
    gain_two = ln2_gain.astype(jnp.float32)
    shift_two = ln2_bias.astype(jnp.float32)
    h_one_full, norm_one_back = jax.vjp(layer_norm, normed_in, gain_one, shift_one)
    h_one = h_one_full.astype(jnp.bfloat16)
    queries = (
        jnp.dot(h_one, w_query, preferred_element_type=jnp.float32) + b_query.astype(jnp.float32)
    ).astype(jnp.bfloat16)
    key_local = (
        jnp.dot(h_one, w_key, preferred_element_type=jnp.float32)
        .astype(jnp.bfloat16)
        .reshape(slot_count, band_rows, model_width)
    )
    value_local = (
        (jnp.dot(h_one, w_value, preferred_element_type=jnp.float32) + b_value.astype(jnp.float32))
        .astype(jnp.bfloat16)
        .reshape(slot_count, band_rows, model_width)
    )
    keys_all, values_all = (
        lax.all_gather(key_local, "band", axis=1, tiled=True),
        lax.all_gather(value_local, "band", axis=1, tiled=True),
    )
    q_slots = queries.reshape(slot_count, band_rows, model_width)
    attended_list = []
    totals_list = []
    for slot_index in range(slot_count):
        attended, log_totals = attend_forward(
            q_slots[slot_index], keys_all[slot_index], values_all[slot_index], key_mask[slot_index]
        )
        attended_list.append(attended)
        totals_list.append(log_totals)
    attn_full = jnp.concatenate(attended_list, 0)
    attn_low = attn_full.astype(jnp.bfloat16)
    residual = (
        normed_in
        + jnp.dot(attn_low, w_out, preferred_element_type=jnp.float32)
        + b_out.astype(jnp.float32)
    )
    h_two_full, norm_two_back = jax.vjp(layer_norm, residual, gain_two, shift_two)
    h_two = h_two_full.astype(jnp.bfloat16)
    up_proj = jnp.dot(h_two, w_up, preferred_element_type=jnp.float32) + b_up.astype(jnp.float32)
    activated_full, gelu_back = jax.vjp(gelu_tanh, up_proj)
    activated = activated_full.astype(jnp.bfloat16)
    result = (
        residual
        + jnp.dot(activated, w_down, preferred_element_type=jnp.float32)
        + b_down.astype(jnp.float32)
    )
    output = result.astype(jnp.bfloat16).reshape(slot_count, band_rows, model_width)
    cot_low = cotangent.reshape(-1, model_width)
    cot_full = cot_low.astype(jnp.float32)
    d_w_down = jnp.einsum("tf,td->fd", activated, cot_low, preferred_element_type=jnp.float32)
    d_b_down = jnp.sum(cot_full, 0)
    d_activated = jnp.einsum("td,fd->tf", cot_low, w_down, preferred_element_type=jnp.float32)
    (d_up_full,) = gelu_back(d_activated)
    d_up = d_up_full.astype(jnp.bfloat16)
    d_w_up = jnp.einsum("td,tf->df", h_two, d_up, preferred_element_type=jnp.float32)
    d_b_up = jnp.sum(d_up, 0, dtype=jnp.float32)
    d_h_two = jnp.einsum("tf,df->td", d_up, w_up, preferred_element_type=jnp.float32)
    d_res_norm, d_gain_two, d_shift_two = norm_two_back(d_h_two)
    d_residual = cot_full + d_res_norm
    d_branch = d_residual.astype(jnp.bfloat16)
    d_w_out = jnp.einsum("td,te->de", attn_low, d_branch, preferred_element_type=jnp.float32)
    d_b_out = jnp.sum(d_branch, 0, dtype=jnp.float32)
    d_attn = jnp.einsum("te,de->td", d_branch, w_out, preferred_element_type=jnp.float32).astype(
        jnp.bfloat16
    )
    row_delta = jnp.sum(
        (d_attn.astype(jnp.float32) * attn_full).reshape(slot_count, band_rows, HEADS, HEAD_DIM), -1
    )
    d_attn_slots = d_attn.reshape(slot_count, band_rows, model_width)
    back_keys, back_values = (keys_all, values_all)
    d_q_list = []
    d_k_list = []
    d_v_list = []
    for slot_index in range(slot_count):
        d_q_slot, d_k_slot, d_v_slot = attend_backward(
            q_slots[slot_index],
            back_keys[slot_index],
            back_values[slot_index],
            key_mask[slot_index],
            d_attn_slots[slot_index],
            row_delta[slot_index],
            totals_list[slot_index],
        )
        d_q_list.append(d_q_slot)
        d_k_list.append(d_k_slot)
        d_v_list.append(d_v_slot)
    d_keys_mine, d_values_mine = (
        lax.psum_scatter(
            jnp.stack(d_k_list).astype(jnp.bfloat16), "band", scatter_dimension=1, tiled=True
        ).astype(jnp.float32),
        lax.psum_scatter(
            jnp.stack(d_v_list).astype(jnp.bfloat16), "band", scatter_dimension=1, tiled=True
        ).astype(jnp.float32),
    )
    d_queries = jnp.concatenate(d_q_list, 0).astype(jnp.bfloat16)
    d_keys = d_keys_mine.reshape(-1, model_width).astype(jnp.bfloat16)
    d_values = d_values_mine.reshape(-1, model_width).astype(jnp.bfloat16)
    d_w_query = jnp.einsum("td,te->de", h_one, d_queries, preferred_element_type=jnp.float32)
    d_b_query = jnp.sum(d_queries, 0, dtype=jnp.float32)
    d_w_key = jnp.einsum("td,te->de", h_one, d_keys, preferred_element_type=jnp.float32)
    d_w_value = jnp.einsum("td,te->de", h_one, d_values, preferred_element_type=jnp.float32)
    d_b_value = jnp.sum(d_values, 0, dtype=jnp.float32)
    d_h_one = jnp.einsum("te,de->td", d_queries, w_query, preferred_element_type=jnp.float32)
    d_h_one = d_h_one + jnp.einsum("te,de->td", d_keys, w_key, preferred_element_type=jnp.float32)
    d_h_one = d_h_one + jnp.einsum(
        "te,de->td", d_values, w_value, preferred_element_type=jnp.float32
    )
    d_start_norm, d_gain_one, d_shift_one = norm_one_back(d_h_one)
    d_start = d_residual + d_start_norm
    centred = raw_flat - new_mean
    small_sums = lax.psum(
        (
            jnp.sum(d_start, 0),
            jnp.sum(d_start * centred, 0),
            d_gain_one,
            d_shift_one,
            d_b_query,
            d_b_value,
            d_b_out,
            d_gain_two,
            d_shift_two,
            d_b_up,
            d_b_down,
        ),
        ("items", "band"),
    )
    sum_g = small_sums[0]
    sum_gx = small_sums[1]
    cube = inverse * inverse * inverse
    d_raw = d_start * inverse + row_keep * (
        -0.5 * inverse * sum_g / patch_total
        - 0.5 * cube * sum_gx * (raw_flat - batch_mean) / patch_total
    )
    d_tokens = d_raw.astype(jnp.bfloat16).reshape(slot_count, band_rows, model_width)
    weight_grads = (
        lax.psum_scatter(
            d_w_query.astype(jnp.bfloat16), "items", scatter_dimension=0, tiled=True
        ).astype(jnp.float32),
        lax.psum_scatter(
            d_w_key.astype(jnp.bfloat16), "items", scatter_dimension=0, tiled=True
        ).astype(jnp.float32),
        lax.psum_scatter(
            d_w_value.astype(jnp.bfloat16), "items", scatter_dimension=0, tiled=True
        ).astype(jnp.float32),
        lax.psum_scatter(
            d_w_out.astype(jnp.bfloat16), "items", scatter_dimension=0, tiled=True
        ).astype(jnp.float32),
        lax.psum_scatter(
            d_w_up.astype(jnp.bfloat16), "items", scatter_dimension=0, tiled=True
        ).astype(jnp.float32),
        lax.psum_scatter(
            d_w_down.astype(jnp.bfloat16), "items", scatter_dimension=0, tiled=True
        ).astype(jnp.float32),
    )
    weight_grads = (
        lax.psum_scatter(
            weight_grads[0].astype(jnp.bfloat16), "band", scatter_dimension=1, tiled=True
        ).astype(jnp.float32),
        lax.psum_scatter(
            weight_grads[1].astype(jnp.bfloat16), "band", scatter_dimension=1, tiled=True
        ).astype(jnp.float32),
        lax.psum_scatter(
            weight_grads[2].astype(jnp.bfloat16), "band", scatter_dimension=1, tiled=True
        ).astype(jnp.float32),
        lax.psum_scatter(
            weight_grads[3].astype(jnp.bfloat16), "band", scatter_dimension=1, tiled=True
        ).astype(jnp.float32),
        lax.psum_scatter(
            weight_grads[4].astype(jnp.bfloat16), "band", scatter_dimension=1, tiled=True
        ).astype(jnp.float32),
        lax.psum_scatter(
            weight_grads[5].astype(jnp.bfloat16), "band", scatter_dimension=1, tiled=True
        ).astype(jnp.float32),
    )
    return (
        output,
        d_tokens,
        new_mean,
        new_var,
        small_sums[2],
        small_sums[3],
        weight_grads[0],
        small_sums[4],
        weight_grads[1],
        weight_grads[2],
        small_sums[5],
        weight_grads[3],
        small_sums[6],
        small_sums[7],
        small_sums[8],
        weight_grads[4],
        small_sums[9],
        weight_grads[5],
        small_sums[10],
    )


def solution(mesh):
    columns = mesh.shape["items"] == 8 and mesh.shape["band"] == 4
    return jax.shard_map(
        column_layer if columns else local,
        mesh=mesh,
        in_specs=(
            P("items", "band", None),
            P("items", "band", None),
            P(),
            P(),
            P(),
            P(),
            P(),
            P(),
            P(),
            P(),
            P(),
            P(),
            P(),
            P(),
            P(),
            P(),
            P(),
            P(),
            P(),
            P(),
            P(),
        ),
        out_specs=(
            P("items", "band", None),
            P("items", "band", None),
            P(),
            P(),
            P(),
            P(),
            P("items", "band"),
            P(),
            P("items", "band"),
            P("items", "band"),
            P(),
            P("items", "band"),
            P(),
            P(),
            P(),
            P("items", "band"),
            P(),
            P("items", "band"),
            P(),
        ),
        check_vma=False,
    )
```
